32 devices in a mesh: dp: 8 (over z, core), tensor: 4 (over y, x).
Axes of the slice: x: 2, y: 2, z: 4, core: 2. Of those that a mesh axis runs over, the one named last changes fastest.
Arguments:
- streams: bfloat16 [8192, 4, 2048], P('dp', None, 'tensor'), may hold values from -6 to 6
- segments: int32 [8192], P('dp'), may hold values from 0 to 3, as said below
- positions: int32 [8192], P('dp'), may hold values from 0 to 511, as said below
- mix_in1: float32 [4], replicated, may hold values from 0.2 to 0.8
- mix_res1: float32 [4, 4], replicated, may hold values from -0.6 to 0.6
- mix_out1: float32 [4], replicated, may hold values from 0.5 to 1.5
- mix_in2: float32 [4], replicated, may hold values from 0.2 to 0.8
- mix_res2: float32 [4, 4], replicated, may hold values from -0.6 to 0.6
- mix_out2: float32 [4], replicated, may hold values from 0.5 to 1.5
- w_query: bfloat16 [2048, 2048], P(None, 'tensor'), may hold values from -0.125 to 0.125
- w_key: bfloat16 [2048, 2048], P(None, 'tensor'), may hold values from -0.125 to 0.125
- w_value: bfloat16 [2048, 2048], P(None, 'tensor'), may hold values from -0.125 to 0.125
- w_output: bfloat16 [2048, 2048], P('tensor'), may hold values from -0.375 to 0.375
- w_gate: bfloat16 [2048, 8192], P(None, 'tensor'), may hold values from -0.125 to 0.125
- w_up: bfloat16 [2048, 8192], P(None, 'tensor'), may hold values from -0.125 to 0.125
- w_down: bfloat16 [8192, 2048], P('tensor'), may hold values from -0.0625 to 0.0625
- cotangent: bfloat16 [8192, 4, 2048], P('dp', None, 'tensor'), may hold values from -6 to 6
Outputs:
- new_streams: bfloat16 [8192, 4, 2048], P('dp', None, 'tensor')
- stream_grad: float32 [8192, 4, 2048], P('dp', None, 'tensor')
- grad_w_query: float32 [2048, 2048], P('dp', 'tensor')
- grad_w_key: float32 [2048, 2048], P('dp', 'tensor')
- grad_w_value: float32 [2048, 2048], P('dp', 'tensor')
- grad_w_output: float32 [2048, 2048], P('tensor', 'dp')
- grad_w_gate: float32 [2048, 8192], P('dp', 'tensor')
- grad_w_up: float32 [2048, 8192], P('dp', 'tensor')
- grad_w_down: float32 [8192, 2048], P('tensor', 'dp')
- grad_mix_in1: float32 [4], replicated
- grad_mix_res1: float32 [4, 4], replicated
- grad_mix_out1: float32 [4], replicated
- grad_mix_in2: float32 [4], replicated
- grad_mix_res2: float32 [4, 4], replicated
- grad_mix_out2: float32 [4], replicated
The draws below stay inside these ranges and needn't reach their ends.
Inputs may be any that keep to these rules, and one draw needn't show every extreme that they name: `segments`: within each sequence of 1024 tokens the document numbers never fall, start at 0 and end at 3; every document has at least one token and at most 512, and in every sequence document 1 has exactly 512 tokens. `positions`: each token's place within its document, 0 at the document's first token.
All inputs are finite; a program needn't handle non-finite values.
Results may differ from the reference program's by a relative error of at most 0.025.
Values may be sent and summed in bfloat16 or wider, within the bound.
A program may use at most 320 MiB of HBM per device.

```python
import jax
import jax.numpy as jnp
from jax import lax

D = 2048
HEADS = 16
HEAD = 128
FF = 8192
NS = 4
LENGTH = 1024
WINDOW = 1024
TOKENS = 8192


def document_cuts(key):
    seq_count = TOKENS // LENGTH
    half_length = LENGTH // 2
    first_cut = jax.random.randint(jax.random.fold_in(key, 11), (seq_count, 1), 1, half_length - 1)
    second_cut = first_cut + half_length
    third_cut = jax.random.randint(jax.random.fold_in(key, 12), (seq_count, 1), second_cut + 1, LENGTH)
    return jnp.stack([first_cut, second_cut, third_cut], axis=1).astype(jnp.int32)


def draw_segments(key, part):
    cuts = document_cuts(key)
    places = jnp.arange(LENGTH, dtype=jnp.int32)[None, None, :]
    numbers = jnp.sum((places >= cuts).astype(jnp.int32), axis=1)
    return numbers.reshape(TOKENS).astype(jnp.int32)


def draw_positions(key, part):
    cuts = document_cuts(key)
    places = jnp.arange(LENGTH, dtype=jnp.int32)[None, None, :]
    starts = jnp.max(jnp.where(places >= cuts, cuts, 0), axis=1)
    return (places[:, 0, :] - starts).reshape(TOKENS).astype(jnp.int32)


def block_levels(key, shape, split, smallest, top_value):
    def one(position, blocks):
        draws = jax.random.uniform(jax.random.fold_in(jax.random.fold_in(key, 6), position), (blocks,), jnp.float32, smallest / len(split), top_value / len(split))
        return jnp.repeat(jnp.exp(draws), shape[position] // blocks).reshape((-1,) + (1,) * (len(shape) - position - 1))

    loudness = one(*split[0])
    for cut in split[1:]:
        loudness = loudness * one(*cut)
    return loudness


def noise(stream_key, dims, width, limit, cuts=(), held_as=jnp.bfloat16):
    factor_of = block_levels(stream_key, dims, cuts, -0.22, 0.18) if cuts else 1.0
    values = jax.random.normal(stream_key, dims, jnp.float32) * width * factor_of
    return jnp.minimum(jnp.maximum(values, -limit), limit).astype(held_as)


def setup_inputs(seed: int = 0) -> dict:
    seeds = jax.random.split(jax.random.key(seed), 18)
    streams = noise(seeds[0], (TOKENS, NS, D), 1.0, 6.0, ((0, 8), (2, 4)))
    segments = draw_segments(jax.random.fold_in(seeds[17], 71), 0)
    positions = draw_positions(jax.random.fold_in(seeds[17], 71), 0)
    mix_in1 = jnp.clip(jax.random.uniform(seeds[3], (NS,), jnp.float32, 0.2, 0.8), 0.2, 0.8)
    mix_res1 = jnp.clip(jax.random.uniform(seeds[4], (NS, NS), jnp.float32, -0.6, 0.6), -0.6, 0.6)
    mix_out1 = jnp.clip(jax.random.uniform(seeds[5], (NS,), jnp.float32, 0.5, 1.5), 0.5, 1.5)
    mix_in2 = jnp.clip(jax.random.uniform(seeds[6], (NS,), jnp.float32, 0.2, 0.8), 0.2, 0.8)
    mix_res2 = jnp.clip(jax.random.uniform(seeds[7], (NS, NS), jnp.float32, -0.6, 0.6), -0.6, 0.6)
    mix_out2 = jnp.clip(jax.random.uniform(seeds[8], (NS,), jnp.float32, 0.5, 1.5), 0.5, 1.5)
    w_query = noise(seeds[9], (D, HEADS * HEAD), D ** -0.5, 0.125, ((1, 4),))
    w_key = noise(seeds[10], (D, HEADS * HEAD), D ** -0.5, 0.125, ((1, 4),))
    w_value = noise(seeds[11], (D, HEADS * HEAD), D ** -0.5, 0.125, ((1, 4),))
    w_output = noise(seeds[12], (HEADS * HEAD, D), (D // 8) ** -0.5, 0.375, ((0, 4),))
    w_gate = noise(seeds[13], (D, FF), D ** -0.5, 0.125, ((1, 4),))
    w_up = noise(seeds[14], (D, FF), D ** -0.5, 0.125, ((1, 4),))
    w_down = noise(seeds[15], (FF, D), FF ** -0.5, 0.0625, ((0, 4),))
    cotangent = noise(seeds[16], (TOKENS, NS, D), 1.0, 6.0, ((0, 8), (2, 4)))
    return dict(streams=streams, segments=segments, positions=positions, mix_in1=mix_in1, mix_res1=mix_res1, mix_out1=mix_out1, mix_in2=mix_in2, mix_res2=mix_res2, mix_out2=mix_out2, w_query=w_query, w_key=w_key, w_value=w_value, w_output=w_output, w_gate=w_gate, w_up=w_up, w_down=w_down, cotangent=cotangent)


EPS = 1e-05
PRECISE = lax.Precision.HIGHEST
MASKED = -1e+30

@jax.custom_vjp
def low(v):
    return lax.optimization_barrier(v.astype(jnp.bfloat16)).astype(jnp.float32)

@jax.custom_vjp
def low_back(v):
    return v

def low_keep(v):
    return (low(v), None)

def low_pass(kept, grad):
    return (grad,)

def back_keep(v):
    return (v, None)

def back_low(kept, grad):
    return (low(grad),)
low.defvjp(low_keep, low_pass)
low_back.defvjp(back_keep, back_low)

def normalize(field):
    average = lax.optimization_barrier(jnp.mean(field, axis=-1, keepdims=True))
    centered = field - average
    variance = lax.optimization_barrier(jnp.mean(centered * centered, axis=-1, keepdims=True))
    return centered * lax.rsqrt(variance + EPS)

def rotary(field, places):
    length = field.shape[0]
    head_count = field.shape[1] // HEAD
    half_size = HEAD // 2
    inverse = 1.0 / 10000.0 ** (jnp.arange(half_size, dtype=jnp.float32) * 2.0 / HEAD)
    angles = places.astype(jnp.float32)[:, None] * inverse[None, :]
    cos_table = jnp.concatenate([jnp.cos(angles), jnp.cos(angles)], axis=-1)[:, None, :]
    sin_table = jnp.concatenate([jnp.sin(angles), jnp.sin(angles)], axis=-1)[:, None, :]
    pieces = field.reshape(length, head_count, HEAD)
    turned = jnp.concatenate([-pieces[..., half_size:], pieces[..., :half_size]], axis=-1)
    return (pieces * cos_table + turned * sin_table).reshape(length, head_count * HEAD)

def attend(queries, keys_rot, values, segment):
    length = queries.shape[0]
    head_count = queries.shape[1] // HEAD
    query_three = queries.reshape(length, head_count, HEAD)
    key_three = keys_rot.reshape(length, head_count, HEAD)
    value_three = values.reshape(length, head_count, HEAD)
    raw_scores = jnp.einsum('qhe,khe->hqk', query_three, key_three, precision=PRECISE)
    scores = low_back(raw_scores * HEAD ** (-0.5))
    places = jnp.arange(length)
    allowed = (places[:, None] >= places[None, :]) & (places[:, None] - places[None, :] < WINDOW)
    allowed = allowed & (segment[:, None] == segment[None, :])
    scores = jnp.where(allowed[None], scores, MASKED)
    row_max = lax.optimization_barrier(jnp.max(scores, axis=-1, keepdims=True))
    raised = jnp.exp(scores - row_max)
    prob_rows = low(raised / lax.optimization_barrier(jnp.sum(raised, axis=-1, keepdims=True)))
    mixture = jnp.einsum('hqk,khe->qhe', prob_rows, value_three, precision=PRECISE)
    return low(low_back(mixture.reshape(length, head_count * HEAD)))

def layer(widened, segment, places, params):
    mix_in1, mix_res1, mix_out1, mix_in2, mix_res2, mix_out2, w_query, w_key, w_value, w_output, w_gate, w_up, w_down = params
    entry1 = jnp.einsum('i,tid->td', mix_in1, widened, precision=PRECISE)
    normed1 = low(normalize(entry1))
    queries = low(rotary(low_back(jnp.dot(normed1, w_query, precision=PRECISE)), places))
    keys_rot = low(rotary(low_back(jnp.dot(normed1, w_key, precision=PRECISE)), places))
    values = low(low_back(jnp.dot(normed1, w_value, precision=PRECISE)))
    attended = attend(queries, keys_rot, values, segment)
    branch1 = low_back(jnp.dot(attended, w_output, precision=PRECISE))
    middle = jnp.einsum('ij,tid->tjd', mix_res1, widened, precision=PRECISE) + mix_out1[None, :, None] * branch1[:, None, :]
    entry2 = jnp.einsum('i,tid->td', mix_in2, middle, precision=PRECISE)
    normed2 = low(normalize(entry2))
    gate_pre = low_back(jnp.dot(normed2, w_gate, precision=PRECISE))
    up_pre = low_back(jnp.dot(normed2, w_up, precision=PRECISE))
    hidden = low(jax.nn.silu(gate_pre) * up_pre)
    branch2 = low_back(jnp.dot(hidden, w_down, precision=PRECISE))
    return jnp.einsum('ij,tid->tjd', mix_res2, middle, precision=PRECISE) + mix_out2[None, :, None] * branch2[:, None, :]

def reference(streams, segments, positions, mix_in1, mix_res1, mix_out1, mix_in2, mix_res2, mix_out2, w_query, w_key, w_value, w_output, w_gate, w_up, w_down, cotangent):
    params = (mix_in1, mix_res1, mix_out1, mix_in2, mix_res2, mix_out2, w_query.astype(jnp.float32), w_key.astype(jnp.float32), w_value.astype(jnp.float32), w_output.astype(jnp.float32), w_gate.astype(jnp.float32), w_up.astype(jnp.float32), w_down.astype(jnp.float32))
    seq_count = TOKENS // LENGTH
    widened = streams.astype(jnp.float32).reshape(seq_count, LENGTH, NS, D)
    cot_full = cotangent.astype(jnp.float32).reshape(seq_count, LENGTH, NS, D)
    seg_rows = segments.reshape(seq_count, LENGTH)
    pos_rows = positions.reshape(seq_count, LENGTH)

    def step(totals, inputs):
        block, segment, places, incoming = inputs
        result, pullback = jax.vjp(lambda field, weights: layer(field, segment, places, weights), block, params)
        grad_block, grad_params = pullback(incoming)
        totals = jax.tree.map(lambda left, right: left + right, totals, grad_params)
        return (totals, (result.astype(jnp.bfloat16), grad_block))
    zeros = jax.tree.map(jnp.zeros_like, params)
    totals, (results, grads) = lax.scan(step, zeros, (widened, seg_rows, pos_rows, cot_full))
    return (results.reshape(TOKENS, NS, D), grads.reshape(TOKENS, NS, D), totals[6], totals[7], totals[8], totals[9], totals[10], totals[11], totals[12], totals[0], totals[1], totals[2], totals[3], totals[4], totals[5])
```

```python
import functools

import jax
import jax.numpy as jnp
from jax import lax
from jax.experimental import pallas as pl
from jax.experimental.pallas import tpu as pltpu
from jax.sharding import PartitionSpec as P

HEAD = 128
LENGTH = 1024
LONGEST = 512
EPS = 1e-05
PRECISE = lax.Precision.HIGHEST
MASKED = -1e30
MESH = pl.DeviceIdType.MESH
BF16 = jnp.bfloat16
F32 = jnp.float32
CHUNK = 256
ROWS = 32
MIB = 1 << 20

IN1, OUT2, ENTRY, ENTRY_B, BRANCH, BRANCH_E, MIXED = 0, 4, 8, 12, 13, 17, 18


def contract_rows(left, right):
    return lax.dot_general(
        left, right, (((0,), (0,)), ((), ())), preferred_element_type=F32
    )


def dot_nn(left, right):
    return jnp.dot(left, right, preferred_element_type=F32)


def dot_nt(left, right):
    return lax.dot_general(
        left, right, (((1,), (1,)), ((), ())), preferred_element_type=F32
    )


def partners(n):
    me = lax.axis_index("tensor")
    if n == 4:
        both = (me + 1 - 2 * lax.rem(me, 2), lax.rem(me + 2, 4), 3 - me)
        return me, both, both
    to = tuple(lax.rem(me + k, n) for k in range(1, n))
    source = tuple(lax.rem(me + n - k, n) for k in range(1, n))
    return me, to, source


def enter(n, to):
    barrier = pltpu.get_barrier_semaphore()
    for target in to:
        pl.semaphore_signal(
            barrier, inc=1, device_id={"tensor": target}, device_id_type=MESH
        )
    pl.semaphore_wait(barrier, n - 1)


def remote(source, target, send_sem, recv_sem, device):
    return pltpu.make_async_remote_copy(
        src_ref=source,
        dst_ref=target,
        send_sem=send_sem,
        recv_sem=recv_sem,
        device_id={"tensor": device},
        device_id_type=MESH,
    )


def columns(index, width):
    return pl.ds(pl.multiple_of(index * width, 128), width)


def chunk_rows(c):
    return pl.ds(pl.multiple_of(c * CHUNK, CHUNK), CHUNK)


class Gather:
    def __init__(self, n, buf, width, send_sem, recv_sem):
        self.n, self.buf, self.width = n, buf, width
        self.me, self.to, self.source = partners(n)
        self.send_sem, self.recv_sem = send_sem, recv_sem

    def own(self):
        return columns(self.me, self.width)

    def start(self, c):
        view = self.buf.at[chunk_rows(c), self.own()]
        for k in range(self.n - 1):
            remote(view, view, self.send_sem.at[k, c], self.recv_sem.at[k, c], self.to[k]).start()

    def arrive(self, c):
        for k in range(self.n - 1):
            view = self.buf.at[chunk_rows(c), columns(self.source[k], self.width)]
            remote(view, view, self.send_sem.at[k, c], self.recv_sem.at[k, c], self.to[k]).wait_recv()

    def finish(self, c):
        view = self.buf.at[chunk_rows(c), self.own()]
        for k in range(self.n - 1):
            remote(view, view, self.send_sem.at[k, c], self.recv_sem.at[k, c], self.to[k]).wait_send()


class Scatter:
    def __init__(self, n, part, came, width, send_sem, recv_sem):
        self.n, self.part, self.came, self.width = n, part, came, width
        self.me, self.to, self.source = partners(n)
        self.send_sem, self.recv_sem = send_sem, recv_sem

    def copy(self, c, k):
        return remote(
            self.part.at[chunk_rows(c), columns(self.to[k], self.width)],
            self.came.at[k, chunk_rows(c)],
            self.send_sem.at[k, c],
            self.recv_sem.at[k, c],
            self.to[k],
        )

    def start(self, c):
        for k in range(self.n - 1):
            self.copy(c, k).start()

    def arrive(self, c):
        for k in range(self.n - 1):
            self.copy(c, k).wait_recv()

    def finish(self, c):
        for k in range(self.n - 1):
            self.copy(c, k).wait_send()

    def total(self, rows):
        total = self.part[rows, columns(self.me, self.width)].astype(F32)
        for k in range(self.n - 1):
            total += self.came[k, rows].astype(F32)
        return total


class Stats:
    def __init__(self, n, mine, came, send_sem, recv_sem):
        self.n, self.mine, self.came = n, mine, came
        self.me, self.to, self.source = partners(n)
        self.send_sem, self.recv_sem = send_sem, recv_sem

    def copy(self, c, k):
        return remote(
            self.mine.at[c], self.came.at[k, c], self.send_sem.at[k, c], self.recv_sem.at[k, c], self.to[k]
        )

    start, arrive, finish = Scatter.start, Scatter.arrive, Scatter.finish

    def put(self, c, first, second):
        ones = jnp.ones((8, 128), F32)
        for place, field in ((0, first), (8, second)):
            self.mine[c, place : place + 8] = lax.dot_general(
                ones, field, (((1,), (1,)), ((), ())), precision=PRECISE, preferred_element_type=F32
            )

    def means(self, c, features):
        total = self.mine[c]
        for k in range(self.n - 1):
            total += self.came[k, c]
        share = jnp.full((8, 128), 1.0 / (8 * features), F32)
        return tuple(
            lax.dot_general(
                total[place : place + 8],
                share,
                (((0,), (0,)), ((), ())),
                precision=PRECISE,
                preferred_element_type=F32,
            )
            for place in (0, 8)
        )


def loop(count, body):
    def step(i, carry):
        body(i)
        return carry

    lax.fori_loop(0, count, step, 0)


def sub_rows(c, r):
    return pl.ds(pl.multiple_of(c * CHUNK + r * ROWS, ROWS), ROWS)


def normalize_rows(source, rows, target, target_rows, scale_ref):
    field = source[rows, :].astype(F32)
    features = field.shape[1]
    average = jnp.sum(field, axis=1, keepdims=True) * (1.0 / features)
    centered = field - average
    variance = jnp.sum(centered * centered, axis=1, keepdims=True) * (1.0 / features)
    scaling = lax.rsqrt(variance + EPS)
    target[target_rows, :] = (centered * scaling).astype(BF16)
    scale_ref[rows, :] = jnp.broadcast_to(scaling, (field.shape[0], 128))


def repeat_lanes(field, width):
    return jnp.concatenate([field] * (width // 128), axis=1)


def fold_lanes(field):
    total = field[:, 0:128]
    for j in range(1, field.shape[1] // 128):
        total += field[:, 128 * j : 128 * (j + 1)]
    return total


def rotate(field, cos_rows, sin_rows, sign):
    turned = pltpu.roll(field, HEAD // 2, 1)
    return field * cos_rows + (sign * turned) * sin_rows


def project_kernel(
    n, coef, cos_ref, sin_ref, s_hbm, c_hbm, wq_hbm, wk_hbm, wv_hbm,
    normed_hbm, q_ref, k_ref, v_ref, scale_ref, gb2_hbm,
    s_buf, c_buf, w_buf, all1, all2, normed, in_sem, w_sem, out_sem,
    send1, recv1, send2, recv2,
):
    _, tokens, width = s_buf.shape
    count = tokens // CHUNK
    heads = width // HEAD
    weights = (wq_hbm, wk_hbm, wv_hbm)

    def s_in(c):
        return pltpu.make_async_copy(
            s_hbm.at[:, chunk_rows(c)], s_buf.at[:, chunk_rows(c)], in_sem.at[0, c]
        )

    def c_in(c):
        return pltpu.make_async_copy(
            c_hbm.at[:, chunk_rows(c)], c_buf.at[:, chunk_rows(c)], in_sem.at[1, c]
        )

    def w_in(j):
        return pltpu.make_async_copy(weights[j], w_buf.at[j], w_sem.at[j])

    def normed_out(c):
        return pltpu.make_async_copy(
            normed.at[chunk_rows(c)], normed_hbm.at[chunk_rows(c)], out_sem.at[0, c]
        )

    def gb2_out(c):
        return pltpu.make_async_copy(
            all2.at[chunk_rows(c)], gb2_hbm.at[chunk_rows(c)], out_sem.at[1, c]
        )

    loop(count, lambda c: s_in(c).start())
    for j in range(3):
        w_in(j).start()
    loop(count, lambda c: c_in(c).start())
    first = Gather(n, all1, width, send1, recv1)
    second = Gather(n, all2, width, send2, recv2)
    enter(n, first.to)

    def mix(buf, base, target, gather, c):
        def part(r):
            rows = sub_rows(c, r)
            total = coef[base] * buf[0, rows].astype(F32)
            for i in range(1, buf.shape[0]):
                total += coef[base + i] * buf[i, rows].astype(F32)
            target[rows, gather.own()] = total.astype(BF16)

        loop(CHUNK // ROWS, part)
        gather.start(c)

    def send_first(c):
        s_in(c).wait()
        mix(s_buf, IN1, all1, first, c)

    loop(count, send_first)
    for j in range(3):
        w_in(j).wait()

    def work(c):
        c_in(c).wait()
        mix(c_buf, OUT2, all2, second, c)
        first.arrive(c)
        loop(
            CHUNK // ROWS,
            lambda r: normalize_rows(all1, sub_rows(c, r), normed, sub_rows(c, r), scale_ref),
        )
        normed_out(c).start()
        rows = chunk_rows(c)
        block = normed[rows, :]
        cos_rows, sin_rows = cos_ref[rows, :], sin_ref[rows, :]
        for j, target in ((0, q_ref), (1, k_ref)):
            lin = dot_nn(block, w_buf[j])
            for h in range(heads):
                place = slice(HEAD * h, HEAD * (h + 1))
                target[rows, place] = rotate(lin[:, place], cos_rows, sin_rows, 1.0).astype(BF16)
        v_ref[rows, :] = dot_nn(block, w_buf[2]).astype(BF16)

    loop(count, work)

    def end(c):
        second.arrive(c)
        gb2_out(c).start()

    loop(count, end)

    def drain(c):
        gb2_out(c).wait()
        normed_out(c).wait()
        first.finish(c)
        second.finish(c)

    loop(count, drain)


def window_bias(c, start, extent, segc_ref, segr_ref, bias):
    def part(r):
        rows = pl.ds(pl.multiple_of(r * ROWS, ROWS), ROWS)
        row = c * CHUNK + r * ROWS + lax.broadcasted_iota(jnp.int32, (ROWS, extent), 0)
        column = start + lax.broadcasted_iota(jnp.int32, (ROWS, extent), 1)
        same = segc_ref[sub_rows(c, r), 0:1] == segr_ref[0:1, pl.ds(start, extent)]
        bias[rows, :] = jnp.where((row >= column) & same, 0.0, MASKED)

    loop(CHUNK // ROWS, part)


def window(c, tokens):
    extent = min(tokens, CHUNK * (-(-(LONGEST - 1) // CHUNK) + 1))
    back = extent // CHUNK - 1
    return pl.multiple_of(jnp.maximum(c - back, 0) * CHUNK, CHUNK), extent


def attend_kernel(
    n, coef, q_ref, k_ref, v_ref, segc_ref, segr_ref, wo_ref, s_hbm,
    attended_ref, branch_ref, normed_hbm, scale_ref,
    s_buf, part, came, all2, normed, bias, in_sem, out_sem, send1, recv1, send2, recv2,
):
    tokens, width = q_ref.shape
    count = tokens // CHUNK
    heads = width // HEAD
    s_in = pltpu.make_async_copy(s_hbm, s_buf, in_sem)
    s_in.start()
    scatter = Scatter(n, part, came, width, send1, recv1)
    gather = Gather(n, all2, width, send2, recv2)
    enter(n, gather.to)

    def attend(c):
        rows = chunk_rows(c)
        start, extent = window(c, tokens)
        window_bias(c, start, extent, segc_ref, segr_ref, bias)
        for h in range(heads):
            place = slice(HEAD * h, HEAD * (h + 1))
            scores = dot_nt(q_ref[rows, place], k_ref[pl.ds(start, extent), place])
            scores = scores * HEAD ** (-0.5) + bias[...]
            raised = jnp.exp(scores - jnp.max(scores, axis=1, keepdims=True))
            inverse = 1.0 / jnp.sum(raised, axis=1, keepdims=True)
            probs = (raised * inverse).astype(BF16)
            attended_ref[rows, place] = dot_nn(probs, v_ref[pl.ds(start, extent), place]).astype(BF16)
        part[rows, :] = dot_nn(attended_ref[rows, :], wo_ref[...]).astype(BF16)
        scatter.start(c)

    loop(count, attend)
    s_in.wait()

    def middle(c):
        scatter.arrive(c)

        def piece(r):
            rows = sub_rows(c, r)
            branch = scatter.total(rows)
            branch_ref[rows, :] = branch
            entry = coef[ENTRY_B] * branch
            for i in range(s_buf.shape[0]):
                entry += coef[ENTRY + i] * s_buf[i, rows].astype(F32)
            all2[rows, gather.own()] = entry.astype(BF16)

        loop(CHUNK // ROWS, piece)
        gather.start(c)

    loop(count, middle)

    def normed_out(c):
        return pltpu.make_async_copy(
            normed.at[chunk_rows(c)], normed_hbm.at[chunk_rows(c)], out_sem.at[c]
        )

    def last(c):
        gather.arrive(c)
        loop(
            CHUNK // ROWS,
            lambda r: normalize_rows(all2, sub_rows(c, r), normed, sub_rows(c, r), scale_ref),
        )
        normed_out(c).start()

    loop(count, last)

    def drain(c):
        normed_out(c).wait()
        scatter.finish(c)
        gather.finish(c)

    loop(count, drain)


def units_kernel(normed_ref, grad_ref, wg_ref, wu_ref, wd_ref, hidden_ref, gate_ref, up_ref):
    block = normed_ref[...]
    gate = dot_nn(block, wg_ref[...])
    up = dot_nn(block, wu_ref[...])
    grad = dot_nt(grad_ref[...], wd_ref[...])
    sig = jax.nn.sigmoid(gate)
    act = gate * sig
    hidden_ref[...] = (act * up).astype(BF16)
    gate_ref[...] = (grad * up * sig * (1.0 + gate * (1.0 - sig))).astype(BF16)
    up_ref[...] = (grad * act).astype(BF16)


def stats_part(part32, normed, normed_rows, part, c, first, second):
    def piece(r):
        rows = pl.ds(pl.multiple_of(r * ROWS, ROWS), ROWS)
        field = part32[rows, :]
        first[rows, :] = fold_lanes(field)
        second[rows, :] = fold_lanes(field * normed[normed_rows(r), :].astype(F32))
        part[sub_rows(c, r), :] = field.astype(BF16)

    loop(CHUNK // ROWS, piece)


def units_back_kernel(
    n, coef, gate_ref, up_ref, wg_ref, wu_ref, normed_ref, scale_ref, c_hbm,
    entry_ref, gb1_hbm,
    c_buf, part32, first, second, part, came, mine, others, all1, in_sem, out_sem,
    send1, recv1, send2, recv2, send3, recv3,
):
    tokens, features = normed_ref.shape
    width = entry_ref.shape[1]
    count = tokens // CHUNK
    c_in = pltpu.make_async_copy(c_hbm, c_buf, in_sem)
    c_in.start()
    scatter = Scatter(n, part, came, width, send1, recv1)
    stats = Stats(n, mine, others, send2, recv2)
    gather = Gather(n, all1, width, send3, recv3)
    enter(n, gather.to)

    def work(c):
        rows = chunk_rows(c)
        part32[...] = dot_nt(gate_ref[rows, :], wg_ref[...])
        part32[...] += dot_nt(up_ref[rows, :], wu_ref[...])
        stats_part(part32, normed_ref, lambda r: sub_rows(c, r), part, c, first, second)
        stats.put(c, first[...], second[...])
        stats.start(c)
        scatter.start(c)

    loop(count, work)
    c_in.wait()

    def middle(c):
        scatter.arrive(c)
        stats.arrive(c)
        first[...], second[...] = stats.means(c, features)

        def piece(r):
            rows = sub_rows(c, r)
            local = pl.ds(pl.multiple_of(r * ROWS, ROWS), ROWS)
            standard = normed_ref[rows, gather.own()].astype(F32)
            entry = repeat_lanes(scale_ref[rows, :], width) * (
                scatter.total(rows)
                - repeat_lanes(first[local, :], width)
                - standard * repeat_lanes(second[local, :], width)
            )
            entry_ref[rows, :] = entry
            grad = coef[BRANCH_E] * entry
            for i in range(c_buf.shape[0]):
                grad += coef[BRANCH + i] * c_buf[i, rows].astype(F32)
            all1[rows, gather.own()] = grad.astype(BF16)

        loop(CHUNK // ROWS, piece)
        gather.start(c)

    loop(count, middle)

    def gb1_out(c):
        return pltpu.make_async_copy(
            all1.at[chunk_rows(c)], gb1_hbm.at[chunk_rows(c)], out_sem.at[c]
        )

    def last(c):
        gather.arrive(c)
        gb1_out(c).start()

    loop(count, last)

    def drain(c):
        gb1_out(c).wait()
        scatter.finish(c)
        stats.finish(c)
        gather.finish(c)

    loop(count, drain)


def attend_back_kernel(
    n, q_ref, k_ref, v_ref, segc_ref, segr_ref, cos_ref, sin_ref, wo_ref, wq_ref, wk_ref, wv_ref,
    wd_ref, scale_ref, gb1_hbm, hidden_hbm, normed_hbm,
    dq_ref, dk_ref, dv_ref, branch_ref, entry_ref,
    gb1_buf, hidden_buf, normed_buf, own_buf, bias, dk_t, dv_t, part32, first, second,
    part1, came1, part2, came2, mine, others, in_sem, own_sem,
    send1, recv1, send2, recv2, send3, recv3,
):
    tokens, width = q_ref.shape
    features = part1.shape[1]
    count = tokens // CHUNK
    heads = width // HEAD
    factor = HEAD ** (-0.5)
    down = Scatter(n, part2, came2, width, send1, recv1)
    scatter = Scatter(n, part1, came1, width, send2, recv2)
    stats = Stats(n, mine, others, send3, recv3)

    def inputs(c, slot):
        return tuple(
            pltpu.make_async_copy(source.at[chunk_rows(c)], target.at[slot], in_sem.at[i, slot])
            for i, (source, target) in enumerate(
                ((gb1_hbm, gb1_buf), (hidden_hbm, hidden_buf), (normed_hbm, normed_buf))
            )
        )

    own_in = pltpu.make_async_copy(normed_hbm.at[:, columns(down.me, width)], own_buf, own_sem)
    own_in.start()
    for copy in inputs(count - 1, 0):
        copy.start()
    dk_t[...] = jnp.zeros_like(dk_t)
    dv_t[...] = jnp.zeros_like(dv_t)
    enter(n, scatter.to)

    def work(i):
        c = count - 1 - i
        slot = lax.rem(i, 2)

        @pl.when(i < count - 1)
        def _():
            for copy in inputs(c - 1, 1 - slot):
                copy.start()

        for copy in inputs(c, slot):
            copy.wait()
        rows = chunk_rows(c)
        part2[rows, :] = dot_nn(hidden_buf[slot], wd_ref[...]).astype(BF16)
        down.start(c)
        grad = dot_nt(gb1_buf[slot], wo_ref[...]).astype(BF16)
        start, extent = window(c, tokens)
        keys = pl.ds(start, extent)
        window_bias(c, start, extent, segc_ref, segr_ref, bias)
        cos_rows, sin_rows = cos_ref[rows, :], sin_ref[rows, :]
        for h in range(heads):
            place = slice(HEAD * h, HEAD * (h + 1))
            query, grad_h = q_ref[rows, place], grad[:, place]
            scores = dot_nt(query, k_ref[keys, place]) * factor + bias[...]
            raised = jnp.exp(scores - jnp.max(scores, axis=1, keepdims=True))
            inverse = 1.0 / jnp.sum(raised, axis=1, keepdims=True)
            probs = raised * inverse
            grad_probs = dot_nt(grad_h, v_ref[keys, place])
            centre = jnp.sum(probs * grad_probs, axis=1, keepdims=True)
            grad_scores = (probs * (grad_probs - centre)).astype(BF16)
            dv_t[place, keys] += dot_nn(jnp.transpose(grad_h), probs.astype(BF16))
            dk_t[place, keys] += dot_nn(jnp.transpose(query), grad_scores)
            dq = dot_nn(grad_scores, k_ref[keys, place]) * factor
            dq_ref[rows, place] = rotate(dq, cos_rows, sin_rows, -1.0).astype(BF16)
            dk = jnp.transpose(dk_t[place, rows]) * factor
            dk_ref[rows, place] = rotate(dk, cos_rows, sin_rows, -1.0).astype(BF16)
            dv_ref[rows, place] = jnp.transpose(dv_t[place, rows]).astype(BF16)
        part32[...] = dot_nt(dq_ref[rows, :], wq_ref[...])
        part32[...] += dot_nt(dk_ref[rows, :], wk_ref[...])
        part32[...] += dot_nt(dv_ref[rows, :], wv_ref[...])
        stats_part(
            part32,
            normed_buf.at[slot],
            lambda r: pl.ds(pl.multiple_of(r * ROWS, ROWS), ROWS),
            part1,
            c,
            first,
            second,
        )
        stats.put(c, first[...], second[...])
        stats.start(c)
        scatter.start(c)

    loop(count, work)
    own_in.wait()

    def last(i):
        c = count - 1 - i
        down.arrive(c)

        def sums(r):
            branch_ref[sub_rows(c, r), :] = down.total(sub_rows(c, r))

        loop(CHUNK // ROWS, sums)
        scatter.arrive(c)
        stats.arrive(c)
        first[...], second[...] = stats.means(c, features)

        def piece(r):
            rows = sub_rows(c, r)
            local = pl.ds(pl.multiple_of(r * ROWS, ROWS), ROWS)
            entry_ref[rows, :] = repeat_lanes(scale_ref[rows, :], width) * (
                scatter.total(rows)
                - repeat_lanes(first[local, :], width)
                - own_buf[rows, :].astype(F32) * repeat_lanes(second[local, :], width)
            )

        loop(CHUNK // ROWS, piece)

    loop(count, last)

    def drain(c):
        down.finish(c)
        scatter.finish(c)
        stats.finish(c)

    loop(count, drain)


def streams_kernel(
    coef, s_ref, c_ref, b1_ref, b2_ref, e1_ref, e2_ref, new_ref, grad_ref, sums_ref
):
    @pl.when(pl.program_id(0) == 0)
    def _():
        sums_ref[...] = jnp.zeros_like(sums_ref)

    count = s_ref.shape[0]

    def fold(field):
        field = fold_lanes(field)
        total = field[0:8]
        for j in range(1, field.shape[0] // 8):
            total += field[8 * j : 8 * (j + 1)]
        return total

    def piece(r):
        rows = pl.ds(pl.multiple_of(r * 16, 16), 16)
        s = [s_ref[i, rows].astype(F32) for i in range(count)]
        c = [c_ref[i, rows].astype(F32) for i in range(count)]
        b1, b2, e1, e2 = b1_ref[rows, :], b2_ref[rows, :], e1_ref[rows, :], e2_ref[rows, :]
        for j in range(count):
            new = coef[BRANCH + j] * b1 + coef[OUT2 + j] * b2
            grad = coef[ENTRY + j] * e2 + coef[IN1 + j] * e1
            for k in range(count):
                new += coef[MIXED + count * k + j] * s[k]
                grad += coef[MIXED + count * j + k] * c[k]
            new_ref[rows, j, :] = new.astype(BF16)
            grad_ref[rows, j, :] = grad
        pairs = [(s[i], c[j]) for i in range(count) for j in range(count)]
        pairs += [(s[i], e1) for i in range(count)] + [(s[i], e2) for i in range(count)]
        pairs += [(c[i], b1) for i in range(count)] + [(c[i], b2) for i in range(count)]
        pairs += [(b1, e2)]
        for place, (left, right) in enumerate(pairs):
            sums_ref[place] += fold(left * right)

    loop(s_ref.shape[1] // 16, piece)


def on_device(
    n,
    streams,
    segments,
    positions,
    mix_in1,
    mix_res1,
    mix_out1,
    mix_in2,
    mix_res2,
    mix_out2,
    w_query,
    w_key,
    w_value,
    w_output,
    w_gate,
    w_up,
    w_down,
    cotangent,
):
    tokens, stream_count, width = streams.shape
    features = w_query.shape[0]
    units = w_gate.shape[1]
    chunks = tokens // CHUNK
    assert tokens == LENGTH and stream_count == 4
    any_spec = pl.BlockSpec(memory_space=pl.ANY)
    vmem = pl.BlockSpec(memory_space=pltpu.VMEM)
    smem = pl.BlockSpec(memory_space=pltpu.SMEM)

    def array(shape, dtype):
        return jax.ShapeDtypeStruct(shape, dtype)

    def dma(*shape):
        return pltpu.SemaphoreType.DMA(shape)

    def pair():
        return [dma(n - 1, chunks), dma(n - 1, chunks)]

    def params(identity, mib):
        return pltpu.CompilerParams(
            collective_id=identity, has_side_effects=True, vmem_limit_bytes=mib * MIB
        )

    half = HEAD // 2
    inverse = 1.0 / 10000.0 ** (jnp.arange(half, dtype=F32) * 2.0 / HEAD)
    angles = positions.astype(F32)[:, None] * inverse[None, :]
    cosine, sine = jnp.cos(angles), jnp.sin(angles)
    cos_table = jnp.concatenate([cosine, cosine], axis=-1)
    sin_table = jnp.concatenate([-sine, sine], axis=-1)
    seg_column = jnp.broadcast_to(segments[:, None], (tokens, 128))
    seg_row = jnp.broadcast_to(segments[None, :], (8, tokens))

    def small(form, left, right):
        return jnp.einsum(form, left, right, precision=PRECISE)

    coef = jnp.concatenate(
        [
            mix_in1,
            mix_out2,
            small("ij,j->i", mix_res1, mix_in2),
            small("j,j->", mix_in2, mix_out1)[None],
            small("i,ij->j", mix_out1, mix_res2),
            small("i,i->", mix_out1, mix_in2)[None],
            small("ki,ij->kj", mix_res1, mix_res2).reshape(-1),
        ]
    )
    planes = jnp.transpose(streams, (1, 0, 2))
    cot_planes = jnp.transpose(cotangent, (1, 0, 2))

    normed1, queries, keys, values, scale1, grad_branch2 = pl.pallas_call(
        functools.partial(project_kernel, n),
        name="project",
        out_shape=[
            array((tokens, features), BF16),
            array((tokens, width), BF16),
            array((tokens, width), BF16),
            array((tokens, width), BF16),
            array((tokens, 128), F32),
            array((tokens, features), BF16),
        ],
        in_specs=[smem, vmem, vmem] + [any_spec] * 5,
        out_specs=[any_spec, vmem, vmem, vmem, vmem, any_spec],
        scratch_shapes=[
            pltpu.VMEM((stream_count, tokens, width), BF16),
            pltpu.VMEM((stream_count, tokens, width), BF16),
            pltpu.VMEM((3, features, width), BF16),
            pltpu.VMEM((tokens, features), BF16),
            pltpu.VMEM((tokens, features), BF16),
            pltpu.VMEM((tokens, features), BF16),
            dma(2, chunks),
            dma(3),
            dma(2, chunks),
        ]
        + pair()
        + pair(),
        compiler_params=params(0, 48),
    )(coef, cos_table, sin_table, planes, cot_planes, w_query, w_key, w_value)

    extent = window(0, tokens)[1]
    attended, branch1, normed2, scale2 = pl.pallas_call(
        functools.partial(attend_kernel, n),
        name="attend",
        out_shape=[
            array((tokens, width), BF16),
            array((tokens, width), F32),
            array((tokens, features), BF16),
            array((tokens, 128), F32),
        ],
        in_specs=[smem] + [vmem] * 6 + [any_spec],
        out_specs=[vmem, vmem, any_spec, vmem],
        scratch_shapes=[
            pltpu.VMEM((stream_count, tokens, width), BF16),
            pltpu.VMEM((tokens, features), BF16),
            pltpu.VMEM((n - 1, tokens, width), BF16),
            pltpu.VMEM((tokens, features), BF16),
            pltpu.VMEM((tokens, features), BF16),
            pltpu.VMEM((CHUNK, extent), F32),
            pltpu.SemaphoreType.DMA,
            dma(chunks),
        ]
        + pair()
        + pair(),
        compiler_params=params(1, 48),
    )(coef, queries, keys, values, seg_column, seg_row, w_output, planes)

    block = min(256, units)
    hidden, grad_gate_act, grad_up_act = pl.pallas_call(
        units_kernel,
        name="units",
        grid=(units // block,),
        out_shape=[array((tokens, units), BF16)] * 3,
        in_specs=[
            pl.BlockSpec((tokens, features), lambda f: (0, 0)),
            pl.BlockSpec((tokens, features), lambda f: (0, 0)),
            pl.BlockSpec((features, block), lambda f: (0, f)),
            pl.BlockSpec((features, block), lambda f: (0, f)),
            pl.BlockSpec((block, features), lambda f: (f, 0)),
        ],
        out_specs=[pl.BlockSpec((tokens, block), lambda f: (0, f))] * 3,
        compiler_params=pltpu.CompilerParams(vmem_limit_bytes=48 * MIB),
    )(normed2, grad_branch2, w_gate, w_up, w_down)

    def over_dp(left, right, dimension):
        partial = contract_rows(left, right).astype(BF16)
        return lax.psum_scatter(
            partial, "dp", scatter_dimension=dimension, tiled=True
        ).astype(F32)

    grad_w_down = over_dp(hidden, grad_branch2, 1)
    grad_w_gate = over_dp(normed2, grad_gate_act, 0)
    grad_w_up = over_dp(normed2, grad_up_act, 0)

    grad_entry2, grad_branch1 = pl.pallas_call(
        functools.partial(units_back_kernel, n),
        name="units_back",
        out_shape=[array((tokens, width), F32), array((tokens, features), BF16)],
        in_specs=[smem] + [vmem] * 6 + [any_spec],
        out_specs=[vmem, any_spec],
        scratch_shapes=[
            pltpu.VMEM((stream_count, tokens, width), BF16),
            pltpu.VMEM((CHUNK, features), F32),
            pltpu.VMEM((CHUNK, 128), F32),
            pltpu.VMEM((CHUNK, 128), F32),
            pltpu.VMEM((tokens, features), BF16),
            pltpu.VMEM((n - 1, tokens, width), BF16),
            pltpu.VMEM((chunks, 16, CHUNK), F32),
            pltpu.VMEM((n - 1, chunks, 16, CHUNK), F32),
            pltpu.VMEM((tokens, features), BF16),
            pltpu.SemaphoreType.DMA,
            dma(chunks),
        ]
        + pair()
        + pair()
        + pair(),
        compiler_params=params(2, 58),
    )(coef, grad_gate_act, grad_up_act, w_gate, w_up, normed2, scale2, cot_planes)

    grad_query_lin, grad_key_lin, grad_value_lin, branch2, grad_entry1 = pl.pallas_call(
        functools.partial(attend_back_kernel, n),
        name="attend_back",
        out_shape=[array((tokens, width), BF16)] * 3 + [array((tokens, width), F32)] * 2,
        in_specs=[vmem] * 13 + [any_spec] * 3,
        out_specs=[vmem] * 5,
        scratch_shapes=[
            pltpu.VMEM((2, CHUNK, features), BF16),
            pltpu.VMEM((2, CHUNK, units), BF16),
            pltpu.VMEM((2, CHUNK, features), BF16),
            pltpu.VMEM((tokens, width), BF16),
            pltpu.VMEM((CHUNK, extent), F32),
            pltpu.VMEM((width, tokens), F32),
            pltpu.VMEM((width, tokens), F32),
            pltpu.VMEM((CHUNK, features), F32),
            pltpu.VMEM((CHUNK, 128), F32),
            pltpu.VMEM((CHUNK, 128), F32),
            pltpu.VMEM((tokens, features), BF16),
            pltpu.VMEM((n - 1, tokens, width), BF16),
            pltpu.VMEM((tokens, features), BF16),
            pltpu.VMEM((n - 1, tokens, width), BF16),
            pltpu.VMEM((chunks, 16, CHUNK), F32),
            pltpu.VMEM((n - 1, chunks, 16, CHUNK), F32),
            dma(3, 2),
            pltpu.SemaphoreType.DMA,
        ]
        + pair()
        + pair()
        + pair(),
        compiler_params=params(3, 60),
    )(
        queries, keys, values, seg_column, seg_row, cos_table, sin_table,
        w_output, w_query, w_key, w_value, w_down, scale1, grad_branch1, hidden, normed1,
    )

    grad_w_output = over_dp(attended, grad_branch1, 1)
    grad_w_query = over_dp(normed1, grad_query_lin, 0)
    grad_w_key = over_dp(normed1, grad_key_lin, 0)
    grad_w_value = over_dp(normed1, grad_value_lin, 0)

    rows = 128
    sum_count = 33
    plane_spec = pl.BlockSpec((stream_count, rows, width), lambda t: (0, t, 0))
    field_spec = pl.BlockSpec((rows, width), lambda t: (t, 0))
    stream_spec = pl.BlockSpec((rows, stream_count, width), lambda t: (t, 0, 0))
    new_streams, stream_grad, sums = pl.pallas_call(
        streams_kernel,
        name="streams",
        grid=(tokens // rows,),
        out_shape=[
            array(streams.shape, BF16),
            array(streams.shape, F32),
            array((sum_count, 8, 128), F32),
        ],
        in_specs=[smem, plane_spec, plane_spec] + [field_spec] * 4,
        out_specs=[
            stream_spec,
            stream_spec,
            pl.BlockSpec((sum_count, 8, 128), lambda t: (0, 0, 0)),
        ],
        compiler_params=pltpu.CompilerParams(vmem_limit_bytes=48 * MIB),
    )(coef, planes, cot_planes, branch1, branch2, grad_entry1, grad_entry2)
    sums = lax.psum(jnp.sum(sums, axis=(1, 2)), ("dp", "tensor"))
    s_c = sums[0:16].reshape(4, 4)
    s_e1, s_e2, c_b1, c_b2, b_e = sums[16:20], sums[20:24], sums[24:28], sums[28:32], sums[32]
    grad_mix_in1 = s_e1
    grad_mix_res1 = small("ik,jk->ij", s_c, mix_res2) + s_e2[:, None] * mix_in2[None, :]
    grad_mix_out1 = small("jk,k->j", mix_res2, c_b1) + mix_in2 * b_e
    grad_mix_in2 = small("ki,k->i", mix_res1, s_e2) + mix_out1 * b_e
    grad_mix_res2 = small("ki,kj->ij", mix_res1, s_c) + mix_out1[:, None] * c_b1[None, :]
    grad_mix_out2 = c_b2
    return (
        new_streams,
        stream_grad,
        grad_w_query,
        grad_w_key,
        grad_w_value,
        grad_w_output,
        grad_w_gate,
        grad_w_up,
        grad_w_down,
        grad_mix_in1,
        grad_mix_res1,
        grad_mix_out1,
        grad_mix_in2,
        grad_mix_res2,
        grad_mix_out2,
    )


def solution(mesh):
    return jax.shard_map(
        functools.partial(on_device, mesh.shape["tensor"]),
        mesh=mesh,
        in_specs=(
            P("dp", None, "tensor"),
            P("dp"),
            P("dp"),
            P(),
            P(),
            P(),
            P(),
            P(),
            P(),
            P(None, "tensor"),
            P(None, "tensor"),
            P(None, "tensor"),
            P("tensor", None),
            P(None, "tensor"),
            P(None, "tensor"),
            P("tensor", None),
            P("dp", None, "tensor"),
        ),
        out_specs=(
            P("dp", None, "tensor"),
            P("dp", None, "tensor"),
            P("dp", "tensor"),
            P("dp", "tensor"),
            P("dp", "tensor"),
            P("tensor", "dp"),
            P("dp", "tensor"),
            P("dp", "tensor"),
            P("tensor", "dp"),
            P(),
            P(),
            P(),
            P(),
            P(),
            P(),
        ),
        check_vma=False,
    )
```

```python
import functools

import jax
import jax.numpy as jnp
from jax import lax
from jax.experimental import pallas as pl
from jax.experimental.pallas import tpu as pltpu
from jax.sharding import PartitionSpec as P

HEAD = 128
LENGTH = 1024
LONGEST = 512
EPS = 1e-05
PRECISE = lax.Precision.HIGHEST
MASKED = -1e30
MESH = pl.DeviceIdType.MESH
BF16 = jnp.bfloat16
F32 = jnp.float32
CHUNK = 256
ROWS = 32
MIB = 1 << 20

IN1, OUT2, ENTRY, ENTRY_B, BRANCH, BRANCH_E, MIXED = 0, 4, 8, 12, 13, 17, 18


def contract_rows(left, right):
    return lax.dot_general(
        left, right, (((0,), (0,)), ((), ())), preferred_element_type=F32
    )


def dot_nn(left, right):
    return jnp.dot(left, right, preferred_element_type=F32)


def dot_nt(left, right):
    return lax.dot_general(
        left, right, (((1,), (1,)), ((), ())), preferred_element_type=F32
    )


def partners(n):
    me = lax.axis_index("tensor")
    if n == 4:
        both = (me + 1 - 2 * lax.rem(me, 2), lax.rem(me + 2, 4), 3 - me)
        return me, both, both
    to = tuple(lax.rem(me + k, n) for k in range(1, n))
    source = tuple(lax.rem(me + n - k, n) for k in range(1, n))
    return me, to, source


def enter(n, to):
    barrier = pltpu.get_barrier_semaphore()
    for target in to:
        pl.semaphore_signal(
            barrier, inc=1, device_id={"tensor": target}, device_id_type=MESH
        )
    pl.semaphore_wait(barrier, n - 1)


def remote(source, target, send_sem, recv_sem, device):
    return pltpu.make_async_remote_copy(
        src_ref=source,
        dst_ref=target,
        send_sem=send_sem,
        recv_sem=recv_sem,
        device_id={"tensor": device},
        device_id_type=MESH,
    )


def columns(index, width):
    return pl.ds(pl.multiple_of(index * width, 128), width)


def chunk_rows(c):
    return pl.ds(pl.multiple_of(c * CHUNK, CHUNK), CHUNK)


def half_rows(c, half):
    return pl.ds(pl.multiple_of(c * CHUNK + half * (CHUNK // 2), CHUNK // 2), CHUNK // 2)


class Gather:
    def __init__(self, n, buf, width, send_sem, recv_sem):
        self.n, self.buf, self.width = n, buf, width
        self.me, self.to, self.source = partners(n)
        self.send_sem, self.recv_sem = send_sem, recv_sem

    def own(self):
        return columns(self.me, self.width)

    def copy(self, rows, owner, k, c, target):
        view = self.buf.at[rows, columns(owner, self.width)]
        return remote(view, view, self.send_sem.at[k, c], self.recv_sem.at[k, c], target)

    def direct(self):
        return 2 if self.n == 4 else self.n - 1

    def handed(self, c):
        side, up, _ = self.to
        return (
            self.copy(half_rows(c, 0), side, 2, c, up),
            self.copy(half_rows(c, 1), up, 3, c, side),
        )

    def start(self, c):
        for k in range(self.direct()):
            self.copy(chunk_rows(c), self.me, k, c, self.to[k]).start()

    def relay(self, c):
        if self.n == 4:
            for k, copy in enumerate(self.handed(c)):
                self.copy(chunk_rows(c), self.source[k], k, c, self.to[k]).wait_recv()
                copy.start()

    def arrive(self, c):
        if self.n == 4:
            side, up, across = self.to
            self.copy(half_rows(c, 0), across, 2, c, up).wait_recv()
            self.copy(half_rows(c, 1), across, 3, c, side).wait_recv()
        else:
            for k in range(self.n - 1):
                self.copy(chunk_rows(c), self.source[k], k, c, self.to[k]).wait_recv()

    def finish(self, c):
        for k in range(self.direct()):
            self.copy(chunk_rows(c), self.me, k, c, self.to[k]).wait_send()
        if self.n == 4:
            for copy in self.handed(c):
                copy.wait_send()

    def take(self, count, work):
        self.relay(0)

        def body(c):
            @pl.when(c + 1 < count)
            def _():
                self.relay(c + 1)

            self.arrive(c)
            work(c)

        loop(count, body)


class Scatter:
    def __init__(self, n, part, came, width, send_sem, recv_sem):
        self.n, self.part, self.came, self.width = n, part, came, width
        self.me, self.to, self.source = partners(n)
        self.send_sem, self.recv_sem = send_sem, recv_sem

    def copy(self, rows, owner, slot, k, c, target):
        return remote(
            self.part.at[rows, columns(owner, self.width)],
            self.came.at[slot, rows],
            self.send_sem.at[k, c],
            self.recv_sem.at[k, c],
            target,
        )

    def first(self, c):
        if self.n != 4:
            return tuple(
                (chunk_rows(c), self.to[k], k, k, c, self.to[k]) for k in range(self.n - 1)
            )
        side, up, across = self.to
        return (
            (half_rows(c, 0), across, 2, 0, c, side),
            (half_rows(c, 1), across, 2, 1, c, up),
            (half_rows(c, 0), side, 0, 2, c, side),
            (half_rows(c, 1), up, 1, 3, c, up),
        )

    def second(self, c):
        if self.n != 4:
            return ()
        side, up, _ = self.to
        return (
            (half_rows(c, 0), up, 1, 4, c, up),
            (half_rows(c, 1), side, 0, 5, c, side),
        )

    def start(self, c):
        for place in self.first(c):
            self.copy(*place).start()

    def relay(self, c):
        second = self.second(c)
        first = self.first(c)
        for half in range(len(second)):
            self.copy(*first[half]).wait_recv()
            owner = columns(self.to[1 - half], self.width)
            base = c * CHUNK + half * (CHUNK // 2)

            def add(r):
                rows = pl.ds(pl.multiple_of(base + r * ROWS, ROWS), ROWS)
                total = self.part[rows, owner].astype(F32) + self.came[2, rows].astype(F32)
                self.part[rows, owner] = total.astype(BF16)

            loop(CHUNK // 2 // ROWS, add)
            self.copy(*second[half]).start()

    def arrive(self, c):
        places = self.first(c)
        if self.n == 4:
            places = places[2:] + self.second(c)
        for place in places:
            self.copy(*place).wait_recv()

    def finish(self, c):
        for place in self.first(c) + self.second(c):
            self.copy(*place).wait_send()

    def total(self, rows):
        total = self.part[rows, columns(self.me, self.width)].astype(F32)
        for k in range(2 if self.n == 4 else self.n - 1):
            total += self.came[k, rows].astype(F32)
        return total


class Stats:
    def __init__(self, n, mine, came, send_sem, recv_sem):
        self.n, self.mine, self.came = n, mine, came
        self.me, self.to, self.source = partners(n)
        self.send_sem, self.recv_sem = send_sem, recv_sem

    def copy(self, c, k):
        return remote(
            self.mine.at[c], self.came.at[k, c], self.send_sem.at[k, c], self.recv_sem.at[k, c], self.to[k]
        )

    def start(self, c):
        for k in range(self.n - 1):
            self.copy(c, k).start()

    def arrive(self, c):
        for k in range(self.n - 1):
            self.copy(c, k).wait_recv()

    def finish(self, c):
        for k in range(self.n - 1):
            self.copy(c, k).wait_send()

    def put(self, c, first, second):
        ones = jnp.ones((8, 128), F32)
        for place, field in ((0, first), (8, second)):
            self.mine[c, place : place + 8] = lax.dot_general(
                ones, field, (((1,), (1,)), ((), ())), precision=PRECISE, preferred_element_type=F32
            )

    def moments(self, c, width):
        pieces = [self.mine[c]] + [self.came[k, c] for k in range(self.n - 1)]
        count = float(self.n * width)
        mean = sum(piece[0:8] for piece in pieces) * (1.0 / count)
        squares = sum(
            piece[8:16] + width * (piece[0:8] * (1.0 / width) - mean) ** 2 for piece in pieces
        )
        share = jnp.full((8, 128), 0.125, F32)
        return tuple(
            lax.dot_general(
                row, share, (((0,), (0,)), ((), ())), precision=PRECISE, preferred_element_type=F32
            )
            for row in (mean, lax.rsqrt(squares * (1.0 / count) + EPS))
        )

    def means(self, c, features):
        total = self.mine[c]
        for k in range(self.n - 1):
            total += self.came[k, c]
        share = jnp.full((8, 128), 1.0 / (8 * features), F32)
        return tuple(
            lax.dot_general(
                total[place : place + 8],
                share,
                (((0,), (0,)), ((), ())),
                precision=PRECISE,
                preferred_element_type=F32,
            )
            for place in (0, 8)
        )


def loop(count, body):
    def step(i, carry):
        body(i)
        return carry

    lax.fori_loop(0, count, step, 0)


def sub_rows(c, r):
    return pl.ds(pl.multiple_of(c * CHUNK + r * ROWS, ROWS), ROWS)


def repeat_lanes(field, width):
    return jnp.concatenate([field] * (width // 128), axis=1)


def fold_lanes(field):
    total = field[:, 0:128]
    for j in range(1, field.shape[1] // 128):
        total += field[:, 128 * j : 128 * (j + 1)]
    return total


def local_rows(r):
    return pl.ds(pl.multiple_of(r * ROWS, ROWS), ROWS)


def fold_entry(entry, first, second, rows):
    first[rows, :] = fold_lanes(entry)
    centered = entry - jnp.sum(entry, axis=1, keepdims=True) * (1.0 / entry.shape[1])
    second[rows, :] = fold_lanes(centered * centered)


def standardize(c, stats, gather, first, second, stand_ref, scale_ref):
    width = stand_ref.shape[1]
    stats.arrive(c)
    first[...], second[...] = stats.moments(c, width)

    def piece(r):
        rows, local = sub_rows(c, r), local_rows(r)
        scaling = second[local, :]
        stand = (stand_ref[rows, :] - repeat_lanes(first[local, :], width)) * repeat_lanes(
            scaling, width
        )
        stand_ref[rows, :] = stand
        scale_ref[rows, :] = scaling
        gather.buf[rows, gather.own()] = stand.astype(BF16)

    loop(CHUNK // ROWS, piece)
    gather.start(c)


def rotate(field, cos_rows, sin_rows, sign):
    turned = pltpu.roll(field, HEAD // 2, 1)
    return field * cos_rows + (sign * turned) * sin_rows


def project_kernel(
    n, coef, cos_ref, sin_ref, s_hbm, c_hbm, wq_hbm, wk_hbm, wv_hbm,
    normed_hbm, q_ref, k_ref, v_ref, stand_ref, scale_ref, gb2_hbm,
    s_buf, c_buf, w_buf, all1, all2, first, second, mine, others, in_sem, w_sem, out_sem,
    send1, recv1, send2, recv2, send3, recv3,
):
    _, tokens, width = s_buf.shape
    count = tokens // CHUNK
    heads = width // HEAD
    weights = (wq_hbm, wk_hbm, wv_hbm)

    def s_in(c):
        return pltpu.make_async_copy(
            s_hbm.at[:, chunk_rows(c)], s_buf.at[:, chunk_rows(c)], in_sem.at[0, c]
        )

    def c_in(c):
        return pltpu.make_async_copy(
            c_hbm.at[:, chunk_rows(c)], c_buf.at[:, chunk_rows(c)], in_sem.at[1, c]
        )

    def w_in(j):
        return pltpu.make_async_copy(weights[j], w_buf.at[j], w_sem.at[j])

    def normed_out(c):
        return pltpu.make_async_copy(
            all1.at[chunk_rows(c)], normed_hbm.at[chunk_rows(c)], out_sem.at[0, c]
        )

    def gb2_out(c):
        return pltpu.make_async_copy(
            all2.at[chunk_rows(c)], gb2_hbm.at[chunk_rows(c)], out_sem.at[1, c]
        )

    loop(count, lambda c: s_in(c).start())
    for j in range(3):
        w_in(j).start()
    loop(count, lambda c: c_in(c).start())
    gather = Gather(n, all1, width, send1, recv1)
    incoming = Gather(n, all2, width, send2, recv2)
    stats = Stats(n, mine, others, send3, recv3)
    enter(n, gather.to)

    def mix(buf, base, rows):
        total = coef[base] * buf[0, rows].astype(F32)
        for i in range(1, buf.shape[0]):
            total += coef[base + i] * buf[i, rows].astype(F32)
        return total

    def entry(c):
        s_in(c).wait()

        def piece(r):
            field = mix(s_buf, IN1, sub_rows(c, r))
            stand_ref[sub_rows(c, r), :] = field
            fold_entry(field, first, second, local_rows(r))

        loop(CHUNK // ROWS, piece)
        stats.put(c, first[...], second[...])
        stats.start(c)

    def send(c):
        standardize(c, stats, gather, first, second, stand_ref, scale_ref)

    entry(0)

    def ahead(c):
        entry(c + 1)
        send(c)

    loop(count - 1, ahead)
    send(count - 1)
    for j in range(3):
        w_in(j).wait()

    def work(c):
        c_in(c).wait()

        def piece(r):
            rows = sub_rows(c, r)
            all2[rows, incoming.own()] = mix(c_buf, OUT2, rows).astype(BF16)

        loop(CHUNK // ROWS, piece)
        incoming.start(c)
        normed_out(c).start()
        rows = chunk_rows(c)
        block = all1[rows, :]
        cos_rows, sin_rows = cos_ref[rows, :], sin_ref[rows, :]
        for j, target in ((0, q_ref), (1, k_ref)):
            lin = dot_nn(block, w_buf[j])
            for h in range(heads):
                place = slice(HEAD * h, HEAD * (h + 1))
                target[rows, place] = rotate(lin[:, place], cos_rows, sin_rows, 1.0).astype(BF16)
        v_ref[rows, :] = dot_nn(block, w_buf[2]).astype(BF16)

    gather.take(count, work)
    incoming.take(count, lambda c: gb2_out(c).start())

    def drain(c):
        gb2_out(c).wait()
        normed_out(c).wait()
        stats.finish(c)
        gather.finish(c)
        incoming.finish(c)

    loop(count, drain)


def window_bias(c, start, extent, segc_ref, segr_ref, bias):
    def part(r):
        rows = pl.ds(pl.multiple_of(r * ROWS, ROWS), ROWS)
        row = c * CHUNK + r * ROWS + lax.broadcasted_iota(jnp.int32, (ROWS, extent), 0)
        column = start + lax.broadcasted_iota(jnp.int32, (ROWS, extent), 1)
        same = segc_ref[sub_rows(c, r), 0:1] == segr_ref[0:1, pl.ds(start, extent)]
        bias[rows, :] = jnp.where((row >= column) & same, 0.0, MASKED)

    loop(CHUNK // ROWS, part)


def window(c, tokens):
    extent = min(tokens, CHUNK * (-(-(LONGEST - 1) // CHUNK) + 1))
    back = extent // CHUNK - 1
    return pl.multiple_of(jnp.maximum(c - back, 0) * CHUNK, CHUNK), extent


def attend_kernel(
    n, coef, q_ref, k_ref, v_ref, segc_ref, segr_ref, wo_ref, s_hbm,
    attended_ref, branch_ref, normed_hbm, stand_ref, scale_ref,
    s_buf, part, came, all2, first, second, mine, others, bias, in_sem, out_sem,
    send1, recv1, send2, recv2, send3, recv3,
):
    tokens, width = q_ref.shape
    count = tokens // CHUNK
    heads = width // HEAD
    s_in = pltpu.make_async_copy(s_hbm, s_buf, in_sem)
    s_in.start()
    scatter = Scatter(n, part, came, width, send1, recv1)
    gather = Gather(n, all2, width, send2, recv2)
    stats = Stats(n, mine, others, send3, recv3)
    enter(n, gather.to)

    def attend(c):
        rows = chunk_rows(c)
        start, extent = window(c, tokens)
        window_bias(c, start, extent, segc_ref, segr_ref, bias)
        for h in range(heads):
            place = slice(HEAD * h, HEAD * (h + 1))
            scores = dot_nt(q_ref[rows, place], k_ref[pl.ds(start, extent), place])
            scores = scores * HEAD ** (-0.5) + bias[...]
            raised = jnp.exp(scores - jnp.max(scores, axis=1, keepdims=True))
            inverse = 1.0 / jnp.sum(raised, axis=1, keepdims=True)
            probs = (raised * inverse).astype(BF16)
            attended_ref[rows, place] = dot_nn(probs, v_ref[pl.ds(start, extent), place]).astype(BF16)
        part[rows, :] = dot_nn(attended_ref[rows, :], wo_ref[...]).astype(BF16)
        scatter.start(c)

        @pl.when(c >= 1)
        def _():
            scatter.relay(c - 1)

    loop(count, attend)
    scatter.relay(count - 1)
    s_in.wait()

    def middle(c):
        scatter.arrive(c)

        def piece(r):
            rows = sub_rows(c, r)
            branch = scatter.total(rows)
            branch_ref[rows, :] = branch
            entry = coef[ENTRY_B] * branch
            for i in range(s_buf.shape[0]):
                entry += coef[ENTRY + i] * s_buf[i, rows].astype(F32)
            stand_ref[rows, :] = entry
            fold_entry(entry, first, second, local_rows(r))

        loop(CHUNK // ROWS, piece)
        stats.put(c, first[...], second[...])
        stats.start(c)

    def send(c):
        standardize(c, stats, gather, first, second, stand_ref, scale_ref)

    middle(0)

    def ahead(c):
        middle(c + 1)
        send(c)

    loop(count - 1, ahead)
    send(count - 1)

    def normed_out(c):
        return pltpu.make_async_copy(
            all2.at[chunk_rows(c)], normed_hbm.at[chunk_rows(c)], out_sem.at[c]
        )

    gather.take(count, lambda c: normed_out(c).start())

    def drain(c):
        normed_out(c).wait()
        scatter.finish(c)
        stats.finish(c)
        gather.finish(c)

    loop(count, drain)


def units_kernel(
    normed_ref, grad_ref, wg_ref, wu_ref, wd_ref, hidden_ref, acts_hbm, buf, sem
):
    step, steps = pl.program_id(0), pl.num_programs(0)
    slot = lax.rem(step, 2)
    width = buf.shape[3]

    def out(at, part):
        place = (part * steps + at) * width
        return pltpu.make_async_copy(
            buf.at[lax.rem(at, 2), part],
            acts_hbm.at[:, pl.ds(pl.multiple_of(place, width), width)],
            sem.at[lax.rem(at, 2), part],
        )

    @pl.when(step >= 2)
    def _():
        out(step - 2, 0).wait()
        out(step - 2, 1).wait()

    block = normed_ref[...]
    gate = dot_nn(block, wg_ref[...])
    up = dot_nn(block, wu_ref[...])
    grad = dot_nt(grad_ref[...], wd_ref[...])
    sig = jax.nn.sigmoid(gate)
    act = gate * sig
    hidden_ref[...] = (act * up).astype(BF16)
    buf[slot, 0] = (grad * up * sig * (1.0 + gate * (1.0 - sig))).astype(BF16)
    buf[slot, 1] = (grad * act).astype(BF16)
    out(step, 0).start()
    out(step, 1).start()

    @pl.when(step == steps - 1)
    def _():
        @pl.when(step >= 1)
        def _():
            out(step - 1, 0).wait()
            out(step - 1, 1).wait()

        out(step, 0).wait()
        out(step, 1).wait()


def stats_part(part32, normed, normed_rows, part, c, first, second):
    def piece(r):
        rows = pl.ds(pl.multiple_of(r * ROWS, ROWS), ROWS)
        field = part32[rows, :]
        first[rows, :] = fold_lanes(field)
        second[rows, :] = fold_lanes(field * normed[normed_rows(r), :].astype(F32))
        part[sub_rows(c, r), :] = field.astype(BF16)

    loop(CHUNK // ROWS, piece)


def units_back_kernel(
    n, coef, acts_ref, wg_ref, wu_ref, normed_ref, stand_ref, scale_ref, c_hbm, _down, _gate_up,
    entry_ref, gb1_hbm,
    c_buf, part32, first, second, part, came, mine, others, all1, in_sem, out_sem,
    send1, recv1, send2, recv2, send3, recv3,
):
    tokens, features = normed_ref.shape
    width = entry_ref.shape[1]
    count = tokens // CHUNK
    c_in = pltpu.make_async_copy(c_hbm, c_buf, in_sem)
    c_in.start()
    scatter = Scatter(n, part, came, width, send1, recv1)
    stats = Stats(n, mine, others, send2, recv2)
    gather = Gather(n, all1, width, send3, recv3)
    enter(n, gather.to)

    def work(c):
        rows = chunk_rows(c)
        units = wg_ref.shape[1]
        part32[...] = dot_nt(acts_ref[rows, 0:units], wg_ref[...])
        part32[...] += dot_nt(acts_ref[rows, units : 2 * units], wu_ref[...])
        stats_part(part32, normed_ref, lambda r: sub_rows(c, r), part, c, first, second)
        stats.put(c, first[...], second[...])
        stats.start(c)
        scatter.start(c)

        @pl.when(c >= 1)
        def _():
            scatter.relay(c - 1)

    loop(count, work)
    scatter.relay(count - 1)
    c_in.wait()

    def middle(c):
        scatter.arrive(c)
        stats.arrive(c)
        first[...], second[...] = stats.means(c, features)

        def piece(r):
            rows = sub_rows(c, r)
            local = pl.ds(pl.multiple_of(r * ROWS, ROWS), ROWS)
            standard = stand_ref[rows, :]
            entry = repeat_lanes(scale_ref[rows, :], width) * (
                scatter.total(rows)
                - repeat_lanes(first[local, :], width)
                - standard * repeat_lanes(second[local, :], width)
            )
            entry_ref[rows, :] = entry
            grad = coef[BRANCH_E] * entry
            for i in range(c_buf.shape[0]):
                grad += coef[BRANCH + i] * c_buf[i, rows].astype(F32)
            all1[rows, gather.own()] = grad.astype(BF16)

        loop(CHUNK // ROWS, piece)
        gather.start(c)

    loop(count, middle)

    def gb1_out(c):
        return pltpu.make_async_copy(
            all1.at[chunk_rows(c)], gb1_hbm.at[chunk_rows(c)], out_sem.at[c]
        )

    gather.take(count, lambda c: gb1_out(c).start())

    def drain(c):
        gb1_out(c).wait()
        scatter.finish(c)
        stats.finish(c)
        gather.finish(c)

    loop(count, drain)


def attend_back_kernel(
    n, q_ref, k_ref, v_ref, segc_ref, segr_ref, cos_ref, sin_ref, wo_ref, wq_ref, wk_ref, wv_ref,
    wd_ref, stand_ref, scale_ref, gb1_hbm, hidden_hbm, normed_hbm, _output, _down,
    lin_ref, branch_ref, entry_ref,
    gb1_buf, hidden_buf, normed_buf, bias, dk_t, dv_t, part32, first, second,
    part1, came1, part2, came2, mine, others, in_sem,
    send1, recv1, send2, recv2, send3, recv3,
):
    tokens, width = q_ref.shape
    features = part1.shape[1]
    count = tokens // CHUNK
    heads = width // HEAD
    factor = HEAD ** (-0.5)
    down = Scatter(n, part2, came2, width, send1, recv1)
    scatter = Scatter(n, part1, came1, width, send2, recv2)
    stats = Stats(n, mine, others, send3, recv3)

    def inputs(c, slot):
        return tuple(
            pltpu.make_async_copy(source.at[chunk_rows(c)], target.at[slot], in_sem.at[i, slot])
            for i, (source, target) in enumerate(
                ((gb1_hbm, gb1_buf), (hidden_hbm, hidden_buf), (normed_hbm, normed_buf))
            )
        )

    for copy in inputs(count - 1, 0):
        copy.start()
    dk_t[...] = jnp.zeros_like(dk_t)
    dv_t[...] = jnp.zeros_like(dv_t)
    enter(n, scatter.to)

    def work(i):
        c = count - 1 - i
        slot = lax.rem(i, 2)

        @pl.when(i < count - 1)
        def _():
            for copy in inputs(c - 1, 1 - slot):
                copy.start()

        for copy in inputs(c, slot):
            copy.wait()
        rows = chunk_rows(c)
        part2[rows, :] = dot_nn(hidden_buf[slot], wd_ref[...]).astype(BF16)
        down.start(c)
        grad = dot_nt(gb1_buf[slot], wo_ref[...]).astype(BF16)
        start, extent = window(c, tokens)
        keys = pl.ds(start, extent)
        window_bias(c, start, extent, segc_ref, segr_ref, bias)
        cos_rows, sin_rows = cos_ref[rows, :], sin_ref[rows, :]
        for h in range(heads):
            place = slice(HEAD * h, HEAD * (h + 1))
            query, grad_h = q_ref[rows, place], grad[:, place]
            scores = dot_nt(query, k_ref[keys, place]) * factor + bias[...]
            raised = jnp.exp(scores - jnp.max(scores, axis=1, keepdims=True))
            inverse = 1.0 / jnp.sum(raised, axis=1, keepdims=True)
            probs = raised * inverse
            grad_probs = dot_nt(grad_h, v_ref[keys, place])
            centre = jnp.sum(probs * grad_probs, axis=1, keepdims=True)
            grad_scores = (probs * (grad_probs - centre)).astype(BF16)
            dv_t[place, keys] += dot_nn(jnp.transpose(grad_h), probs.astype(BF16))
            dk_t[place, keys] += dot_nn(jnp.transpose(query), grad_scores)
            dq = dot_nn(grad_scores, k_ref[keys, place]) * factor
            lin_ref[rows, place] = rotate(dq, cos_rows, sin_rows, -1.0).astype(BF16)
            dk = jnp.transpose(dk_t[place, rows]) * factor
            lin_ref[rows, slice(width + HEAD * h, width + HEAD * (h + 1))] = rotate(dk, cos_rows, sin_rows, -1.0).astype(BF16)
            lin_ref[rows, slice(2 * width + HEAD * h, 2 * width + HEAD * (h + 1))] = jnp.transpose(dv_t[place, rows]).astype(BF16)
        part32[...] = dot_nt(lin_ref[rows, 0:width], wq_ref[...])
        part32[...] += dot_nt(lin_ref[rows, width : 2 * width], wk_ref[...])
        part32[...] += dot_nt(lin_ref[rows, 2 * width : 3 * width], wv_ref[...])
        stats_part(
            part32,
            normed_buf.at[slot],
            lambda r: pl.ds(pl.multiple_of(r * ROWS, ROWS), ROWS),
            part1,
            c,
            first,
            second,
        )
        stats.put(c, first[...], second[...])
        stats.start(c)
        scatter.start(c)
        down.relay(c)

        @pl.when(i >= 1)
        def _():
            scatter.relay(c + 1)

    loop(count, work)
    scatter.relay(0)

    def last(i):
        c = count - 1 - i
        down.arrive(c)

        def sums(r):
            branch_ref[sub_rows(c, r), :] = down.total(sub_rows(c, r))

        loop(CHUNK // ROWS, sums)
        scatter.arrive(c)
        stats.arrive(c)
        first[...], second[...] = stats.means(c, features)

        def piece(r):
            rows = sub_rows(c, r)
            local = pl.ds(pl.multiple_of(r * ROWS, ROWS), ROWS)
            entry_ref[rows, :] = repeat_lanes(scale_ref[rows, :], width) * (
                scatter.total(rows)
                - repeat_lanes(first[local, :], width)
                - stand_ref[rows, :] * repeat_lanes(second[local, :], width)
            )

        loop(CHUNK // ROWS, piece)

    loop(count, last)

    def drain(c):
        down.finish(c)
        scatter.finish(c)
        stats.finish(c)

    loop(count, drain)


def streams_kernel(
    coef, s_ref, c_ref, b1_ref, b2_ref, e1_ref, e2_ref, _gate_up, new_ref, grad_ref, sums_ref
):
    @pl.when(pl.program_id(0) == 0)
    def _():
        sums_ref[...] = jnp.zeros_like(sums_ref)

    count = s_ref.shape[0]

    def fold(field):
        field = fold_lanes(field)
        total = field[0:8]
        for j in range(1, field.shape[0] // 8):
            total += field[8 * j : 8 * (j + 1)]
        return total

    def piece(r):
        rows = pl.ds(pl.multiple_of(r * 16, 16), 16)
        s = [s_ref[i, rows].astype(F32) for i in range(count)]
        c = [c_ref[i, rows].astype(F32) for i in range(count)]
        b1, b2, e1, e2 = b1_ref[rows, :], b2_ref[rows, :], e1_ref[rows, :], e2_ref[rows, :]
        for j in range(count):
            new = coef[BRANCH + j] * b1 + coef[OUT2 + j] * b2
            grad = coef[ENTRY + j] * e2 + coef[IN1 + j] * e1
            for k in range(count):
                new += coef[MIXED + count * k + j] * s[k]
                grad += coef[MIXED + count * j + k] * c[k]
            new_ref[rows, j, :] = new.astype(BF16)
            grad_ref[rows, j, :] = grad
        pairs = [(s[i], c[j]) for i in range(count) for j in range(count)]
        pairs += [(s[i], e1) for i in range(count)] + [(s[i], e2) for i in range(count)]
        pairs += [(c[i], b1) for i in range(count)] + [(c[i], b2) for i in range(count)]
        pairs += [(b1, e2)]
        for place, (left, right) in enumerate(pairs):
            sums_ref[place] += fold(left * right)

    loop(s_ref.shape[1] // 16, piece)


def on_device(
    n,
    streams,
    segments,
    positions,
    mix_in1,
    mix_res1,
    mix_out1,
    mix_in2,
    mix_res2,
    mix_out2,
    w_query,
    w_key,
    w_value,
    w_output,
    w_gate,
    w_up,
    w_down,
    cotangent,
):
    tokens, stream_count, width = streams.shape
    features = w_query.shape[0]
    units = w_gate.shape[1]
    chunks = tokens // CHUNK
    assert tokens == LENGTH and stream_count == 4
    any_spec = pl.BlockSpec(memory_space=pl.ANY)
    vmem = pl.BlockSpec(memory_space=pltpu.VMEM)
    smem = pl.BlockSpec(memory_space=pltpu.SMEM)

    def array(shape, dtype):
        return jax.ShapeDtypeStruct(shape, dtype)

    def dma(*shape):
        return pltpu.SemaphoreType.DMA(shape)

    def pair(lanes):
        return [dma(lanes, chunks), dma(lanes, chunks)]

    gather_sems = pair(4 if n == 4 else n - 1)
    scatter_sems = pair(6 if n == 4 else n - 1)
    stats_sems = pair(n - 1)

    def lasts(micros):
        return pl.CostEstimate(
            flops=int(micros * 1.0e9), bytes_accessed=int(micros * 3.6e6), transcendentals=0
        )

    def params(identity, mib):
        return pltpu.CompilerParams(
            collective_id=identity, has_side_effects=True, vmem_limit_bytes=mib * MIB
        )

    half = HEAD // 2
    inverse = 1.0 / 10000.0 ** (jnp.arange(half, dtype=F32) * 2.0 / HEAD)
    angles = positions.astype(F32)[:, None] * inverse[None, :]
    cosine, sine = jnp.cos(angles), jnp.sin(angles)
    cos_table = jnp.concatenate([cosine, cosine], axis=-1)
    sin_table = jnp.concatenate([-sine, sine], axis=-1)
    seg_column = jnp.broadcast_to(segments[:, None], (tokens, 128))
    seg_row = jnp.broadcast_to(segments[None, :], (8, tokens))

    def small(form, left, right):
        return jnp.einsum(form, left, right, precision=PRECISE)

    coef = jnp.concatenate(
        [
            mix_in1,
            mix_out2,
            small("ij,j->i", mix_res1, mix_in2),
            small("j,j->", mix_in2, mix_out1)[None],
            small("i,ij->j", mix_out1, mix_res2),
            small("i,i->", mix_out1, mix_in2)[None],
            small("ki,ij->kj", mix_res1, mix_res2).reshape(-1),
        ]
    )
    planes = jnp.transpose(streams, (1, 0, 2))
    cot_planes = jnp.transpose(cotangent, (1, 0, 2))

    def stats_scratch():
        return [
            pltpu.VMEM((CHUNK, 128), F32),
            pltpu.VMEM((CHUNK, 128), F32),
            pltpu.VMEM((chunks, 16, CHUNK), F32),
            pltpu.VMEM((n - 1, chunks, 16, CHUNK), F32),
        ]

    normed1, queries, keys, values, stand1, scale1, grad_branch2 = pl.pallas_call(
        functools.partial(project_kernel, n),
        name="project",
        cost_estimate=lasts(100),
        out_shape=[
            array((tokens, features), BF16),
            array((tokens, width), BF16),
            array((tokens, width), BF16),
            array((tokens, width), BF16),
            array((tokens, width), F32),
            array((tokens, 128), F32),
            array((tokens, features), BF16),
        ],
        in_specs=[smem, vmem, vmem] + [any_spec] * 5,
        out_specs=[any_spec, vmem, vmem, vmem, vmem, vmem, any_spec],
        scratch_shapes=[
            pltpu.VMEM((stream_count, tokens, width), BF16),
            pltpu.VMEM((stream_count, tokens, width), BF16),
            pltpu.VMEM((3, features, width), BF16),
            pltpu.VMEM((tokens, features), BF16),
            pltpu.VMEM((tokens, features), BF16),
        ]
        + stats_scratch()
        + [dma(2, chunks), dma(3), dma(2, chunks)]
        + gather_sems
        + gather_sems
        + stats_sems,
        compiler_params=params(0, 48),
    )(coef, cos_table, sin_table, planes, cot_planes, w_query, w_key, w_value)

    extent = window(0, tokens)[1]
    attended, branch1, normed2, stand2, scale2 = pl.pallas_call(
        functools.partial(attend_kernel, n),
        name="attend",
        cost_estimate=lasts(100),
        out_shape=[
            array((tokens, width), BF16),
            array((tokens, width), F32),
            array((tokens, features), BF16),
            array((tokens, width), F32),
            array((tokens, 128), F32),
        ],
        in_specs=[smem] + [vmem] * 6 + [any_spec],
        out_specs=[vmem, vmem, any_spec, vmem, vmem],
        scratch_shapes=[
            pltpu.VMEM((stream_count, tokens, width), BF16),
            pltpu.VMEM((tokens, features), BF16),
            pltpu.VMEM((n - 1, tokens, width), BF16),
            pltpu.VMEM((tokens, features), BF16),
        ]
        + stats_scratch()
        + [pltpu.VMEM((CHUNK, extent), F32), pltpu.SemaphoreType.DMA, dma(chunks)]
        + scatter_sems
        + gather_sems
        + stats_sems,
        compiler_params=params(1, 48),
    )(coef, queries, keys, values, seg_column, seg_row, w_output, planes)

    block = min(256, units)
    hidden, grad_acts = pl.pallas_call(
        units_kernel,
        name="units",
        cost_estimate=lasts(35),
        grid=(units // block,),
        out_shape=[array((tokens, units), BF16), array((tokens, 2 * units), BF16)],
        in_specs=[
            pl.BlockSpec((tokens, features), lambda f: (0, 0)),
            pl.BlockSpec((tokens, features), lambda f: (0, 0)),
            pl.BlockSpec((features, block), lambda f: (0, f)),
            pl.BlockSpec((features, block), lambda f: (0, f)),
            pl.BlockSpec((block, features), lambda f: (f, 0)),
        ],
        out_specs=[pl.BlockSpec((tokens, block), lambda f: (0, f)), any_spec],
        scratch_shapes=[pltpu.VMEM((2, 2, tokens, block), BF16), dma(2, 2)],
        compiler_params=pltpu.CompilerParams(vmem_limit_bytes=48 * MIB),
    )(normed2, grad_branch2, w_gate, w_up, w_down)

    def over_dp(partial, dimension):
        return lax.psum_scatter(partial, "dp", scatter_dimension=dimension, tiled=True)

    part_down = contract_rows(hidden, grad_branch2).astype(BF16)
    part_gate_up = contract_rows(normed2, grad_acts).astype(BF16)
    grad_down = over_dp(part_down, 1)
    grad_gate_up = over_dp(part_gate_up, 0)
    grad_w_down = grad_down.astype(F32)
    grad_w_gate = grad_gate_up[:, :units].astype(F32)
    grad_w_up = grad_gate_up[:, units:].astype(F32)

    grad_entry2, grad_branch1 = pl.pallas_call(
        functools.partial(units_back_kernel, n),
        name="units_back",
        cost_estimate=lasts(400),
        out_shape=[array((tokens, width), F32), array((tokens, features), BF16)],
        in_specs=[smem] + [vmem] * 6 + [any_spec] * 3,
        out_specs=[vmem, any_spec],
        scratch_shapes=[
            pltpu.VMEM((stream_count, tokens, width), BF16),
            pltpu.VMEM((CHUNK, features), F32),
            pltpu.VMEM((CHUNK, 128), F32),
            pltpu.VMEM((CHUNK, 128), F32),
            pltpu.VMEM((tokens, features), BF16),
            pltpu.VMEM((n - 1, tokens, width), BF16),
            pltpu.VMEM((chunks, 16, CHUNK), F32),
            pltpu.VMEM((n - 1, chunks, 16, CHUNK), F32),
            pltpu.VMEM((tokens, features), BF16),
            pltpu.SemaphoreType.DMA,
            dma(chunks),
        ]
        + scatter_sems
        + stats_sems
        + gather_sems,
        compiler_params=params(2, 60),
    )(
        coef, grad_acts, w_gate, w_up, normed2, stand2, scale2, cot_planes,
        part_down, part_gate_up,
    )

    part_output = contract_rows(grad_branch1, attended).astype(BF16)

    grad_lin, branch2, grad_entry1 = pl.pallas_call(
        functools.partial(attend_back_kernel, n),
        name="attend_back",
        cost_estimate=lasts(2),
        out_shape=[array((tokens, 3 * width), BF16)] + [array((tokens, width), F32)] * 2,
        in_specs=[vmem] * 14 + [any_spec] * 5,
        out_specs=[vmem] * 3,
        scratch_shapes=[
            pltpu.VMEM((2, CHUNK, features), BF16),
            pltpu.VMEM((2, CHUNK, units), BF16),
            pltpu.VMEM((2, CHUNK, features), BF16),
            pltpu.VMEM((CHUNK, extent), F32),
            pltpu.VMEM((width, tokens), F32),
            pltpu.VMEM((width, tokens), F32),
            pltpu.VMEM((CHUNK, features), F32),
            pltpu.VMEM((CHUNK, 128), F32),
            pltpu.VMEM((CHUNK, 128), F32),
            pltpu.VMEM((tokens, features), BF16),
            pltpu.VMEM((n - 1, tokens, width), BF16),
            pltpu.VMEM((tokens, features), BF16),
            pltpu.VMEM((n - 1, tokens, width), BF16),
            pltpu.VMEM((chunks, 16, CHUNK), F32),
            pltpu.VMEM((n - 1, chunks, 16, CHUNK), F32),
            dma(3, 2),
        ]
        + scatter_sems
        + scatter_sems
        + stats_sems,
        compiler_params=params(3, 60),
    )(
        queries, keys, values, seg_column, seg_row, cos_table, sin_table,
        w_output, w_query, w_key, w_value, w_down, stand1, scale1,
        grad_branch1, hidden, normed1, part_output, grad_down,
    )

    part_lin = contract_rows(normed1, grad_lin).astype(BF16)
    grad_lin_w = over_dp(jnp.concatenate([part_lin, part_output], axis=1), 0)
    grad_w_output = jnp.transpose(grad_lin_w[:, 3 * width :]).astype(F32)
    grad_w_query, grad_w_key, grad_w_value = (
        grad_lin_w[:, width * j : width * (j + 1)].astype(F32) for j in range(3)
    )

    rows = 128
    sum_count = 33
    plane_spec = pl.BlockSpec((stream_count, rows, width), lambda t: (0, t, 0))
    field_spec = pl.BlockSpec((rows, width), lambda t: (t, 0))
    stream_spec = pl.BlockSpec((rows, stream_count, width), lambda t: (t, 0, 0))
    new_streams, stream_grad, sums = pl.pallas_call(
        streams_kernel,
        name="streams",
        cost_estimate=lasts(2),
        grid=(tokens // rows,),
        out_shape=[
            array(streams.shape, BF16),
            array(streams.shape, F32),
            array((sum_count, 8, 128), F32),
        ],
        in_specs=[smem, plane_spec, plane_spec] + [field_spec] * 4 + [any_spec],
        out_specs=[
            stream_spec,
            stream_spec,
            pl.BlockSpec((sum_count, 8, 128), lambda t: (0, 0, 0)),
        ],
        compiler_params=pltpu.CompilerParams(vmem_limit_bytes=48 * MIB),
    )(coef, planes, cot_planes, branch1, branch2, grad_entry1, grad_entry2, grad_gate_up)
    sums = lax.psum(jnp.sum(sums, axis=(1, 2)), ("dp", "tensor"))
    s_c = sums[0:16].reshape(4, 4)
    s_e1, s_e2, c_b1, c_b2, b_e = sums[16:20], sums[20:24], sums[24:28], sums[28:32], sums[32]
    grad_mix_in1 = s_e1
    grad_mix_res1 = small("ik,jk->ij", s_c, mix_res2) + s_e2[:, None] * mix_in2[None, :]
    grad_mix_out1 = small("jk,k->j", mix_res2, c_b1) + mix_in2 * b_e
    grad_mix_in2 = small("ki,k->i", mix_res1, s_e2) + mix_out1 * b_e
    grad_mix_res2 = small("ki,kj->ij", mix_res1, s_c) + mix_out1[:, None] * c_b1[None, :]
    grad_mix_out2 = c_b2
    return (
        new_streams,
        stream_grad,
        grad_w_query,
        grad_w_key,
        grad_w_value,
        grad_w_output,
        grad_w_gate,
        grad_w_up,
        grad_w_down,
        grad_mix_in1,
        grad_mix_res1,
        grad_mix_out1,
        grad_mix_in2,
        grad_mix_res2,
        grad_mix_out2,
    )


def solution(mesh):
    return jax.shard_map(
        functools.partial(on_device, mesh.shape["tensor"]),
        mesh=mesh,
        in_specs=(
            P("dp", None, "tensor"),
            P("dp"),
            P("dp"),
            P(),
            P(),
            P(),
            P(),
            P(),
            P(),
            P(None, "tensor"),
            P(None, "tensor"),
            P(None, "tensor"),
            P("tensor", None),
            P(None, "tensor"),
            P(None, "tensor"),
            P("tensor", None),
            P("dp", None, "tensor"),
        ),
        out_specs=(
            P("dp", None, "tensor"),
            P("dp", None, "tensor"),
            P("dp", "tensor"),
            P("dp", "tensor"),
            P("dp", "tensor"),
            P("tensor", "dp"),
            P("dp", "tensor"),
            P("dp", "tensor"),
            P("tensor", "dp"),
            P(),
            P(),
            P(),
            P(),
            P(),
            P(),
        ),
        check_vma=False,
    )
```

```python
import functools
import math

import jax
import jax.numpy as jnp
from jax import lax
from jax.experimental import pallas as pl
from jax.experimental.pallas import tpu as pltpu
from jax.sharding import PartitionSpec as P

HEAD = 128
LENGTH = 1024
LONGEST = 512
EPS = 1e-05
PRECISE = lax.Precision.HIGHEST
MASKED = -1e30
MESH = pl.DeviceIdType.MESH
BF16 = jnp.bfloat16
F32 = jnp.float32
CHUNK = 256
ROWS = 32
MIB = 1 << 20


def inner(left, right):
    total = left[0] * right[0]
    for a, b in zip(left[1:], right[1:]):
        total += a * b
    return total


class Mixing:
    def __init__(self, refs):
        vectors = [[ref[i] for i in range(4)] for ref in refs[:4]]
        self.in1, self.out1, self.in2, self.out2 = vectors
        self.res1, self.res2 = (
            [[ref[i, j] for j in range(4)] for i in range(4)] for ref in refs[4:]
        )
        self.entry = [inner(row, self.in2) for row in self.res1]
        self.branch = [inner(self.out1, column) for column in zip(*self.res2)]
        self.across = inner(self.out1, self.in2)

    def mixed(self, k, j):
        return inner(self.res1[k], [row[j] for row in self.res2])


def contract_rows(left, right):
    return lax.dot_general(
        left, right, (((0,), (0,)), ((), ())), preferred_element_type=F32
    )


def dot_nn(left, right):
    return jnp.dot(left, right, preferred_element_type=F32)


def dot_nt(left, right):
    return lax.dot_general(
        left, right, (((1,), (1,)), ((), ())), preferred_element_type=F32
    )


def partners(n):
    me = lax.axis_index("tensor")
    if n == 4:
        both = (me + 1 - 2 * lax.rem(me, 2), lax.rem(me + 2, 4), 3 - me)
        return me, both, both
    to = tuple(lax.rem(me + k, n) for k in range(1, n))
    source = tuple(lax.rem(me + n - k, n) for k in range(1, n))
    return me, to, source


def enter(n, to):
    barrier = pltpu.get_barrier_semaphore()
    for target in to:
        pl.semaphore_signal(
            barrier, inc=1, device_id={"tensor": target}, device_id_type=MESH
        )
    pl.semaphore_wait(barrier, n - 1)


def remote(source, target, send_sem, recv_sem, device):
    return pltpu.make_async_remote_copy(
        src_ref=source,
        dst_ref=target,
        send_sem=send_sem,
        recv_sem=recv_sem,
        device_id={"tensor": device},
        device_id_type=MESH,
    )


def columns(index, width):
    return pl.ds(pl.multiple_of(index * width, 128), width)


def chunk_rows(c):
    return pl.ds(pl.multiple_of(c * CHUNK, CHUNK), CHUNK)


def half_rows(c, half):
    return pl.ds(pl.multiple_of(c * CHUNK + half * (CHUNK // 2), CHUNK // 2), CHUNK // 2)


class Gather:
    def __init__(self, n, buf, width, send_sem, recv_sem):
        self.n, self.buf, self.width = n, buf, width
        self.me, self.to, self.source = partners(n)
        self.send_sem, self.recv_sem = send_sem, recv_sem

    def own(self):
        return columns(self.me, self.width)

    def copy(self, rows, owner, k, c, target):
        view = self.buf.at[rows, columns(owner, self.width)]
        return remote(view, view, self.send_sem.at[k, c], self.recv_sem.at[k, c], target)

    def direct(self):
        return 2 if self.n == 4 else self.n - 1

    def handed(self, c):
        side, up, _ = self.to
        return (
            self.copy(half_rows(c, 0), side, 2, c, up),
            self.copy(half_rows(c, 1), up, 3, c, side),
        )

    def start(self, c):
        for k in range(self.direct()):
            self.copy(chunk_rows(c), self.me, k, c, self.to[k]).start()

    def relay(self, c):
        if self.n == 4:
            for k, copy in enumerate(self.handed(c)):
                self.copy(chunk_rows(c), self.source[k], k, c, self.to[k]).wait_recv()
                copy.start()

    def arrive(self, c):
        if self.n == 4:
            side, up, across = self.to
            self.copy(half_rows(c, 0), across, 2, c, up).wait_recv()
            self.copy(half_rows(c, 1), across, 3, c, side).wait_recv()
        else:
            for k in range(self.n - 1):
                self.copy(chunk_rows(c), self.source[k], k, c, self.to[k]).wait_recv()

    def finish(self, c):
        for k in range(self.direct()):
            self.copy(chunk_rows(c), self.me, k, c, self.to[k]).wait_send()
        if self.n == 4:
            for copy in self.handed(c):
                copy.wait_send()

    def take(self, count, work):
        self.relay(0)

        def body(c):
            @pl.when(c + 1 < count)
            def _():
                self.relay(c + 1)

            self.arrive(c)
            work(c)

        loop(count, body)


class Scatter:
    def __init__(self, n, part, came, width, send_sem, recv_sem):
        self.n, self.part, self.came, self.width = n, part, came, width
        self.me, self.to, self.source = partners(n)
        self.send_sem, self.recv_sem = send_sem, recv_sem

    def copy(self, rows, owner, slot, k, c, target):
        return remote(
            self.part.at[rows, columns(owner, self.width)],
            self.came.at[slot, rows],
            self.send_sem.at[k, c],
            self.recv_sem.at[k, c],
            target,
        )

    def first(self, c):
        if self.n != 4:
            return tuple(
                (chunk_rows(c), self.to[k], k, k, c, self.to[k]) for k in range(self.n - 1)
            )
        side, up, across = self.to
        return (
            (half_rows(c, 0), across, 2, 0, c, side),
            (half_rows(c, 1), across, 2, 1, c, up),
            (half_rows(c, 0), side, 0, 2, c, side),
            (half_rows(c, 1), up, 1, 3, c, up),
        )

    def second(self, c):
        if self.n != 4:
            return ()
        side, up, _ = self.to
        return (
            (half_rows(c, 0), up, 1, 4, c, up),
            (half_rows(c, 1), side, 0, 5, c, side),
        )

    def start(self, c):
        for place in self.first(c):
            self.copy(*place).start()

    def relay(self, c):
        second = self.second(c)
        first = self.first(c)
        for half in range(len(second)):
            self.copy(*first[half]).wait_recv()
            owner = columns(self.to[1 - half], self.width)
            base = c * CHUNK + half * (CHUNK // 2)

            def add(r):
                rows = pl.ds(pl.multiple_of(base + r * ROWS, ROWS), ROWS)
                total = self.part[rows, owner].astype(F32) + self.came[2, rows].astype(F32)
                self.part[rows, owner] = total.astype(BF16)

            loop(CHUNK // 2 // ROWS, add)
            self.copy(*second[half]).start()

    def arrive(self, c):
        places = self.first(c)
        if self.n == 4:
            places = places[2:] + self.second(c)
        for place in places:
            self.copy(*place).wait_recv()

    def finish(self, c):
        for place in self.first(c) + self.second(c):
            self.copy(*place).wait_send()

    def total(self, rows):
        total = self.part[rows, columns(self.me, self.width)].astype(F32)
        for k in range(2 if self.n == 4 else self.n - 1):
            total += self.came[k, rows].astype(F32)
        return total


class Stats:
    def __init__(self, n, mine, came, send_sem, recv_sem):
        self.n, self.mine, self.came = n, mine, came
        self.me, self.to, self.source = partners(n)
        self.send_sem, self.recv_sem = send_sem, recv_sem

    def copy(self, c, k):
        return remote(
            self.mine.at[c], self.came.at[k, c], self.send_sem.at[k, c], self.recv_sem.at[k, c], self.to[k]
        )

    def start(self, c):
        for k in range(self.n - 1):
            self.copy(c, k).start()

    def arrive(self, c):
        for k in range(self.n - 1):
            self.copy(c, k).wait_recv()

    def finish(self, c):
        for k in range(self.n - 1):
            self.copy(c, k).wait_send()

    def put(self, c, first, second):
        ones = jnp.ones((8, 128), F32)
        for place, field in ((0, first), (8, second)):
            self.mine[c, place : place + 8] = lax.dot_general(
                ones, field, (((1,), (1,)), ((), ())), precision=PRECISE, preferred_element_type=F32
            )

    def moments(self, c, width):
        pieces = [self.mine[c]] + [self.came[k, c] for k in range(self.n - 1)]
        count = float(self.n * width)
        mean = sum(piece[0:8] for piece in pieces) * (1.0 / count)
        squares = sum(
            piece[8:16] + width * (piece[0:8] * (1.0 / width) - mean) ** 2 for piece in pieces
        )
        share = jnp.full((8, 128), 0.125, F32)
        return tuple(
            lax.dot_general(
                row, share, (((0,), (0,)), ((), ())), precision=PRECISE, preferred_element_type=F32
            )
            for row in (mean, lax.rsqrt(squares * (1.0 / count) + EPS))
        )

    def means(self, c, features):
        total = self.mine[c]
        for k in range(self.n - 1):
            total += self.came[k, c]
        share = jnp.full((8, 128), 1.0 / (8 * features), F32)
        return tuple(
            lax.dot_general(
                total[place : place + 8],
                share,
                (((0,), (0,)), ((), ())),
                precision=PRECISE,
                preferred_element_type=F32,
            )
            for place in (0, 8)
        )


def loop(count, body):
    def step(i, carry):
        body(i)
        return carry

    lax.fori_loop(0, count, step, 0)


def sub_rows(c, r):
    return pl.ds(pl.multiple_of(c * CHUNK + r * ROWS, ROWS), ROWS)


def repeat_lanes(field, width):
    return jnp.concatenate([field] * (width // 128), axis=1)


def fold_lanes(field):
    total = field[:, 0:128]
    for j in range(1, field.shape[1] // 128):
        total += field[:, 128 * j : 128 * (j + 1)]
    return total


def local_rows(r):
    return pl.ds(pl.multiple_of(r * ROWS, ROWS), ROWS)


def fold_entry(entry, first, second, rows):
    first[rows, :] = fold_lanes(entry)
    centered = entry - jnp.sum(entry, axis=1, keepdims=True) * (1.0 / entry.shape[1])
    second[rows, :] = fold_lanes(centered * centered)


def standardize(c, stats, gather, first, second, stand_ref, scale_ref):
    width = stand_ref.shape[1]
    stats.arrive(c)
    first[...], second[...] = stats.moments(c, width)

    def piece(r):
        rows, local = sub_rows(c, r), local_rows(r)
        scaling = second[local, :]
        stand = (stand_ref[rows, :] - repeat_lanes(first[local, :], width)) * repeat_lanes(
            scaling, width
        )
        stand_ref[rows, :] = stand
        scale_ref[rows, :] = scaling
        gather.buf[rows, gather.own()] = stand.astype(BF16)

    loop(CHUNK // ROWS, piece)
    gather.start(c)


def rotate(field, cos_rows, sin_rows, sign):
    turned = pltpu.roll(field, HEAD // 2, 1)
    return field * cos_rows + (sign * turned) * sin_rows


def spread(row):
    share = jnp.full((8, 128), 0.125, F32)
    return lax.dot_general(
        jnp.broadcast_to(row, (8, 128)),
        share,
        (((0,), (0,)), ((), ())),
        precision=PRECISE,
        preferred_element_type=F32,
    )


def project_kernel(
    n, in1, out2, positions_ref, segments_ref, s_hbm, c_hbm, wq_hbm, wk_hbm, wv_hbm,
    normed_hbm, q_ref, k_ref, v_ref, stand_ref, scale_ref, gb2_hbm, planes_hbm, cot_hbm,
    cos_ref, sin_ref, segc_ref, segr_ref,
    s_buf, c_buf, planes, cot_planes, w_buf, all1, all2, first, second, mine, others,
    in_sem, w_sem, out_sem, send1, recv1, send2, recv2, send3, recv3,
):
    tokens, streams, width = s_buf.shape
    count = tokens // CHUNK
    heads = width // HEAD
    weights = (wq_hbm, wk_hbm, wv_hbm)

    def s_in(c):
        return pltpu.make_async_copy(
            s_hbm.at[chunk_rows(c)], s_buf.at[chunk_rows(c)], in_sem.at[0, c]
        )

    def c_in(c):
        return pltpu.make_async_copy(
            c_hbm.at[chunk_rows(c)], c_buf.at[chunk_rows(c)], in_sem.at[1, c]
        )

    def w_in(j):
        return pltpu.make_async_copy(weights[j], w_buf.at[j], w_sem.at[j])

    def out(c, i):
        rows = chunk_rows(c)
        source, target = (
            (all1.at[rows], normed_hbm.at[rows]),
            (all2.at[rows], gb2_hbm.at[rows]),
            (planes.at[:, rows], planes_hbm.at[:, rows]),
            (cot_planes.at[:, rows], cot_hbm.at[:, rows]),
        )[i]
        return pltpu.make_async_copy(source, target, out_sem.at[i, c])

    c_in(0).start()
    loop(count, lambda c: s_in(c).start())
    loop(count - 1, lambda c: c_in(c + 1).start())
    for j in range(3):
        w_in(j).start()
    gather = Gather(n, all1, width, send1, recv1)
    incoming = Gather(n, all2, width, send2, recv2)
    stats = Stats(n, mine, others, send3, recv3)
    enter(n, gather.to)

    def mix(buf, weight, target, rows):
        block = buf[rows].astype(F32)
        total = None
        for i in range(streams):
            field = block[:, i, :]
            target[i, rows] = field.astype(BF16)
            total = weight[i] * field if total is None else total + weight[i] * field
        return total

    def entry(c):
        s_in(c).wait()

        def piece(r):
            field = mix(s_buf, in1, planes, sub_rows(c, r))
            stand_ref[sub_rows(c, r), :] = field
            fold_entry(field, first, second, local_rows(r))

        loop(CHUNK // ROWS, piece)
        stats.put(c, first[...], second[...])
        stats.start(c)

    def send(c):
        standardize(c, stats, gather, first, second, stand_ref, scale_ref)

    def grad(c):
        c_in(c).wait()

        def piece(r):
            rows = sub_rows(c, r)
            all2[rows, incoming.own()] = mix(c_buf, out2, cot_planes, rows).astype(BF16)

        loop(CHUNK // ROWS, piece)
        incoming.start(c)
        out(c, 3).start()

    grad(0)
    entry(0)

    def ahead(c):
        entry(c + 1)
        send(c)

    loop(count - 1, ahead)
    grad(1)
    send(count - 1)
    loop(count - 2, lambda c: grad(c + 2))

    segr_ref[...] = jnp.concatenate(
        [
            jnp.broadcast_to(segments_ref[a : a + 1, :].astype(F32), (8, 128))
            for a in range(tokens // 128)
        ],
        axis=1,
    )
    lane = lax.broadcasted_iota(jnp.int32, (128, 128), 1)
    exponent = lax.rem(lane, HEAD // 2).astype(F32) * (-2.0 / HEAD * math.log(10000.0))
    inverse = jnp.exp(exponent)
    for a in range(tokens // 128):
        rows = slice(128 * a, 128 * (a + 1))
        segc_ref[rows, :] = spread(segments_ref[a : a + 1, :].astype(F32))
        angles = spread(positions_ref[a : a + 1, :].astype(F32)) * inverse
        cos_ref[rows, :] = jnp.cos(angles)
        sine = jnp.sin(angles)
        sin_ref[rows, :] = jnp.where(lane < HEAD // 2, -sine, sine)
    for j in range(3):
        w_in(j).wait()

    def work(c):
        for i in (0, 2):
            out(c, i).start()
        rows = chunk_rows(c)
        block = all1[rows, :]
        cos_rows, sin_rows = cos_ref[rows, :], sin_ref[rows, :]
        for j, target in ((0, q_ref), (1, k_ref)):
            lin = dot_nn(block, w_buf[j])
            for h in range(heads):
                place = slice(HEAD * h, HEAD * (h + 1))
                target[rows, place] = rotate(lin[:, place], cos_rows, sin_rows, 1.0).astype(BF16)
        v_ref[rows, :] = dot_nn(block, w_buf[2]).astype(BF16)
        incoming.relay(c)

    gather.take(count, work)

    def end(c):
        incoming.arrive(c)
        out(c, 1).start()

    loop(count, end)

    def drain(c):
        for i in range(4):
            out(c, i).wait()
        stats.finish(c)
        gather.finish(c)
        incoming.finish(c)

    loop(count, drain)


def window_bias(c, start, extent, segc_ref, segr_ref, bias):
    def part(r):
        rows = pl.ds(pl.multiple_of(r * ROWS, ROWS), ROWS)
        row = c * CHUNK + r * ROWS + lax.broadcasted_iota(jnp.int32, (ROWS, extent), 0)
        column = start + lax.broadcasted_iota(jnp.int32, (ROWS, extent), 1)
        same = segc_ref[sub_rows(c, r), 0:1] == segr_ref[0:1, pl.ds(start, extent)]
        bias[rows, :] = jnp.where((row >= column) & same, 0.0, MASKED)

    loop(CHUNK // ROWS, part)


def window(c, tokens):
    extent = min(tokens, CHUNK * (-(-(LONGEST - 1) // CHUNK) + 1))
    back = extent // CHUNK - 1
    return pl.multiple_of(jnp.maximum(c - back, 0) * CHUNK, CHUNK), extent


def attend_kernel(
    n, in1, out1, in2, out2, res1, res2, q_ref, k_ref, v_ref, segc_ref, segr_ref, wo_ref,
    s_hbm, gb2_hbm, wg_hbm, wu_hbm, wd_hbm,
    attended_ref, branch_ref, normed_hbm, stand_ref, scale_ref, hidden_hbm, acts_hbm,
    s_buf, gb2_buf, wg_buf, wu_buf, wd_buf, hidden_buf, gate_buf, up_buf,
    part, came, all2, first, second, mine, others, bias,
    s_sem, gb2_sem, w_sem, normed_sem, out_sem, send1, recv1, send2, recv2, send3, recv3,
):
    tokens, width = q_ref.shape
    units = wg_buf.shape[1]
    count = tokens // CHUNK
    heads = width // HEAD
    block = min(units, 512)
    mixing = Mixing((in1, out1, in2, out2, res1, res2))

    def s_in(c):
        slot = lax.rem(c, 2)
        return pltpu.make_async_copy(s_hbm.at[:, chunk_rows(c)], s_buf.at[slot], s_sem.at[slot])

    def gb2_in(c):
        slot = lax.rem(c, 2)
        return pltpu.make_async_copy(gb2_hbm.at[chunk_rows(c)], gb2_buf.at[slot], gb2_sem.at[slot])

    def normed_out(c):
        return pltpu.make_async_copy(
            all2.at[chunk_rows(c)], normed_hbm.at[chunk_rows(c)], normed_sem.at[c]
        )

    def outs(c):
        slot, rows = lax.rem(c, 2), chunk_rows(c)
        return tuple(
            pltpu.make_async_copy(buf.at[slot], target, out_sem.at[i, slot])
            for i, (buf, target) in enumerate(
                (
                    (hidden_buf, hidden_hbm.at[rows]),
                    (gate_buf, acts_hbm.at[rows, 0:units]),
                    (up_buf, acts_hbm.at[rows, units : 2 * units]),
                )
            )
        )

    weights = tuple(
        pltpu.make_async_copy(source, target, w_sem.at[i])
        for i, (source, target) in enumerate(
            ((wg_hbm, wg_buf), (wu_hbm, wu_buf), (wd_hbm, wd_buf))
        )
    )
    s_in(0).start()
    gb2_in(0).start()
    for copy in weights:
        copy.start()
    scatter = Scatter(n, part, came, width, send1, recv1)
    gather = Gather(n, all2, width, send2, recv2)
    stats = Stats(n, mine, others, send3, recv3)
    enter(n, gather.to)

    def attend(c):
        rows = chunk_rows(c)
        start, extent = window(c, tokens)
        window_bias(c, start, extent, segc_ref, segr_ref, bias)
        for h in range(heads):
            place = slice(HEAD * h, HEAD * (h + 1))
            scores = dot_nt(q_ref[rows, place], k_ref[pl.ds(start, extent), place])
            scores = scores * HEAD ** (-0.5) + bias[...]
            raised = jnp.exp(scores - jnp.max(scores, axis=1, keepdims=True))
            inverse = 1.0 / jnp.sum(raised, axis=1, keepdims=True)
            probs = (raised * inverse).astype(BF16)
            attended_ref[rows, place] = dot_nn(probs, v_ref[pl.ds(start, extent), place]).astype(BF16)
        part[rows, :] = dot_nn(attended_ref[rows, :], wo_ref[...]).astype(BF16)

    def middle(c):
        @pl.when(c + 1 < count)
        def _():
            s_in(c + 1).start()

        s_in(c).wait()
        slot = lax.rem(c, 2)
        scatter.arrive(c)

        def piece(r):
            rows = sub_rows(c, r)
            branch = scatter.total(rows)
            branch_ref[rows, :] = branch
            entry = mixing.across * branch
            for i in range(s_buf.shape[1]):
                entry += mixing.entry[i] * s_buf[slot, i, local_rows(r)].astype(F32)
            stand_ref[rows, :] = entry
            fold_entry(entry, first, second, local_rows(r))

        loop(CHUNK // ROWS, piece)
        stats.put(c, first[...], second[...])
        stats.start(c)

    def send(c):
        standardize(c, stats, gather, first, second, stand_ref, scale_ref)

    def work(c):
        normed_out(c).start()
        slot = lax.rem(c, 2)

        @pl.when(c + 1 < count)
        def _():
            gb2_in(c + 1).start()

        @pl.when(c >= 2)
        def _():
            for copy in outs(c - 2):
                copy.wait()

        gb2_in(c).wait()

        def piece(f):
            place = columns(f, block)
            gate = dot_nn(all2[chunk_rows(c), :], wg_buf[:, place])
            up = dot_nn(all2[chunk_rows(c), :], wu_buf[:, place])
            grad = dot_nt(gb2_buf[slot], wd_buf[place, :])
            sig = jax.nn.sigmoid(gate)
            act = gate * sig
            hidden_buf[slot, :, place] = (act * up).astype(BF16)
            gate_buf[slot, :, place] = (grad * up * sig * (1.0 + gate * (1.0 - sig))).astype(BF16)
            up_buf[slot, :, place] = (grad * act).astype(BF16)

        loop(units // block, piece)
        for copy in outs(c):
            copy.start()

    def attend_send(c):
        attend(c)
        scatter.start(c)

        @pl.when(c >= 1)
        def _():
            scatter.relay(c - 1)

    end = count - 1
    loop(end, attend_send)
    middle(0)
    attend(end)
    send(0)
    scatter.start(end)
    scatter.relay(end - 1)

    def ahead(c):
        middle(c)
        send(c)

    loop(end - 2, lambda c: ahead(c + 1))
    scatter.relay(end)
    middle(end - 1)
    gather.relay(0)
    send(end - 1)
    for copy in weights:
        copy.wait()
    gather.arrive(0)
    work(0)
    middle(end)
    gather.relay(1)
    send(end)

    def rest(c):
        gather.arrive(c)
        work(c)

        @pl.when(c + 1 < count)
        def _():
            gather.relay(c + 1)

    loop(end, lambda c: rest(c + 1))
    for c in range(max(count - 2, 0), count):
        for copy in outs(c):
            copy.wait()

    def drain(c):
        normed_out(c).wait()
        scatter.finish(c)
        stats.finish(c)
        gather.finish(c)

    loop(count, drain)


def stats_part(part32, normed, normed_rows, part, c, first, second):
    def piece(r):
        rows = pl.ds(pl.multiple_of(r * ROWS, ROWS), ROWS)
        field = part32[rows, :]
        first[rows, :] = fold_lanes(field)
        second[rows, :] = fold_lanes(field * normed[normed_rows(r), :].astype(F32))
        part[sub_rows(c, r), :] = field.astype(BF16)

    loop(CHUNK // ROWS, piece)


def units_back_kernel(
    n, in1, out1, in2, out2, res1, res2, acts_ref, wg_ref, wu_ref, normed_ref, stand_ref, scale_ref, c_hbm, _down, _gate_up,
    entry_ref, gb1_hbm,
    c_buf, part32, first, second, part, came, mine, others, all1, in_sem, out_sem,
    send1, recv1, send2, recv2, send3, recv3,
):
    tokens, features = normed_ref.shape
    width = entry_ref.shape[1]
    count = tokens // CHUNK
    mixing = Mixing((in1, out1, in2, out2, res1, res2))
    c_in = pltpu.make_async_copy(c_hbm, c_buf, in_sem)
    c_in.start()
    scatter = Scatter(n, part, came, width, send1, recv1)
    stats = Stats(n, mine, others, send2, recv2)
    gather = Gather(n, all1, width, send3, recv3)
    enter(n, gather.to)

    def work(c):
        rows = chunk_rows(c)
        units = wg_ref.shape[1]
        part32[...] = dot_nt(acts_ref[rows, 0:units], wg_ref[...])
        part32[...] += dot_nt(acts_ref[rows, units : 2 * units], wu_ref[...])
        stats_part(part32, normed_ref, lambda r: sub_rows(c, r), part, c, first, second)
        stats.put(c, first[...], second[...])
        stats.start(c)
        scatter.start(c)

        @pl.when(c >= 1)
        def _():
            scatter.relay(c - 1)

    loop(count, work)
    scatter.relay(count - 1)
    c_in.wait()

    def middle(c):
        scatter.arrive(c)
        stats.arrive(c)
        first[...], second[...] = stats.means(c, features)

        def piece(r):
            rows = sub_rows(c, r)
            local = pl.ds(pl.multiple_of(r * ROWS, ROWS), ROWS)
            standard = stand_ref[rows, :]
            entry = repeat_lanes(scale_ref[rows, :], width) * (
                scatter.total(rows)
                - repeat_lanes(first[local, :], width)
                - standard * repeat_lanes(second[local, :], width)
            )
            entry_ref[rows, :] = entry
            grad = mixing.across * entry
            for i in range(c_buf.shape[0]):
                grad += mixing.branch[i] * c_buf[i, rows].astype(F32)
            all1[rows, gather.own()] = grad.astype(BF16)

        loop(CHUNK // ROWS, piece)
        gather.start(c)

    loop(count, middle)

    def gb1_out(c):
        return pltpu.make_async_copy(
            all1.at[chunk_rows(c)], gb1_hbm.at[chunk_rows(c)], out_sem.at[c]
        )

    gather.take(count, lambda c: gb1_out(c).start())

    def drain(c):
        gb1_out(c).wait()
        scatter.finish(c)
        stats.finish(c)
        gather.finish(c)

    loop(count, drain)


def attend_back_kernel(
    n, q_ref, k_ref, v_ref, segc_ref, segr_ref, cos_ref, sin_ref, wo_ref, wq_ref, wk_ref, wv_ref,
    wd_ref, stand_ref, scale_ref, gb1_hbm, hidden_hbm, normed_hbm, _output, _down,
    lin_ref, branch_ref, entry_ref,
    gb1_buf, hidden_buf, normed_buf, bias, dk_t, dv_t, part32, first, second,
    part1, came1, part2, came2, mine, others, in_sem,
    send1, recv1, send2, recv2, send3, recv3,
):
    tokens, width = q_ref.shape
    features = part1.shape[1]
    count = tokens // CHUNK
    heads = width // HEAD
    factor = HEAD ** (-0.5)
    down = Scatter(n, part2, came2, width, send1, recv1)
    scatter = Scatter(n, part1, came1, width, send2, recv2)
    stats = Stats(n, mine, others, send3, recv3)

    def inputs(c, slot):
        return tuple(
            pltpu.make_async_copy(source.at[chunk_rows(c)], target.at[slot], in_sem.at[i, slot])
            for i, (source, target) in enumerate(
                ((gb1_hbm, gb1_buf), (hidden_hbm, hidden_buf), (normed_hbm, normed_buf))
            )
        )

    for copy in inputs(count - 1, 0):
        copy.start()
    dk_t[...] = jnp.zeros_like(dk_t)
    dv_t[...] = jnp.zeros_like(dv_t)
    enter(n, scatter.to)

    def work(i):
        c = count - 1 - i
        slot = lax.rem(i, 2)

        @pl.when(i < count - 1)
        def _():
            for copy in inputs(c - 1, 1 - slot):
                copy.start()

        for copy in inputs(c, slot):
            copy.wait()
        rows = chunk_rows(c)
        part2[rows, :] = dot_nn(hidden_buf[slot], wd_ref[...]).astype(BF16)
        down.start(c)
        grad = dot_nt(gb1_buf[slot], wo_ref[...]).astype(BF16)
        start, extent = window(c, tokens)
        keys = pl.ds(start, extent)
        window_bias(c, start, extent, segc_ref, segr_ref, bias)
        cos_rows, sin_rows = cos_ref[rows, :], sin_ref[rows, :]
        for h in range(heads):
            place = slice(HEAD * h, HEAD * (h + 1))
            query, grad_h = q_ref[rows, place], grad[:, place]
            scores = dot_nt(query, k_ref[keys, place]) * factor + bias[...]
            raised = jnp.exp(scores - jnp.max(scores, axis=1, keepdims=True))
            inverse = 1.0 / jnp.sum(raised, axis=1, keepdims=True)
            probs = raised * inverse
            grad_probs = dot_nt(grad_h, v_ref[keys, place])
            centre = jnp.sum(probs * grad_probs, axis=1, keepdims=True)
            grad_scores = (probs * (grad_probs - centre)).astype(BF16)
            dv_t[place, keys] += dot_nn(jnp.transpose(grad_h), probs.astype(BF16))
            dk_t[place, keys] += dot_nn(jnp.transpose(query), grad_scores)
            dq = dot_nn(grad_scores, k_ref[keys, place]) * factor
            lin_ref[rows, place] = rotate(dq, cos_rows, sin_rows, -1.0).astype(BF16)
            dk = jnp.transpose(dk_t[place, rows]) * factor
            lin_ref[rows, slice(width + HEAD * h, width + HEAD * (h + 1))] = rotate(dk, cos_rows, sin_rows, -1.0).astype(BF16)
            lin_ref[rows, slice(2 * width + HEAD * h, 2 * width + HEAD * (h + 1))] = jnp.transpose(dv_t[place, rows]).astype(BF16)
        part32[...] = dot_nt(lin_ref[rows, 0:width], wq_ref[...])
        part32[...] += dot_nt(lin_ref[rows, width : 2 * width], wk_ref[...])
        part32[...] += dot_nt(lin_ref[rows, 2 * width : 3 * width], wv_ref[...])
        stats_part(
            part32,
            normed_buf.at[slot],
            lambda r: pl.ds(pl.multiple_of(r * ROWS, ROWS), ROWS),
            part1,
            c,
            first,
            second,
        )
        stats.put(c, first[...], second[...])
        stats.start(c)
        scatter.start(c)
        down.relay(c)

        @pl.when(i >= 1)
        def _():
            scatter.relay(c + 1)

    loop(count, work)
    scatter.relay(0)

    def last(i):
        c = count - 1 - i
        down.arrive(c)

        def sums(r):
            branch_ref[sub_rows(c, r), :] = down.total(sub_rows(c, r))

        loop(CHUNK // ROWS, sums)
        scatter.arrive(c)
        stats.arrive(c)
        first[...], second[...] = stats.means(c, features)

        def piece(r):
            rows = sub_rows(c, r)
            local = pl.ds(pl.multiple_of(r * ROWS, ROWS), ROWS)
            entry_ref[rows, :] = repeat_lanes(scale_ref[rows, :], width) * (
                scatter.total(rows)
                - repeat_lanes(first[local, :], width)
                - stand_ref[rows, :] * repeat_lanes(second[local, :], width)
            )

        loop(CHUNK // ROWS, piece)

    loop(count, last)

    def drain(c):
        down.finish(c)
        scatter.finish(c)
        stats.finish(c)

    loop(count, drain)


def streams_kernel(
    in1, out1, in2, out2, res1, res2, s_ref, c_ref, b1_ref, b2_ref, e1_ref, e2_ref, new_ref, grad_ref, sums_ref
):
    @pl.when(pl.program_id(0) == 0)
    def _():
        sums_ref[...] = jnp.zeros_like(sums_ref)

    count = s_ref.shape[0]
    mixing = Mixing((in1, out1, in2, out2, res1, res2))
    mixed = [[mixing.mixed(k, j) for j in range(count)] for k in range(count)]

    def fold(field):
        field = fold_lanes(field)
        total = field[0:8]
        for j in range(1, field.shape[0] // 8):
            total += field[8 * j : 8 * (j + 1)]
        return total

    def piece(r):
        rows = pl.ds(pl.multiple_of(r * 16, 16), 16)
        s = [s_ref[i, rows].astype(F32) for i in range(count)]
        c = [c_ref[i, rows].astype(F32) for i in range(count)]
        b1, b2, e1, e2 = b1_ref[rows, :], b2_ref[rows, :], e1_ref[rows, :], e2_ref[rows, :]
        for j in range(count):
            new = mixing.branch[j] * b1 + mixing.out2[j] * b2
            grad = mixing.entry[j] * e2 + mixing.in1[j] * e1
            for k in range(count):
                new += mixed[k][j] * s[k]
                grad += mixed[j][k] * c[k]
            new_ref[rows, j, :] = new.astype(BF16)
            grad_ref[rows, j, :] = grad
        pairs = [(s[i], c[j]) for i in range(count) for j in range(count)]
        pairs += [(s[i], e1) for i in range(count)] + [(s[i], e2) for i in range(count)]
        pairs += [(c[i], b1) for i in range(count)] + [(c[i], b2) for i in range(count)]
        pairs += [(b1, e2)]
        for place, (left, right) in enumerate(pairs):
            sums_ref[place] += fold(left * right)

    loop(s_ref.shape[1] // 16, piece)


PLANES = 4
CORES = 2
SUMS = 33
SUM_ROWS = 40


def finish_kernel(
    n, first_hbm, last_hbm, sums_ref,
    q_out, k_out, v_out, o_out, sums_out,
    own, core, right, left, by_core, by_plane, by_tensor,
    own_sem, core_send, core_recv, right_send, right_recv, left_send, left_recv, sum_send, sum_recv,
):
    _, pieces, height, width = own.shape
    me = lax.axis_index("dp")
    plane, mine = lax.div(me, CORES), lax.rem(me, CORES)
    partner = me + 1 - 2 * mine
    here, peers, peer_source = partners(n)
    planes_to = [lax.rem(plane + k, PLANES) for k in range(1, PLANES)]
    planes_from = [lax.rem(plane + PLANES - k, PLANES) for k in range(1, PLANES)]

    def dp_at(position):
        return position * CORES + mine

    def rows_of(position, half):
        return pl.ds(pl.multiple_of((position * CORES + half) * height, height), height)

    def block(position, half, p):
        if p < pieces - 1:
            return first_hbm.at[rows_of(position, half), p * width : (p + 1) * width]
        return last_hbm.at[rows_of(position, half)]

    def over_dp(source, target, send_sem, recv_sem, device):
        return pltpu.make_async_remote_copy(
            src_ref=source, dst_ref=target, send_sem=send_sem, recv_sem=recv_sem,
            device_id={"dp": device}, device_id_type=MESH,
        )

    def own_in(position, p):
        return pltpu.make_async_copy(
            block(position, mine, p), own.at[position, p], own_sem.at[position, p]
        )

    def core_in(position, p):
        return over_dp(
            block(position, 1 - mine, p), core.at[position, p],
            core_send.at[position, p], core_recv.at[position, p], partner,
        )

    def rightward(step, p):
        return over_dp(
            own.at[lax.rem(plane + PLANES - step, PLANES), p], right.at[step - 1, p],
            right_send.at[step - 1, p], right_recv.at[step - 1, p], lax.rem(me + CORES, PLANES * CORES),
        )

    def leftward(step, p):
        return over_dp(
            own.at[lax.rem(plane + step, PLANES), p], left.at[step - 1, p],
            left_send.at[step - 1, p], left_recv.at[step - 1, p],
            lax.rem(me + (PLANES - 1) * CORES, PLANES * CORES),
        )

    order = (3, 0, 2, 1)
    for position in order:
        for p in range(pieces):
            own_in(position, p).start()

    barrier = pltpu.get_barrier_semaphore()
    pl.semaphore_signal(barrier, inc=1, device_id={"dp": partner}, device_id_type=MESH)
    for k in range(PLANES - 1):
        pl.semaphore_signal(
            barrier, inc=1, device_id={"dp": dp_at(planes_to[k])}, device_id_type=MESH
        )
    for k in range(n - 1):
        pl.semaphore_signal(barrier, inc=1, device_id={"tensor": peers[k]}, device_id_type=MESH)
    pl.semaphore_wait(barrier, 1 + PLANES - 1 + n - 1)

    by_core[mine] = jnp.zeros((SUM_ROWS, 128), F32)
    by_core[mine, 0:SUMS] = jnp.sum(sums_ref[...], axis=1)
    over_dp(
        by_core.at[mine], by_core.at[mine], sum_send.at[0], sum_recv.at[0], partner
    ).start()
    for position in order:
        for p in range(pieces):
            core_in(position, p).start()
    over_dp(
        by_core.at[1 - mine], by_core.at[1 - mine], sum_send.at[0], sum_recv.at[0], partner
    ).wait_recv()
    by_plane[plane] = by_core[0] + by_core[1]

    def plane_sums(k, at):
        return over_dp(
            by_plane.at[at], by_plane.at[at], sum_send.at[1 + k], sum_recv.at[1 + k],
            dp_at(planes_to[k]),
        )

    def tensor_sums(k, at):
        at = by_tensor.at[at]
        return remote(at, at, sum_send.at[PLANES + k], sum_recv.at[PLANES + k], peers[k])

    for k in range(PLANES - 1):
        plane_sums(k, plane).start()

    def gather_pair(position):
        def piece(p):
            pltpu.make_async_copy(
                own.at[position, p], own.at[position, p], own_sem.at[position, p]
            ).wait()
            over_dp(
                core.at[position, p], core.at[position, p],
                core_send.at[position, p], core_recv.at[position, p], partner,
            ).wait_recv()
            add(own.at[position, p], core.at[position, p])

        loop(pieces, piece)

    def add(target, source):
        def part(r):
            rows = local_rows(r)
            target[rows, :] = (target[rows, :].astype(F32) + source[rows, :].astype(F32)).astype(BF16)

        loop(height // ROWS, part)

    def send_step(step):
        def piece(p):
            @pl.when(plane <= step - 1)
            def _():
                if step >= 2:

                    @pl.when(plane >= 1)
                    def _():
                        rightward(step - 1, p).wait_recv()
                        add(own.at[lax.rem(plane + PLANES - step, PLANES), p], right.at[step - 2, p])

                rightward(step, p).start()

            @pl.when(plane >= PLANES - step)
            def _():
                if step >= 2:

                    @pl.when(plane <= PLANES - 2)
                    def _():
                        leftward(step - 1, p).wait_recv()
                        add(own.at[lax.rem(plane + step, PLANES), p], left.at[step - 2, p])

                leftward(step, p).start()

        loop(pieces, piece)

    gather_pair(3)
    gather_pair(0)
    send_step(1)
    gather_pair(2)
    gather_pair(1)
    for k in range(PLANES - 1):
        plane_sums(k, planes_from[k]).wait_recv()
    by_tensor[here] = sum((by_plane[i] for i in range(1, PLANES)), by_plane[0])
    for k in range(n - 1):
        tensor_sums(k, here).start()
    for step in range(2, PLANES):
        send_step(step)
    for k in range(n - 1):
        tensor_sums(k, peer_source[k]).wait_recv()
    sums_out[...] = sum((by_tensor[i] for i in range(1, n)), by_tensor[0])

    for p, target in enumerate((q_out, k_out, v_out, o_out)):
        steps = PLANES - 2

        @pl.when(plane >= 1)
        def _():
            rightward(PLANES - 1, p).wait_recv()

        @pl.when(plane <= PLANES - 2)
        def _():
            leftward(PLANES - 1, p).wait_recv()

        total = own[plane, p].astype(F32)
        total += jnp.where(plane >= 1, right[steps, p].astype(F32), 0.0)
        total += jnp.where(plane <= PLANES - 2, left[steps, p].astype(F32), 0.0)
        target[...] = total if p < pieces - 1 else jnp.transpose(total)

    over_dp(by_core.at[mine], by_core.at[mine], sum_send.at[0], sum_recv.at[0], partner).wait_send()
    for k in range(PLANES - 1):
        plane_sums(k, plane).wait_send()
    for k in range(n - 1):
        tensor_sums(k, here).wait_send()
    for p in range(pieces):
        for position in range(PLANES):
            core_in(position, p).wait_send()
        for step in range(1, PLANES):

            @pl.when(plane <= step - 1)
            def _():
                rightward(step, p).wait_send()

            @pl.when(plane >= PLANES - step)
            def _():
                leftward(step, p).wait_send()


def on_device(
    n,
    replicas,
    streams,
    segments,
    positions,
    mix_in1,
    mix_res1,
    mix_out1,
    mix_in2,
    mix_res2,
    mix_out2,
    w_query,
    w_key,
    w_value,
    w_output,
    w_gate,
    w_up,
    w_down,
    cotangent,
):
    tokens, stream_count, width = streams.shape
    features = w_query.shape[0]
    units = w_gate.shape[1]
    chunks = tokens // CHUNK
    assert tokens == LENGTH and stream_count == 4
    any_spec = pl.BlockSpec(memory_space=pl.ANY)
    vmem = pl.BlockSpec(memory_space=pltpu.VMEM)
    smem = pl.BlockSpec(memory_space=pltpu.SMEM)

    def array(shape, dtype):
        return jax.ShapeDtypeStruct(shape, dtype)

    def dma(*shape):
        return pltpu.SemaphoreType.DMA(shape)

    def pair(lanes):
        return [dma(lanes, chunks), dma(lanes, chunks)]

    gather_sems = pair(4 if n == 4 else n - 1)
    scatter_sems = pair(6 if n == 4 else n - 1)
    stats_sems = pair(n - 1)

    def lasts(micros):
        return pl.CostEstimate(
            flops=int(micros * 1.0e9), bytes_accessed=int(micros * 3.6e6), transcendentals=0
        )

    def params(identity, mib):
        return pltpu.CompilerParams(
            collective_id=identity, has_side_effects=True, vmem_limit_bytes=mib * MIB
        )

    def small(form, left, right):
        return jnp.einsum(form, left, right, precision=PRECISE)

    mixes = (mix_in1, mix_out1, mix_in2, mix_out2, mix_res1, mix_res2)

    def stats_scratch():
        return [
            pltpu.VMEM((CHUNK, 128), F32),
            pltpu.VMEM((CHUNK, 128), F32),
            pltpu.VMEM((chunks, 16, CHUNK), F32),
            pltpu.VMEM((n - 1, chunks, 16, CHUNK), F32),
        ]

    (
        normed1, queries, keys, values, stand1, scale1, grad_branch2, planes, cot_planes,
        cos_table, sin_table, seg_column, seg_row,
    ) = pl.pallas_call(
        functools.partial(project_kernel, n),
        name="project",
        cost_estimate=lasts(100),
        out_shape=[
            array((tokens, features), BF16),
            array((tokens, width), BF16),
            array((tokens, width), BF16),
            array((tokens, width), BF16),
            array((tokens, width), F32),
            array((tokens, 128), F32),
            array((tokens, features), BF16),
            array((stream_count, tokens, width), BF16),
            array((stream_count, tokens, width), BF16),
            array((tokens, HEAD), F32),
            array((tokens, HEAD), F32),
            array((tokens, 128), F32),
            array((8, tokens), F32),
        ],
        in_specs=[smem, smem, vmem, vmem] + [any_spec] * 5,
        out_specs=[any_spec] + [vmem] * 5 + [any_spec] * 3 + [vmem] * 4,
        scratch_shapes=[
            pltpu.VMEM((tokens, stream_count, width), BF16),
            pltpu.VMEM((tokens, stream_count, width), BF16),
            pltpu.VMEM((stream_count, tokens, width), BF16),
            pltpu.VMEM((stream_count, tokens, width), BF16),
            pltpu.VMEM((3, features, width), BF16),
            pltpu.VMEM((tokens, features), BF16),
            pltpu.VMEM((tokens, features), BF16),
        ]
        + stats_scratch()
        + [dma(2, chunks), dma(3), dma(4, chunks)]
        + gather_sems
        + gather_sems
        + stats_sems,
        compiler_params=params(0, 56),
    )(
        mix_in1, mix_out2,
        positions.reshape(tokens // 128, 128), segments.reshape(tokens // 128, 128),
        streams, cotangent, w_query, w_key, w_value,
    )

    extent = window(0, tokens)[1]
    attended, branch1, normed2, stand2, scale2, hidden, grad_acts = pl.pallas_call(
        functools.partial(attend_kernel, n),
        name="attend",
        cost_estimate=lasts(100),
        out_shape=[
            array((tokens, width), BF16),
            array((tokens, width), F32),
            array((tokens, features), BF16),
            array((tokens, width), F32),
            array((tokens, 128), F32),
            array((tokens, units), BF16),
            array((tokens, 2 * units), BF16),
        ],
        in_specs=[smem] * 6 + [vmem] * 6 + [any_spec] * 5,
        out_specs=[vmem, vmem, any_spec, vmem, vmem, any_spec, any_spec],
        scratch_shapes=[
            pltpu.VMEM((2, stream_count, CHUNK, width), BF16),
            pltpu.VMEM((2, CHUNK, features), BF16),
            pltpu.VMEM((features, units), BF16),
            pltpu.VMEM((features, units), BF16),
            pltpu.VMEM((units, features), BF16),
            pltpu.VMEM((2, CHUNK, units), BF16),
            pltpu.VMEM((2, CHUNK, units), BF16),
            pltpu.VMEM((2, CHUNK, units), BF16),
            pltpu.VMEM((tokens, features), BF16),
            pltpu.VMEM((n - 1, tokens, width), BF16),
            pltpu.VMEM((tokens, features), BF16),
        ]
        + stats_scratch()
        + [pltpu.VMEM((CHUNK, extent), F32), dma(2), dma(2), dma(3), dma(chunks), dma(3, 2)]
        + scatter_sems
        + gather_sems
        + stats_sems,
        compiler_params=params(1, 62),
    )(
        *mixes, queries, keys, values, seg_column, seg_row, w_output, planes,
        grad_branch2, w_gate, w_up, w_down,
    )

    def over_dp(partial, dimension):
        return lax.psum_scatter(partial, "dp", scatter_dimension=dimension, tiled=True)

    part_down = contract_rows(hidden, grad_branch2).astype(BF16)
    part_gate_up = contract_rows(normed2, grad_acts).astype(BF16)
    grad_down = over_dp(part_down, 1)
    grad_gate_up = over_dp(part_gate_up, 0)
    grad_w_down = grad_down.astype(F32)
    grad_w_gate = grad_gate_up[:, :units].astype(F32)
    grad_w_up = grad_gate_up[:, units:].astype(F32)

    grad_entry2, grad_branch1 = pl.pallas_call(
        functools.partial(units_back_kernel, n),
        name="units_back",
        cost_estimate=lasts(400),
        out_shape=[array((tokens, width), F32), array((tokens, features), BF16)],
        in_specs=[smem] * 6 + [vmem] * 6 + [any_spec] * 3,
        out_specs=[vmem, any_spec],
        scratch_shapes=[
            pltpu.VMEM((stream_count, tokens, width), BF16),
            pltpu.VMEM((CHUNK, features), F32),
            pltpu.VMEM((CHUNK, 128), F32),
            pltpu.VMEM((CHUNK, 128), F32),
            pltpu.VMEM((tokens, features), BF16),
            pltpu.VMEM((n - 1, tokens, width), BF16),
            pltpu.VMEM((chunks, 16, CHUNK), F32),
            pltpu.VMEM((n - 1, chunks, 16, CHUNK), F32),
            pltpu.VMEM((tokens, features), BF16),
            pltpu.SemaphoreType.DMA,
            dma(chunks),
        ]
        + scatter_sems
        + stats_sems
        + gather_sems,
        compiler_params=params(2, 60),
    )(
        *mixes, grad_acts, w_gate, w_up, normed2, stand2, scale2, cot_planes,
        part_down, part_gate_up,
    )

    part_output = contract_rows(grad_branch1, attended).astype(BF16)

    grad_lin, branch2, grad_entry1 = pl.pallas_call(
        functools.partial(attend_back_kernel, n),
        name="attend_back",
        cost_estimate=lasts(2),
        out_shape=[array((tokens, 3 * width), BF16)] + [array((tokens, width), F32)] * 2,
        in_specs=[vmem] * 14 + [any_spec] * 5,
        out_specs=[vmem] * 3,
        scratch_shapes=[
            pltpu.VMEM((2, CHUNK, features), BF16),
            pltpu.VMEM((2, CHUNK, units), BF16),
            pltpu.VMEM((2, CHUNK, features), BF16),
            pltpu.VMEM((CHUNK, extent), F32),
            pltpu.VMEM((width, tokens), F32),
            pltpu.VMEM((width, tokens), F32),
            pltpu.VMEM((CHUNK, features), F32),
            pltpu.VMEM((CHUNK, 128), F32),
            pltpu.VMEM((CHUNK, 128), F32),
            pltpu.VMEM((tokens, features), BF16),
            pltpu.VMEM((n - 1, tokens, width), BF16),
            pltpu.VMEM((tokens, features), BF16),
            pltpu.VMEM((n - 1, tokens, width), BF16),
            pltpu.VMEM((chunks, 16, CHUNK), F32),
            pltpu.VMEM((n - 1, chunks, 16, CHUNK), F32),
            dma(3, 2),
        ]
        + scatter_sems
        + scatter_sems
        + stats_sems,
        compiler_params=params(3, 60),
    )(
        queries, keys, values, seg_column, seg_row, cos_table, sin_table,
        w_output, w_query, w_key, w_value, w_down, stand1, scale1,
        grad_branch1, hidden, normed1, part_output, grad_down,
    )

    part_lin = contract_rows(normed1, grad_lin).astype(BF16)

    rows = 128
    plane_spec = pl.BlockSpec((stream_count, rows, width), lambda t: (0, t, 0))
    field_spec = pl.BlockSpec((rows, width), lambda t: (t, 0))
    stream_spec = pl.BlockSpec((rows, stream_count, width), lambda t: (t, 0, 0))
    new_streams, stream_grad, sums = pl.pallas_call(
        streams_kernel,
        name="streams",
        cost_estimate=lasts(2),
        grid=(tokens // rows,),
        out_shape=[
            array(streams.shape, BF16),
            array(streams.shape, F32),
            array((SUMS, 8, 128), F32),
        ],
        in_specs=[smem] * 6 + [plane_spec, plane_spec] + [field_spec] * 4,
        out_specs=[
            stream_spec,
            stream_spec,
            pl.BlockSpec((SUMS, 8, 128), lambda t: (0, 0, 0)),
        ],
        compiler_params=pltpu.CompilerParams(vmem_limit_bytes=48 * MIB),
    )(*mixes, planes, cot_planes, branch1, branch2, grad_entry1, grad_entry2)
    height = features // replicas
    if replicas == PLANES * CORES and stream_count == 4:
        steps = PLANES - 1
        grad_w_query, grad_w_key, grad_w_value, grad_w_output, sums = pl.pallas_call(
            functools.partial(finish_kernel, n),
            name="finish",
            cost_estimate=lasts(2),
            out_shape=[array((height, width), F32)] * 3
            + [array((width, height), F32), array((SUM_ROWS, 128), F32)],
            in_specs=[any_spec, any_spec, vmem],
            out_specs=[vmem] * 5,
            scratch_shapes=[
                pltpu.VMEM((PLANES, 4, height, width), BF16),
                pltpu.VMEM((PLANES, 4, height, width), BF16),
                pltpu.VMEM((steps, 4, height, width), BF16),
                pltpu.VMEM((steps, 4, height, width), BF16),
                pltpu.VMEM((CORES, SUM_ROWS, 128), F32),
                pltpu.VMEM((PLANES, SUM_ROWS, 128), F32),
                pltpu.VMEM((n, SUM_ROWS, 128), F32),
                dma(PLANES, 4),
                dma(PLANES, 4),
                dma(PLANES, 4),
                dma(steps, 4),
                dma(steps, 4),
                dma(steps, 4),
                dma(steps, 4),
                dma(PLANES + n - 1),
                dma(PLANES + n - 1),
            ],
            compiler_params=params(4, 48),
        )(part_lin, part_output, sums)
        sums = jnp.sum(sums[:SUMS], axis=1)
    else:
        grad_w_query, grad_w_key, grad_w_value = (
            over_dp(part_lin[:, width * j : width * (j + 1)], 0).astype(F32) for j in range(3)
        )
        grad_w_output = jnp.transpose(over_dp(part_output, 0)).astype(F32)
        sums = lax.psum(jnp.sum(sums, axis=(1, 2)), ("dp", "tensor"))
    s_c = sums[0:16].reshape(4, 4)
    s_e1, s_e2, c_b1, c_b2, b_e = sums[16:20], sums[20:24], sums[24:28], sums[28:32], sums[32]
    grad_mix_in1 = s_e1
    grad_mix_res1 = small("ik,jk->ij", s_c, mix_res2) + s_e2[:, None] * mix_in2[None, :]
    grad_mix_out1 = small("jk,k->j", mix_res2, c_b1) + mix_in2 * b_e
    grad_mix_in2 = small("ki,k->i", mix_res1, s_e2) + mix_out1 * b_e
    grad_mix_res2 = small("ki,kj->ij", mix_res1, s_c) + mix_out1[:, None] * c_b1[None, :]
    grad_mix_out2 = c_b2
    return (
        new_streams,
        stream_grad,
        grad_w_query,
        grad_w_key,
        grad_w_value,
        grad_w_output,
        grad_w_gate,
        grad_w_up,
        grad_w_down,
        grad_mix_in1,
        grad_mix_res1,
        grad_mix_out1,
        grad_mix_in2,
        grad_mix_res2,
        grad_mix_out2,
    )


def solution(mesh):
    return jax.shard_map(
        functools.partial(on_device, mesh.shape["tensor"], mesh.shape["dp"]),
        mesh=mesh,
        in_specs=(
            P("dp", None, "tensor"),
            P("dp"),
            P("dp"),
            P(),
            P(),
            P(),
            P(),
            P(),
            P(),
            P(None, "tensor"),
            P(None, "tensor"),
            P(None, "tensor"),
            P("tensor", None),
            P(None, "tensor"),
            P(None, "tensor"),
            P("tensor", None),
            P("dp", None, "tensor"),
        ),
        out_specs=(
            P("dp", None, "tensor"),
            P("dp", None, "tensor"),
            P("dp", "tensor"),
            P("dp", "tensor"),
            P("dp", "tensor"),
            P("tensor", "dp"),
            P("dp", "tensor"),
            P("dp", "tensor"),
            P("tensor", "dp"),
            P(),
            P(),
            P(),
            P(),
            P(),
            P(),
        ),
        check_vma=False,
    )
```

```python
import functools
import math

import jax
import jax.numpy as jnp
from jax import lax
from jax.experimental import pallas as pl
from jax.experimental.pallas import tpu as pltpu
from jax.sharding import PartitionSpec as P

HEAD = 128
LENGTH = 1024
LONGEST = 512
EPS = 1e-05
PRECISE = lax.Precision.HIGHEST
MASKED = -1e30
MESH = pl.DeviceIdType.MESH
BF16 = jnp.bfloat16
F32 = jnp.float32
CHUNK = 256
ROWS = 32
MIB = 1 << 20


def inner(left, right):
    total = left[0] * right[0]
    for a, b in zip(left[1:], right[1:]):
        total += a * b
    return total


class Mixing:
    def __init__(self, refs):
        vectors = [[ref[i] for i in range(4)] for ref in refs[:4]]
        self.in1, self.out1, self.in2, self.out2 = vectors
        self.res1, self.res2 = (
            [[ref[i, j] for j in range(4)] for i in range(4)] for ref in refs[4:]
        )
        self.entry = [inner(row, self.in2) for row in self.res1]
        self.branch = [inner(self.out1, column) for column in zip(*self.res2)]
        self.across = inner(self.out1, self.in2)

    def mixed(self, k, j):
        return inner(self.res1[k], [row[j] for row in self.res2])


def contract_rows(left, right):
    return lax.dot_general(
        left, right, (((0,), (0,)), ((), ())), preferred_element_type=F32
    )


def dot_nn(left, right):
    return jnp.dot(left, right, preferred_element_type=F32)


def dot_nt(left, right):
    return lax.dot_general(
        left, right, (((1,), (1,)), ((), ())), preferred_element_type=F32
    )


def partners(n):
    me = lax.axis_index("tensor")
    if n == 4:
        both = (me + 1 - 2 * lax.rem(me, 2), lax.rem(me + 2, 4), 3 - me)
        return me, both, both
    to = tuple(lax.rem(me + k, n) for k in range(1, n))
    source = tuple(lax.rem(me + n - k, n) for k in range(1, n))
    return me, to, source


def enter(n, to):
    barrier = pltpu.get_barrier_semaphore()
    for target in to:
        pl.semaphore_signal(
            barrier, inc=1, device_id={"tensor": target}, device_id_type=MESH
        )
    pl.semaphore_wait(barrier, n - 1)


def remote(source, target, send_sem, recv_sem, device):
    return pltpu.make_async_remote_copy(
        src_ref=source,
        dst_ref=target,
        send_sem=send_sem,
        recv_sem=recv_sem,
        device_id={"tensor": device},
        device_id_type=MESH,
    )


def columns(index, width):
    return pl.ds(pl.multiple_of(index * width, 128), width)


def chunk_rows(c):
    return pl.ds(pl.multiple_of(c * CHUNK, CHUNK), CHUNK)


def half_rows(c, half):
    return pl.ds(pl.multiple_of(c * CHUNK + half * (CHUNK // 2), CHUNK // 2), CHUNK // 2)


class Gather:
    def __init__(self, n, buf, width, send_sem, recv_sem):
        self.n, self.buf, self.width = n, buf, width
        self.me, self.to, self.source = partners(n)
        self.send_sem, self.recv_sem = send_sem, recv_sem

    def own(self):
        return columns(self.me, self.width)

    def copy(self, rows, owner, k, c, target):
        view = self.buf.at[rows, columns(owner, self.width)]
        return remote(view, view, self.send_sem.at[k, c], self.recv_sem.at[k, c], target)

    def direct(self):
        return 2 if self.n == 4 else self.n - 1

    def handed(self, c):
        side, up, _ = self.to
        return (
            self.copy(half_rows(c, 0), side, 2, c, up),
            self.copy(half_rows(c, 1), up, 3, c, side),
        )

    def start(self, c):
        for k in range(self.direct()):
            self.copy(chunk_rows(c), self.me, k, c, self.to[k]).start()

    def relay(self, c):
        if self.n == 4:
            for k, copy in enumerate(self.handed(c)):
                self.copy(chunk_rows(c), self.source[k], k, c, self.to[k]).wait_recv()
                copy.start()

    def arrive(self, c):
        if self.n == 4:
            side, up, across = self.to
            self.copy(half_rows(c, 0), across, 2, c, up).wait_recv()
            self.copy(half_rows(c, 1), across, 3, c, side).wait_recv()
        else:
            for k in range(self.n - 1):
                self.copy(chunk_rows(c), self.source[k], k, c, self.to[k]).wait_recv()

    def finish(self, c):
        for k in range(self.direct()):
            self.copy(chunk_rows(c), self.me, k, c, self.to[k]).wait_send()
        if self.n == 4:
            for copy in self.handed(c):
                copy.wait_send()


class Scatter:
    def __init__(self, n, part, came, width, send_sem, recv_sem):
        self.n, self.part, self.came, self.width = n, part, came, width
        self.me, self.to, self.source = partners(n)
        self.send_sem, self.recv_sem = send_sem, recv_sem

    def copy(self, rows, owner, slot, k, c, target):
        return remote(
            self.part.at[rows, columns(owner, self.width)],
            self.came.at[slot, rows],
            self.send_sem.at[k, c],
            self.recv_sem.at[k, c],
            target,
        )

    def first(self, c):
        if self.n != 4:
            return tuple(
                (chunk_rows(c), self.to[k], k, k, c, self.to[k]) for k in range(self.n - 1)
            )
        side, up, across = self.to
        return (
            (half_rows(c, 0), across, 2, 0, c, side),
            (half_rows(c, 1), across, 2, 1, c, up),
            (half_rows(c, 0), side, 0, 2, c, side),
            (half_rows(c, 1), up, 1, 3, c, up),
        )

    def second(self, c):
        if self.n != 4:
            return ()
        side, up, _ = self.to
        return (
            (half_rows(c, 0), up, 1, 4, c, up),
            (half_rows(c, 1), side, 0, 5, c, side),
        )

    def start(self, c):
        for place in self.first(c):
            self.copy(*place).start()

    def relay(self, c):
        second = self.second(c)
        first = self.first(c)
        for half in range(len(second)):
            self.copy(*first[half]).wait_recv()
            owner = columns(self.to[1 - half], self.width)
            base = c * CHUNK + half * (CHUNK // 2)

            def add(r):
                rows = pl.ds(pl.multiple_of(base + r * ROWS, ROWS), ROWS)
                total = self.part[rows, owner].astype(F32) + self.came[2, rows].astype(F32)
                self.part[rows, owner] = total.astype(BF16)

            loop(CHUNK // 2 // ROWS, add)
            self.copy(*second[half]).start()

    def arrive(self, c):
        places = self.first(c)
        if self.n == 4:
            places = places[2:] + self.second(c)
        for place in places:
            self.copy(*place).wait_recv()

    def finish(self, c):
        for place in self.first(c) + self.second(c):
            self.copy(*place).wait_send()

    def total(self, rows):
        total = self.part[rows, columns(self.me, self.width)].astype(F32)
        for k in range(2 if self.n == 4 else self.n - 1):
            total += self.came[k, rows].astype(F32)
        return total


class Stats:
    def __init__(self, n, mine, came, send_sem, recv_sem):
        self.n, self.mine, self.came = n, mine, came
        self.me, self.to, self.source = partners(n)
        self.send_sem, self.recv_sem = send_sem, recv_sem

    def copy(self, c, k):
        return remote(
            self.mine.at[c], self.came.at[k, c], self.send_sem.at[k, c], self.recv_sem.at[k, c], self.to[k]
        )

    def start(self, c):
        for k in range(self.n - 1):
            self.copy(c, k).start()

    def arrive(self, c):
        for k in range(self.n - 1):
            self.copy(c, k).wait_recv()

    def finish(self, c):
        for k in range(self.n - 1):
            self.copy(c, k).wait_send()

    def put(self, c, first, second):
        ones = jnp.ones((8, 128), F32)
        for place, field in ((0, first), (8, second)):
            self.mine[c, place : place + 8] = lax.dot_general(
                ones, field, (((1,), (1,)), ((), ())), precision=PRECISE, preferred_element_type=F32
            )

    def moments(self, c, width):
        pieces = [self.mine[c]] + [self.came[k, c] for k in range(self.n - 1)]
        count = float(self.n * width)
        mean = sum(piece[0:8] for piece in pieces) * (1.0 / count)
        squares = sum(
            piece[8:16] + width * (piece[0:8] * (1.0 / width) - mean) ** 2 for piece in pieces
        )
        share = jnp.full((8, 128), 0.125, F32)
        return tuple(
            lax.dot_general(
                row, share, (((0,), (0,)), ((), ())), precision=PRECISE, preferred_element_type=F32
            )
            for row in (mean, lax.rsqrt(squares * (1.0 / count) + EPS))
        )

    def means(self, c, features):
        total = self.mine[c]
        for k in range(self.n - 1):
            total += self.came[k, c]
        share = jnp.full((8, 128), 1.0 / (8 * features), F32)
        return tuple(
            lax.dot_general(
                total[place : place + 8],
                share,
                (((0,), (0,)), ((), ())),
                precision=PRECISE,
                preferred_element_type=F32,
            )
            for place in (0, 8)
        )


def loop(count, body):
    def step(i, carry):
        body(i)
        return carry

    lax.fori_loop(0, count, step, 0)


def sub_rows(c, r):
    return pl.ds(pl.multiple_of(c * CHUNK + r * ROWS, ROWS), ROWS)


def repeat_lanes(field, width):
    return jnp.concatenate([field] * (width // 128), axis=1)


def fold_lanes(field):
    total = field[:, 0:128]
    for j in range(1, field.shape[1] // 128):
        total += field[:, 128 * j : 128 * (j + 1)]
    return total


def local_rows(r):
    return pl.ds(pl.multiple_of(r * ROWS, ROWS), ROWS)


def fold_entry(entry, first, second, rows):
    first[rows, :] = fold_lanes(entry)
    centered = entry - jnp.sum(entry, axis=1, keepdims=True) * (1.0 / entry.shape[1])
    second[rows, :] = fold_lanes(centered * centered)


def standardize(c, stats, gather, first, second, stand_ref, scale_ref):
    width = stand_ref.shape[1]
    stats.arrive(c)
    first[...], second[...] = stats.moments(c, width)

    def piece(r):
        rows, local = sub_rows(c, r), local_rows(r)
        scaling = second[local, :]
        stand = (stand_ref[rows, :] - repeat_lanes(first[local, :], width)) * repeat_lanes(
            scaling, width
        )
        stand_ref[rows, :] = stand
        scale_ref[rows, :] = scaling
        gather.buf[rows, gather.own()] = stand.astype(BF16)

    loop(CHUNK // ROWS, piece)
    gather.start(c)


def rotate(field, cos_rows, sin_rows, sign):
    turned = pltpu.roll(field, HEAD // 2, 1)
    return field * cos_rows + (sign * turned) * sin_rows


def spread(row):
    share = jnp.full((8, 128), 0.125, F32)
    return lax.dot_general(
        jnp.broadcast_to(row, (8, 128)),
        share,
        (((0,), (0,)), ((), ())),
        precision=PRECISE,
        preferred_element_type=F32,
    )


def project_kernel(
    n, in1, out2, positions_ref, segments_ref, s_hbm, c_hbm, wq_hbm, wk_hbm, wv_hbm,
    normed_hbm, q_ref, k_ref, v_ref, stand_ref, scale_ref, gb2_hbm, cot_hbm,
    cos_ref, sin_ref, segc_ref, segr_ref,
    s_buf, c_buf, cot_planes, w_buf, all1, all2, first, second, mine, others,
    in_sem, w_sem, out_sem, send1, recv1, send2, recv2, send3, recv3,
):
    streams, tokens, width = s_buf.shape
    count = tokens // CHUNK
    heads = width // HEAD
    weights = (wq_hbm, wk_hbm, wv_hbm)

    def s_in(c):
        return pltpu.make_async_copy(
            s_hbm.at[:, chunk_rows(c)], s_buf.at[:, chunk_rows(c)], in_sem.at[0, c]
        )

    def c_in(c):
        return pltpu.make_async_copy(
            c_hbm.at[chunk_rows(c)], c_buf.at[chunk_rows(c)], in_sem.at[1, c]
        )

    def w_in(j):
        return pltpu.make_async_copy(weights[j], w_buf.at[j], w_sem.at[j])

    def out(c, i):
        rows = chunk_rows(c)
        source, target = (
            (all1.at[rows], normed_hbm.at[rows]),
            (all2.at[rows], gb2_hbm.at[rows]),
            (cot_planes.at[:, rows], cot_hbm.at[:, rows]),
        )[i]
        return pltpu.make_async_copy(source, target, out_sem.at[i, c])

    loop(count, lambda c: s_in(c).start())
    loop(count, lambda c: c_in(c).start())
    for j in range(3):
        w_in(j).start()
    gather = Gather(n, all1, width, send1, recv1)
    incoming = Gather(n, all2, width, send2, recv2)
    stats = Stats(n, mine, others, send3, recv3)
    enter(n, gather.to)

    def entry(c):
        s_in(c).wait()

        def piece(r):
            rows = sub_rows(c, r)
            field = in1[0] * s_buf[0, rows].astype(F32)
            for i in range(1, streams):
                field += in1[i] * s_buf[i, rows].astype(F32)
            stand_ref[sub_rows(c, r), :] = field
            fold_entry(field, first, second, local_rows(r))

        loop(CHUNK // ROWS, piece)
        stats.put(c, first[...], second[...])
        stats.start(c)

    def send(c):
        standardize(c, stats, gather, first, second, stand_ref, scale_ref)

    def grad(c):
        c_in(c).wait()

        def piece(r):
            rows = sub_rows(c, r)
            block = c_buf[rows].astype(F32)
            total = None
            for i in range(streams):
                field = block[:, i, :]
                cot_planes[i, rows] = field.astype(BF16)
                total = out2[i] * field if total is None else total + out2[i] * field
            all2[rows, incoming.own()] = total.astype(BF16)

        loop(CHUNK // ROWS, piece)
        incoming.start(c)
        out(c, 2).start()

    entry(0)

    def ahead(c):
        entry(c + 1)
        send(c)

    loop(count - 1, ahead)
    send(count - 1)
    grad(0)
    gather.relay(0)
    grad(1)
    gather.relay(1)
    incoming.relay(0)

    segr_ref[...] = jnp.concatenate(
        [
            jnp.broadcast_to(segments_ref[a : a + 1, :].astype(F32), (8, 128))
            for a in range(tokens // 128)
        ],
        axis=1,
    )
    lane = lax.broadcasted_iota(jnp.int32, (128, 128), 1)
    exponent = lax.rem(lane, HEAD // 2).astype(F32) * (-2.0 / HEAD * math.log(10000.0))
    inverse = jnp.exp(exponent)
    for a in range(tokens // 128):
        rows = slice(128 * a, 128 * (a + 1))
        segc_ref[rows, :] = spread(segments_ref[a : a + 1, :].astype(F32))
        angles = spread(positions_ref[a : a + 1, :].astype(F32)) * inverse
        cos_ref[rows, :] = jnp.cos(angles)
        sine = jnp.sin(angles)
        sin_ref[rows, :] = jnp.where(lane < HEAD // 2, -sine, sine)
    grad(2)
    gather.relay(2)
    grad(3)
    gather.relay(3)
    incoming.relay(1)
    for j in range(3):
        w_in(j).wait()

    def work(c):
        gather.arrive(c)
        out(c, 0).start()
        rows = chunk_rows(c)
        block = all1[rows, :]
        cos_rows, sin_rows = cos_ref[rows, :], sin_ref[rows, :]
        for j, target in ((0, q_ref), (1, k_ref)):
            lin = dot_nn(block, w_buf[j])
            for h in range(heads):
                place = slice(HEAD * h, HEAD * (h + 1))
                target[rows, place] = rotate(lin[:, place], cos_rows, sin_rows, 1.0).astype(BF16)
        v_ref[rows, :] = dot_nn(block, w_buf[2]).astype(BF16)

        @pl.when(c + 2 < count)
        def _():
            incoming.relay(c + 2)

    loop(count, work)

    def end(c):
        incoming.arrive(c)
        out(c, 1).start()

    loop(count, end)

    def drain(c):
        for i in range(3):
            out(c, i).wait()
        stats.finish(c)
        gather.finish(c)
        incoming.finish(c)

    loop(count, drain)


def window_bias(c, start, extent, segc_ref, segr_ref, bias):
    def part(r):
        rows = pl.ds(pl.multiple_of(r * ROWS, ROWS), ROWS)
        row = c * CHUNK + r * ROWS + lax.broadcasted_iota(jnp.int32, (ROWS, extent), 0)
        column = start + lax.broadcasted_iota(jnp.int32, (ROWS, extent), 1)
        same = segc_ref[sub_rows(c, r), 0:1] == segr_ref[0:1, pl.ds(start, extent)]
        bias[rows, :] = jnp.where((row >= column) & same, 0.0, MASKED)

    loop(CHUNK // ROWS, part)


def window(c, tokens):
    extent = min(tokens, CHUNK * (-(-(LONGEST - 1) // CHUNK) + 1))
    back = extent // CHUNK - 1
    return pl.multiple_of(jnp.maximum(c - back, 0) * CHUNK, CHUNK), extent


def attend_kernel(
    n, in1, out1, in2, out2, res1, res2, q_ref, k_ref, v_ref, segc_ref, segr_ref, wo_ref,
    s_hbm, gb2_hbm, wg_hbm, wu_hbm, wd_hbm,
    attended_ref, branch_ref, normed_hbm, stand_ref, scale_ref, hidden_hbm, acts_hbm, grads_hbm,
    s_buf, gb2_buf, wg_buf, wu_buf, wd_buf, hidden_buf, gate_buf, up_buf,
    part, came, all2, first, second, mine, others, bias,
    s_sem, gb2_sem, grad_sem, w_sem, normed_sem, out_sem, send1, recv1, send2, recv2, send3, recv3,
):
    tokens, width = q_ref.shape
    units = wg_buf.shape[1]
    count = tokens // CHUNK
    heads = width // HEAD
    block = min(units, 512)
    mixing = Mixing((in1, out1, in2, out2, res1, res2))

    def s_in(c):
        slot = lax.rem(c, 2)
        return pltpu.make_async_copy(s_hbm.at[:, chunk_rows(c)], s_buf.at[slot], s_sem.at[slot])

    def gb2_in(c):
        slot = lax.rem(c, 2)
        return pltpu.make_async_copy(gb2_hbm.at[chunk_rows(c)], gb2_buf.at[slot], gb2_sem.at[slot])

    def grads_out(c):
        slot = lax.rem(c, 2)
        return pltpu.make_async_copy(
            gate_buf.at[slot], grads_hbm.at[chunk_rows(c)], grad_sem.at[0, slot]
        )

    def grads_in(c):
        slot = lax.rem(c, 2)
        return pltpu.make_async_copy(
            grads_hbm.at[chunk_rows(c)], gb2_buf.at[slot, :, 0:units], grad_sem.at[1, slot]
        )

    def normed_out(c):
        return pltpu.make_async_copy(
            all2.at[chunk_rows(c)], normed_hbm.at[chunk_rows(c)], normed_sem.at[c]
        )

    def outs(c):
        slot, rows = lax.rem(c, 2), chunk_rows(c)
        return tuple(
            pltpu.make_async_copy(buf.at[slot], target, out_sem.at[i, slot])
            for i, (buf, target) in enumerate(
                (
                    (hidden_buf, hidden_hbm.at[rows]),
                    (gate_buf, acts_hbm.at[rows, 0:units]),
                    (up_buf, acts_hbm.at[rows, units : 2 * units]),
                )
            )
        )

    weights = tuple(
        pltpu.make_async_copy(source, target, w_sem.at[i])
        for i, (source, target) in enumerate(
            ((wd_hbm, wd_buf), (wg_hbm, wg_buf), (wu_hbm, wu_buf))
        )
    )
    s_in(0).start()
    gb2_in(0).start()
    gb2_in(1).start()
    for copy in weights:
        copy.start()
    scatter = Scatter(n, part, came, width, send1, recv1)
    gather = Gather(n, all2, width, send2, recv2)
    stats = Stats(n, mine, others, send3, recv3)
    enter(n, gather.to)

    def attend(c):
        rows = chunk_rows(c)
        start, extent = window(c, tokens)
        window_bias(c, start, extent, segc_ref, segr_ref, bias)
        for h in range(heads):
            place = slice(HEAD * h, HEAD * (h + 1))
            scores = dot_nt(q_ref[rows, place], k_ref[pl.ds(start, extent), place])
            scores = scores * HEAD ** (-0.5) + bias[...]
            raised = jnp.exp(scores - jnp.max(scores, axis=1, keepdims=True))
            inverse = 1.0 / jnp.sum(raised, axis=1, keepdims=True)
            probs = (raised * inverse).astype(BF16)
            attended_ref[rows, place] = dot_nn(probs, v_ref[pl.ds(start, extent), place]).astype(BF16)
        part[rows, :] = dot_nn(attended_ref[rows, :], wo_ref[...]).astype(BF16)

    def middle(c):
        @pl.when(c + 1 < count)
        def _():
            s_in(c + 1).start()

        s_in(c).wait()
        slot = lax.rem(c, 2)
        scatter.arrive(c)

        def piece(r):
            rows = sub_rows(c, r)
            branch = scatter.total(rows)
            branch_ref[rows, :] = branch
            entry = mixing.across * branch
            for i in range(s_buf.shape[1]):
                entry += mixing.entry[i] * s_buf[slot, i, local_rows(r)].astype(F32)
            stand_ref[rows, :] = entry
            fold_entry(entry, first, second, local_rows(r))

        loop(CHUNK // ROWS, piece)
        stats.put(c, first[...], second[...])
        stats.start(c)

    def send(c):
        standardize(c, stats, gather, first, second, stand_ref, scale_ref)

    def work(c):
        gather.arrive(c)
        normed_out(c).start()
        slot = lax.rem(c, 2)

        @pl.when(c >= 2)
        def _():
            for copy in outs(c - 2):
                copy.wait()

        grads_in(c).wait()

        def piece(f):
            place = columns(f, block)
            gate = dot_nn(all2[chunk_rows(c), :], wg_buf[:, place])
            up = dot_nn(all2[chunk_rows(c), :], wu_buf[:, place])
            grad = gb2_buf[slot, :, place].astype(F32)
            sig = jax.nn.sigmoid(gate)
            act = gate * sig
            hidden_buf[slot, :, place] = (act * up).astype(BF16)
            gate_buf[slot, :, place] = (grad * up * sig * (1.0 + gate * (1.0 - sig))).astype(BF16)
            up_buf[slot, :, place] = (grad * act).astype(BF16)

        loop(units // block, piece)
        for copy in outs(c):
            copy.start()

        @pl.when(c + 2 < count)
        def _():
            grads_in(c + 2).start()
            gather.relay(c + 2)

    def grads(c):
        slot = lax.rem(c, 2)
        if c >= 2:
            grads_out(c - 2).wait()
        gb2_in(c).wait()

        def piece(f):
            place = columns(f, block)
            gate_buf[slot, :, place] = dot_nt(gb2_buf[slot], wd_buf[place, :]).astype(BF16)

        loop(units // block, piece)
        grads_out(c).start()
        if c + 2 < count:
            gb2_in(c + 2).start()

    def attend_send(c):
        attend(c)
        scatter.start(c)

        @pl.when(c >= 1)
        def _():
            scatter.relay(c - 1)

    loop(count, attend_send)
    middle(0)
    weights[0].wait()
    grads(0)
    scatter.relay(3)
    middle(1)
    send(0)
    grads(1)
    middle(2)
    send(1)
    grads(2)
    middle(3)
    grads(3)
    gather.relay(0)
    send(2)
    gather.relay(1)
    send(3)
    grads_out(2).wait()
    grads_out(3).wait()
    grads_in(0).start()
    grads_in(1).start()
    weights[1].wait()
    weights[2].wait()
    loop(count, work)
    for c in range(max(count - 2, 0), count):
        for copy in outs(c):
            copy.wait()

    def drain(c):
        normed_out(c).wait()
        scatter.finish(c)
        stats.finish(c)
        gather.finish(c)

    loop(count, drain)


def stats_part(part32, normed, normed_rows, part, c, first, second):
    def piece(r):
        rows = pl.ds(pl.multiple_of(r * ROWS, ROWS), ROWS)
        field = part32[rows, :]
        first[rows, :] = fold_lanes(field)
        second[rows, :] = fold_lanes(field * normed[normed_rows(r), :].astype(F32))
        part[sub_rows(c, r), :] = field.astype(BF16)

    loop(CHUNK // ROWS, piece)


def units_back_kernel(
    n, in1, out1, in2, out2, res1, res2, acts_ref, wg_ref, wu_ref, normed_ref, stand_ref, scale_ref, c_hbm, _down, _gate_up,
    entry_ref, gb1_hbm,
    c_buf, part32, first, second, part, came, mine, others, all1, in_sem, out_sem,
    send1, recv1, send2, recv2, send3, recv3,
):
    tokens, features = normed_ref.shape
    width = entry_ref.shape[1]
    count = tokens // CHUNK
    mixing = Mixing((in1, out1, in2, out2, res1, res2))
    c_in = pltpu.make_async_copy(c_hbm, c_buf, in_sem)
    c_in.start()
    scatter = Scatter(n, part, came, width, send1, recv1)
    stats = Stats(n, mine, others, send2, recv2)
    gather = Gather(n, all1, width, send3, recv3)
    enter(n, gather.to)

    def work(c):
        rows = chunk_rows(c)
        units = wg_ref.shape[1]
        part32[...] = dot_nt(acts_ref[rows, 0:units], wg_ref[...])
        part32[...] += dot_nt(acts_ref[rows, units : 2 * units], wu_ref[...])
        stats_part(part32, normed_ref, lambda r: sub_rows(c, r), part, c, first, second)
        stats.put(c, first[...], second[...])
        stats.start(c)
        scatter.start(c)

        @pl.when(c >= 1)
        def _():
            scatter.relay(c - 1)

    def middle(c):
        scatter.arrive(c)
        stats.arrive(c)
        first[...], second[...] = stats.means(c, features)

        def piece(r):
            rows = sub_rows(c, r)
            local = pl.ds(pl.multiple_of(r * ROWS, ROWS), ROWS)
            standard = stand_ref[rows, :]
            entry = repeat_lanes(scale_ref[rows, :], width) * (
                scatter.total(rows)
                - repeat_lanes(first[local, :], width)
                - standard * repeat_lanes(second[local, :], width)
            )
            entry_ref[rows, :] = entry
            grad = mixing.across * entry
            for i in range(c_buf.shape[0]):
                grad += mixing.branch[i] * c_buf[i, rows].astype(F32)
            all1[rows, gather.own()] = grad.astype(BF16)

        loop(CHUNK // ROWS, piece)
        gather.start(c)

    c_in.wait()

    def ahead(c):
        work(c)

        @pl.when(c >= 2)
        def _():
            middle(c - 2)

    loop(count, ahead)
    scatter.relay(count - 1)
    middle(count - 2)
    gather.relay(0)
    middle(count - 1)
    for c in range(1, count):
        gather.relay(c)

    def gb1_out(c):
        return pltpu.make_async_copy(
            all1.at[chunk_rows(c)], gb1_hbm.at[chunk_rows(c)], out_sem.at[c]
        )

    def last(c):
        gather.arrive(c)
        gb1_out(c).start()

    loop(count, last)

    def drain(c):
        gb1_out(c).wait()
        scatter.finish(c)
        stats.finish(c)
        gather.finish(c)

    loop(count, drain)


def attend_back_kernel(
    n, q_ref, k_ref, v_ref, segc_ref, segr_ref, cos_ref, sin_ref, wo_ref, wq_ref, wk_ref, wv_ref,
    wd_ref, stand_ref, scale_ref, gb1_hbm, hidden_hbm, normed_hbm, _output, _down,
    lin_ref, branch_ref, entry_ref,
    gb1_buf, hidden_buf, normed_buf, bias, dk_t, dv_t, part32, first, second,
    part1, came1, part2, came2, mine, others, in_sem,
    send1, recv1, send2, recv2, send3, recv3,
):
    tokens, width = q_ref.shape
    features = part1.shape[1]
    count = tokens // CHUNK
    heads = width // HEAD
    factor = HEAD ** (-0.5)
    down = Scatter(n, part2, came2, width, send1, recv1)
    scatter = Scatter(n, part1, came1, width, send2, recv2)
    stats = Stats(n, mine, others, send3, recv3)

    def inputs(c, slot):
        return tuple(
            pltpu.make_async_copy(source.at[chunk_rows(c)], target.at[slot], in_sem.at[i, slot])
            for i, (source, target) in enumerate(
                ((gb1_hbm, gb1_buf), (hidden_hbm, hidden_buf), (normed_hbm, normed_buf))
            )
        )

    for copy in inputs(count - 1, 0):
        copy.start()
    dk_t[...] = jnp.zeros_like(dk_t)
    dv_t[...] = jnp.zeros_like(dv_t)
    enter(n, scatter.to)

    def work(i):
        c = count - 1 - i
        slot = lax.rem(i, 2)

        @pl.when(i < count - 1)
        def _():
            for copy in inputs(c - 1, 1 - slot):
                copy.start()

        for copy in inputs(c, slot):
            copy.wait()
        rows = chunk_rows(c)
        part2[rows, :] = dot_nn(hidden_buf[slot], wd_ref[...]).astype(BF16)
        down.start(c)
        grad = dot_nt(gb1_buf[slot], wo_ref[...]).astype(BF16)
        start, extent = window(c, tokens)
        keys = pl.ds(start, extent)
        window_bias(c, start, extent, segc_ref, segr_ref, bias)
        cos_rows, sin_rows = cos_ref[rows, :], sin_ref[rows, :]
        for h in range(heads):
            place = slice(HEAD * h, HEAD * (h + 1))
            query, grad_h = q_ref[rows, place], grad[:, place]
            scores = dot_nt(query, k_ref[keys, place]) * factor + bias[...]
            raised = jnp.exp(scores - jnp.max(scores, axis=1, keepdims=True))
            inverse = 1.0 / jnp.sum(raised, axis=1, keepdims=True)
            probs = raised * inverse
            grad_probs = dot_nt(grad_h, v_ref[keys, place])
            centre = jnp.sum(probs * grad_probs, axis=1, keepdims=True)
            grad_scores = (probs * (grad_probs - centre)).astype(BF16)
            dv_t[place, keys] += dot_nn(jnp.transpose(grad_h), probs.astype(BF16))
            dk_t[place, keys] += dot_nn(jnp.transpose(query), grad_scores)
            dq = dot_nn(grad_scores, k_ref[keys, place]) * factor
            lin_ref[rows, place] = rotate(dq, cos_rows, sin_rows, -1.0).astype(BF16)
            dk = jnp.transpose(dk_t[place, rows]) * factor
            lin_ref[rows, slice(width + HEAD * h, width + HEAD * (h + 1))] = rotate(dk, cos_rows, sin_rows, -1.0).astype(BF16)
            lin_ref[rows, slice(2 * width + HEAD * h, 2 * width + HEAD * (h + 1))] = jnp.transpose(dv_t[place, rows]).astype(BF16)
        part32[...] = dot_nt(lin_ref[rows, 0:width], wq_ref[...])
        part32[...] += dot_nt(lin_ref[rows, width : 2 * width], wk_ref[...])
        part32[...] += dot_nt(lin_ref[rows, 2 * width : 3 * width], wv_ref[...])
        stats_part(
            part32,
            normed_buf.at[slot],
            lambda r: pl.ds(pl.multiple_of(r * ROWS, ROWS), ROWS),
            part1,
            c,
            first,
            second,
        )
        stats.put(c, first[...], second[...])
        stats.start(c)
        scatter.start(c)
        down.relay(c)

        @pl.when(i >= 1)
        def _():
            scatter.relay(c + 1)

    loop(count, work)
    scatter.relay(0)

    def last(i):
        c = count - 1 - i
        down.arrive(c)

        def sums(r):
            branch_ref[sub_rows(c, r), :] = down.total(sub_rows(c, r))

        loop(CHUNK // ROWS, sums)
        scatter.arrive(c)
        stats.arrive(c)
        first[...], second[...] = stats.means(c, features)

        def piece(r):
            rows = sub_rows(c, r)
            local = pl.ds(pl.multiple_of(r * ROWS, ROWS), ROWS)
            entry_ref[rows, :] = repeat_lanes(scale_ref[rows, :], width) * (
                scatter.total(rows)
                - repeat_lanes(first[local, :], width)
                - stand_ref[rows, :] * repeat_lanes(second[local, :], width)
            )

        loop(CHUNK // ROWS, piece)

    loop(count, last)

    def drain(c):
        down.finish(c)
        scatter.finish(c)
        stats.finish(c)

    loop(count, drain)


def streams_kernel(
    in1, out1, in2, out2, res1, res2, s_ref, c_ref, b1_ref, b2_ref, e1_ref, e2_ref, new_ref, grad_ref, sums_ref
):
    @pl.when(pl.program_id(0) == 0)
    def _():
        sums_ref[...] = jnp.zeros_like(sums_ref)

    count = s_ref.shape[0]
    mixing = Mixing((in1, out1, in2, out2, res1, res2))
    mixed = [[mixing.mixed(k, j) for j in range(count)] for k in range(count)]

    def fold(field):
        field = fold_lanes(field)
        total = field[0:8]
        for j in range(1, field.shape[0] // 8):
            total += field[8 * j : 8 * (j + 1)]
        return total

    def piece(r):
        rows = pl.ds(pl.multiple_of(r * 16, 16), 16)
        s = [s_ref[i, rows].astype(F32) for i in range(count)]
        c = [c_ref[i, rows].astype(F32) for i in range(count)]
        b1, b2, e1, e2 = b1_ref[rows, :], b2_ref[rows, :], e1_ref[rows, :], e2_ref[rows, :]
        for j in range(count):
            new = mixing.branch[j] * b1 + mixing.out2[j] * b2
            grad = mixing.entry[j] * e2 + mixing.in1[j] * e1
            for k in range(count):
                new += mixed[k][j] * s[k]
                grad += mixed[j][k] * c[k]
            new_ref[rows, j, :] = new.astype(BF16)
            grad_ref[rows, j, :] = grad
        pairs = [(s[i], c[j]) for i in range(count) for j in range(count)]
        pairs += [(s[i], e1) for i in range(count)] + [(s[i], e2) for i in range(count)]
        pairs += [(c[i], b1) for i in range(count)] + [(c[i], b2) for i in range(count)]
        pairs += [(b1, e2)]
        for place, (left, right) in enumerate(pairs):
            sums_ref[place] += fold(left * right)

    loop(s_ref.shape[1] // 16, piece)


PLANES = 4
CORES = 2
SUMS = 33
SUM_ROWS = 40


def finish_kernel(
    n, first_hbm, last_hbm, sums_ref,
    q_out, k_out, v_out, o_out, sums_out,
    own, core, right, left, by_core, by_plane, by_tensor,
    own_sem, core_send, core_recv, right_send, right_recv, left_send, left_recv, sum_send, sum_recv,
):
    _, pieces, height, width = own.shape
    me = lax.axis_index("dp")
    plane, mine = lax.div(me, CORES), lax.rem(me, CORES)
    partner = me + 1 - 2 * mine
    here, peers, peer_source = partners(n)
    planes_to = [lax.rem(plane + k, PLANES) for k in range(1, PLANES)]
    planes_from = [lax.rem(plane + PLANES - k, PLANES) for k in range(1, PLANES)]

    def dp_at(position):
        return position * CORES + mine

    def rows_of(position, half):
        return pl.ds(pl.multiple_of((position * CORES + half) * height, height), height)

    def block(position, half, p):
        if p < pieces - 1:
            return first_hbm.at[rows_of(position, half), p * width : (p + 1) * width]
        return last_hbm.at[rows_of(position, half)]

    def over_dp(source, target, send_sem, recv_sem, device):
        return pltpu.make_async_remote_copy(
            src_ref=source, dst_ref=target, send_sem=send_sem, recv_sem=recv_sem,
            device_id={"dp": device}, device_id_type=MESH,
        )

    def own_in(position, p):
        return pltpu.make_async_copy(
            block(position, mine, p), own.at[position, p], own_sem.at[position, p]
        )

    def core_in(position, p):
        return over_dp(
            block(position, 1 - mine, p), core.at[position, p],
            core_send.at[position, p], core_recv.at[position, p], partner,
        )

    def rightward(step, p):
        return over_dp(
            own.at[lax.rem(plane + PLANES - step, PLANES), p], right.at[step - 1, p],
            right_send.at[step - 1, p], right_recv.at[step - 1, p], lax.rem(me + CORES, PLANES * CORES),
        )

    def leftward(step, p):
        return over_dp(
            own.at[lax.rem(plane + step, PLANES), p], left.at[step - 1, p],
            left_send.at[step - 1, p], left_recv.at[step - 1, p],
            lax.rem(me + (PLANES - 1) * CORES, PLANES * CORES),
        )

    order = (3, 0, 2, 1)
    for position in order:
        for p in range(pieces):
            own_in(position, p).start()

    barrier = pltpu.get_barrier_semaphore()
    pl.semaphore_signal(barrier, inc=1, device_id={"dp": partner}, device_id_type=MESH)
    for k in range(PLANES - 1):
        pl.semaphore_signal(
            barrier, inc=1, device_id={"dp": dp_at(planes_to[k])}, device_id_type=MESH
        )
    for k in range(n - 1):
        pl.semaphore_signal(barrier, inc=1, device_id={"tensor": peers[k]}, device_id_type=MESH)
    pl.semaphore_wait(barrier, 1 + PLANES - 1 + n - 1)

    by_core[mine] = jnp.zeros((SUM_ROWS, 128), F32)
    by_core[mine, 0:SUMS] = jnp.sum(sums_ref[...], axis=1)
    over_dp(
        by_core.at[mine], by_core.at[mine], sum_send.at[0], sum_recv.at[0], partner
    ).start()
    for position in order:
        for p in range(pieces):
            core_in(position, p).start()
    over_dp(
        by_core.at[1 - mine], by_core.at[1 - mine], sum_send.at[0], sum_recv.at[0], partner
    ).wait_recv()
    by_plane[plane] = by_core[0] + by_core[1]

    def plane_sums(k, at):
        return over_dp(
            by_plane.at[at], by_plane.at[at], sum_send.at[1 + k], sum_recv.at[1 + k],
            dp_at(planes_to[k]),
        )

    def tensor_sums(k, at):
        at = by_tensor.at[at]
        return remote(at, at, sum_send.at[PLANES + k], sum_recv.at[PLANES + k], peers[k])

    for k in range(PLANES - 1):
        plane_sums(k, plane).start()

    def gather_pair(position):
        def piece(p):
            pltpu.make_async_copy(
                own.at[position, p], own.at[position, p], own_sem.at[position, p]
            ).wait()
            over_dp(
                core.at[position, p], core.at[position, p],
                core_send.at[position, p], core_recv.at[position, p], partner,
            ).wait_recv()
            add(own.at[position, p], core.at[position, p])

        loop(pieces, piece)

    def add(target, source):
        def part(r):
            rows = local_rows(r)
            target[rows, :] = (target[rows, :].astype(F32) + source[rows, :].astype(F32)).astype(BF16)

        loop(height // ROWS, part)

    def send_step(step):
        def piece(p):
            @pl.when(plane <= step - 1)
            def _():
                if step >= 2:

                    @pl.when(plane >= 1)
                    def _():
                        rightward(step - 1, p).wait_recv()
                        add(own.at[lax.rem(plane + PLANES - step, PLANES), p], right.at[step - 2, p])

                rightward(step, p).start()

            @pl.when(plane >= PLANES - step)
            def _():
                if step >= 2:

                    @pl.when(plane <= PLANES - 2)
                    def _():
                        leftward(step - 1, p).wait_recv()
                        add(own.at[lax.rem(plane + step, PLANES), p], left.at[step - 2, p])

                leftward(step, p).start()

        loop(pieces, piece)

    gather_pair(3)
    gather_pair(0)
    send_step(1)
    gather_pair(2)
    gather_pair(1)
    for k in range(PLANES - 1):
        plane_sums(k, planes_from[k]).wait_recv()
    by_tensor[here] = sum((by_plane[i] for i in range(1, PLANES)), by_plane[0])
    for k in range(n - 1):
        tensor_sums(k, here).start()
    for step in range(2, PLANES):
        send_step(step)
    for k in range(n - 1):
        tensor_sums(k, peer_source[k]).wait_recv()
    sums_out[...] = sum((by_tensor[i] for i in range(1, n)), by_tensor[0])

    for p, target in enumerate((q_out, k_out, v_out, o_out)):
        steps = PLANES - 2

        @pl.when(plane >= 1)
        def _():
            rightward(PLANES - 1, p).wait_recv()

        @pl.when(plane <= PLANES - 2)
        def _():
            leftward(PLANES - 1, p).wait_recv()

        total = own[plane, p].astype(F32)
        total += jnp.where(plane >= 1, right[steps, p].astype(F32), 0.0)
        total += jnp.where(plane <= PLANES - 2, left[steps, p].astype(F32), 0.0)
        target[...] = total if p < pieces - 1 else jnp.transpose(total)

    over_dp(by_core.at[mine], by_core.at[mine], sum_send.at[0], sum_recv.at[0], partner).wait_send()
    for k in range(PLANES - 1):
        plane_sums(k, plane).wait_send()
    for k in range(n - 1):
        tensor_sums(k, here).wait_send()
    for p in range(pieces):
        for position in range(PLANES):
            core_in(position, p).wait_send()
        for step in range(1, PLANES):

            @pl.when(plane <= step - 1)
            def _():
                rightward(step, p).wait_send()

            @pl.when(plane >= PLANES - step)
            def _():
                leftward(step, p).wait_send()


def on_device(
    n,
    replicas,
    streams,
    segments,
    positions,
    mix_in1,
    mix_res1,
    mix_out1,
    mix_in2,
    mix_res2,
    mix_out2,
    w_query,
    w_key,
    w_value,
    w_output,
    w_gate,
    w_up,
    w_down,
    cotangent,
):
    tokens, stream_count, width = streams.shape
    features = w_query.shape[0]
    units = w_gate.shape[1]
    chunks = tokens // CHUNK
    assert tokens == LENGTH == 4 * CHUNK and stream_count == 4
    any_spec = pl.BlockSpec(memory_space=pl.ANY)
    vmem = pl.BlockSpec(memory_space=pltpu.VMEM)
    smem = pl.BlockSpec(memory_space=pltpu.SMEM)

    def array(shape, dtype):
        return jax.ShapeDtypeStruct(shape, dtype)

    def dma(*shape):
        return pltpu.SemaphoreType.DMA(shape)

    def pair(lanes):
        return [dma(lanes, chunks), dma(lanes, chunks)]

    gather_sems = pair(4 if n == 4 else n - 1)
    scatter_sems = pair(6 if n == 4 else n - 1)
    stats_sems = pair(n - 1)

    def lasts(micros):
        return pl.CostEstimate(
            flops=int(micros * 1.0e9), bytes_accessed=int(micros * 3.6e6), transcendentals=0
        )

    def params(identity, mib):
        return pltpu.CompilerParams(
            collective_id=identity, has_side_effects=True, vmem_limit_bytes=mib * MIB
        )

    def small(form, left, right):
        return jnp.einsum(form, left, right, precision=PRECISE)

    planes = jnp.transpose(streams, (1, 0, 2))
    mixes = (mix_in1, mix_out1, mix_in2, mix_out2, mix_res1, mix_res2)

    def stats_scratch():
        return [
            pltpu.VMEM((CHUNK, 128), F32),
            pltpu.VMEM((CHUNK, 128), F32),
            pltpu.VMEM((chunks, 16, CHUNK), F32),
            pltpu.VMEM((n - 1, chunks, 16, CHUNK), F32),
        ]

    (
        normed1, queries, keys, values, stand1, scale1, grad_branch2, cot_planes,
        cos_table, sin_table, seg_column, seg_row,
    ) = pl.pallas_call(
        functools.partial(project_kernel, n),
        name="project",
        cost_estimate=lasts(100),
        out_shape=[
            array((tokens, features), BF16),
            array((tokens, width), BF16),
            array((tokens, width), BF16),
            array((tokens, width), BF16),
            array((tokens, width), F32),
            array((tokens, 128), F32),
            array((tokens, features), BF16),
            array((stream_count, tokens, width), BF16),
            array((tokens, HEAD), F32),
            array((tokens, HEAD), F32),
            array((tokens, 128), F32),
            array((8, tokens), F32),
        ],
        in_specs=[smem, smem, vmem, vmem] + [any_spec] * 5,
        out_specs=[any_spec] + [vmem] * 5 + [any_spec] * 2 + [vmem] * 4,
        scratch_shapes=[
            pltpu.VMEM((stream_count, tokens, width), BF16),
            pltpu.VMEM((tokens, stream_count, width), BF16),
            pltpu.VMEM((stream_count, tokens, width), BF16),
            pltpu.VMEM((3, features, width), BF16),
            pltpu.VMEM((tokens, features), BF16),
            pltpu.VMEM((tokens, features), BF16),
        ]
        + stats_scratch()
        + [dma(2, chunks), dma(3), dma(3, chunks)]
        + gather_sems
        + gather_sems
        + stats_sems,
        compiler_params=params(0, 56),
    )(
        mix_in1, mix_out2,
        positions.reshape(tokens // 128, 128), segments.reshape(tokens // 128, 128),
        planes, cotangent, w_query, w_key, w_value,
    )

    extent = window(0, tokens)[1]
    attended, branch1, normed2, stand2, scale2, hidden, grad_acts, _ = pl.pallas_call(
        functools.partial(attend_kernel, n),
        name="attend",
        cost_estimate=lasts(100),
        out_shape=[
            array((tokens, width), BF16),
            array((tokens, width), F32),
            array((tokens, features), BF16),
            array((tokens, width), F32),
            array((tokens, 128), F32),
            array((tokens, units), BF16),
            array((tokens, 2 * units), BF16),
            array((tokens, units), BF16),
        ],
        in_specs=[smem] * 6 + [vmem] * 6 + [any_spec] * 5,
        out_specs=[vmem, vmem, any_spec, vmem, vmem, any_spec, any_spec, any_spec],
        scratch_shapes=[
            pltpu.VMEM((2, stream_count, CHUNK, width), BF16),
            pltpu.VMEM((2, CHUNK, features), BF16),
            pltpu.VMEM((features, units), BF16),
            pltpu.VMEM((features, units), BF16),
            pltpu.VMEM((units, features), BF16),
            pltpu.VMEM((2, CHUNK, units), BF16),
            pltpu.VMEM((2, CHUNK, units), BF16),
            pltpu.VMEM((2, CHUNK, units), BF16),
            pltpu.VMEM((tokens, features), BF16),
            pltpu.VMEM((n - 1, tokens, width), BF16),
            pltpu.VMEM((tokens, features), BF16),
        ]
        + stats_scratch()
        + [pltpu.VMEM((CHUNK, extent), F32), dma(2), dma(2), dma(2, 2)]
        + [dma(3), dma(chunks), dma(3, 2)]
        + scatter_sems
        + gather_sems
        + stats_sems,
        compiler_params=params(1, 62),
    )(
        *mixes, queries, keys, values, seg_column, seg_row, w_output, planes,
        grad_branch2, w_gate, w_up, w_down,
    )

    def over_dp(partial, dimension):
        return lax.psum_scatter(partial, "dp", scatter_dimension=dimension, tiled=True)

    part_down = contract_rows(hidden, grad_branch2).astype(BF16)
    part_gate_up = contract_rows(normed2, grad_acts).astype(BF16)
    grad_down = over_dp(part_down, 1)
    grad_gate_up = over_dp(part_gate_up, 0)
    grad_w_down = grad_down.astype(F32)
    grad_w_gate = grad_gate_up[:, :units].astype(F32)
    grad_w_up = grad_gate_up[:, units:].astype(F32)

    grad_entry2, grad_branch1 = pl.pallas_call(
        functools.partial(units_back_kernel, n),
        name="units_back",
        cost_estimate=lasts(400),
        out_shape=[array((tokens, width), F32), array((tokens, features), BF16)],
        in_specs=[smem] * 6 + [vmem] * 6 + [any_spec] * 3,
        out_specs=[vmem, any_spec],
        scratch_shapes=[
            pltpu.VMEM((stream_count, tokens, width), BF16),
            pltpu.VMEM((CHUNK, features), F32),
            pltpu.VMEM((CHUNK, 128), F32),
            pltpu.VMEM((CHUNK, 128), F32),
            pltpu.VMEM((tokens, features), BF16),
            pltpu.VMEM((n - 1, tokens, width), BF16),
            pltpu.VMEM((chunks, 16, CHUNK), F32),
            pltpu.VMEM((n - 1, chunks, 16, CHUNK), F32),
            pltpu.VMEM((tokens, features), BF16),
            pltpu.SemaphoreType.DMA,
            dma(chunks),
        ]
        + scatter_sems
        + stats_sems
        + gather_sems,
        compiler_params=params(2, 60),
    )(
        *mixes, grad_acts, w_gate, w_up, normed2, stand2, scale2, cot_planes,
        part_down, part_gate_up,
    )

    part_output = contract_rows(grad_branch1, attended).astype(BF16)

    grad_lin, branch2, grad_entry1 = pl.pallas_call(
        functools.partial(attend_back_kernel, n),
        name="attend_back",
        cost_estimate=lasts(2),
        out_shape=[array((tokens, 3 * width), BF16)] + [array((tokens, width), F32)] * 2,
        in_specs=[vmem] * 14 + [any_spec] * 5,
        out_specs=[vmem] * 3,
        scratch_shapes=[
            pltpu.VMEM((2, CHUNK, features), BF16),
            pltpu.VMEM((2, CHUNK, units), BF16),
            pltpu.VMEM((2, CHUNK, features), BF16),
            pltpu.VMEM((CHUNK, extent), F32),
            pltpu.VMEM((width, tokens), F32),
            pltpu.VMEM((width, tokens), F32),
            pltpu.VMEM((CHUNK, features), F32),
            pltpu.VMEM((CHUNK, 128), F32),
            pltpu.VMEM((CHUNK, 128), F32),
            pltpu.VMEM((tokens, features), BF16),
            pltpu.VMEM((n - 1, tokens, width), BF16),
            pltpu.VMEM((tokens, features), BF16),
            pltpu.VMEM((n - 1, tokens, width), BF16),
            pltpu.VMEM((chunks, 16, CHUNK), F32),
            pltpu.VMEM((n - 1, chunks, 16, CHUNK), F32),
            dma(3, 2),
        ]
        + scatter_sems
        + scatter_sems
        + stats_sems,
        compiler_params=params(3, 60),
    )(
        queries, keys, values, seg_column, seg_row, cos_table, sin_table,
        w_output, w_query, w_key, w_value, w_down, stand1, scale1,
        grad_branch1, hidden, normed1, part_output, grad_down,
    )

    part_lin = contract_rows(normed1, grad_lin).astype(BF16)

    rows = 128
    plane_spec = pl.BlockSpec((stream_count, rows, width), lambda t: (0, t, 0))
    field_spec = pl.BlockSpec((rows, width), lambda t: (t, 0))
    stream_spec = pl.BlockSpec((rows, stream_count, width), lambda t: (t, 0, 0))
    new_streams, stream_grad, sums = pl.pallas_call(
        streams_kernel,
        name="streams",
        cost_estimate=lasts(2),
        grid=(tokens // rows,),
        out_shape=[
            array(streams.shape, BF16),
            array(streams.shape, F32),
            array((SUMS, 8, 128), F32),
        ],
        in_specs=[smem] * 6 + [plane_spec, plane_spec] + [field_spec] * 4,
        out_specs=[
            stream_spec,
            stream_spec,
            pl.BlockSpec((SUMS, 8, 128), lambda t: (0, 0, 0)),
        ],
        compiler_params=pltpu.CompilerParams(vmem_limit_bytes=48 * MIB),
    )(*mixes, planes, cot_planes, branch1, branch2, grad_entry1, grad_entry2)
    height = features // replicas
    if replicas == PLANES * CORES and stream_count == 4:
        steps = PLANES - 1
        grad_w_query, grad_w_key, grad_w_value, grad_w_output, sums = pl.pallas_call(
            functools.partial(finish_kernel, n),
            name="finish",
            cost_estimate=lasts(2),
            out_shape=[array((height, width), F32)] * 3
            + [array((width, height), F32), array((SUM_ROWS, 128), F32)],
            in_specs=[any_spec, any_spec, vmem],
            out_specs=[vmem] * 5,
            scratch_shapes=[
                pltpu.VMEM((PLANES, 4, height, width), BF16),
                pltpu.VMEM((PLANES, 4, height, width), BF16),
                pltpu.VMEM((steps, 4, height, width), BF16),
                pltpu.VMEM((steps, 4, height, width), BF16),
                pltpu.VMEM((CORES, SUM_ROWS, 128), F32),
                pltpu.VMEM((PLANES, SUM_ROWS, 128), F32),
                pltpu.VMEM((n, SUM_ROWS, 128), F32),
                dma(PLANES, 4),
                dma(PLANES, 4),
                dma(PLANES, 4),
                dma(steps, 4),
                dma(steps, 4),
                dma(steps, 4),
                dma(steps, 4),
                dma(PLANES + n - 1),
                dma(PLANES + n - 1),
            ],
            compiler_params=params(4, 48),
        )(part_lin, part_output, sums)
        sums = jnp.sum(sums[:SUMS], axis=1)
    else:
        grad_w_query, grad_w_key, grad_w_value = (
            over_dp(part_lin[:, width * j : width * (j + 1)], 0).astype(F32) for j in range(3)
        )
        grad_w_output = jnp.transpose(over_dp(part_output, 0)).astype(F32)
        sums = lax.psum(jnp.sum(sums, axis=(1, 2)), ("dp", "tensor"))
    s_c = sums[0:16].reshape(4, 4)
    s_e1, s_e2, c_b1, c_b2, b_e = sums[16:20], sums[20:24], sums[24:28], sums[28:32], sums[32]
    grad_mix_in1 = s_e1
    grad_mix_res1 = small("ik,jk->ij", s_c, mix_res2) + s_e2[:, None] * mix_in2[None, :]
    grad_mix_out1 = small("jk,k->j", mix_res2, c_b1) + mix_in2 * b_e
    grad_mix_in2 = small("ki,k->i", mix_res1, s_e2) + mix_out1 * b_e
    grad_mix_res2 = small("ki,kj->ij", mix_res1, s_c) + mix_out1[:, None] * c_b1[None, :]
    grad_mix_out2 = c_b2
    return (
        new_streams,
        stream_grad,
        grad_w_query,
        grad_w_key,
        grad_w_value,
        grad_w_output,
        grad_w_gate,
        grad_w_up,
        grad_w_down,
        grad_mix_in1,
        grad_mix_res1,
        grad_mix_out1,
        grad_mix_in2,
        grad_mix_res2,
        grad_mix_out2,
    )


def solution(mesh):
    return jax.shard_map(
        functools.partial(on_device, mesh.shape["tensor"], mesh.shape["dp"]),
        mesh=mesh,
        in_specs=(
            P("dp", None, "tensor"),
            P("dp"),
            P("dp"),
            P(),
            P(),
            P(),
            P(),
            P(),
            P(),
            P(None, "tensor"),
            P(None, "tensor"),
            P(None, "tensor"),
            P("tensor", None),
            P(None, "tensor"),
            P(None, "tensor"),
            P("tensor", None),
            P("dp", None, "tensor"),
        ),
        out_specs=(
            P("dp", None, "tensor"),
            P("dp", None, "tensor"),
            P("dp", "tensor"),
            P("dp", "tensor"),
            P("dp", "tensor"),
            P("tensor", "dp"),
            P("dp", "tensor"),
            P("dp", "tensor"),
            P("tensor", "dp"),
            P(),
            P(),
            P(),
            P(),
            P(),
            P(),
        ),
        check_vma=False,
    )
```

```python
import functools
import math

import jax
import jax.numpy as jnp
from jax import lax
from jax.experimental import pallas as pl
from jax.experimental.pallas import tpu as pltpu
from jax.sharding import PartitionSpec as P

HEAD = 128
LENGTH = 1024
LONGEST = 512
EPS = 1e-05
PRECISE = lax.Precision.HIGHEST
MASKED = -1e30
MESH = pl.DeviceIdType.MESH
BF16 = jnp.bfloat16
F32 = jnp.float32
CHUNK = 256
ROWS = 32
MIB = 1 << 20


def inner(left, right):
    total = left[0] * right[0]
    for a, b in zip(left[1:], right[1:]):
        total += a * b
    return total


class Mixing:
    def __init__(self, refs):
        vectors = [[ref[i] for i in range(4)] for ref in refs[:4]]
        self.in1, self.out1, self.in2, self.out2 = vectors
        self.res1, self.res2 = (
            [[ref[i, j] for j in range(4)] for i in range(4)] for ref in refs[4:]
        )
        self.entry = [inner(row, self.in2) for row in self.res1]
        self.branch = [inner(self.out1, column) for column in zip(*self.res2)]
        self.across = inner(self.out1, self.in2)

    def mixed(self, k, j):
        return inner(self.res1[k], [row[j] for row in self.res2])


def contract_rows(left, right):
    return lax.dot_general(
        left, right, (((0,), (0,)), ((), ())), preferred_element_type=F32
    )


def dot_nn(left, right):
    return jnp.dot(left, right, preferred_element_type=F32)


def dot_nt(left, right):
    return lax.dot_general(
        left, right, (((1,), (1,)), ((), ())), preferred_element_type=F32
    )


def partners(n):
    me = lax.axis_index("tensor")
    if n == 4:
        both = (me + 1 - 2 * lax.rem(me, 2), lax.rem(me + 2, 4), 3 - me)
        return me, both, both
    to = tuple(lax.rem(me + k, n) for k in range(1, n))
    source = tuple(lax.rem(me + n - k, n) for k in range(1, n))
    return me, to, source


def enter(n, to):
    barrier = pltpu.get_barrier_semaphore()
    for target in to:
        pl.semaphore_signal(
            barrier, inc=1, device_id={"tensor": target}, device_id_type=MESH
        )
    pl.semaphore_wait(barrier, n - 1)


def remote(source, target, send_sem, recv_sem, device):
    return pltpu.make_async_remote_copy(
        src_ref=source,
        dst_ref=target,
        send_sem=send_sem,
        recv_sem=recv_sem,
        device_id={"tensor": device},
        device_id_type=MESH,
    )


def columns(index, width):
    return pl.ds(pl.multiple_of(index * width, 128), width)


def chunk_rows(c):
    return pl.ds(pl.multiple_of(c * CHUNK, CHUNK), CHUNK)


def half_rows(c, half):
    return pl.ds(pl.multiple_of(c * CHUNK + half * (CHUNK // 2), CHUNK // 2), CHUNK // 2)


class Gather:
    def __init__(self, n, buf, width, send_sem, recv_sem):
        self.n, self.buf, self.width = n, buf, width
        self.me, self.to, self.source = partners(n)
        self.send_sem, self.recv_sem = send_sem, recv_sem

    def own(self):
        return columns(self.me, self.width)

    def copy(self, rows, owner, k, c, target):
        view = self.buf.at[rows, columns(owner, self.width)]
        return remote(view, view, self.send_sem.at[k, c], self.recv_sem.at[k, c], target)

    def direct(self):
        return 2 if self.n == 4 else self.n - 1

    def handed(self, c):
        side, up, _ = self.to
        return (
            self.copy(half_rows(c, 0), side, 2, c, up),
            self.copy(half_rows(c, 1), up, 3, c, side),
        )

    def start(self, c):
        for k in range(self.direct()):
            self.copy(chunk_rows(c), self.me, k, c, self.to[k]).start()

    def relay(self, c):
        if self.n == 4:
            for k, copy in enumerate(self.handed(c)):
                self.copy(chunk_rows(c), self.source[k], k, c, self.to[k]).wait_recv()
                copy.start()

    def arrive(self, c):
        if self.n == 4:
            side, up, across = self.to
            self.copy(half_rows(c, 0), across, 2, c, up).wait_recv()
            self.copy(half_rows(c, 1), across, 3, c, side).wait_recv()
        else:
            for k in range(self.n - 1):
                self.copy(chunk_rows(c), self.source[k], k, c, self.to[k]).wait_recv()

    def finish(self, c):
        for k in range(self.direct()):
            self.copy(chunk_rows(c), self.me, k, c, self.to[k]).wait_send()
        if self.n == 4:
            for copy in self.handed(c):
                copy.wait_send()


class Scatter:
    def __init__(self, n, part, came, width, send_sem, recv_sem):
        self.n, self.part, self.came, self.width = n, part, came, width
        self.me, self.to, self.source = partners(n)
        self.send_sem, self.recv_sem = send_sem, recv_sem

    def copy(self, rows, owner, slot, k, c, target):
        return remote(
            self.part.at[rows, columns(owner, self.width)],
            self.came.at[slot, rows],
            self.send_sem.at[k, c],
            self.recv_sem.at[k, c],
            target,
        )

    def first(self, c):
        if self.n != 4:
            return tuple(
                (chunk_rows(c), self.to[k], k, k, c, self.to[k]) for k in range(self.n - 1)
            )
        side, up, across = self.to
        return (
            (half_rows(c, 0), across, 2, 0, c, side),
            (half_rows(c, 1), across, 2, 1, c, up),
            (half_rows(c, 0), side, 0, 2, c, side),
            (half_rows(c, 1), up, 1, 3, c, up),
        )

    def second(self, c):
        if self.n != 4:
            return ()
        side, up, _ = self.to
        return (
            (half_rows(c, 0), up, 1, 4, c, up),
            (half_rows(c, 1), side, 0, 5, c, side),
        )

    def start(self, c):
        for place in self.first(c):
            self.copy(*place).start()

    def relay(self, c):
        second = self.second(c)
        first = self.first(c)
        for half in range(len(second)):
            self.copy(*first[half]).wait_recv()
            owner = columns(self.to[1 - half], self.width)
            base = c * CHUNK + half * (CHUNK // 2)

            def add(r):
                rows = pl.ds(pl.multiple_of(base + r * ROWS, ROWS), ROWS)
                total = self.part[rows, owner].astype(F32) + self.came[2, rows].astype(F32)
                self.part[rows, owner] = total.astype(BF16)

            loop(CHUNK // 2 // ROWS, add)
            self.copy(*second[half]).start()

    def arrive(self, c):
        places = self.first(c)
        if self.n == 4:
            places = places[2:] + self.second(c)
        for place in places:
            self.copy(*place).wait_recv()

    def finish(self, c):
        for place in self.first(c) + self.second(c):
            self.copy(*place).wait_send()

    def total(self, rows):
        total = self.part[rows, columns(self.me, self.width)].astype(F32)
        for k in range(2 if self.n == 4 else self.n - 1):
            total += self.came[k, rows].astype(F32)
        return total


class Stats:
    def __init__(self, n, mine, came, send_sem, recv_sem):
        self.n, self.mine, self.came = n, mine, came
        self.me, self.to, self.source = partners(n)
        self.send_sem, self.recv_sem = send_sem, recv_sem

    def copy(self, c, k):
        return remote(
            self.mine.at[c], self.came.at[k, c], self.send_sem.at[k, c], self.recv_sem.at[k, c], self.to[k]
        )

    def start(self, c):
        for k in range(self.n - 1):
            self.copy(c, k).start()

    def arrive(self, c):
        for k in range(self.n - 1):
            self.copy(c, k).wait_recv()

    def finish(self, c):
        for k in range(self.n - 1):
            self.copy(c, k).wait_send()

    def put(self, c, first, second):
        ones = jnp.ones((8, 128), F32)
        for place, field in ((0, first), (8, second)):
            self.mine[c, place : place + 8] = lax.dot_general(
                ones, field, (((1,), (1,)), ((), ())), precision=PRECISE, preferred_element_type=F32
            )

    def moments(self, c, width):
        pieces = [self.mine[c]] + [self.came[k, c] for k in range(self.n - 1)]
        count = float(self.n * width)
        mean = sum(piece[0:8] for piece in pieces) * (1.0 / count)
        squares = sum(
            piece[8:16] + width * (piece[0:8] * (1.0 / width) - mean) ** 2 for piece in pieces
        )
        share = jnp.full((8, 128), 0.125, F32)
        return tuple(
            lax.dot_general(
                row, share, (((0,), (0,)), ((), ())), precision=PRECISE, preferred_element_type=F32
            )
            for row in (mean, lax.rsqrt(squares * (1.0 / count) + EPS))
        )

    def means(self, c, features):
        total = self.mine[c]
        for k in range(self.n - 1):
            total += self.came[k, c]
        share = jnp.full((8, 128), 1.0 / (8 * features), F32)
        return tuple(
            lax.dot_general(
                total[place : place + 8],
                share,
                (((0,), (0,)), ((), ())),
                precision=PRECISE,
                preferred_element_type=F32,
            )
            for place in (0, 8)
        )


def loop(count, body):
    def step(i, carry):
        body(i)
        return carry

    lax.fori_loop(0, count, step, 0)


def sub_rows(c, r):
    return pl.ds(pl.multiple_of(c * CHUNK + r * ROWS, ROWS), ROWS)


def repeat_lanes(field, width):
    return jnp.concatenate([field] * (width // 128), axis=1)


def fold_lanes(field):
    total = field[:, 0:128]
    for j in range(1, field.shape[1] // 128):
        total += field[:, 128 * j : 128 * (j + 1)]
    return total


def local_rows(r):
    return pl.ds(pl.multiple_of(r * ROWS, ROWS), ROWS)


def fold_entry(entry, first, second, rows):
    first[rows, :] = fold_lanes(entry)
    centered = entry - jnp.sum(entry, axis=1, keepdims=True) * (1.0 / entry.shape[1])
    second[rows, :] = fold_lanes(centered * centered)


def standardize(c, stats, gather, first, second, stand_ref, scale_ref):
    width = stand_ref.shape[1]
    stats.arrive(c)
    first[...], second[...] = stats.moments(c, width)

    def piece(r):
        rows, local = sub_rows(c, r), local_rows(r)
        scaling = second[local, :]
        stand = (stand_ref[rows, :] - repeat_lanes(first[local, :], width)) * repeat_lanes(
            scaling, width
        )
        stand_ref[rows, :] = stand
        scale_ref[rows, :] = scaling
        gather.buf[rows, gather.own()] = stand.astype(BF16)

    loop(CHUNK // ROWS, piece)
    gather.start(c)


def rotate(field, cos_rows, sin_rows, sign):
    turned = pltpu.roll(field, HEAD // 2, 1)
    return field * cos_rows + (sign * turned) * sin_rows


def spread(row):
    share = jnp.full((8, 128), 0.125, F32)
    return lax.dot_general(
        jnp.broadcast_to(row, (8, 128)),
        share,
        (((0,), (0,)), ((), ())),
        precision=PRECISE,
        preferred_element_type=F32,
    )


def project_kernel(
    n, in1, out2, positions_ref, segments_ref, s_hbm, c_hbm, wq_hbm, wk_hbm, wv_hbm,
    normed_hbm, q_ref, k_ref, v_ref, stand_ref, scale_ref, gb2_hbm, cot_hbm,
    cos_ref, sin_ref, segc_ref, segr_ref,
    s_buf, c_buf, cot_planes, w_buf, all1, all2, first, second, mine, others,
    in_sem, w_sem, out_sem, send1, recv1, send2, recv2, send3, recv3,
):
    streams, tokens, width = s_buf.shape
    count = tokens // CHUNK
    heads = width // HEAD
    weights = (wq_hbm, wk_hbm, wv_hbm)

    def s_in(c):
        return pltpu.make_async_copy(
            s_hbm.at[:, chunk_rows(c)], s_buf.at[:, chunk_rows(c)], in_sem.at[0, c]
        )

    def c_in(c):
        return pltpu.make_async_copy(
            c_hbm.at[chunk_rows(c)], c_buf.at[chunk_rows(c)], in_sem.at[1, c]
        )

    def w_in(j):
        return pltpu.make_async_copy(weights[j], w_buf.at[j], w_sem.at[j])

    def out(c, i):
        rows = chunk_rows(c)
        source, target = (
            (all1.at[rows], normed_hbm.at[rows]),
            (all2.at[rows], gb2_hbm.at[rows]),
            (cot_planes.at[:, rows], cot_hbm.at[:, rows]),
        )[i]
        return pltpu.make_async_copy(source, target, out_sem.at[i, c])

    loop(count, lambda c: s_in(c).start())
    loop(count, lambda c: c_in(c).start())
    for j in range(3):
        w_in(j).start()
    gather = Gather(n, all1, width, send1, recv1)
    incoming = Gather(n, all2, width, send2, recv2)
    stats = Stats(n, mine, others, send3, recv3)
    enter(n, gather.to)

    def entry(c):
        s_in(c).wait()

        def piece(r):
            rows = sub_rows(c, r)
            field = in1[0] * s_buf[0, rows].astype(F32)
            for i in range(1, streams):
                field += in1[i] * s_buf[i, rows].astype(F32)
            stand_ref[sub_rows(c, r), :] = field
            fold_entry(field, first, second, local_rows(r))

        loop(CHUNK // ROWS, piece)
        stats.put(c, first[...], second[...])
        stats.start(c)

    def send(c):
        standardize(c, stats, gather, first, second, stand_ref, scale_ref)

    def grad(c):
        c_in(c).wait()

        def piece(r):
            rows = sub_rows(c, r)
            block = c_buf[rows].astype(F32)
            total = None
            for i in range(streams):
                field = block[:, i, :]
                cot_planes[i, rows] = field.astype(BF16)
                total = out2[i] * field if total is None else total + out2[i] * field
            all2[rows, incoming.own()] = total.astype(BF16)

        loop(CHUNK // ROWS, piece)
        incoming.start(c)
        out(c, 2).start()

    entry(0)

    def ahead(c):
        entry(c + 1)
        send(c)

    loop(count - 1, ahead)
    send(count - 1)
    grad(0)
    gather.relay(0)
    grad(1)
    gather.relay(1)
    incoming.relay(0)

    segr_ref[...] = jnp.concatenate(
        [
            jnp.broadcast_to(segments_ref[a : a + 1, :].astype(F32), (8, 128))
            for a in range(tokens // 128)
        ],
        axis=1,
    )
    lane = lax.broadcasted_iota(jnp.int32, (128, 128), 1)
    exponent = lax.rem(lane, HEAD // 2).astype(F32) * (-2.0 / HEAD * math.log(10000.0))
    inverse = jnp.exp(exponent)
    for a in range(tokens // 128):
        rows = slice(128 * a, 128 * (a + 1))
        segc_ref[rows, :] = spread(segments_ref[a : a + 1, :].astype(F32))
        angles = spread(positions_ref[a : a + 1, :].astype(F32)) * inverse
        cos_ref[rows, :] = jnp.cos(angles)
        sine = jnp.sin(angles)
        sin_ref[rows, :] = jnp.where(lane < HEAD // 2, -sine, sine)
    grad(2)
    gather.relay(2)
    grad(3)
    gather.relay(3)
    incoming.relay(1)
    for j in range(3):
        w_in(j).wait()

    def work(c):
        gather.arrive(c)
        out(c, 0).start()
        rows = chunk_rows(c)
        block = all1[rows, :]
        cos_rows, sin_rows = cos_ref[rows, :], sin_ref[rows, :]
        for j, target in ((0, q_ref), (1, k_ref)):
            lin = dot_nn(block, w_buf[j])
            for h in range(heads):
                place = slice(HEAD * h, HEAD * (h + 1))
                target[rows, place] = rotate(lin[:, place], cos_rows, sin_rows, 1.0).astype(BF16)
        v_ref[rows, :] = dot_nn(block, w_buf[2]).astype(BF16)

        @pl.when(c + 2 < count)
        def _():
            incoming.relay(c + 2)

    loop(count, work)

    def end(c):
        incoming.arrive(c)
        out(c, 1).start()

    loop(count, end)

    def drain(c):
        for i in range(3):
            out(c, i).wait()
        stats.finish(c)
        gather.finish(c)
        incoming.finish(c)

    loop(count, drain)


def window_bias(c, start, extent, segc_ref, segr_ref, bias):
    def part(r):
        rows = pl.ds(pl.multiple_of(r * ROWS, ROWS), ROWS)
        row = c * CHUNK + r * ROWS + lax.broadcasted_iota(jnp.int32, (ROWS, extent), 0)
        column = start + lax.broadcasted_iota(jnp.int32, (ROWS, extent), 1)
        same = segc_ref[sub_rows(c, r), 0:1] == segr_ref[0:1, pl.ds(start, extent)]
        bias[rows, :] = jnp.where((row >= column) & same, 0.0, MASKED)

    loop(CHUNK // ROWS, part)


def window(c, tokens):
    extent = min(tokens, CHUNK * (-(-(LONGEST - 1) // CHUNK) + 1))
    back = extent // CHUNK - 1
    return pl.multiple_of(jnp.maximum(c - back, 0) * CHUNK, CHUNK), extent


def attend_kernel(
    n, in1, out1, in2, out2, res1, res2, q_ref, k_ref, v_ref, segc_ref, segr_ref, wo_ref,
    s_hbm, gb2_hbm, wg_hbm, wu_hbm, wd_hbm,
    attended_ref, branch_ref, normed_hbm, stand_ref, scale_ref, hidden_hbm, acts_hbm, grads_hbm,
    s_buf, gb2_buf, wg_buf, wu_buf, wd_buf, hidden_buf, gate_buf, up_buf,
    part, came, all2, first, second, mine, others, bias,
    s_sem, gb2_sem, grad_sem, w_sem, normed_sem, out_sem, send1, recv1, send2, recv2, send3, recv3,
):
    tokens, width = q_ref.shape
    units = wg_buf.shape[1]
    count = tokens // CHUNK
    heads = width // HEAD
    block = min(units, 512)
    mixing = Mixing((in1, out1, in2, out2, res1, res2))

    def s_in(c):
        slot = lax.rem(c, 2)
        return pltpu.make_async_copy(s_hbm.at[:, chunk_rows(c)], s_buf.at[slot], s_sem.at[slot])

    def gb2_in(c):
        slot = lax.rem(c, 2)
        return pltpu.make_async_copy(gb2_hbm.at[chunk_rows(c)], gb2_buf.at[slot], gb2_sem.at[slot])

    def grads_out(c):
        slot = lax.rem(c, 2)
        return pltpu.make_async_copy(
            gate_buf.at[slot], grads_hbm.at[chunk_rows(c)], grad_sem.at[0, slot]
        )

    def grads_in(c):
        slot = lax.rem(c, 2)
        return pltpu.make_async_copy(
            grads_hbm.at[chunk_rows(c)], gb2_buf.at[slot, :, 0:units], grad_sem.at[1, slot]
        )

    def normed_out(c):
        return pltpu.make_async_copy(
            all2.at[chunk_rows(c)], normed_hbm.at[chunk_rows(c)], normed_sem.at[c]
        )

    def outs(c):
        slot, rows = lax.rem(c, 2), chunk_rows(c)
        return tuple(
            pltpu.make_async_copy(buf.at[slot], target, out_sem.at[i, slot])
            for i, (buf, target) in enumerate(
                (
                    (hidden_buf, hidden_hbm.at[rows]),
                    (gate_buf, acts_hbm.at[rows, 0:units]),
                    (up_buf, acts_hbm.at[rows, units : 2 * units]),
                )
            )
        )

    weights = tuple(
        pltpu.make_async_copy(source, target, w_sem.at[i])
        for i, (source, target) in enumerate(
            ((wd_hbm, wd_buf), (wg_hbm, wg_buf), (wu_hbm, wu_buf))
        )
    )
    s_in(0).start()
    gb2_in(0).start()
    gb2_in(1).start()
    for copy in weights:
        copy.start()
    scatter = Scatter(n, part, came, width, send1, recv1)
    gather = Gather(n, all2, width, send2, recv2)
    stats = Stats(n, mine, others, send3, recv3)
    enter(n, gather.to)

    def attend(c):
        rows = chunk_rows(c)
        start, extent = window(c, tokens)
        window_bias(c, start, extent, segc_ref, segr_ref, bias)
        for h in range(heads):
            place = slice(HEAD * h, HEAD * (h + 1))
            scores = dot_nt(q_ref[rows, place], k_ref[pl.ds(start, extent), place])
            scores = scores * HEAD ** (-0.5) + bias[...]
            raised = jnp.exp(scores - jnp.max(scores, axis=1, keepdims=True))
            inverse = 1.0 / jnp.sum(raised, axis=1, keepdims=True)
            probs = (raised * inverse).astype(BF16)
            attended_ref[rows, place] = dot_nn(probs, v_ref[pl.ds(start, extent), place]).astype(BF16)
        part[rows, :] = dot_nn(attended_ref[rows, :], wo_ref[...]).astype(BF16)

    def middle(c):
        @pl.when(c + 1 < count)
        def _():
            s_in(c + 1).start()

        s_in(c).wait()
        slot = lax.rem(c, 2)
        scatter.arrive(c)

        def piece(r):
            rows = sub_rows(c, r)
            branch = scatter.total(rows)
            branch_ref[rows, :] = branch
            entry = mixing.across * branch
            for i in range(s_buf.shape[1]):
                entry += mixing.entry[i] * s_buf[slot, i, local_rows(r)].astype(F32)
            stand_ref[rows, :] = entry
            fold_entry(entry, first, second, local_rows(r))

        loop(CHUNK // ROWS, piece)
        stats.put(c, first[...], second[...])
        stats.start(c)

    def send(c):
        standardize(c, stats, gather, first, second, stand_ref, scale_ref)

    def work(c):
        gather.arrive(c)
        normed_out(c).start()
        slot = lax.rem(c, 2)

        @pl.when(c >= 2)
        def _():
            for copy in outs(c - 2):
                copy.wait()

        grads_in(c).wait()

        def piece(f):
            place = columns(f, block)
            gate = dot_nn(all2[chunk_rows(c), :], wg_buf[:, place])
            up = dot_nn(all2[chunk_rows(c), :], wu_buf[:, place])
            grad = gb2_buf[slot, :, place].astype(F32)
            sig = jax.nn.sigmoid(gate)
            act = gate * sig
            hidden_buf[slot, :, place] = (act * up).astype(BF16)
            gate_buf[slot, :, place] = (grad * up * sig * (1.0 + gate * (1.0 - sig))).astype(BF16)
            up_buf[slot, :, place] = (grad * act).astype(BF16)

        loop(units // block, piece)
        for copy in outs(c):
            copy.start()

        @pl.when(c + 2 < count)
        def _():
            grads_in(c + 2).start()
            gather.relay(c + 2)

    def grads(c):
        slot = lax.rem(c, 2)
        if c >= 2:
            grads_out(c - 2).wait()
        gb2_in(c).wait()

        def piece(f):
            place = columns(f, block)
            gate_buf[slot, :, place] = dot_nt(gb2_buf[slot], wd_buf[place, :]).astype(BF16)

        loop(units // block, piece)
        grads_out(c).start()
        if c + 2 < count:
            gb2_in(c + 2).start()

    def attend_send(c):
        attend(c)
        scatter.start(c)

        @pl.when(c >= 1)
        def _():
            scatter.relay(c - 1)

    loop(count, attend_send)
    middle(0)
    weights[0].wait()
    grads(0)
    scatter.relay(3)
    middle(1)
    send(0)
    grads(1)
    middle(2)
    send(1)
    grads(2)
    middle(3)
    grads(3)
    gather.relay(0)
    send(2)
    gather.relay(1)
    send(3)
    grads_out(2).wait()
    grads_out(3).wait()
    grads_in(0).start()
    grads_in(1).start()
    weights[1].wait()
    weights[2].wait()
    loop(count, work)
    for c in range(max(count - 2, 0), count):
        for copy in outs(c):
            copy.wait()

    def drain(c):
        normed_out(c).wait()
        scatter.finish(c)
        stats.finish(c)
        gather.finish(c)

    loop(count, drain)


def stats_part(part32, normed, normed_rows, part, c, first, second):
    def piece(r):
        rows = pl.ds(pl.multiple_of(r * ROWS, ROWS), ROWS)
        field = part32[rows, :]
        first[rows, :] = fold_lanes(field)
        second[rows, :] = fold_lanes(field * normed[normed_rows(r), :].astype(F32))
        part[sub_rows(c, r), :] = field.astype(BF16)

    loop(CHUNK // ROWS, piece)


def units_back_kernel(
    n, in1, out1, in2, out2, res1, res2, acts_ref, wg_ref, wu_ref, normed_ref, stand_ref, scale_ref, c_hbm, _down, _gate_up,
    entry_ref, gb1_hbm,
    c_buf, part32, first, second, part, came, mine, others, all1, in_sem, out_sem,
    send1, recv1, send2, recv2, send3, recv3,
):
    tokens, features = normed_ref.shape
    width = entry_ref.shape[1]
    count = tokens // CHUNK
    mixing = Mixing((in1, out1, in2, out2, res1, res2))
    c_in = pltpu.make_async_copy(c_hbm, c_buf, in_sem)
    c_in.start()
    scatter = Scatter(n, part, came, width, send1, recv1)
    stats = Stats(n, mine, others, send2, recv2)
    gather = Gather(n, all1, width, send3, recv3)
    enter(n, gather.to)

    def work(c):
        rows = chunk_rows(c)
        units = wg_ref.shape[1]
        part32[...] = dot_nt(acts_ref[rows, 0:units], wg_ref[...])
        part32[...] += dot_nt(acts_ref[rows, units : 2 * units], wu_ref[...])
        stats_part(part32, normed_ref, lambda r: sub_rows(c, r), part, c, first, second)
        stats.put(c, first[...], second[...])
        stats.start(c)
        scatter.start(c)

        @pl.when(c >= 1)
        def _():
            scatter.relay(c - 1)

    def middle(c):
        scatter.arrive(c)
        stats.arrive(c)
        first[...], second[...] = stats.means(c, features)

        def piece(r):
            rows = sub_rows(c, r)
            local = pl.ds(pl.multiple_of(r * ROWS, ROWS), ROWS)
            standard = stand_ref[rows, :]
            entry = repeat_lanes(scale_ref[rows, :], width) * (
                scatter.total(rows)
                - repeat_lanes(first[local, :], width)
                - standard * repeat_lanes(second[local, :], width)
            )
            entry_ref[rows, :] = entry
            grad = mixing.across * entry
            for i in range(c_buf.shape[0]):
                grad += mixing.branch[i] * c_buf[i, rows].astype(F32)
            all1[rows, gather.own()] = grad.astype(BF16)

        loop(CHUNK // ROWS, piece)
        gather.start(c)

    c_in.wait()

    def ahead(c):
        work(c)

        @pl.when(c >= 2)
        def _():
            middle(c - 2)

    loop(count, ahead)
    scatter.relay(count - 1)
    middle(count - 2)
    gather.relay(0)
    middle(count - 1)
    for c in range(1, count):
        gather.relay(c)

    def gb1_out(c):
        return pltpu.make_async_copy(
            all1.at[chunk_rows(c)], gb1_hbm.at[chunk_rows(c)], out_sem.at[c]
        )

    def last(c):
        gather.arrive(c)
        gb1_out(c).start()

    loop(count, last)

    def drain(c):
        gb1_out(c).wait()
        scatter.finish(c)
        stats.finish(c)
        gather.finish(c)

    loop(count, drain)


def attend_back_kernel(
    n, q_ref, k_ref, v_ref, segc_ref, segr_ref, cos_ref, sin_ref, wo_ref, wq_ref, wk_ref, wv_ref,
    wd_ref, stand_ref, scale_ref, gb1_hbm, hidden_hbm, normed_hbm, _output, _down,
    lin_ref, branch_ref, entry_ref,
    gb1_buf, hidden_buf, normed_buf, bias, dk_t, dv_t, part32, first, second,
    part1, came1, part2, came2, mine, others, in_sem,
    send1, recv1, send2, recv2, send3, recv3,
):
    tokens, width = q_ref.shape
    features = part1.shape[1]
    count = tokens // CHUNK
    heads = width // HEAD
    factor = HEAD ** (-0.5)
    down = Scatter(n, part2, came2, width, send1, recv1)
    scatter = Scatter(n, part1, came1, width, send2, recv2)
    stats = Stats(n, mine, others, send3, recv3)

    def inputs(c, slot):
        return tuple(
            pltpu.make_async_copy(source.at[chunk_rows(c)], target.at[slot], in_sem.at[i, slot])
            for i, (source, target) in enumerate(
                ((gb1_hbm, gb1_buf), (hidden_hbm, hidden_buf), (normed_hbm, normed_buf))
            )
        )

    for copy in inputs(count - 1, 0):
        copy.start()
    dk_t[...] = jnp.zeros_like(dk_t)
    dv_t[...] = jnp.zeros_like(dv_t)
    enter(n, scatter.to)

    def work(i):
        c = count - 1 - i
        slot = lax.rem(i, 2)

        @pl.when(i < count - 1)
        def _():
            for copy in inputs(c - 1, 1 - slot):
                copy.start()

        for copy in inputs(c, slot):
            copy.wait()
        rows = chunk_rows(c)
        part2[rows, :] = dot_nn(hidden_buf[slot], wd_ref[...]).astype(BF16)
        down.start(c)
        grad = dot_nt(gb1_buf[slot], wo_ref[...]).astype(BF16)
        start, extent = window(c, tokens)
        keys = pl.ds(start, extent)
        window_bias(c, start, extent, segc_ref, segr_ref, bias)
        cos_rows, sin_rows = cos_ref[rows, :], sin_ref[rows, :]
        for h in range(heads):
            place = slice(HEAD * h, HEAD * (h + 1))
            query, grad_h = q_ref[rows, place], grad[:, place]
            scores = dot_nt(query, k_ref[keys, place]) * factor + bias[...]
            raised = jnp.exp(scores - jnp.max(scores, axis=1, keepdims=True))
            inverse = 1.0 / jnp.sum(raised, axis=1, keepdims=True)
            probs = raised * inverse
            grad_probs = dot_nt(grad_h, v_ref[keys, place])
            centre = jnp.sum(probs * grad_probs, axis=1, keepdims=True)
            grad_scores = (probs * (grad_probs - centre)).astype(BF16)
            dv_t[place, keys] += dot_nn(jnp.transpose(grad_h), probs.astype(BF16))
            dk_t[place, keys] += dot_nn(jnp.transpose(query), grad_scores)
            dq = dot_nn(grad_scores, k_ref[keys, place]) * factor
            lin_ref[rows, place] = rotate(dq, cos_rows, sin_rows, -1.0).astype(BF16)
            dk = jnp.transpose(dk_t[place, rows]) * factor
            lin_ref[rows, slice(width + HEAD * h, width + HEAD * (h + 1))] = rotate(dk, cos_rows, sin_rows, -1.0).astype(BF16)
            lin_ref[rows, slice(2 * width + HEAD * h, 2 * width + HEAD * (h + 1))] = jnp.transpose(dv_t[place, rows]).astype(BF16)
        part32[...] = dot_nt(lin_ref[rows, 0:width], wq_ref[...])
        part32[...] += dot_nt(lin_ref[rows, width : 2 * width], wk_ref[...])
        part32[...] += dot_nt(lin_ref[rows, 2 * width : 3 * width], wv_ref[...])
        stats_part(
            part32,
            normed_buf.at[slot],
            lambda r: pl.ds(pl.multiple_of(r * ROWS, ROWS), ROWS),
            part1,
            c,
            first,
            second,
        )
        stats.put(c, first[...], second[...])
        stats.start(c)
        scatter.start(c)
        down.relay(c)

        @pl.when(i >= 1)
        def _():
            scatter.relay(c + 1)

    loop(count, work)
    scatter.relay(0)

    def last(i):
        c = count - 1 - i
        down.arrive(c)

        def sums(r):
            branch_ref[sub_rows(c, r), :] = down.total(sub_rows(c, r))

        loop(CHUNK // ROWS, sums)
        scatter.arrive(c)
        stats.arrive(c)
        first[...], second[...] = stats.means(c, features)

        def piece(r):
            rows = sub_rows(c, r)
            local = pl.ds(pl.multiple_of(r * ROWS, ROWS), ROWS)
            entry_ref[rows, :] = repeat_lanes(scale_ref[rows, :], width) * (
                scatter.total(rows)
                - repeat_lanes(first[local, :], width)
                - stand_ref[rows, :] * repeat_lanes(second[local, :], width)
            )

        loop(CHUNK // ROWS, piece)

    loop(count, last)

    def drain(c):
        down.finish(c)
        scatter.finish(c)
        stats.finish(c)

    loop(count, drain)


def streams_kernel(
    in1, out1, in2, out2, res1, res2, s_ref, c_ref, b1_ref, b2_ref, e1_ref, e2_ref, new_ref, grad_ref, sums_ref
):
    @pl.when(pl.program_id(0) == 0)
    def _():
        sums_ref[...] = jnp.zeros_like(sums_ref)

    count = s_ref.shape[0]
    mixing = Mixing((in1, out1, in2, out2, res1, res2))
    mixed = [[mixing.mixed(k, j) for j in range(count)] for k in range(count)]

    def fold(field):
        field = fold_lanes(field)
        total = field[0:8]
        for j in range(1, field.shape[0] // 8):
            total += field[8 * j : 8 * (j + 1)]
        return total

    def piece(r):
        rows = pl.ds(pl.multiple_of(r * 16, 16), 16)
        s = [s_ref[i, rows].astype(F32) for i in range(count)]
        c = [c_ref[i, rows].astype(F32) for i in range(count)]
        b1, b2, e1, e2 = b1_ref[rows, :], b2_ref[rows, :], e1_ref[rows, :], e2_ref[rows, :]
        for j in range(count):
            new = mixing.branch[j] * b1 + mixing.out2[j] * b2
            grad = mixing.entry[j] * e2 + mixing.in1[j] * e1
            for k in range(count):
                new += mixed[k][j] * s[k]
                grad += mixed[j][k] * c[k]
            new_ref[rows, j, :] = new.astype(BF16)
            grad_ref[rows, j, :] = grad
        pairs = [(s[i], c[j]) for i in range(count) for j in range(count)]
        pairs += [(s[i], e1) for i in range(count)] + [(s[i], e2) for i in range(count)]
        pairs += [(c[i], b1) for i in range(count)] + [(c[i], b2) for i in range(count)]
        pairs += [(b1, e2)]
        for place, (left, right) in enumerate(pairs):
            sums_ref[place] += fold(left * right)

    loop(s_ref.shape[1] // 16, piece)


PLANES = 4
CORES = 2
SUMS = 33
SUM_ROWS = 40


def pair_kernel(
    left_hbm, right_hbm, out_hbm, left, right, turned, sent, came, mine_buf,
    left_sem, right_sem, out_sem, send_sem, recv_sem,
):
    steps, height, width = came.shape
    block = height // 2
    piece = right_sem.shape[0]
    across = width // piece
    me = lax.axis_index("dp")
    mine = lax.rem(me, CORES)
    partner = me + 1 - 2 * mine

    def left_in(step, half, part):
        index = (2 * step + part) * CORES + half
        return pltpu.make_async_copy(
            left_hbm.at[:, columns(index, block)],
            left.at[2 * step + part, half],
            left_sem.at[2 * step + part, half],
        )

    def right_in(f):
        return pltpu.make_async_copy(
            right_hbm.at[:, columns(f, across)], right.at[:, columns(f, across)], right_sem.at[f]
        )

    def swap(step):
        return pltpu.make_async_remote_copy(
            src_ref=sent.at[step],
            dst_ref=came.at[step],
            send_sem=send_sem.at[step],
            recv_sem=recv_sem.at[step],
            device_id={"dp": partner},
            device_id_type=MESH,
        )

    def out(step):
        rows = pl.ds(pl.multiple_of(step * height, height), height)
        return pltpu.make_async_copy(mine_buf.at[step], out_hbm.at[rows], out_sem.at[step])

    for part in range(2):
        left_in(0, 1 - mine, part).start()
    for f in range(piece):
        right_in(f).start()
    for half in (1 - mine, mine):
        for step in range(steps):
            for part in range(2):
                if half is mine or step > 0:
                    left_in(step, half, part).start()
    barrier = pltpu.get_barrier_semaphore()
    pl.semaphore_signal(barrier, inc=1, device_id={"dp": partner}, device_id_type=MESH)
    pl.semaphore_wait(barrier, 1)

    def turn(step, half):
        for part in range(2):
            left_in(step, half, part).wait()
            turned[part * block : (part + 1) * block, :] = jnp.transpose(left[2 * step + part, half])

    def other(step):
        turn(step, 1 - mine)

        def part(f):
            @pl.when(step == 0)
            def _():
                right_in(f).wait()

            place = columns(f, across)
            sent[step, :, place] = dot_nn(turned[...], right[:, place]).astype(BF16)

        loop(piece, part)
        swap(step).start()

    loop(steps, other)

    def own(step):
        turn(step, mine)
        swap(step).wait_recv()

        def part(f):
            place = columns(f, across)
            total = dot_nn(turned[...], right[:, place]) + came[step, :, place].astype(F32)
            mine_buf[step, :, place] = total.astype(BF16)

        loop(piece, part)
        out(step).start()

    loop(steps, own)

    def drain(step):
        swap(step).wait_send()
        out(step).wait()

    loop(steps, drain)


def finish_kernel(
    n, first_hbm, last_hbm, sums_ref,
    q_out, k_out, v_out, o_out, sums_out,
    own, core, right, left, by_core, by_plane, by_tensor,
    own_sem, core_send, core_recv, right_send, right_recv, left_send, left_recv, sum_send, sum_recv,
):
    _, pieces, height, width = own.shape
    me = lax.axis_index("dp")
    plane, mine = lax.div(me, CORES), lax.rem(me, CORES)
    partner = me + 1 - 2 * mine
    here, peers, peer_source = partners(n)
    planes_to = [lax.rem(plane + k, PLANES) for k in range(1, PLANES)]
    planes_from = [lax.rem(plane + PLANES - k, PLANES) for k in range(1, PLANES)]

    def dp_at(position):
        return position * CORES + mine

    def rows_of(position, half):
        return pl.ds(pl.multiple_of((position * CORES + half) * height, height), height)

    def block(position, half, p):
        if p < pieces - 1:
            return first_hbm.at[rows_of(position, half), p * width : (p + 1) * width]
        return last_hbm.at[rows_of(position, half)]

    def over_dp(source, target, send_sem, recv_sem, device):
        return pltpu.make_async_remote_copy(
            src_ref=source, dst_ref=target, send_sem=send_sem, recv_sem=recv_sem,
            device_id={"dp": device}, device_id_type=MESH,
        )

    def own_in(position, p):
        return pltpu.make_async_copy(
            block(position, mine, p), own.at[position, p], own_sem.at[position, p]
        )

    def core_in(position, p):
        return over_dp(
            block(position, 1 - mine, p), core.at[position, p],
            core_send.at[position, p], core_recv.at[position, p], partner,
        )

    def rightward(step, p):
        return over_dp(
            own.at[lax.rem(plane + PLANES - step, PLANES), p], right.at[step - 1, p],
            right_send.at[step - 1, p], right_recv.at[step - 1, p], lax.rem(me + CORES, PLANES * CORES),
        )

    def leftward(step, p):
        return over_dp(
            own.at[lax.rem(plane + step, PLANES), p], left.at[step - 1, p],
            left_send.at[step - 1, p], left_recv.at[step - 1, p],
            lax.rem(me + (PLANES - 1) * CORES, PLANES * CORES),
        )

    order = (3, 0, 2, 1)
    for position in order:
        for p in range(pieces):
            own_in(position, p).start()

    barrier = pltpu.get_barrier_semaphore()
    pl.semaphore_signal(barrier, inc=1, device_id={"dp": partner}, device_id_type=MESH)
    for k in range(PLANES - 1):
        pl.semaphore_signal(
            barrier, inc=1, device_id={"dp": dp_at(planes_to[k])}, device_id_type=MESH
        )
    for k in range(n - 1):
        pl.semaphore_signal(barrier, inc=1, device_id={"tensor": peers[k]}, device_id_type=MESH)
    pl.semaphore_wait(barrier, 1 + PLANES - 1 + n - 1)

    by_core[mine] = jnp.zeros((SUM_ROWS, 128), F32)
    by_core[mine, 0:SUMS] = jnp.sum(sums_ref[...], axis=1)
    over_dp(
        by_core.at[mine], by_core.at[mine], sum_send.at[0], sum_recv.at[0], partner
    ).start()
    for position in order:
        for p in range(pieces):
            core_in(position, p).start()
    over_dp(
        by_core.at[1 - mine], by_core.at[1 - mine], sum_send.at[0], sum_recv.at[0], partner
    ).wait_recv()
    by_plane[plane] = by_core[0] + by_core[1]

    def plane_sums(k, at):
        return over_dp(
            by_plane.at[at], by_plane.at[at], sum_send.at[1 + k], sum_recv.at[1 + k],
            dp_at(planes_to[k]),
        )

    def tensor_sums(k, at):
        at = by_tensor.at[at]
        return remote(at, at, sum_send.at[PLANES + k], sum_recv.at[PLANES + k], peers[k])

    for k in range(PLANES - 1):
        plane_sums(k, plane).start()

    def gather_pair(position):
        def piece(p):
            pltpu.make_async_copy(
                own.at[position, p], own.at[position, p], own_sem.at[position, p]
            ).wait()
            over_dp(
                core.at[position, p], core.at[position, p],
                core_send.at[position, p], core_recv.at[position, p], partner,
            ).wait_recv()
            add(own.at[position, p], core.at[position, p])

        loop(pieces, piece)

    def add(target, source):
        def part(r):
            rows = local_rows(r)
            target[rows, :] = (target[rows, :].astype(F32) + source[rows, :].astype(F32)).astype(BF16)

        loop(height // ROWS, part)

    def send_step(step):
        def piece(p):
            @pl.when(plane <= step - 1)
            def _():
                if step >= 2:

                    @pl.when(plane >= 1)
                    def _():
                        rightward(step - 1, p).wait_recv()
                        add(own.at[lax.rem(plane + PLANES - step, PLANES), p], right.at[step - 2, p])

                rightward(step, p).start()

            @pl.when(plane >= PLANES - step)
            def _():
                if step >= 2:

                    @pl.when(plane <= PLANES - 2)
                    def _():
                        leftward(step - 1, p).wait_recv()
                        add(own.at[lax.rem(plane + step, PLANES), p], left.at[step - 2, p])

                leftward(step, p).start()

        loop(pieces, piece)

    gather_pair(3)
    gather_pair(0)
    send_step(1)
    gather_pair(2)
    gather_pair(1)
    for k in range(PLANES - 1):
        plane_sums(k, planes_from[k]).wait_recv()
    by_tensor[here] = sum((by_plane[i] for i in range(1, PLANES)), by_plane[0])
    for k in range(n - 1):
        tensor_sums(k, here).start()
    for step in range(2, PLANES):
        send_step(step)
    for k in range(n - 1):
        tensor_sums(k, peer_source[k]).wait_recv()
    sums_out[...] = sum((by_tensor[i] for i in range(1, n)), by_tensor[0])

    for p, target in enumerate((q_out, k_out, v_out, o_out)):
        steps = PLANES - 2

        @pl.when(plane >= 1)
        def _():
            rightward(PLANES - 1, p).wait_recv()

        @pl.when(plane <= PLANES - 2)
        def _():
            leftward(PLANES - 1, p).wait_recv()

        total = own[plane, p].astype(F32)
        total += jnp.where(plane >= 1, right[steps, p].astype(F32), 0.0)
        total += jnp.where(plane <= PLANES - 2, left[steps, p].astype(F32), 0.0)
        target[...] = total if p < pieces - 1 else jnp.transpose(total)

    over_dp(by_core.at[mine], by_core.at[mine], sum_send.at[0], sum_recv.at[0], partner).wait_send()
    for k in range(PLANES - 1):
        plane_sums(k, plane).wait_send()
    for k in range(n - 1):
        tensor_sums(k, here).wait_send()
    for p in range(pieces):
        for position in range(PLANES):
            core_in(position, p).wait_send()
        for step in range(1, PLANES):

            @pl.when(plane <= step - 1)
            def _():
                rightward(step, p).wait_send()

            @pl.when(plane >= PLANES - step)
            def _():
                leftward(step, p).wait_send()


def on_device(
    n,
    replicas,
    streams,
    segments,
    positions,
    mix_in1,
    mix_res1,
    mix_out1,
    mix_in2,
    mix_res2,
    mix_out2,
    w_query,
    w_key,
    w_value,
    w_output,
    w_gate,
    w_up,
    w_down,
    cotangent,
):
    tokens, stream_count, width = streams.shape
    features = w_query.shape[0]
    units = w_gate.shape[1]
    chunks = tokens // CHUNK
    assert tokens == LENGTH == 4 * CHUNK and stream_count == 4
    any_spec = pl.BlockSpec(memory_space=pl.ANY)
    vmem = pl.BlockSpec(memory_space=pltpu.VMEM)
    smem = pl.BlockSpec(memory_space=pltpu.SMEM)

    def array(shape, dtype):
        return jax.ShapeDtypeStruct(shape, dtype)

    def dma(*shape):
        return pltpu.SemaphoreType.DMA(shape)

    def pair(lanes):
        return [dma(lanes, chunks), dma(lanes, chunks)]

    gather_sems = pair(4 if n == 4 else n - 1)
    scatter_sems = pair(6 if n == 4 else n - 1)
    stats_sems = pair(n - 1)

    def lasts(micros):
        return pl.CostEstimate(
            flops=int(micros * 1.0e9), bytes_accessed=int(micros * 3.6e6), transcendentals=0
        )

    def params(identity, mib):
        return pltpu.CompilerParams(
            collective_id=identity, has_side_effects=True, vmem_limit_bytes=mib * MIB
        )

    def small(form, left, right):
        return jnp.einsum(form, left, right, precision=PRECISE)

    planes = jnp.transpose(streams, (1, 0, 2))
    mixes = (mix_in1, mix_out1, mix_in2, mix_out2, mix_res1, mix_res2)

    def stats_scratch():
        return [
            pltpu.VMEM((CHUNK, 128), F32),
            pltpu.VMEM((CHUNK, 128), F32),
            pltpu.VMEM((chunks, 16, CHUNK), F32),
            pltpu.VMEM((n - 1, chunks, 16, CHUNK), F32),
        ]

    (
        normed1, queries, keys, values, stand1, scale1, grad_branch2, cot_planes,
        cos_table, sin_table, seg_column, seg_row,
    ) = pl.pallas_call(
        functools.partial(project_kernel, n),
        name="project",
        cost_estimate=lasts(100),
        out_shape=[
            array((tokens, features), BF16),
            array((tokens, width), BF16),
            array((tokens, width), BF16),
            array((tokens, width), BF16),
            array((tokens, width), F32),
            array((tokens, 128), F32),
            array((tokens, features), BF16),
            array((stream_count, tokens, width), BF16),
            array((tokens, HEAD), F32),
            array((tokens, HEAD), F32),
            array((tokens, 128), F32),
            array((8, tokens), F32),
        ],
        in_specs=[smem, smem, vmem, vmem] + [any_spec] * 5,
        out_specs=[any_spec] + [vmem] * 5 + [any_spec] * 2 + [vmem] * 4,
        scratch_shapes=[
            pltpu.VMEM((stream_count, tokens, width), BF16),
            pltpu.VMEM((tokens, stream_count, width), BF16),
            pltpu.VMEM((stream_count, tokens, width), BF16),
            pltpu.VMEM((3, features, width), BF16),
            pltpu.VMEM((tokens, features), BF16),
            pltpu.VMEM((tokens, features), BF16),
        ]
        + stats_scratch()
        + [dma(2, chunks), dma(3), dma(3, chunks)]
        + gather_sems
        + gather_sems
        + stats_sems,
        compiler_params=params(0, 56),
    )(
        mix_in1, mix_out2,
        positions.reshape(tokens // 128, 128), segments.reshape(tokens // 128, 128),
        planes, cotangent, w_query, w_key, w_value,
    )

    extent = window(0, tokens)[1]
    attended, branch1, normed2, stand2, scale2, hidden, grad_acts, _ = pl.pallas_call(
        functools.partial(attend_kernel, n),
        name="attend",
        cost_estimate=lasts(100),
        out_shape=[
            array((tokens, width), BF16),
            array((tokens, width), F32),
            array((tokens, features), BF16),
            array((tokens, width), F32),
            array((tokens, 128), F32),
            array((tokens, units), BF16),
            array((tokens, 2 * units), BF16),
            array((tokens, units), BF16),
        ],
        in_specs=[smem] * 6 + [vmem] * 6 + [any_spec] * 5,
        out_specs=[vmem, vmem, any_spec, vmem, vmem, any_spec, any_spec, any_spec],
        scratch_shapes=[
            pltpu.VMEM((2, stream_count, CHUNK, width), BF16),
            pltpu.VMEM((2, CHUNK, features), BF16),
            pltpu.VMEM((features, units), BF16),
            pltpu.VMEM((features, units), BF16),
            pltpu.VMEM((units, features), BF16),
            pltpu.VMEM((2, CHUNK, units), BF16),
            pltpu.VMEM((2, CHUNK, units), BF16),
            pltpu.VMEM((2, CHUNK, units), BF16),
            pltpu.VMEM((tokens, features), BF16),
            pltpu.VMEM((n - 1, tokens, width), BF16),
            pltpu.VMEM((tokens, features), BF16),
        ]
        + stats_scratch()
        + [pltpu.VMEM((CHUNK, extent), F32), dma(2), dma(2), dma(2, 2)]
        + [dma(3), dma(chunks), dma(3, 2)]
        + scatter_sems
        + gather_sems
        + stats_sems,
        compiler_params=params(1, 62),
    )(
        *mixes, queries, keys, values, seg_column, seg_row, w_output, planes,
        grad_branch2, w_gate, w_up, w_down,
    )

    def over_dp(partial, dimension):
        return lax.psum_scatter(partial, "dp", scatter_dimension=dimension, tiled=True)

    height = features // replicas
    paired = replicas == PLANES * CORES

    def weight_sum(identity, left, right):
        if not paired:
            partial = contract_rows(left, right).astype(BF16)
            return over_dp(partial, 0), partial
        steps, columns_in = PLANES // 2, right.shape[1]
        pieces = max(columns_in // 1024, 1)
        partial = pl.pallas_call(
            pair_kernel,
            name="pair",
            cost_estimate=lasts(20),
            out_shape=array((features // CORES, columns_in), BF16),
            in_specs=[any_spec, any_spec],
            out_specs=any_spec,
            scratch_shapes=[
                pltpu.VMEM((PLANES, CORES, tokens, height), BF16),
                pltpu.VMEM((tokens, columns_in), BF16),
                pltpu.VMEM((2 * height, tokens), BF16),
                pltpu.VMEM((steps, 2 * height, columns_in), BF16),
                pltpu.VMEM((steps, 2 * height, columns_in), BF16),
                pltpu.VMEM((steps, 2 * height, columns_in), BF16),
                dma(PLANES, CORES),
                dma(pieces),
                dma(steps),
                dma(steps),
                dma(steps),
            ],
            compiler_params=params(identity, 56),
        )(left, right)
        groups = [[CORES * plane + c for plane in range(PLANES)] for c in range(CORES)]
        total = lax.psum_scatter(
            partial, "dp", scatter_dimension=0, tiled=True, axis_index_groups=groups
        )
        return total, partial

    grad_down, part_down = weight_sum(5, grad_branch2, hidden)
    grad_gate_up, part_gate_up = weight_sum(6, normed2, grad_acts)
    grad_w_down = jnp.transpose(grad_down).astype(F32)
    grad_w_gate = grad_gate_up[:, :units].astype(F32)
    grad_w_up = grad_gate_up[:, units:].astype(F32)

    grad_entry2, grad_branch1 = pl.pallas_call(
        functools.partial(units_back_kernel, n),
        name="units_back",
        cost_estimate=lasts(400),
        out_shape=[array((tokens, width), F32), array((tokens, features), BF16)],
        in_specs=[smem] * 6 + [vmem] * 6 + [any_spec] * 3,
        out_specs=[vmem, any_spec],
        scratch_shapes=[
            pltpu.VMEM((stream_count, tokens, width), BF16),
            pltpu.VMEM((CHUNK, features), F32),
            pltpu.VMEM((CHUNK, 128), F32),
            pltpu.VMEM((CHUNK, 128), F32),
            pltpu.VMEM((tokens, features), BF16),
            pltpu.VMEM((n - 1, tokens, width), BF16),
            pltpu.VMEM((chunks, 16, CHUNK), F32),
            pltpu.VMEM((n - 1, chunks, 16, CHUNK), F32),
            pltpu.VMEM((tokens, features), BF16),
            pltpu.SemaphoreType.DMA,
            dma(chunks),
        ]
        + scatter_sems
        + stats_sems
        + gather_sems,
        compiler_params=params(2, 60),
    )(
        *mixes, grad_acts, w_gate, w_up, normed2, stand2, scale2, cot_planes,
        part_down, part_gate_up,
    )

    part_output = contract_rows(grad_branch1, attended).astype(BF16)

    grad_lin, branch2, grad_entry1 = pl.pallas_call(
        functools.partial(attend_back_kernel, n),
        name="attend_back",
        cost_estimate=lasts(2),
        out_shape=[array((tokens, 3 * width), BF16)] + [array((tokens, width), F32)] * 2,
        in_specs=[vmem] * 14 + [any_spec] * 5,
        out_specs=[vmem] * 3,
        scratch_shapes=[
            pltpu.VMEM((2, CHUNK, features), BF16),
            pltpu.VMEM((2, CHUNK, units), BF16),
            pltpu.VMEM((2, CHUNK, features), BF16),
            pltpu.VMEM((CHUNK, extent), F32),
            pltpu.VMEM((width, tokens), F32),
            pltpu.VMEM((width, tokens), F32),
            pltpu.VMEM((CHUNK, features), F32),
            pltpu.VMEM((CHUNK, 128), F32),
            pltpu.VMEM((CHUNK, 128), F32),
            pltpu.VMEM((tokens, features), BF16),
            pltpu.VMEM((n - 1, tokens, width), BF16),
            pltpu.VMEM((tokens, features), BF16),
            pltpu.VMEM((n - 1, tokens, width), BF16),
            pltpu.VMEM((chunks, 16, CHUNK), F32),
            pltpu.VMEM((n - 1, chunks, 16, CHUNK), F32),
            dma(3, 2),
        ]
        + scatter_sems
        + scatter_sems
        + stats_sems,
        compiler_params=params(3, 60),
    )(
        queries, keys, values, seg_column, seg_row, cos_table, sin_table,
        w_output, w_query, w_key, w_value, w_down, stand1, scale1,
        grad_branch1, hidden, normed1, part_output, grad_w_down,
    )

    part_lin = contract_rows(normed1, grad_lin).astype(BF16)

    rows = 128
    plane_spec = pl.BlockSpec((stream_count, rows, width), lambda t: (0, t, 0))
    field_spec = pl.BlockSpec((rows, width), lambda t: (t, 0))
    stream_spec = pl.BlockSpec((rows, stream_count, width), lambda t: (t, 0, 0))
    new_streams, stream_grad, sums = pl.pallas_call(
        streams_kernel,
        name="streams",
        cost_estimate=lasts(2),
        grid=(tokens // rows,),
        out_shape=[
            array(streams.shape, BF16),
            array(streams.shape, F32),
            array((SUMS, 8, 128), F32),
        ],
        in_specs=[smem] * 6 + [plane_spec, plane_spec] + [field_spec] * 4,
        out_specs=[
            stream_spec,
            stream_spec,
            pl.BlockSpec((SUMS, 8, 128), lambda t: (0, 0, 0)),
        ],
        compiler_params=pltpu.CompilerParams(vmem_limit_bytes=48 * MIB),
    )(*mixes, planes, cot_planes, branch1, branch2, grad_entry1, grad_entry2)
    if paired:
        steps = PLANES - 1
        grad_w_query, grad_w_key, grad_w_value, grad_w_output, sums = pl.pallas_call(
            functools.partial(finish_kernel, n),
            name="finish",
            cost_estimate=lasts(2),
            out_shape=[array((height, width), F32)] * 3
            + [array((width, height), F32), array((SUM_ROWS, 128), F32)],
            in_specs=[any_spec, any_spec, vmem],
            out_specs=[vmem] * 5,
            scratch_shapes=[
                pltpu.VMEM((PLANES, 4, height, width), BF16),
                pltpu.VMEM((PLANES, 4, height, width), BF16),
                pltpu.VMEM((steps, 4, height, width), BF16),
                pltpu.VMEM((steps, 4, height, width), BF16),
                pltpu.VMEM((CORES, SUM_ROWS, 128), F32),
                pltpu.VMEM((PLANES, SUM_ROWS, 128), F32),
                pltpu.VMEM((n, SUM_ROWS, 128), F32),
                dma(PLANES, 4),
                dma(PLANES, 4),
                dma(PLANES, 4),
                dma(steps, 4),
                dma(steps, 4),
                dma(steps, 4),
                dma(steps, 4),
                dma(PLANES + n - 1),
                dma(PLANES + n - 1),
            ],
            compiler_params=params(4, 48),
        )(part_lin, part_output, sums)
        sums = jnp.sum(sums[:SUMS], axis=1)
    else:
        grad_w_query, grad_w_key, grad_w_value = (
            over_dp(part_lin[:, width * j : width * (j + 1)], 0).astype(F32) for j in range(3)
        )
        grad_w_output = jnp.transpose(over_dp(part_output, 0)).astype(F32)
        sums = lax.psum(jnp.sum(sums, axis=(1, 2)), ("dp", "tensor"))
    s_c = sums[0:16].reshape(4, 4)
    s_e1, s_e2, c_b1, c_b2, b_e = sums[16:20], sums[20:24], sums[24:28], sums[28:32], sums[32]
    grad_mix_in1 = s_e1
    grad_mix_res1 = small("ik,jk->ij", s_c, mix_res2) + s_e2[:, None] * mix_in2[None, :]
    grad_mix_out1 = small("jk,k->j", mix_res2, c_b1) + mix_in2 * b_e
    grad_mix_in2 = small("ki,k->i", mix_res1, s_e2) + mix_out1 * b_e
    grad_mix_res2 = small("ki,kj->ij", mix_res1, s_c) + mix_out1[:, None] * c_b1[None, :]
    grad_mix_out2 = c_b2
    return (
        new_streams,
        stream_grad,
        grad_w_query,
        grad_w_key,
        grad_w_value,
        grad_w_output,
        grad_w_gate,
        grad_w_up,
        grad_w_down,
        grad_mix_in1,
        grad_mix_res1,
        grad_mix_out1,
        grad_mix_in2,
        grad_mix_res2,
        grad_mix_out2,
    )


def solution(mesh):
    return jax.shard_map(
        functools.partial(on_device, mesh.shape["tensor"], mesh.shape["dp"]),
        mesh=mesh,
        in_specs=(
            P("dp", None, "tensor"),
            P("dp"),
            P("dp"),
            P(),
            P(),
            P(),
            P(),
            P(),
            P(),
            P(None, "tensor"),
            P(None, "tensor"),
            P(None, "tensor"),
            P("tensor", None),
            P(None, "tensor"),
            P(None, "tensor"),
            P("tensor", None),
            P("dp", None, "tensor"),
        ),
        out_specs=(
            P("dp", None, "tensor"),
            P("dp", None, "tensor"),
            P("dp", "tensor"),
            P("dp", "tensor"),
            P("dp", "tensor"),
            P("tensor", "dp"),
            P("dp", "tensor"),
            P("dp", "tensor"),
            P("tensor", "dp"),
            P(),
            P(),
            P(),
            P(),
            P(),
            P(),
        ),
        check_vma=False,
    )
```

```python
import functools
import math

import jax
import jax.numpy as jnp
from jax import lax
from jax.experimental import pallas as pl
from jax.experimental.pallas import tpu as pltpu
from jax.sharding import PartitionSpec as P

HEAD = 128
LENGTH = 1024
LONGEST = 512
EPS = 1e-05
PRECISE = lax.Precision.HIGHEST
MASKED = -1e30
MESH = pl.DeviceIdType.MESH
BF16 = jnp.bfloat16
F32 = jnp.float32
CHUNK = 256
ROWS = 32
MIB = 1 << 20


def inner(left, right):
    total = left[0] * right[0]
    for a, b in zip(left[1:], right[1:]):
        total += a * b
    return total


class Mixing:
    def __init__(self, refs):
        vectors = [[ref[i] for i in range(4)] for ref in refs[:4]]
        self.in1, self.out1, self.in2, self.out2 = vectors
        self.res1, self.res2 = (
            [[ref[i, j] for j in range(4)] for i in range(4)] for ref in refs[4:]
        )
        self.entry = [inner(row, self.in2) for row in self.res1]
        self.branch = [inner(self.out1, column) for column in zip(*self.res2)]
        self.across = inner(self.out1, self.in2)

    def mixed(self, k, j):
        return inner(self.res1[k], [row[j] for row in self.res2])


def contract_rows(left, right):
    return lax.dot_general(
        left, right, (((0,), (0,)), ((), ())), preferred_element_type=F32
    )


def dot_nn(left, right):
    return jnp.dot(left, right, preferred_element_type=F32)


def dot_nt(left, right):
    return lax.dot_general(
        left, right, (((1,), (1,)), ((), ())), preferred_element_type=F32
    )


def partners(n):
    me = lax.axis_index("tensor")
    if n == 4:
        both = (me + 1 - 2 * lax.rem(me, 2), lax.rem(me + 2, 4), 3 - me)
        return me, both, both
    to = tuple(lax.rem(me + k, n) for k in range(1, n))
    source = tuple(lax.rem(me + n - k, n) for k in range(1, n))
    return me, to, source


def enter(n, to):
    barrier = pltpu.get_barrier_semaphore()
    for target in to:
        pl.semaphore_signal(
            barrier, inc=1, device_id={"tensor": target}, device_id_type=MESH
        )
    pl.semaphore_wait(barrier, n - 1)


def remote(source, target, send_sem, recv_sem, device):
    return pltpu.make_async_remote_copy(
        src_ref=source,
        dst_ref=target,
        send_sem=send_sem,
        recv_sem=recv_sem,
        device_id={"tensor": device},
        device_id_type=MESH,
    )


def columns(index, width):
    return pl.ds(pl.multiple_of(index * width, 128), width)


def chunk_rows(c):
    return pl.ds(pl.multiple_of(c * CHUNK, CHUNK), CHUNK)


def half_rows(c, half):
    return pl.ds(pl.multiple_of(c * CHUNK + half * (CHUNK // 2), CHUNK // 2), CHUNK // 2)


class Gather:
    def __init__(self, n, buf, width, send_sem, recv_sem):
        self.n, self.buf, self.width = n, buf, width
        self.me, self.to, self.source = partners(n)
        self.send_sem, self.recv_sem = send_sem, recv_sem

    def own(self):
        return columns(self.me, self.width)

    def copy(self, rows, owner, k, c, target):
        view = self.buf.at[rows, columns(owner, self.width)]
        return remote(view, view, self.send_sem.at[k, c], self.recv_sem.at[k, c], target)

    def direct(self):
        return 2 if self.n == 4 else self.n - 1

    def handed(self, c):
        side, up, _ = self.to
        return (
            self.copy(half_rows(c, 0), side, 2, c, up),
            self.copy(half_rows(c, 1), up, 3, c, side),
        )

    def start(self, c):
        for k in range(self.direct()):
            self.copy(chunk_rows(c), self.me, k, c, self.to[k]).start()

    def relay(self, c):
        if self.n == 4:
            for k, copy in enumerate(self.handed(c)):
                self.copy(chunk_rows(c), self.source[k], k, c, self.to[k]).wait_recv()
                copy.start()

    def arrive(self, c):
        if self.n == 4:
            side, up, across = self.to
            self.copy(half_rows(c, 0), across, 2, c, up).wait_recv()
            self.copy(half_rows(c, 1), across, 3, c, side).wait_recv()
        else:
            for k in range(self.n - 1):
                self.copy(chunk_rows(c), self.source[k], k, c, self.to[k]).wait_recv()

    def finish(self, c):
        for k in range(self.direct()):
            self.copy(chunk_rows(c), self.me, k, c, self.to[k]).wait_send()
        if self.n == 4:
            for copy in self.handed(c):
                copy.wait_send()


class Scatter:
    def __init__(self, n, part, came, width, send_sem, recv_sem):
        self.n, self.part, self.came, self.width = n, part, came, width
        self.me, self.to, self.source = partners(n)
        self.send_sem, self.recv_sem = send_sem, recv_sem

    def copy(self, rows, owner, slot, k, c, target):
        return remote(
            self.part.at[rows, columns(owner, self.width)],
            self.came.at[slot, rows],
            self.send_sem.at[k, c],
            self.recv_sem.at[k, c],
            target,
        )

    def first(self, c):
        if self.n != 4:
            return tuple(
                (chunk_rows(c), self.to[k], k, k, c, self.to[k]) for k in range(self.n - 1)
            )
        side, up, across = self.to
        return (
            (half_rows(c, 0), across, 2, 0, c, side),
            (half_rows(c, 1), across, 2, 1, c, up),
            (half_rows(c, 0), side, 0, 2, c, side),
            (half_rows(c, 1), up, 1, 3, c, up),
        )

    def second(self, c):
        if self.n != 4:
            return ()
        side, up, _ = self.to
        return (
            (half_rows(c, 0), up, 1, 4, c, up),
            (half_rows(c, 1), side, 0, 5, c, side),
        )

    def start(self, c):
        for place in self.first(c):
            self.copy(*place).start()

    def relay(self, c):
        second = self.second(c)
        first = self.first(c)
        for half in range(len(second)):
            self.copy(*first[half]).wait_recv()
            owner = columns(self.to[1 - half], self.width)
            base = c * CHUNK + half * (CHUNK // 2)

            def add(r):
                rows = pl.ds(pl.multiple_of(base + r * ROWS, ROWS), ROWS)
                total = self.part[rows, owner].astype(F32) + self.came[2, rows].astype(F32)
                self.part[rows, owner] = total.astype(BF16)

            loop(CHUNK // 2 // ROWS, add)
            self.copy(*second[half]).start()

    def arrive(self, c):
        places = self.first(c)
        if self.n == 4:
            places = places[2:] + self.second(c)
        for place in places:
            self.copy(*place).wait_recv()

    def finish(self, c):
        for place in self.first(c) + self.second(c):
            self.copy(*place).wait_send()

    def total(self, rows):
        total = self.part[rows, columns(self.me, self.width)].astype(F32)
        for k in range(2 if self.n == 4 else self.n - 1):
            total += self.came[k, rows].astype(F32)
        return total


class Stats:
    def __init__(self, n, mine, came, send_sem, recv_sem):
        self.n, self.mine, self.came = n, mine, came
        self.me, self.to, self.source = partners(n)
        self.send_sem, self.recv_sem = send_sem, recv_sem

    def copy(self, c, k):
        return remote(
            self.mine.at[c], self.came.at[k, c], self.send_sem.at[k, c], self.recv_sem.at[k, c], self.to[k]
        )

    def start(self, c):
        for k in range(self.n - 1):
            self.copy(c, k).start()

    def arrive(self, c):
        for k in range(self.n - 1):
            self.copy(c, k).wait_recv()

    def finish(self, c):
        for k in range(self.n - 1):
            self.copy(c, k).wait_send()

    def put(self, c, first, second):
        ones = jnp.ones((8, 128), F32)
        for place, field in ((0, first), (8, second)):
            self.mine[c, place : place + 8] = lax.dot_general(
                ones, field, (((1,), (1,)), ((), ())), precision=PRECISE, preferred_element_type=F32
            )

    def moments(self, c, width):
        pieces = [self.mine[c]] + [self.came[k, c] for k in range(self.n - 1)]
        count = float(self.n * width)
        mean = sum(piece[0:8] for piece in pieces) * (1.0 / count)
        squares = sum(
            piece[8:16] + width * (piece[0:8] * (1.0 / width) - mean) ** 2 for piece in pieces
        )
        share = jnp.full((8, 128), 0.125, F32)
        return tuple(
            lax.dot_general(
                row, share, (((0,), (0,)), ((), ())), precision=PRECISE, preferred_element_type=F32
            )
            for row in (mean, lax.rsqrt(squares * (1.0 / count) + EPS))
        )

    def means(self, c, features):
        total = self.mine[c]
        for k in range(self.n - 1):
            total += self.came[k, c]
        share = jnp.full((8, 128), 1.0 / (8 * features), F32)
        return tuple(
            lax.dot_general(
                total[place : place + 8],
                share,
                (((0,), (0,)), ((), ())),
                precision=PRECISE,
                preferred_element_type=F32,
            )
            for place in (0, 8)
        )


def loop(count, body):
    def step(i, carry):
        body(i)
        return carry

    lax.fori_loop(0, count, step, 0)


def sub_rows(c, r):
    return pl.ds(pl.multiple_of(c * CHUNK + r * ROWS, ROWS), ROWS)


def repeat_lanes(field, width):
    return jnp.concatenate([field] * (width // 128), axis=1)


def fold_lanes(field):
    total = field[:, 0:128]
    for j in range(1, field.shape[1] // 128):
        total += field[:, 128 * j : 128 * (j + 1)]
    return total


def local_rows(r):
    return pl.ds(pl.multiple_of(r * ROWS, ROWS), ROWS)


def fold_entry(entry, first, second, rows):
    first[rows, :] = fold_lanes(entry)
    centered = entry - jnp.sum(entry, axis=1, keepdims=True) * (1.0 / entry.shape[1])
    second[rows, :] = fold_lanes(centered * centered)


def standardize(c, stats, gather, first, second, stand_ref, scale_ref):
    width = stand_ref.shape[1]
    stats.arrive(c)
    first[...], second[...] = stats.moments(c, width)

    def piece(r):
        rows, local = sub_rows(c, r), local_rows(r)
        scaling = second[local, :]
        stand = (stand_ref[rows, :] - repeat_lanes(first[local, :], width)) * repeat_lanes(
            scaling, width
        )
        stand_ref[rows, :] = stand
        scale_ref[rows, :] = scaling
        gather.buf[rows, gather.own()] = stand.astype(BF16)

    loop(CHUNK // ROWS, piece)
    gather.start(c)


def rotate(field, cos_rows, sin_rows, sign):
    turned = pltpu.roll(field, HEAD // 2, 1)
    return field * cos_rows + (sign * turned) * sin_rows


def spread(row):
    share = jnp.full((8, 128), 0.125, F32)
    return lax.dot_general(
        jnp.broadcast_to(row, (8, 128)),
        share,
        (((0,), (0,)), ((), ())),
        precision=PRECISE,
        preferred_element_type=F32,
    )


def project_kernel(
    n, in1, out2, positions_ref, segments_ref, s_hbm, c_hbm, wq_hbm, wk_hbm, wv_hbm,
    normed_hbm, q_ref, k_ref, v_ref, stand_ref, scale_ref, gb2_hbm, cot_hbm,
    cos_ref, sin_ref, segc_ref, segr_ref,
    s_buf, c_buf, cot_planes, w_buf, all1, all2, first, second, mine, others,
    in_sem, w_sem, out_sem, send1, recv1, send2, recv2, send3, recv3,
):
    streams, tokens, width = s_buf.shape
    count = tokens // CHUNK
    heads = width // HEAD
    weights = (wq_hbm, wk_hbm, wv_hbm)

    def s_in(c):
        return pltpu.make_async_copy(
            s_hbm.at[:, chunk_rows(c)], s_buf.at[:, chunk_rows(c)], in_sem.at[0, c]
        )

    def c_in(c):
        return pltpu.make_async_copy(
            c_hbm.at[chunk_rows(c)], c_buf.at[chunk_rows(c)], in_sem.at[1, c]
        )

    def w_in(j):
        return pltpu.make_async_copy(weights[j], w_buf.at[j], w_sem.at[j])

    def out(c, i):
        rows = chunk_rows(c)
        source, target = (
            (all1.at[rows], normed_hbm.at[rows]),
            (all2.at[rows], gb2_hbm.at[rows]),
            (cot_planes.at[:, rows], cot_hbm.at[:, rows]),
        )[i]
        return pltpu.make_async_copy(source, target, out_sem.at[i, c])

    loop(count, lambda c: s_in(c).start())
    loop(count, lambda c: c_in(c).start())
    for j in range(3):
        w_in(j).start()
    gather = Gather(n, all1, width, send1, recv1)
    incoming = Gather(n, all2, width, send2, recv2)
    stats = Stats(n, mine, others, send3, recv3)
    enter(n, gather.to)

    def entry(c):
        s_in(c).wait()

        def piece(r):
            rows = sub_rows(c, r)
            field = in1[0] * s_buf[0, rows].astype(F32)
            for i in range(1, streams):
                field += in1[i] * s_buf[i, rows].astype(F32)
            stand_ref[sub_rows(c, r), :] = field
            fold_entry(field, first, second, local_rows(r))

        loop(CHUNK // ROWS, piece)
        stats.put(c, first[...], second[...])
        stats.start(c)

    def send(c):
        standardize(c, stats, gather, first, second, stand_ref, scale_ref)

    def grad(c):
        c_in(c).wait()

        def piece(r):
            rows = sub_rows(c, r)
            block = c_buf[rows].astype(F32)
            total = None
            for i in range(streams):
                field = block[:, i, :]
                cot_planes[i, rows] = field.astype(BF16)
                total = out2[i] * field if total is None else total + out2[i] * field
            all2[rows, incoming.own()] = total.astype(BF16)

        loop(CHUNK // ROWS, piece)
        incoming.start(c)
        out(c, 2).start()

    entry(0)

    def ahead(c):
        entry(c + 1)
        send(c)

    loop(count - 1, ahead)
    send(count - 1)
    grad(0)
    gather.relay(0)
    grad(1)
    gather.relay(1)
    incoming.relay(0)

    segr_ref[...] = jnp.concatenate(
        [
            jnp.broadcast_to(segments_ref[a : a + 1, :].astype(F32), (8, 128))
            for a in range(tokens // 128)
        ],
        axis=1,
    )
    lane = lax.broadcasted_iota(jnp.int32, (128, 128), 1)
    exponent = lax.rem(lane, HEAD // 2).astype(F32) * (-2.0 / HEAD * math.log(10000.0))
    inverse = jnp.exp(exponent)
    for a in range(tokens // 128):
        rows = slice(128 * a, 128 * (a + 1))
        segc_ref[rows, :] = spread(segments_ref[a : a + 1, :].astype(F32))
        angles = spread(positions_ref[a : a + 1, :].astype(F32)) * inverse
        cos_ref[rows, :] = jnp.cos(angles)
        sine = jnp.sin(angles)
        sin_ref[rows, :] = jnp.where(lane < HEAD // 2, -sine, sine)
    grad(2)
    gather.relay(2)
    grad(3)
    gather.relay(3)
    incoming.relay(1)
    for j in range(3):
        w_in(j).wait()

    def work(c):
        gather.arrive(c)
        out(c, 0).start()
        rows = chunk_rows(c)
        block = all1[rows, :]
        cos_rows, sin_rows = cos_ref[rows, :], sin_ref[rows, :]
        for j, target in ((0, q_ref), (1, k_ref)):
            lin = dot_nn(block, w_buf[j])
            for h in range(heads):
                place = slice(HEAD * h, HEAD * (h + 1))
                target[rows, place] = rotate(lin[:, place], cos_rows, sin_rows, 1.0).astype(BF16)
        v_ref[rows, :] = dot_nn(block, w_buf[2]).astype(BF16)

        @pl.when(c + 2 < count)
        def _():
            incoming.relay(c + 2)

    loop(count, work)

    def end(c):
        incoming.arrive(c)
        out(c, 1).start()

    loop(count, end)

    def drain(c):
        for i in range(3):
            out(c, i).wait()
        stats.finish(c)
        gather.finish(c)
        incoming.finish(c)

    loop(count, drain)


def window_bias(c, start, extent, segc_ref, segr_ref, bias):
    def part(r):
        rows = pl.ds(pl.multiple_of(r * ROWS, ROWS), ROWS)
        row = c * CHUNK + r * ROWS + lax.broadcasted_iota(jnp.int32, (ROWS, extent), 0)
        column = start + lax.broadcasted_iota(jnp.int32, (ROWS, extent), 1)
        same = segc_ref[sub_rows(c, r), 0:1] == segr_ref[0:1, pl.ds(start, extent)]
        bias[rows, :] = jnp.where((row >= column) & same, 0.0, MASKED)

    loop(CHUNK // ROWS, part)


def window(c, tokens):
    extent = min(tokens, CHUNK * (-(-(LONGEST - 1) // CHUNK) + 1))
    back = extent // CHUNK - 1
    return pl.multiple_of(jnp.maximum(c - back, 0) * CHUNK, CHUNK), extent


def attend_kernel(
    n, in1, out1, in2, out2, res1, res2, q_ref, k_ref, v_ref, segc_ref, segr_ref, wo_ref,
    s_hbm, gb2_hbm, wg_hbm, wu_hbm, wd_hbm,
    attended_ref, branch_ref, normed_hbm, stand_ref, scale_ref, hidden_hbm, acts_hbm, grads_hbm,
    s_buf, gb2_buf, wg_buf, wu_buf, wd_buf, hidden_buf, gate_buf, up_buf,
    part, came, all2, first, second, mine, others, bias,
    s_sem, gb2_sem, grad_sem, w_sem, normed_sem, out_sem, send1, recv1, send2, recv2, send3, recv3,
):
    tokens, width = q_ref.shape
    units = wg_buf.shape[1]
    count = tokens // CHUNK
    heads = width // HEAD
    block = min(units, 512)
    mixing = Mixing((in1, out1, in2, out2, res1, res2))

    def s_in(c):
        slot = lax.rem(c, 2)
        return pltpu.make_async_copy(s_hbm.at[:, chunk_rows(c)], s_buf.at[slot], s_sem.at[slot])

    def gb2_in(c):
        slot = lax.rem(c, 2)
        return pltpu.make_async_copy(gb2_hbm.at[chunk_rows(c)], gb2_buf.at[slot], gb2_sem.at[slot])

    def grads_out(c):
        slot = lax.rem(c, 2)
        return pltpu.make_async_copy(
            gate_buf.at[slot], grads_hbm.at[chunk_rows(c)], grad_sem.at[0, slot]
        )

    def grads_in(c):
        slot = lax.rem(c, 2)
        return pltpu.make_async_copy(
            grads_hbm.at[chunk_rows(c)], gb2_buf.at[slot, :, 0:units], grad_sem.at[1, slot]
        )

    def normed_out(c):
        return pltpu.make_async_copy(
            all2.at[chunk_rows(c)], normed_hbm.at[chunk_rows(c)], normed_sem.at[c]
        )

    def outs(c):
        slot, rows = lax.rem(c, 2), chunk_rows(c)
        return tuple(
            pltpu.make_async_copy(buf.at[slot], target, out_sem.at[i, slot])
            for i, (buf, target) in enumerate(
                (
                    (hidden_buf, hidden_hbm.at[rows]),
                    (gate_buf, acts_hbm.at[rows, 0:units]),
                    (up_buf, acts_hbm.at[rows, units : 2 * units]),
                )
            )
        )

    weights = tuple(
        pltpu.make_async_copy(source, target, w_sem.at[i])
        for i, (source, target) in enumerate(
            ((wd_hbm, wd_buf), (wg_hbm, wg_buf), (wu_hbm, wu_buf))
        )
    )
    s_in(0).start()
    gb2_in(0).start()
    gb2_in(1).start()
    for copy in weights:
        copy.start()
    scatter = Scatter(n, part, came, width, send1, recv1)
    gather = Gather(n, all2, width, send2, recv2)
    stats = Stats(n, mine, others, send3, recv3)
    enter(n, gather.to)

    def attend(c):
        rows = chunk_rows(c)
        start, extent = window(c, tokens)
        window_bias(c, start, extent, segc_ref, segr_ref, bias)
        for h in range(heads):
            place = slice(HEAD * h, HEAD * (h + 1))
            scores = dot_nt(q_ref[rows, place], k_ref[pl.ds(start, extent), place])
            scores = scores * HEAD ** (-0.5) + bias[...]
            raised = jnp.exp(scores - jnp.max(scores, axis=1, keepdims=True))
            inverse = 1.0 / jnp.sum(raised, axis=1, keepdims=True)
            probs = (raised * inverse).astype(BF16)
            attended_ref[rows, place] = dot_nn(probs, v_ref[pl.ds(start, extent), place]).astype(BF16)
        part[rows, :] = dot_nn(attended_ref[rows, :], wo_ref[...]).astype(BF16)

    def middle(c):
        @pl.when(c + 1 < count)
        def _():
            s_in(c + 1).start()

        s_in(c).wait()
        slot = lax.rem(c, 2)
        scatter.arrive(c)

        def piece(r):
            rows = sub_rows(c, r)
            branch = scatter.total(rows)
            branch_ref[rows, :] = branch
            entry = mixing.across * branch
            for i in range(s_buf.shape[1]):
                entry += mixing.entry[i] * s_buf[slot, i, local_rows(r)].astype(F32)
            stand_ref[rows, :] = entry
            fold_entry(entry, first, second, local_rows(r))

        loop(CHUNK // ROWS, piece)
        stats.put(c, first[...], second[...])
        stats.start(c)

    def send(c):
        standardize(c, stats, gather, first, second, stand_ref, scale_ref)

    def work(c):
        gather.arrive(c)
        normed_out(c).start()
        slot = lax.rem(c, 2)

        @pl.when(c >= 2)
        def _():
            for copy in outs(c - 2):
                copy.wait()

        grads_in(c).wait()

        def piece(f):
            place = columns(f, block)
            gate = dot_nn(all2[chunk_rows(c), :], wg_buf[:, place])
            up = dot_nn(all2[chunk_rows(c), :], wu_buf[:, place])
            grad = gb2_buf[slot, :, place].astype(F32)
            sig = jax.nn.sigmoid(gate)
            act = gate * sig
            hidden_buf[slot, :, place] = (act * up).astype(BF16)
            gate_buf[slot, :, place] = (grad * up * sig * (1.0 + gate * (1.0 - sig))).astype(BF16)
            up_buf[slot, :, place] = (grad * act).astype(BF16)

        loop(units // block, piece)
        for copy in outs(c):
            copy.start()

        @pl.when(c + 2 < count)
        def _():
            grads_in(c + 2).start()
            gather.relay(c + 2)

    def grads(c):
        slot = lax.rem(c, 2)
        if c >= 2:
            grads_out(c - 2).wait()
        gb2_in(c).wait()

        def piece(f):
            place = columns(f, block)
            gate_buf[slot, :, place] = dot_nt(gb2_buf[slot], wd_buf[place, :]).astype(BF16)

        loop(units // block, piece)
        grads_out(c).start()
        if c + 2 < count:
            gb2_in(c + 2).start()

    def attend_send(c):
        attend(c)
        scatter.start(c)

        @pl.when(c >= 1)
        def _():
            scatter.relay(c - 1)

    loop(count, attend_send)
    middle(0)
    weights[0].wait()
    grads(0)
    scatter.relay(3)
    middle(1)
    send(0)
    grads(1)
    middle(2)
    send(1)
    grads(2)
    middle(3)
    grads(3)
    gather.relay(0)
    send(2)
    gather.relay(1)
    send(3)
    grads_out(2).wait()
    grads_out(3).wait()
    grads_in(0).start()
    grads_in(1).start()
    weights[1].wait()
    weights[2].wait()
    loop(count, work)
    for c in range(max(count - 2, 0), count):
        for copy in outs(c):
            copy.wait()

    def drain(c):
        normed_out(c).wait()
        scatter.finish(c)
        stats.finish(c)
        gather.finish(c)

    loop(count, drain)


def stats_part(part32, normed, normed_rows, part, c, first, second):
    def piece(r):
        rows = pl.ds(pl.multiple_of(r * ROWS, ROWS), ROWS)
        field = part32[rows, :]
        first[rows, :] = fold_lanes(field)
        second[rows, :] = fold_lanes(field * normed[normed_rows(r), :].astype(F32))
        part[sub_rows(c, r), :] = field.astype(BF16)

    loop(CHUNK // ROWS, piece)


def units_back_kernel(
    n, in1, out1, in2, out2, res1, res2, acts_ref, wg_ref, wu_ref, normed_ref, stand_ref, scale_ref, c_hbm, _down, _gate_up,
    entry_ref, gb1_hbm,
    c_buf, part32, first, second, part, came, mine, others, all1, in_sem, out_sem,
    send1, recv1, send2, recv2, send3, recv3,
):
    tokens, features = normed_ref.shape
    width = entry_ref.shape[1]
    count = tokens // CHUNK
    mixing = Mixing((in1, out1, in2, out2, res1, res2))
    c_in = pltpu.make_async_copy(c_hbm, c_buf, in_sem)
    c_in.start()
    scatter = Scatter(n, part, came, width, send1, recv1)
    stats = Stats(n, mine, others, send2, recv2)
    gather = Gather(n, all1, width, send3, recv3)
    enter(n, gather.to)

    def work(c):
        rows = chunk_rows(c)
        units = wg_ref.shape[1]
        part32[...] = dot_nt(acts_ref[rows, 0:units], wg_ref[...])
        part32[...] += dot_nt(acts_ref[rows, units : 2 * units], wu_ref[...])
        stats_part(part32, normed_ref, lambda r: sub_rows(c, r), part, c, first, second)
        stats.put(c, first[...], second[...])
        stats.start(c)
        scatter.start(c)

        @pl.when(c >= 1)
        def _():
            scatter.relay(c - 1)

    def middle(c):
        scatter.arrive(c)
        stats.arrive(c)
        first[...], second[...] = stats.means(c, features)

        def piece(r):
            rows = sub_rows(c, r)
            local = pl.ds(pl.multiple_of(r * ROWS, ROWS), ROWS)
            standard = stand_ref[rows, :]
            entry = repeat_lanes(scale_ref[rows, :], width) * (
                scatter.total(rows)
                - repeat_lanes(first[local, :], width)
                - standard * repeat_lanes(second[local, :], width)
            )
            entry_ref[rows, :] = entry
            grad = mixing.across * entry
            for i in range(c_buf.shape[0]):
                grad += mixing.branch[i] * c_buf[i, rows].astype(F32)
            all1[rows, gather.own()] = grad.astype(BF16)

        loop(CHUNK // ROWS, piece)
        gather.start(c)

    c_in.wait()

    def ahead(c):
        work(c)

        @pl.when(c >= 2)
        def _():
            middle(c - 2)

    loop(count, ahead)
    scatter.relay(count - 1)
    middle(count - 2)
    gather.relay(0)
    middle(count - 1)
    for c in range(1, count):
        gather.relay(c)

    def gb1_out(c):
        return pltpu.make_async_copy(
            all1.at[chunk_rows(c)], gb1_hbm.at[chunk_rows(c)], out_sem.at[c]
        )

    def last(c):
        gather.arrive(c)
        gb1_out(c).start()

    loop(count, last)

    def drain(c):
        gb1_out(c).wait()
        scatter.finish(c)
        stats.finish(c)
        gather.finish(c)

    loop(count, drain)


def attend_back_kernel(
    n, q_ref, k_ref, v_ref, segc_ref, segr_ref, cos_ref, sin_ref, wo_ref, wq_ref, wk_ref, wv_ref,
    wd_ref, stand_ref, scale_ref, gb1_hbm, hidden_hbm, normed_hbm, _output, _down,
    lin_ref, branch_ref, entry_ref,
    gb1_buf, hidden_buf, normed_buf, bias, dk_t, dv_t, part32, first, second,
    part1, came1, part2, came2, mine, others, in_sem,
    send1, recv1, send2, recv2, send3, recv3,
):
    tokens, width = q_ref.shape
    features = part1.shape[1]
    count = tokens // CHUNK
    heads = width // HEAD
    factor = HEAD ** (-0.5)
    down = Scatter(n, part2, came2, width, send1, recv1)
    scatter = Scatter(n, part1, came1, width, send2, recv2)
    stats = Stats(n, mine, others, send3, recv3)

    def inputs(c, slot):
        return tuple(
            pltpu.make_async_copy(source.at[chunk_rows(c)], target.at[slot], in_sem.at[i, slot])
            for i, (source, target) in enumerate(
                ((gb1_hbm, gb1_buf), (hidden_hbm, hidden_buf), (normed_hbm, normed_buf))
            )
        )

    for copy in inputs(count - 1, 0):
        copy.start()
    dk_t[...] = jnp.zeros_like(dk_t)
    dv_t[...] = jnp.zeros_like(dv_t)
    enter(n, scatter.to)

    def work(i):
        c = count - 1 - i
        slot = lax.rem(i, 2)

        @pl.when(i < count - 1)
        def _():
            for copy in inputs(c - 1, 1 - slot):
                copy.start()

        for copy in inputs(c, slot):
            copy.wait()
        rows = chunk_rows(c)
        part2[rows, :] = dot_nn(hidden_buf[slot], wd_ref[...]).astype(BF16)
        down.start(c)
        grad = dot_nt(gb1_buf[slot], wo_ref[...]).astype(BF16)
        start, extent = window(c, tokens)
        keys = pl.ds(start, extent)
        window_bias(c, start, extent, segc_ref, segr_ref, bias)
        cos_rows, sin_rows = cos_ref[rows, :], sin_ref[rows, :]
        for h in range(heads):
            place = slice(HEAD * h, HEAD * (h + 1))
            query, grad_h = q_ref[rows, place], grad[:, place]
            scores = dot_nt(query, k_ref[keys, place]) * factor + bias[...]
            raised = jnp.exp(scores - jnp.max(scores, axis=1, keepdims=True))
            inverse = 1.0 / jnp.sum(raised, axis=1, keepdims=True)
            probs = raised * inverse
            grad_probs = dot_nt(grad_h, v_ref[keys, place])
            centre = jnp.sum(probs * grad_probs, axis=1, keepdims=True)
            grad_scores = (probs * (grad_probs - centre)).astype(BF16)
            dv_t[place, keys] += dot_nn(jnp.transpose(grad_h), probs.astype(BF16))
            dk_t[place, keys] += dot_nn(jnp.transpose(query), grad_scores)
            dq = dot_nn(grad_scores, k_ref[keys, place]) * factor
            lin_ref[rows, place] = rotate(dq, cos_rows, sin_rows, -1.0).astype(BF16)
            dk = jnp.transpose(dk_t[place, rows]) * factor
            lin_ref[rows, slice(width + HEAD * h, width + HEAD * (h + 1))] = rotate(dk, cos_rows, sin_rows, -1.0).astype(BF16)
            lin_ref[rows, slice(2 * width + HEAD * h, 2 * width + HEAD * (h + 1))] = jnp.transpose(dv_t[place, rows]).astype(BF16)
        part32[...] = dot_nt(lin_ref[rows, 0:width], wq_ref[...])
        part32[...] += dot_nt(lin_ref[rows, width : 2 * width], wk_ref[...])
        part32[...] += dot_nt(lin_ref[rows, 2 * width : 3 * width], wv_ref[...])
        stats_part(
            part32,
            normed_buf.at[slot],
            lambda r: pl.ds(pl.multiple_of(r * ROWS, ROWS), ROWS),
            part1,
            c,
            first,
            second,
        )
        stats.put(c, first[...], second[...])
        stats.start(c)
        scatter.start(c)
        down.relay(c)

        @pl.when(i >= 1)
        def _():
            scatter.relay(c + 1)

    loop(count, work)
    scatter.relay(0)

    def last(i):
        c = count - 1 - i
        down.arrive(c)

        def sums(r):
            branch_ref[sub_rows(c, r), :] = down.total(sub_rows(c, r))

        loop(CHUNK // ROWS, sums)
        scatter.arrive(c)
        stats.arrive(c)
        first[...], second[...] = stats.means(c, features)

        def piece(r):
            rows = sub_rows(c, r)
            local = pl.ds(pl.multiple_of(r * ROWS, ROWS), ROWS)
            entry_ref[rows, :] = repeat_lanes(scale_ref[rows, :], width) * (
                scatter.total(rows)
                - repeat_lanes(first[local, :], width)
                - stand_ref[rows, :] * repeat_lanes(second[local, :], width)
            )

        loop(CHUNK // ROWS, piece)

    loop(count, last)

    def drain(c):
        down.finish(c)
        scatter.finish(c)
        stats.finish(c)

    loop(count, drain)


def turn_kernel(source_ref, target_ref):
    target_ref[...] = jnp.transpose(source_ref[...].astype(F32))


def streams_kernel(
    in1, out1, in2, out2, res1, res2, s_ref, c_ref, b1_ref, b2_ref, e1_ref, e2_ref,
    new_ref, grad_ref, mix_ref, sums_ref,
):
    @pl.when(pl.program_id(0) == 0)
    def _():
        sums_ref[...] = jnp.zeros_like(sums_ref)

    count = s_ref.shape[0]
    mixing = Mixing((in1, out1, in2, out2, res1, res2))
    mixed = [[mixing.mixed(k, j) for j in range(count)] for k in range(count)]

    def fold(field):
        field = fold_lanes(field)
        total = field[0:8]
        for j in range(1, field.shape[0] // 8):
            total += field[8 * j : 8 * (j + 1)]
        return total

    def piece(r):
        rows = pl.ds(pl.multiple_of(r * 16, 16), 16)
        s = [s_ref[i, rows].astype(F32) for i in range(count)]
        c = [c_ref[i, rows].astype(F32) for i in range(count)]
        b1, b2, e1, e2 = b1_ref[rows, :], b2_ref[rows, :], e1_ref[rows, :], e2_ref[rows, :]
        for j in range(count):
            new = mixing.branch[j] * b1 + mixing.out2[j] * b2
            grad = mixing.entry[j] * e2 + mixing.in1[j] * e1
            for k in range(count):
                new += mixed[k][j] * s[k]
                grad += mixed[j][k] * c[k]
            new_ref[rows, j, :] = new.astype(BF16)
            grad_ref[rows, j, :] = grad
        pairs = [(s[i], c[j]) for i in range(count) for j in range(count)]
        pairs += [(s[i], e1) for i in range(count)] + [(s[i], e2) for i in range(count)]
        pairs += [(c[i], b1) for i in range(count)] + [(c[i], b2) for i in range(count)]
        pairs += [(b1, e2)]
        for place, (left, right) in enumerate(pairs):
            sums_ref[place] += fold(left * right)

    loop(s_ref.shape[1] // 16, piece)

    @pl.when(pl.program_id(0) == pl.num_programs(0) - 1)
    def _():
        sums = [sums_ref[place] for place in range(PRODUCTS)]
        s_c = [sums[count * i : count * (i + 1)] for i in range(count)]
        s_e1, s_e2, c_b1, c_b2 = (sums[16 + 4 * k : 20 + 4 * k] for k in range(4))
        b_e = sums[32]
        every = range(count)
        row1, row2 = mixing.res1, mixing.res2
        grads = [s_e1[i] for i in every]
        grads += [inner(row2[j], s_c[i]) + mixing.in2[j] * s_e2[i] for i in every for j in every]
        grads += [inner(row2[j], c_b1) + mixing.in2[j] * b_e for j in every]
        turned1 = [[row1[k][i] for k in every] for i in every]
        grads += [inner(turned1[i], s_e2) + mixing.out1[i] * b_e for i in every]
        grads += [
            inner(turned1[i], [s_c[k][j] for k in every]) + mixing.out1[i] * c_b1[j]
            for i in every
            for j in every
        ]
        grads += [c_b2[j] for j in every]
        for place, field in enumerate(grads):
            mix_ref[place] = field


PLANES = 4
CORES = 2
PRODUCTS = 33
SUMS = 48


def pair_kernel(
    left_hbm, right_hbm, out_hbm, left, right, turned, sent, came, mine_buf,
    left_sem, right_sem, out_sem, send_sem, recv_sem,
):
    steps, height, width = came.shape
    block = height // 2
    piece = right_sem.shape[0]
    across = width // piece
    me = lax.axis_index("dp")
    mine = lax.rem(me, CORES)
    partner = me + 1 - 2 * mine

    def left_in(step, half, part):
        index = (2 * step + part) * CORES + half
        return pltpu.make_async_copy(
            left_hbm.at[:, columns(index, block)],
            left.at[2 * step + part, half],
            left_sem.at[2 * step + part, half],
        )

    def right_in(f):
        return pltpu.make_async_copy(
            right_hbm.at[:, columns(f, across)], right.at[:, columns(f, across)], right_sem.at[f]
        )

    def swap(step):
        return pltpu.make_async_remote_copy(
            src_ref=sent.at[step],
            dst_ref=came.at[step],
            send_sem=send_sem.at[step],
            recv_sem=recv_sem.at[step],
            device_id={"dp": partner},
            device_id_type=MESH,
        )

    def out(step):
        rows = pl.ds(pl.multiple_of(step * height, height), height)
        return pltpu.make_async_copy(mine_buf.at[step], out_hbm.at[rows], out_sem.at[step])

    for part in range(2):
        left_in(0, 1 - mine, part).start()
    for f in range(piece):
        right_in(f).start()
    for half in (1 - mine, mine):
        for step in range(steps):
            for part in range(2):
                if half is mine or step > 0:
                    left_in(step, half, part).start()
    barrier = pltpu.get_barrier_semaphore()
    pl.semaphore_signal(barrier, inc=1, device_id={"dp": partner}, device_id_type=MESH)
    pl.semaphore_wait(barrier, 1)

    def turn(step, half):
        for part in range(2):
            left_in(step, half, part).wait()
            turned[part * block : (part + 1) * block, :] = jnp.transpose(left[2 * step + part, half])

    def other(step):
        turn(step, 1 - mine)

        def part(f):
            @pl.when(step == 0)
            def _():
                right_in(f).wait()

            place = columns(f, across)
            sent[step, :, place] = dot_nn(turned[...], right[:, place]).astype(BF16)

        loop(piece, part)
        swap(step).start()

    loop(steps, other)

    def own(step):
        turn(step, mine)
        swap(step).wait_recv()

        def part(f):
            place = columns(f, across)
            total = dot_nn(turned[...], right[:, place]) + came[step, :, place].astype(F32)
            mine_buf[step, :, place] = total.astype(BF16)

        loop(piece, part)
        out(step).start()

    loop(steps, own)

    def drain(step):
        swap(step).wait_send()
        out(step).wait()

    loop(steps, drain)


def finish_kernel(
    n, first_hbm, last_hbm, sums_ref,
    q_out, k_out, v_out, o_out, sums_out,
    own, core, right, left, by_core, by_plane, by_tensor,
    own_sem, core_send, core_recv, right_send, right_recv, left_send, left_recv, sum_send, sum_recv,
):
    _, pieces, height, width = own.shape
    me = lax.axis_index("dp")
    plane, mine = lax.div(me, CORES), lax.rem(me, CORES)
    partner = me + 1 - 2 * mine
    here, peers, peer_source = partners(n)
    planes_to = [lax.rem(plane + k, PLANES) for k in range(1, PLANES)]
    planes_from = [lax.rem(plane + PLANES - k, PLANES) for k in range(1, PLANES)]

    def dp_at(position):
        return position * CORES + mine

    def rows_of(position, half):
        return pl.ds(pl.multiple_of((position * CORES + half) * height, height), height)

    def block(position, half, p):
        if p < pieces - 1:
            return first_hbm.at[rows_of(position, half), p * width : (p + 1) * width]
        return last_hbm.at[rows_of(position, half)]

    def over_dp(source, target, send_sem, recv_sem, device):
        return pltpu.make_async_remote_copy(
            src_ref=source, dst_ref=target, send_sem=send_sem, recv_sem=recv_sem,
            device_id={"dp": device}, device_id_type=MESH,
        )

    def own_in(position, p):
        return pltpu.make_async_copy(
            block(position, mine, p), own.at[position, p], own_sem.at[position, p]
        )

    def core_in(position, p):
        return over_dp(
            block(position, 1 - mine, p), core.at[position, p],
            core_send.at[position, p], core_recv.at[position, p], partner,
        )

    def rightward(step, p):
        return over_dp(
            own.at[lax.rem(plane + PLANES - step, PLANES), p], right.at[step - 1, p],
            right_send.at[step - 1, p], right_recv.at[step - 1, p], lax.rem(me + CORES, PLANES * CORES),
        )

    def leftward(step, p):
        return over_dp(
            own.at[lax.rem(plane + step, PLANES), p], left.at[step - 1, p],
            left_send.at[step - 1, p], left_recv.at[step - 1, p],
            lax.rem(me + (PLANES - 1) * CORES, PLANES * CORES),
        )

    order = (3, 0, 2, 1)
    for position in order:
        for p in range(pieces):
            own_in(position, p).start()

    barrier = pltpu.get_barrier_semaphore()
    pl.semaphore_signal(barrier, inc=1, device_id={"dp": partner}, device_id_type=MESH)
    for k in range(PLANES - 1):
        pl.semaphore_signal(
            barrier, inc=1, device_id={"dp": dp_at(planes_to[k])}, device_id_type=MESH
        )
    for k in range(n - 1):
        pl.semaphore_signal(barrier, inc=1, device_id={"tensor": peers[k]}, device_id_type=MESH)
    pl.semaphore_wait(barrier, 1 + PLANES - 1 + n - 1)

    by_core[mine] = jnp.sum(sums_ref[...], axis=1)
    over_dp(
        by_core.at[mine], by_core.at[mine], sum_send.at[0], sum_recv.at[0], partner
    ).start()
    for position in order:
        for p in range(pieces):
            core_in(position, p).start()
    over_dp(
        by_core.at[1 - mine], by_core.at[1 - mine], sum_send.at[0], sum_recv.at[0], partner
    ).wait_recv()
    by_plane[plane] = by_core[0] + by_core[1]

    def plane_sums(k, at):
        return over_dp(
            by_plane.at[at], by_plane.at[at], sum_send.at[1 + k], sum_recv.at[1 + k],
            dp_at(planes_to[k]),
        )

    def tensor_sums(k, at):
        at = by_tensor.at[at]
        return remote(at, at, sum_send.at[PLANES + k], sum_recv.at[PLANES + k], peers[k])

    for k in range(PLANES - 1):
        plane_sums(k, plane).start()

    def gather_pair(position):
        def piece(p):
            pltpu.make_async_copy(
                own.at[position, p], own.at[position, p], own_sem.at[position, p]
            ).wait()
            over_dp(
                core.at[position, p], core.at[position, p],
                core_send.at[position, p], core_recv.at[position, p], partner,
            ).wait_recv()
            add(own.at[position, p], core.at[position, p])

        loop(pieces, piece)

    def add(target, source):
        def part(r):
            rows = local_rows(r)
            target[rows, :] = (target[rows, :].astype(F32) + source[rows, :].astype(F32)).astype(BF16)

        loop(height // ROWS, part)

    def send_step(step):
        def piece(p):
            @pl.when(plane <= step - 1)
            def _():
                if step >= 2:

                    @pl.when(plane >= 1)
                    def _():
                        rightward(step - 1, p).wait_recv()
                        add(own.at[lax.rem(plane + PLANES - step, PLANES), p], right.at[step - 2, p])

                rightward(step, p).start()

            @pl.when(plane >= PLANES - step)
            def _():
                if step >= 2:

                    @pl.when(plane <= PLANES - 2)
                    def _():
                        leftward(step - 1, p).wait_recv()
                        add(own.at[lax.rem(plane + step, PLANES), p], left.at[step - 2, p])

                leftward(step, p).start()

        loop(pieces, piece)

    gather_pair(3)
    gather_pair(0)
    send_step(1)
    gather_pair(2)
    gather_pair(1)
    for k in range(PLANES - 1):
        plane_sums(k, planes_from[k]).wait_recv()
    by_tensor[here] = sum((by_plane[i] for i in range(1, PLANES)), by_plane[0])
    for k in range(n - 1):
        tensor_sums(k, here).start()
    for step in range(2, PLANES):
        send_step(step)
    for k in range(n - 1):
        tensor_sums(k, peer_source[k]).wait_recv()
    sums_out[...] = sum((by_tensor[i] for i in range(1, n)), by_tensor[0])

    for p, target in enumerate((q_out, k_out, v_out, o_out)):
        steps = PLANES - 2

        @pl.when(plane >= 1)
        def _():
            rightward(PLANES - 1, p).wait_recv()

        @pl.when(plane <= PLANES - 2)
        def _():
            leftward(PLANES - 1, p).wait_recv()

        total = own[plane, p].astype(F32)
        total += jnp.where(plane >= 1, right[steps, p].astype(F32), 0.0)
        total += jnp.where(plane <= PLANES - 2, left[steps, p].astype(F32), 0.0)
        target[...] = total if p < pieces - 1 else jnp.transpose(total)

    over_dp(by_core.at[mine], by_core.at[mine], sum_send.at[0], sum_recv.at[0], partner).wait_send()
    for k in range(PLANES - 1):
        plane_sums(k, plane).wait_send()
    for k in range(n - 1):
        tensor_sums(k, here).wait_send()
    for p in range(pieces):
        for position in range(PLANES):
            core_in(position, p).wait_send()
        for step in range(1, PLANES):

            @pl.when(plane <= step - 1)
            def _():
                rightward(step, p).wait_send()

            @pl.when(plane >= PLANES - step)
            def _():
                leftward(step, p).wait_send()


def on_device(
    n,
    replicas,
    streams,
    segments,
    positions,
    mix_in1,
    mix_res1,
    mix_out1,
    mix_in2,
    mix_res2,
    mix_out2,
    w_query,
    w_key,
    w_value,
    w_output,
    w_gate,
    w_up,
    w_down,
    cotangent,
):
    tokens, stream_count, width = streams.shape
    features = w_query.shape[0]
    units = w_gate.shape[1]
    chunks = tokens // CHUNK
    assert tokens == LENGTH == 4 * CHUNK and stream_count == 4
    any_spec = pl.BlockSpec(memory_space=pl.ANY)
    vmem = pl.BlockSpec(memory_space=pltpu.VMEM)
    smem = pl.BlockSpec(memory_space=pltpu.SMEM)

    def array(shape, dtype):
        return jax.ShapeDtypeStruct(shape, dtype)

    def dma(*shape):
        return pltpu.SemaphoreType.DMA(shape)

    def pair(lanes):
        return [dma(lanes, chunks), dma(lanes, chunks)]

    gather_sems = pair(4 if n == 4 else n - 1)
    scatter_sems = pair(6 if n == 4 else n - 1)
    stats_sems = pair(n - 1)

    def lasts(micros):
        return pl.CostEstimate(
            flops=int(micros * 1.0e9), bytes_accessed=int(micros * 3.6e6), transcendentals=0
        )

    def params(identity, mib):
        return pltpu.CompilerParams(
            collective_id=identity, has_side_effects=True, vmem_limit_bytes=mib * MIB
        )

    planes = jnp.transpose(streams, (1, 0, 2))
    mixes = (mix_in1, mix_out1, mix_in2, mix_out2, mix_res1, mix_res2)

    def stats_scratch():
        return [
            pltpu.VMEM((CHUNK, 128), F32),
            pltpu.VMEM((CHUNK, 128), F32),
            pltpu.VMEM((chunks, 16, CHUNK), F32),
            pltpu.VMEM((n - 1, chunks, 16, CHUNK), F32),
        ]

    (
        normed1, queries, keys, values, stand1, scale1, grad_branch2, cot_planes,
        cos_table, sin_table, seg_column, seg_row,
    ) = pl.pallas_call(
        functools.partial(project_kernel, n),
        name="project",
        cost_estimate=lasts(100),
        out_shape=[
            array((tokens, features), BF16),
            array((tokens, width), BF16),
            array((tokens, width), BF16),
            array((tokens, width), BF16),
            array((tokens, width), F32),
            array((tokens, 128), F32),
            array((tokens, features), BF16),
            array((stream_count, tokens, width), BF16),
            array((tokens, HEAD), F32),
            array((tokens, HEAD), F32),
            array((tokens, 128), F32),
            array((8, tokens), F32),
        ],
        in_specs=[smem, smem, vmem, vmem] + [any_spec] * 5,
        out_specs=[any_spec] + [vmem] * 5 + [any_spec] * 2 + [vmem] * 4,
        scratch_shapes=[
            pltpu.VMEM((stream_count, tokens, width), BF16),
            pltpu.VMEM((tokens, stream_count, width), BF16),
            pltpu.VMEM((stream_count, tokens, width), BF16),
            pltpu.VMEM((3, features, width), BF16),
            pltpu.VMEM((tokens, features), BF16),
            pltpu.VMEM((tokens, features), BF16),
        ]
        + stats_scratch()
        + [dma(2, chunks), dma(3), dma(3, chunks)]
        + gather_sems
        + gather_sems
        + stats_sems,
        compiler_params=params(0, 56),
    )(
        mix_in1, mix_out2,
        positions.reshape(tokens // 128, 128), segments.reshape(tokens // 128, 128),
        planes, cotangent, w_query, w_key, w_value,
    )

    extent = window(0, tokens)[1]
    attended, branch1, normed2, stand2, scale2, hidden, grad_acts, _ = pl.pallas_call(
        functools.partial(attend_kernel, n),
        name="attend",
        cost_estimate=lasts(100),
        out_shape=[
            array((tokens, width), BF16),
            array((tokens, width), F32),
            array((tokens, features), BF16),
            array((tokens, width), F32),
            array((tokens, 128), F32),
            array((tokens, units), BF16),
            array((tokens, 2 * units), BF16),
            array((tokens, units), BF16),
        ],
        in_specs=[smem] * 6 + [vmem] * 6 + [any_spec] * 5,
        out_specs=[vmem, vmem, any_spec, vmem, vmem, any_spec, any_spec, any_spec],
        scratch_shapes=[
            pltpu.VMEM((2, stream_count, CHUNK, width), BF16),
            pltpu.VMEM((2, CHUNK, features), BF16),
            pltpu.VMEM((features, units), BF16),
            pltpu.VMEM((features, units), BF16),
            pltpu.VMEM((units, features), BF16),
            pltpu.VMEM((2, CHUNK, units), BF16),
            pltpu.VMEM((2, CHUNK, units), BF16),
            pltpu.VMEM((2, CHUNK, units), BF16),
            pltpu.VMEM((tokens, features), BF16),
            pltpu.VMEM((n - 1, tokens, width), BF16),
            pltpu.VMEM((tokens, features), BF16),
        ]
        + stats_scratch()
        + [pltpu.VMEM((CHUNK, extent), F32), dma(2), dma(2), dma(2, 2)]
        + [dma(3), dma(chunks), dma(3, 2)]
        + scatter_sems
        + gather_sems
        + stats_sems,
        compiler_params=params(1, 62),
    )(
        *mixes, queries, keys, values, seg_column, seg_row, w_output, planes,
        grad_branch2, w_gate, w_up, w_down,
    )

    def over_dp(partial, dimension):
        return lax.psum_scatter(partial, "dp", scatter_dimension=dimension, tiled=True)

    height = features // replicas
    paired = replicas == PLANES * CORES

    def weight_sum(identity, left, right):
        if not paired:
            partial = contract_rows(left, right).astype(BF16)
            return over_dp(partial, 0), partial
        steps, columns_in = PLANES // 2, right.shape[1]
        pieces = max(columns_in // 1024, 1)
        partial = pl.pallas_call(
            pair_kernel,
            name="pair",
            cost_estimate=lasts(20),
            out_shape=array((features // CORES, columns_in), BF16),
            in_specs=[any_spec, any_spec],
            out_specs=any_spec,
            scratch_shapes=[
                pltpu.VMEM((PLANES, CORES, tokens, height), BF16),
                pltpu.VMEM((tokens, columns_in), BF16),
                pltpu.VMEM((2 * height, tokens), BF16),
                pltpu.VMEM((steps, 2 * height, columns_in), BF16),
                pltpu.VMEM((steps, 2 * height, columns_in), BF16),
                pltpu.VMEM((steps, 2 * height, columns_in), BF16),
                dma(PLANES, CORES),
                dma(pieces),
                dma(steps),
                dma(steps),
                dma(steps),
            ],
            compiler_params=params(identity, 56),
        )(left, right)
        groups = [[CORES * plane + c for plane in range(PLANES)] for c in range(CORES)]
        total = lax.psum_scatter(
            partial, "dp", scatter_dimension=0, tiled=True, axis_index_groups=groups
        )
        return total, partial

    grad_down, part_down = weight_sum(5, grad_branch2, hidden)
    part_gate_up = contract_rows(normed2, grad_acts).astype(BF16)
    grad_gate_up = over_dp(part_gate_up, 0)
    grad_w_down = pl.pallas_call(
        turn_kernel,
        name="turn",
        cost_estimate=lasts(2),
        out_shape=array((units, height), F32),
        in_specs=[vmem],
        out_specs=vmem,
        compiler_params=pltpu.CompilerParams(vmem_limit_bytes=32 * MIB),
    )(grad_down)
    grad_w_gate = grad_gate_up[:, :units].astype(F32)
    grad_w_up = grad_gate_up[:, units:].astype(F32)

    grad_entry2, grad_branch1 = pl.pallas_call(
        functools.partial(units_back_kernel, n),
        name="units_back",
        cost_estimate=lasts(400),
        out_shape=[array((tokens, width), F32), array((tokens, features), BF16)],
        in_specs=[smem] * 6 + [vmem] * 6 + [any_spec] * 3,
        out_specs=[vmem, any_spec],
        scratch_shapes=[
            pltpu.VMEM((stream_count, tokens, width), BF16),
            pltpu.VMEM((CHUNK, features), F32),
            pltpu.VMEM((CHUNK, 128), F32),
            pltpu.VMEM((CHUNK, 128), F32),
            pltpu.VMEM((tokens, features), BF16),
            pltpu.VMEM((n - 1, tokens, width), BF16),
            pltpu.VMEM((chunks, 16, CHUNK), F32),
            pltpu.VMEM((n - 1, chunks, 16, CHUNK), F32),
            pltpu.VMEM((tokens, features), BF16),
            pltpu.SemaphoreType.DMA,
            dma(chunks),
        ]
        + scatter_sems
        + stats_sems
        + gather_sems,
        compiler_params=params(2, 60),
    )(
        *mixes, grad_acts, w_gate, w_up, normed2, stand2, scale2, cot_planes,
        part_down, part_gate_up,
    )

    part_output = contract_rows(grad_branch1, attended).astype(BF16)

    grad_lin, branch2, grad_entry1 = pl.pallas_call(
        functools.partial(attend_back_kernel, n),
        name="attend_back",
        cost_estimate=lasts(2),
        out_shape=[array((tokens, 3 * width), BF16)] + [array((tokens, width), F32)] * 2,
        in_specs=[vmem] * 14 + [any_spec] * 5,
        out_specs=[vmem] * 3,
        scratch_shapes=[
            pltpu.VMEM((2, CHUNK, features), BF16),
            pltpu.VMEM((2, CHUNK, units), BF16),
            pltpu.VMEM((2, CHUNK, features), BF16),
            pltpu.VMEM((CHUNK, extent), F32),
            pltpu.VMEM((width, tokens), F32),
            pltpu.VMEM((width, tokens), F32),
            pltpu.VMEM((CHUNK, features), F32),
            pltpu.VMEM((CHUNK, 128), F32),
            pltpu.VMEM((CHUNK, 128), F32),
            pltpu.VMEM((tokens, features), BF16),
            pltpu.VMEM((n - 1, tokens, width), BF16),
            pltpu.VMEM((tokens, features), BF16),
            pltpu.VMEM((n - 1, tokens, width), BF16),
            pltpu.VMEM((chunks, 16, CHUNK), F32),
            pltpu.VMEM((n - 1, chunks, 16, CHUNK), F32),
            dma(3, 2),
        ]
        + scatter_sems
        + scatter_sems
        + stats_sems,
        compiler_params=params(3, 60),
    )(
        queries, keys, values, seg_column, seg_row, cos_table, sin_table,
        w_output, w_query, w_key, w_value, w_down, stand1, scale1,
        grad_branch1, hidden, normed1, part_output, grad_w_down,
    )

    part_lin = contract_rows(normed1, grad_lin).astype(BF16)

    rows = 128
    plane_spec = pl.BlockSpec((stream_count, rows, width), lambda t: (0, t, 0))
    field_spec = pl.BlockSpec((rows, width), lambda t: (t, 0))
    stream_spec = pl.BlockSpec((rows, stream_count, width), lambda t: (t, 0, 0))
    new_streams, stream_grad, sums = pl.pallas_call(
        streams_kernel,
        name="streams",
        cost_estimate=lasts(2),
        grid=(tokens // rows,),
        out_shape=[
            array(streams.shape, BF16),
            array(streams.shape, F32),
            array((SUMS, 8, 128), F32),
        ],
        in_specs=[smem] * 6 + [plane_spec, plane_spec] + [field_spec] * 4,
        out_specs=[
            stream_spec,
            stream_spec,
            pl.BlockSpec((SUMS, 8, 128), lambda t: (0, 0, 0)),
        ],
        scratch_shapes=[pltpu.VMEM((PRODUCTS, 8, 128), F32)],
        compiler_params=pltpu.CompilerParams(vmem_limit_bytes=48 * MIB),
    )(*mixes, planes, cot_planes, branch1, branch2, grad_entry1, grad_entry2)
    if paired:
        steps = PLANES - 1
        grad_w_query, grad_w_key, grad_w_value, grad_w_output, sums = pl.pallas_call(
            functools.partial(finish_kernel, n),
            name="finish",
            cost_estimate=lasts(2),
            out_shape=[array((height, width), F32)] * 3
            + [array((width, height), F32), array((SUMS, 128), F32)],
            in_specs=[any_spec, any_spec, vmem],
            out_specs=[vmem] * 5,
            scratch_shapes=[
                pltpu.VMEM((PLANES, 4, height, width), BF16),
                pltpu.VMEM((PLANES, 4, height, width), BF16),
                pltpu.VMEM((steps, 4, height, width), BF16),
                pltpu.VMEM((steps, 4, height, width), BF16),
                pltpu.VMEM((CORES, SUMS, 128), F32),
                pltpu.VMEM((PLANES, SUMS, 128), F32),
                pltpu.VMEM((n, SUMS, 128), F32),
                dma(PLANES, 4),
                dma(PLANES, 4),
                dma(PLANES, 4),
                dma(steps, 4),
                dma(steps, 4),
                dma(steps, 4),
                dma(steps, 4),
                dma(PLANES + n - 1),
                dma(PLANES + n - 1),
            ],
            compiler_params=params(4, 48),
        )(part_lin, part_output, sums)
        sums = jnp.sum(sums, axis=1)
    else:
        grad_w_query, grad_w_key, grad_w_value = (
            over_dp(part_lin[:, width * j : width * (j + 1)], 0).astype(F32) for j in range(3)
        )
        grad_w_output = jnp.transpose(over_dp(part_output, 0)).astype(F32)
        sums = lax.psum(jnp.sum(sums, axis=(1, 2)), ("dp", "tensor"))
    grad_mix_in1, grad_mix_res1 = sums[0:4], sums[4:20].reshape(4, 4)
    grad_mix_out1, grad_mix_in2 = sums[20:24], sums[24:28]
    grad_mix_res2, grad_mix_out2 = sums[28:44].reshape(4, 4), sums[44:48]
    return (
        new_streams,
        stream_grad,
        grad_w_query,
        grad_w_key,
        grad_w_value,
        grad_w_output,
        grad_w_gate,
        grad_w_up,
        grad_w_down,
        grad_mix_in1,
        grad_mix_res1,
        grad_mix_out1,
        grad_mix_in2,
        grad_mix_res2,
        grad_mix_out2,
    )


def solution(mesh):
    return jax.shard_map(
        functools.partial(on_device, mesh.shape["tensor"], mesh.shape["dp"]),
        mesh=mesh,
        in_specs=(
            P("dp", None, "tensor"),
            P("dp"),
            P("dp"),
            P(),
            P(),
            P(),
            P(),
            P(),
            P(),
            P(None, "tensor"),
            P(None, "tensor"),
            P(None, "tensor"),
            P("tensor", None),
            P(None, "tensor"),
            P(None, "tensor"),
            P("tensor", None),
            P("dp", None, "tensor"),
        ),
        out_specs=(
            P("dp", None, "tensor"),
            P("dp", None, "tensor"),
            P("dp", "tensor"),
            P("dp", "tensor"),
            P("dp", "tensor"),
            P("tensor", "dp"),
            P("dp", "tensor"),
            P("dp", "tensor"),
            P("tensor", "dp"),
            P(),
            P(),
            P(),
            P(),
            P(),
            P(),
        ),
        check_vma=False,
    )
```

```python
import functools
import math

import jax
import jax.numpy as jnp
from jax import lax
from jax.experimental import pallas as pl
from jax.experimental.pallas import tpu as pltpu
from jax.sharding import PartitionSpec as P

HEAD = 128
LENGTH = 1024
LONGEST = 512
EPS = 1e-05
PRECISE = lax.Precision.HIGHEST
MASKED = -1e30
MESH = pl.DeviceIdType.MESH
BF16 = jnp.bfloat16
F32 = jnp.float32
CHUNK = 256
ROWS = 32
MIB = 1 << 20


def inner(left, right):
    total = left[0] * right[0]
    for a, b in zip(left[1:], right[1:]):
        total += a * b
    return total


class Mixing:
    def __init__(self, refs):
        vectors = [[ref[i] for i in range(4)] for ref in refs[:4]]
        self.in1, self.out1, self.in2, self.out2 = vectors
        self.res1, self.res2 = (
            [[ref[i, j] for j in range(4)] for i in range(4)] for ref in refs[4:]
        )
        self.entry = [inner(row, self.in2) for row in self.res1]
        self.branch = [inner(self.out1, column) for column in zip(*self.res2)]
        self.across = inner(self.out1, self.in2)

    def mixed(self, k, j):
        return inner(self.res1[k], [row[j] for row in self.res2])


def contract_rows(left, right):
    return lax.dot_general(
        left, right, (((0,), (0,)), ((), ())), preferred_element_type=F32
    )


def dot_nn(left, right):
    return jnp.dot(left, right, preferred_element_type=F32)


def dot_nt(left, right):
    return lax.dot_general(
        left, right, (((1,), (1,)), ((), ())), preferred_element_type=F32
    )


def partners(n):
    me = lax.axis_index("tensor")
    if n == 4:
        both = (me + 1 - 2 * lax.rem(me, 2), lax.rem(me + 2, 4), 3 - me)
        return me, both, both
    to = tuple(lax.rem(me + k, n) for k in range(1, n))
    source = tuple(lax.rem(me + n - k, n) for k in range(1, n))
    return me, to, source


def enter(n, to):
    barrier = pltpu.get_barrier_semaphore()
    for target in to:
        pl.semaphore_signal(
            barrier, inc=1, device_id={"tensor": target}, device_id_type=MESH
        )
    pl.semaphore_wait(barrier, n - 1)


def remote(source, target, send_sem, recv_sem, device):
    return pltpu.make_async_remote_copy(
        src_ref=source,
        dst_ref=target,
        send_sem=send_sem,
        recv_sem=recv_sem,
        device_id={"tensor": device},
        device_id_type=MESH,
    )


def columns(index, width):
    return pl.ds(pl.multiple_of(index * width, 128), width)


def chunk_rows(c):
    return pl.ds(pl.multiple_of(c * CHUNK, CHUNK), CHUNK)


def half_rows(c, half):
    return pl.ds(pl.multiple_of(c * CHUNK + half * (CHUNK // 2), CHUNK // 2), CHUNK // 2)


class Gather:
    def __init__(self, n, buf, width, send_sem, recv_sem):
        self.n, self.buf, self.width = n, buf, width
        self.me, self.to, self.source = partners(n)
        self.send_sem, self.recv_sem = send_sem, recv_sem

    def own(self):
        return columns(self.me, self.width)

    def copy(self, rows, owner, k, c, target):
        view = self.buf.at[rows, columns(owner, self.width)]
        return remote(view, view, self.send_sem.at[k, c], self.recv_sem.at[k, c], target)

    def direct(self):
        return 2 if self.n == 4 else self.n - 1

    def handed(self, c):
        side, up, _ = self.to
        return (
            self.copy(half_rows(c, 0), side, 2, c, up),
            self.copy(half_rows(c, 1), up, 3, c, side),
        )

    def start(self, c):
        for k in range(self.direct()):
            self.copy(chunk_rows(c), self.me, k, c, self.to[k]).start()

    def relay(self, c):
        if self.n == 4:
            for k, copy in enumerate(self.handed(c)):
                self.copy(chunk_rows(c), self.source[k], k, c, self.to[k]).wait_recv()
                copy.start()

    def arrive(self, c):
        if self.n == 4:
            side, up, across = self.to
            self.copy(half_rows(c, 0), across, 2, c, up).wait_recv()
            self.copy(half_rows(c, 1), across, 3, c, side).wait_recv()
        else:
            for k in range(self.n - 1):
                self.copy(chunk_rows(c), self.source[k], k, c, self.to[k]).wait_recv()

    def finish(self, c):
        for k in range(self.direct()):
            self.copy(chunk_rows(c), self.me, k, c, self.to[k]).wait_send()
        if self.n == 4:
            for copy in self.handed(c):
                copy.wait_send()


class Scatter:
    def __init__(self, n, part, came, width, send_sem, recv_sem):
        self.n, self.part, self.came, self.width = n, part, came, width
        self.me, self.to, self.source = partners(n)
        self.send_sem, self.recv_sem = send_sem, recv_sem

    def copy(self, rows, owner, slot, k, c, target):
        return remote(
            self.part.at[rows, columns(owner, self.width)],
            self.came.at[slot, rows],
            self.send_sem.at[k, c],
            self.recv_sem.at[k, c],
            target,
        )

    def first(self, c):
        if self.n != 4:
            return tuple(
                (chunk_rows(c), self.to[k], k, k, c, self.to[k]) for k in range(self.n - 1)
            )
        side, up, across = self.to
        return (
            (half_rows(c, 0), across, 2, 0, c, side),
            (half_rows(c, 1), across, 2, 1, c, up),
            (half_rows(c, 0), side, 0, 2, c, side),
            (half_rows(c, 1), up, 1, 3, c, up),
        )

    def second(self, c):
        if self.n != 4:
            return ()
        side, up, _ = self.to
        return (
            (half_rows(c, 0), up, 1, 4, c, up),
            (half_rows(c, 1), side, 0, 5, c, side),
        )

    def start(self, c):
        for place in self.first(c):
            self.copy(*place).start()

    def relay(self, c):
        second = self.second(c)
        first = self.first(c)
        for half in range(len(second)):
            self.copy(*first[half]).wait_recv()
            owner = columns(self.to[1 - half], self.width)
            base = c * CHUNK + half * (CHUNK // 2)

            def add(r):
                rows = pl.ds(pl.multiple_of(base + r * ROWS, ROWS), ROWS)
                total = self.part[rows, owner].astype(F32) + self.came[2, rows].astype(F32)
                self.part[rows, owner] = total.astype(BF16)

            loop(CHUNK // 2 // ROWS, add)
            self.copy(*second[half]).start()

    def arrive(self, c):
        places = self.first(c)
        if self.n == 4:
            places = places[2:] + self.second(c)
        for place in places:
            self.copy(*place).wait_recv()

    def finish(self, c):
        for place in self.first(c) + self.second(c):
            self.copy(*place).wait_send()

    def total(self, rows):
        total = self.part[rows, columns(self.me, self.width)].astype(F32)
        for k in range(2 if self.n == 4 else self.n - 1):
            total += self.came[k, rows].astype(F32)
        return total


class Stats:
    def __init__(self, n, mine, came, send_sem, recv_sem):
        self.n, self.mine, self.came = n, mine, came
        self.me, self.to, self.source = partners(n)
        self.send_sem, self.recv_sem = send_sem, recv_sem

    def copy(self, c, k):
        return remote(
            self.mine.at[c], self.came.at[k, c], self.send_sem.at[k, c], self.recv_sem.at[k, c], self.to[k]
        )

    def start(self, c):
        for k in range(self.n - 1):
            self.copy(c, k).start()

    def arrive(self, c):
        for k in range(self.n - 1):
            self.copy(c, k).wait_recv()

    def finish(self, c):
        for k in range(self.n - 1):
            self.copy(c, k).wait_send()

    def put(self, c, first, second):
        ones = jnp.ones((8, 128), F32)
        for place, field in ((0, first), (8, second)):
            self.mine[c, place : place + 8] = lax.dot_general(
                ones, field, (((1,), (1,)), ((), ())), precision=PRECISE, preferred_element_type=F32
            )

    def moments(self, c, width):
        pieces = [self.mine[c]] + [self.came[k, c] for k in range(self.n - 1)]
        count = float(self.n * width)
        mean = sum(piece[0:8] for piece in pieces) * (1.0 / count)
        squares = sum(
            piece[8:16] + width * (piece[0:8] * (1.0 / width) - mean) ** 2 for piece in pieces
        )
        share = jnp.full((8, 128), 0.125, F32)
        return tuple(
            lax.dot_general(
                row, share, (((0,), (0,)), ((), ())), precision=PRECISE, preferred_element_type=F32
            )
            for row in (mean, lax.rsqrt(squares * (1.0 / count) + EPS))
        )

    def means(self, c, features):
        total = self.mine[c]
        for k in range(self.n - 1):
            total += self.came[k, c]
        share = jnp.full((8, 128), 1.0 / (8 * features), F32)
        return tuple(
            lax.dot_general(
                total[place : place + 8],
                share,
                (((0,), (0,)), ((), ())),
                precision=PRECISE,
                preferred_element_type=F32,
            )
            for place in (0, 8)
        )


def loop(count, body):
    def step(i, carry):
        body(i)
        return carry

    lax.fori_loop(0, count, step, 0)


def sub_rows(c, r):
    return pl.ds(pl.multiple_of(c * CHUNK + r * ROWS, ROWS), ROWS)


def repeat_lanes(field, width):
    return jnp.concatenate([field] * (width // 128), axis=1)


def fold_lanes(field):
    total = field[:, 0:128]
    for j in range(1, field.shape[1] // 128):
        total += field[:, 128 * j : 128 * (j + 1)]
    return total


def local_rows(r):
    return pl.ds(pl.multiple_of(r * ROWS, ROWS), ROWS)


def fold_entry(entry, first, second, rows):
    first[rows, :] = fold_lanes(entry)
    centered = entry - jnp.sum(entry, axis=1, keepdims=True) * (1.0 / entry.shape[1])
    second[rows, :] = fold_lanes(centered * centered)


def standardize(c, stats, gather, first, second, stand_ref, scale_ref):
    width = stand_ref.shape[1]
    stats.arrive(c)
    first[...], second[...] = stats.moments(c, width)

    def piece(r):
        rows, local = sub_rows(c, r), local_rows(r)
        scaling = second[local, :]
        stand = (stand_ref[rows, :] - repeat_lanes(first[local, :], width)) * repeat_lanes(
            scaling, width
        )
        stand_ref[rows, :] = stand
        scale_ref[rows, :] = scaling
        gather.buf[rows, gather.own()] = stand.astype(BF16)

    loop(CHUNK // ROWS, piece)
    gather.start(c)


def rotate(field, cos_rows, sin_rows, sign):
    turned = pltpu.roll(field, HEAD // 2, 1)
    return field * cos_rows + (sign * turned) * sin_rows


def spread(row):
    share = jnp.full((8, 128), 0.125, F32)
    return lax.dot_general(
        jnp.broadcast_to(row, (8, 128)),
        share,
        (((0,), (0,)), ((), ())),
        precision=PRECISE,
        preferred_element_type=F32,
    )


def project_kernel(
    n, in1, out2, positions_ref, segments_ref, s_hbm, c_hbm, wq_hbm, wk_hbm, wv_hbm,
    normed_hbm, q_ref, k_ref, v_ref, stand_ref, scale_ref, gb2_hbm, cot_hbm,
    cos_ref, sin_ref, segc_ref, segr_ref,
    s_buf, c_buf, cot_planes, w_buf, all1, all2, first, second, mine, others,
    in_sem, w_sem, out_sem, send1, recv1, send2, recv2, send3, recv3,
):
    streams, tokens, width = s_buf.shape
    count = tokens // CHUNK
    heads = width // HEAD
    weights = (wq_hbm, wk_hbm, wv_hbm)

    def s_in(c):
        return pltpu.make_async_copy(
            s_hbm.at[:, chunk_rows(c)], s_buf.at[:, chunk_rows(c)], in_sem.at[0, c]
        )

    def c_in(c):
        return pltpu.make_async_copy(
            c_hbm.at[chunk_rows(c)], c_buf.at[chunk_rows(c)], in_sem.at[1, c]
        )

    def w_in(j):
        return pltpu.make_async_copy(weights[j], w_buf.at[j], w_sem.at[j])

    def out(c, i):
        rows = chunk_rows(c)
        source, target = (
            (all1.at[rows], normed_hbm.at[rows]),
            (all2.at[rows], gb2_hbm.at[rows]),
            (cot_planes.at[:, rows], cot_hbm.at[:, rows]),
        )[i]
        return pltpu.make_async_copy(source, target, out_sem.at[i, c])

    loop(count, lambda c: s_in(c).start())
    loop(count, lambda c: c_in(c).start())
    for j in range(3):
        w_in(j).start()
    gather = Gather(n, all1, width, send1, recv1)
    incoming = Gather(n, all2, width, send2, recv2)
    stats = Stats(n, mine, others, send3, recv3)
    enter(n, gather.to)

    def entry(c):
        s_in(c).wait()

        def piece(r):
            rows = sub_rows(c, r)
            field = in1[0] * s_buf[0, rows].astype(F32)
            for i in range(1, streams):
                field += in1[i] * s_buf[i, rows].astype(F32)
            stand_ref[sub_rows(c, r), :] = field
            fold_entry(field, first, second, local_rows(r))

        loop(CHUNK // ROWS, piece)
        stats.put(c, first[...], second[...])
        stats.start(c)

    def send(c):
        standardize(c, stats, gather, first, second, stand_ref, scale_ref)

    def grad(c):
        c_in(c).wait()

        def piece(r):
            rows = sub_rows(c, r)
            block = c_buf[rows].astype(F32)
            total = None
            for i in range(streams):
                field = block[:, i, :]
                cot_planes[i, rows] = field.astype(BF16)
                total = out2[i] * field if total is None else total + out2[i] * field
            all2[rows, incoming.own()] = total.astype(BF16)

        loop(CHUNK // ROWS, piece)
        incoming.start(c)
        out(c, 2).start()

    entry(0)

    def ahead(c):
        entry(c + 1)
        send(c)

    loop(count - 1, ahead)
    send(count - 1)
    grad(0)
    gather.relay(0)
    grad(1)
    gather.relay(1)
    incoming.relay(0)

    segr_ref[...] = jnp.concatenate(
        [
            jnp.broadcast_to(segments_ref[a : a + 1, :].astype(F32), (8, 128))
            for a in range(tokens // 128)
        ],
        axis=1,
    )
    lane = lax.broadcasted_iota(jnp.int32, (128, 128), 1)
    exponent = lax.rem(lane, HEAD // 2).astype(F32) * (-2.0 / HEAD * math.log(10000.0))
    inverse = jnp.exp(exponent)
    for a in range(tokens // 128):
        rows = slice(128 * a, 128 * (a + 1))
        segc_ref[rows, :] = spread(segments_ref[a : a + 1, :].astype(F32))
        angles = spread(positions_ref[a : a + 1, :].astype(F32)) * inverse
        cos_ref[rows, :] = jnp.cos(angles)
        sine = jnp.sin(angles)
        sin_ref[rows, :] = jnp.where(lane < HEAD // 2, -sine, sine)
    grad(2)
    gather.relay(2)
    grad(3)
    gather.relay(3)
    incoming.relay(1)
    for j in range(3):
        w_in(j).wait()

    def work(c):
        gather.arrive(c)
        out(c, 0).start()
        rows = chunk_rows(c)
        block = all1[rows, :]
        cos_rows, sin_rows = cos_ref[rows, :], sin_ref[rows, :]
        for j, target in ((0, q_ref), (1, k_ref)):
            lin = dot_nn(block, w_buf[j])
            for h in range(heads):
                place = slice(HEAD * h, HEAD * (h + 1))
                target[rows, place] = rotate(lin[:, place], cos_rows, sin_rows, 1.0).astype(BF16)
        v_ref[rows, :] = dot_nn(block, w_buf[2]).astype(BF16)

        @pl.when(c + 2 < count)
        def _():
            incoming.relay(c + 2)

    loop(count, work)

    def end(c):
        incoming.arrive(c)
        out(c, 1).start()

    loop(count, end)

    def drain(c):
        for i in range(3):
            out(c, i).wait()
        stats.finish(c)
        gather.finish(c)
        incoming.finish(c)

    loop(count, drain)


def window_bias(c, start, extent, segc_ref, segr_ref, bias):
    def part(r):
        rows = pl.ds(pl.multiple_of(r * ROWS, ROWS), ROWS)
        row = c * CHUNK + r * ROWS + lax.broadcasted_iota(jnp.int32, (ROWS, extent), 0)
        column = start + lax.broadcasted_iota(jnp.int32, (ROWS, extent), 1)
        same = segc_ref[sub_rows(c, r), 0:1] == segr_ref[0:1, pl.ds(start, extent)]
        bias[rows, :] = jnp.where((row >= column) & same, 0.0, MASKED)

    loop(CHUNK // ROWS, part)


def window(c, tokens):
    extent = min(tokens, CHUNK * (-(-(LONGEST - 1) // CHUNK) + 1))
    back = extent // CHUNK - 1
    return pl.multiple_of(jnp.maximum(c - back, 0) * CHUNK, CHUNK), extent


def attend_kernel(
    n, in1, out1, in2, out2, res1, res2, q_ref, k_ref, v_ref, segc_ref, segr_ref, wo_ref,
    s_hbm, gb2_hbm, wg_hbm, wu_hbm, wd_hbm,
    attended_ref, branch_ref, normed_hbm, stand_ref, scale_ref, hidden_hbm, acts_hbm, grads_hbm,
    s_buf, gb2_buf, wg_buf, wu_buf, wd_buf, hidden_buf, gate_buf, up_buf,
    part, came, all2, first, second, mine, others, bias,
    s_sem, gb2_sem, grad_sem, w_sem, normed_sem, out_sem, send1, recv1, send2, recv2, send3, recv3,
):
    tokens, width = q_ref.shape
    units = wg_buf.shape[1]
    count = tokens // CHUNK
    heads = width // HEAD
    block = min(units, 512)
    mixing = Mixing((in1, out1, in2, out2, res1, res2))

    def s_in(c):
        slot = lax.rem(c, 2)
        return pltpu.make_async_copy(s_hbm.at[:, chunk_rows(c)], s_buf.at[slot], s_sem.at[slot])

    def gb2_in(c):
        slot = lax.rem(c, 2)
        return pltpu.make_async_copy(gb2_hbm.at[chunk_rows(c)], gb2_buf.at[slot], gb2_sem.at[slot])

    def grads_out(c):
        slot = lax.rem(c, 2)
        return pltpu.make_async_copy(
            gate_buf.at[slot], grads_hbm.at[chunk_rows(c)], grad_sem.at[0, slot]
        )

    def grads_in(c):
        slot = lax.rem(c, 2)
        return pltpu.make_async_copy(
            grads_hbm.at[chunk_rows(c)], gb2_buf.at[slot, :, 0:units], grad_sem.at[1, slot]
        )

    def normed_out(c):
        return pltpu.make_async_copy(
            all2.at[chunk_rows(c)], normed_hbm.at[chunk_rows(c)], normed_sem.at[c]
        )

    def outs(c):
        slot, rows = lax.rem(c, 2), chunk_rows(c)
        return tuple(
            pltpu.make_async_copy(buf.at[slot], target, out_sem.at[i, slot])
            for i, (buf, target) in enumerate(
                (
                    (hidden_buf, hidden_hbm.at[rows]),
                    (gate_buf, acts_hbm.at[rows, 0:units]),
                    (up_buf, acts_hbm.at[rows, units : 2 * units]),
                )
            )
        )

    weights = tuple(
        pltpu.make_async_copy(source, target, w_sem.at[i])
        for i, (source, target) in enumerate(
            ((wd_hbm, wd_buf), (wg_hbm, wg_buf), (wu_hbm, wu_buf))
        )
    )
    s_in(0).start()
    gb2_in(0).start()
    gb2_in(1).start()
    for copy in weights:
        copy.start()
    scatter = Scatter(n, part, came, width, send1, recv1)
    gather = Gather(n, all2, width, send2, recv2)
    stats = Stats(n, mine, others, send3, recv3)
    enter(n, gather.to)

    def attend(c):
        rows = chunk_rows(c)
        start, extent = window(c, tokens)
        window_bias(c, start, extent, segc_ref, segr_ref, bias)
        for h in range(heads):
            place = slice(HEAD * h, HEAD * (h + 1))
            scores = dot_nt(q_ref[rows, place], k_ref[pl.ds(start, extent), place])
            scores = scores * HEAD ** (-0.5) + bias[...]
            raised = jnp.exp(scores - jnp.max(scores, axis=1, keepdims=True))
            inverse = 1.0 / jnp.sum(raised, axis=1, keepdims=True)
            probs = (raised * inverse).astype(BF16)
            attended_ref[rows, place] = dot_nn(probs, v_ref[pl.ds(start, extent), place]).astype(BF16)
        part[rows, :] = dot_nn(attended_ref[rows, :], wo_ref[...]).astype(BF16)

    def middle(c):
        @pl.when(c + 1 < count)
        def _():
            s_in(c + 1).start()

        s_in(c).wait()
        slot = lax.rem(c, 2)
        scatter.arrive(c)

        def piece(r):
            rows = sub_rows(c, r)
            branch = scatter.total(rows)
            branch_ref[rows, :] = branch
            entry = mixing.across * branch
            for i in range(s_buf.shape[1]):
                entry += mixing.entry[i] * s_buf[slot, i, local_rows(r)].astype(F32)
            stand_ref[rows, :] = entry
            fold_entry(entry, first, second, local_rows(r))

        loop(CHUNK // ROWS, piece)
        stats.put(c, first[...], second[...])
        stats.start(c)

    def send(c):
        standardize(c, stats, gather, first, second, stand_ref, scale_ref)

    def work(c):
        gather.arrive(c)
        normed_out(c).start()
        slot = lax.rem(c, 2)

        @pl.when(c >= 2)
        def _():
            for copy in outs(c - 2):
                copy.wait()

        grads_in(c).wait()

        def piece(f):
            place = columns(f, block)
            gate = dot_nn(all2[chunk_rows(c), :], wg_buf[:, place])
            up = dot_nn(all2[chunk_rows(c), :], wu_buf[:, place])
            grad = gb2_buf[slot, :, place].astype(F32)
            sig = jax.nn.sigmoid(gate)
            act = gate * sig
            hidden_buf[slot, :, place] = (act * up).astype(BF16)
            gate_buf[slot, :, place] = (grad * up * sig * (1.0 + gate * (1.0 - sig))).astype(BF16)
            up_buf[slot, :, place] = (grad * act).astype(BF16)

        loop(units // block, piece)
        for copy in outs(c):
            copy.start()

        @pl.when(c + 2 < count)
        def _():
            grads_in(c + 2).start()
            gather.relay(c + 2)

    def grads(c):
        slot = lax.rem(c, 2)
        if c >= 2:
            grads_out(c - 2).wait()
        gb2_in(c).wait()

        def piece(f):
            place = columns(f, block)
            gate_buf[slot, :, place] = dot_nt(gb2_buf[slot], wd_buf[place, :]).astype(BF16)

        loop(units // block, piece)
        grads_out(c).start()
        if c + 2 < count:
            gb2_in(c + 2).start()

    def attend_send(c):
        attend(c)
        scatter.start(c)

        @pl.when(c >= 1)
        def _():
            scatter.relay(c - 1)

    loop(count, attend_send)
    middle(0)
    weights[0].wait()
    grads(0)
    scatter.relay(3)
    middle(1)
    send(0)
    grads(1)
    middle(2)
    send(1)
    grads(2)
    middle(3)
    grads(3)
    gather.relay(0)
    send(2)
    gather.relay(1)
    send(3)
    grads_out(2).wait()
    grads_out(3).wait()
    grads_in(0).start()
    grads_in(1).start()
    weights[1].wait()
    weights[2].wait()
    loop(count, work)
    for c in range(max(count - 2, 0), count):
        for copy in outs(c):
            copy.wait()

    def drain(c):
        normed_out(c).wait()
        scatter.finish(c)
        stats.finish(c)
        gather.finish(c)

    loop(count, drain)


def stats_part(part32, normed, normed_rows, part, c, first, second):
    def piece(r):
        rows = pl.ds(pl.multiple_of(r * ROWS, ROWS), ROWS)
        field = part32[rows, :]
        first[rows, :] = fold_lanes(field)
        second[rows, :] = fold_lanes(field * normed[normed_rows(r), :].astype(F32))
        part[sub_rows(c, r), :] = field.astype(BF16)

    loop(CHUNK // ROWS, piece)


def units_back_kernel(
    n, in1, out1, in2, out2, res1, res2, scale_ref, acts_hbm, wg_hbm, wu_hbm, normed_hbm, stand_hbm, c_hbm, _down, _gate_up,
    entry_ref, gb1_hbm,
    acts_ref, wg_ref, wu_ref, normed_ref, stand_ref, c_buf, part32, first, second, part, came, mine, others, all1, acts_sem, in_sem, out_sem,
    send1, recv1, send2, recv2, send3, recv3,
):
    tokens, features = normed_ref.shape
    width = entry_ref.shape[1]
    count = tokens // CHUNK
    mixing = Mixing((in1, out1, in2, out2, res1, res2))

    def acts_in(c):
        return pltpu.make_async_copy(
            acts_hbm.at[chunk_rows(c)], acts_ref.at[chunk_rows(c)], acts_sem.at[c]
        )

    wg_in, wu_in, normed_in, stand_in, c_in = (
        pltpu.make_async_copy(source, target, in_sem.at[i])
        for i, (source, target) in enumerate(
            (
                (wg_hbm, wg_ref),
                (wu_hbm, wu_ref),
                (normed_hbm, normed_ref),
                (stand_hbm, stand_ref),
                (c_hbm, c_buf),
            )
        )
    )
    acts_in(0).start()
    wg_in.start()
    wu_in.start()
    normed_in.start()
    loop(count - 1, lambda c: acts_in(c + 1).start())
    stand_in.start()
    c_in.start()
    scatter = Scatter(n, part, came, width, send1, recv1)
    stats = Stats(n, mine, others, send2, recv2)
    gather = Gather(n, all1, width, send3, recv3)
    enter(n, gather.to)

    def work(c):
        rows = chunk_rows(c)
        units = wg_ref.shape[1]
        acts_in(c).wait()

        @pl.when(c == 0)
        def _():
            wg_in.wait()

        part32[...] = dot_nt(acts_ref[rows, 0:units], wg_ref[...])

        @pl.when(c == 0)
        def _():
            wu_in.wait()
            normed_in.wait()

        part32[...] += dot_nt(acts_ref[rows, units : 2 * units], wu_ref[...])
        stats_part(part32, normed_ref, lambda r: sub_rows(c, r), part, c, first, second)
        stats.put(c, first[...], second[...])
        stats.start(c)
        scatter.start(c)

        @pl.when(c >= 1)
        def _():
            scatter.relay(c - 1)

    def middle(c):
        scatter.arrive(c)
        stats.arrive(c)
        first[...], second[...] = stats.means(c, features)

        def piece(r):
            rows = sub_rows(c, r)
            local = pl.ds(pl.multiple_of(r * ROWS, ROWS), ROWS)
            standard = stand_ref[rows, :]
            entry = repeat_lanes(scale_ref[rows, :], width) * (
                scatter.total(rows)
                - repeat_lanes(first[local, :], width)
                - standard * repeat_lanes(second[local, :], width)
            )
            entry_ref[rows, :] = entry
            grad = mixing.across * entry
            for i in range(c_buf.shape[0]):
                grad += mixing.branch[i] * c_buf[i, rows].astype(F32)
            all1[rows, gather.own()] = grad.astype(BF16)

        loop(CHUNK // ROWS, piece)
        gather.start(c)

    def ahead(c):
        work(c)

        @pl.when(c == 1)
        def _():
            stand_in.wait()
            c_in.wait()

        @pl.when(c >= 2)
        def _():
            middle(c - 2)

    loop(count, ahead)
    scatter.relay(count - 1)
    middle(count - 2)
    gather.relay(0)
    middle(count - 1)
    for c in range(1, count):
        gather.relay(c)

    def gb1_out(c):
        return pltpu.make_async_copy(
            all1.at[chunk_rows(c)], gb1_hbm.at[chunk_rows(c)], out_sem.at[c]
        )

    def last(c):
        gather.arrive(c)
        gb1_out(c).start()

    loop(count, last)

    def drain(c):
        gb1_out(c).wait()
        scatter.finish(c)
        stats.finish(c)
        gather.finish(c)

    loop(count, drain)


def attend_back_kernel(
    n, q_ref, k_ref, v_ref, segc_ref, segr_ref, cos_ref, sin_ref, scale_ref,
    wo_hbm, wq_hbm, wk_hbm, wv_hbm, wd_hbm, stand_hbm, gb1_hbm, hidden_hbm, normed_hbm, _output, _down,
    lin_ref, branch_ref, entry_ref,
    wo_ref, wq_ref, wk_ref, wv_ref, wd_ref, stand_ref, gb1_buf, hidden_buf, normed_buf, bias, dk_t, dv_t, part32, first, second,
    part1, came1, part2, came2, mine, others, in_sem, w_sem,
    send1, recv1, send2, recv2, send3, recv3,
):
    tokens, width = q_ref.shape
    features = part1.shape[1]
    count = tokens // CHUNK
    heads = width // HEAD
    factor = HEAD ** (-0.5)
    down = Scatter(n, part2, came2, width, send1, recv1)
    scatter = Scatter(n, part1, came1, width, send2, recv2)
    stats = Stats(n, mine, others, send3, recv3)

    def inputs(c, slot):
        return tuple(
            pltpu.make_async_copy(source.at[chunk_rows(c)], target.at[slot], in_sem.at[i, slot])
            for i, (source, target) in enumerate(
                ((gb1_hbm, gb1_buf), (hidden_hbm, hidden_buf), (normed_hbm, normed_buf))
            )
        )

    wd_in, wo_in, wq_in, wk_in, wv_in, stand_in = (
        pltpu.make_async_copy(source, target, w_sem.at[i])
        for i, (source, target) in enumerate(
            (
                (wd_hbm, wd_ref),
                (wo_hbm, wo_ref),
                (wq_hbm, wq_ref),
                (wk_hbm, wk_ref),
                (wv_hbm, wv_ref),
                (stand_hbm, stand_ref),
            )
        )
    )
    for copy in inputs(count - 1, 0):
        copy.start()
    for copy in (wd_in, wo_in, wq_in, wk_in, wv_in, stand_in):
        copy.start()
    dk_t[...] = jnp.zeros_like(dk_t)
    dv_t[...] = jnp.zeros_like(dv_t)
    enter(n, scatter.to)

    def work(i):
        c = count - 1 - i
        slot = lax.rem(i, 2)

        @pl.when(i < count - 1)
        def _():
            for copy in inputs(c - 1, 1 - slot):
                copy.start()

        for copy in inputs(c, slot):
            copy.wait()
        rows = chunk_rows(c)

        @pl.when(i == 0)
        def _():
            wd_in.wait()

        part2[rows, :] = dot_nn(hidden_buf[slot], wd_ref[...]).astype(BF16)
        down.start(c)

        @pl.when(i == 0)
        def _():
            for copy in (wo_in, wq_in, wk_in, wv_in):
                copy.wait()

        grad = dot_nt(gb1_buf[slot], wo_ref[...]).astype(BF16)
        start, extent = window(c, tokens)
        keys = pl.ds(start, extent)
        window_bias(c, start, extent, segc_ref, segr_ref, bias)
        cos_rows, sin_rows = cos_ref[rows, :], sin_ref[rows, :]
        for h in range(heads):
            place = slice(HEAD * h, HEAD * (h + 1))
            query, grad_h = q_ref[rows, place], grad[:, place]
            scores = dot_nt(query, k_ref[keys, place]) * factor + bias[...]
            raised = jnp.exp(scores - jnp.max(scores, axis=1, keepdims=True))
            inverse = 1.0 / jnp.sum(raised, axis=1, keepdims=True)
            probs = raised * inverse
            grad_probs = dot_nt(grad_h, v_ref[keys, place])
            centre = jnp.sum(probs * grad_probs, axis=1, keepdims=True)
            grad_scores = (probs * (grad_probs - centre)).astype(BF16)
            dv_t[place, keys] += dot_nn(jnp.transpose(grad_h), probs.astype(BF16))
            dk_t[place, keys] += dot_nn(jnp.transpose(query), grad_scores)
            dq = dot_nn(grad_scores, k_ref[keys, place]) * factor
            lin_ref[rows, place] = rotate(dq, cos_rows, sin_rows, -1.0).astype(BF16)
            dk = jnp.transpose(dk_t[place, rows]) * factor
            lin_ref[rows, slice(width + HEAD * h, width + HEAD * (h + 1))] = rotate(dk, cos_rows, sin_rows, -1.0).astype(BF16)
            lin_ref[rows, slice(2 * width + HEAD * h, 2 * width + HEAD * (h + 1))] = jnp.transpose(dv_t[place, rows]).astype(BF16)
        part32[...] = dot_nt(lin_ref[rows, 0:width], wq_ref[...])
        part32[...] += dot_nt(lin_ref[rows, width : 2 * width], wk_ref[...])
        part32[...] += dot_nt(lin_ref[rows, 2 * width : 3 * width], wv_ref[...])
        stats_part(
            part32,
            normed_buf.at[slot],
            lambda r: pl.ds(pl.multiple_of(r * ROWS, ROWS), ROWS),
            part1,
            c,
            first,
            second,
        )
        stats.put(c, first[...], second[...])
        stats.start(c)
        scatter.start(c)
        down.relay(c)

        @pl.when(i >= 1)
        def _():
            scatter.relay(c + 1)

    loop(count, work)
    scatter.relay(0)
    stand_in.wait()

    def last(i):
        c = count - 1 - i
        down.arrive(c)

        def sums(r):
            branch_ref[sub_rows(c, r), :] = down.total(sub_rows(c, r))

        loop(CHUNK // ROWS, sums)
        scatter.arrive(c)
        stats.arrive(c)
        first[...], second[...] = stats.means(c, features)

        def piece(r):
            rows = sub_rows(c, r)
            local = pl.ds(pl.multiple_of(r * ROWS, ROWS), ROWS)
            entry_ref[rows, :] = repeat_lanes(scale_ref[rows, :], width) * (
                scatter.total(rows)
                - repeat_lanes(first[local, :], width)
                - stand_ref[rows, :] * repeat_lanes(second[local, :], width)
            )

        loop(CHUNK // ROWS, piece)

    loop(count, last)

    def drain(c):
        down.finish(c)
        scatter.finish(c)
        stats.finish(c)

    loop(count, drain)


def turn_kernel(source_ref, target_ref):
    target_ref[...] = jnp.transpose(source_ref[...].astype(F32))


def streams_kernel(
    in1, out1, in2, out2, res1, res2, s_ref, c_ref, b1_ref, b2_ref, e1_ref, e2_ref,
    new_ref, grad_ref, mix_ref, sums_ref,
):
    @pl.when(pl.program_id(0) == 0)
    def _():
        sums_ref[...] = jnp.zeros_like(sums_ref)

    count = s_ref.shape[0]
    mixing = Mixing((in1, out1, in2, out2, res1, res2))
    mixed = [[mixing.mixed(k, j) for j in range(count)] for k in range(count)]

    def fold(field):
        field = fold_lanes(field)
        total = field[0:8]
        for j in range(1, field.shape[0] // 8):
            total += field[8 * j : 8 * (j + 1)]
        return total

    def piece(r):
        rows = pl.ds(pl.multiple_of(r * 16, 16), 16)
        s = [s_ref[i, rows].astype(F32) for i in range(count)]
        c = [c_ref[i, rows].astype(F32) for i in range(count)]
        b1, b2, e1, e2 = b1_ref[rows, :], b2_ref[rows, :], e1_ref[rows, :], e2_ref[rows, :]
        for j in range(count):
            new = mixing.branch[j] * b1 + mixing.out2[j] * b2
            grad = mixing.entry[j] * e2 + mixing.in1[j] * e1
            for k in range(count):
                new += mixed[k][j] * s[k]
                grad += mixed[j][k] * c[k]
            new_ref[rows, j, :] = new.astype(BF16)
            grad_ref[rows, j, :] = grad
        pairs = [(s[i], c[j]) for i in range(count) for j in range(count)]
        pairs += [(s[i], e1) for i in range(count)] + [(s[i], e2) for i in range(count)]
        pairs += [(c[i], b1) for i in range(count)] + [(c[i], b2) for i in range(count)]
        pairs += [(b1, e2)]
        for place, (left, right) in enumerate(pairs):
            sums_ref[place] += fold(left * right)

    loop(s_ref.shape[1] // 16, piece)

    @pl.when(pl.program_id(0) == pl.num_programs(0) - 1)
    def _():
        sums = [sums_ref[place] for place in range(PRODUCTS)]
        s_c = [sums[count * i : count * (i + 1)] for i in range(count)]
        s_e1, s_e2, c_b1, c_b2 = (sums[16 + 4 * k : 20 + 4 * k] for k in range(4))
        b_e = sums[32]
        every = range(count)
        row1, row2 = mixing.res1, mixing.res2
        grads = [s_e1[i] for i in every]
        grads += [inner(row2[j], s_c[i]) + mixing.in2[j] * s_e2[i] for i in every for j in every]
        grads += [inner(row2[j], c_b1) + mixing.in2[j] * b_e for j in every]
        turned1 = [[row1[k][i] for k in every] for i in every]
        grads += [inner(turned1[i], s_e2) + mixing.out1[i] * b_e for i in every]
        grads += [
            inner(turned1[i], [s_c[k][j] for k in every]) + mixing.out1[i] * c_b1[j]
            for i in every
            for j in every
        ]
        grads += [c_b2[j] for j in every]
        for place, field in enumerate(grads):
            mix_ref[place] = field


PLANES = 4
CORES = 2
PRODUCTS = 33
SUMS = 48


def pair_kernel(
    left_hbm, right_hbm, out_hbm, left, right, turned, sent, came, mine_buf,
    left_sem, right_sem, out_sem, send_sem, recv_sem,
):
    steps, height, width = came.shape
    block = height // 2
    piece = right_sem.shape[0]
    across = width // piece
    me = lax.axis_index("dp")
    mine = lax.rem(me, CORES)
    partner = me + 1 - 2 * mine

    def left_in(step, half, part):
        index = (2 * step + part) * CORES + half
        return pltpu.make_async_copy(
            left_hbm.at[:, columns(index, block)],
            left.at[2 * step + part, half],
            left_sem.at[2 * step + part, half],
        )

    def right_in(f):
        return pltpu.make_async_copy(
            right_hbm.at[:, columns(f, across)], right.at[:, columns(f, across)], right_sem.at[f]
        )

    def swap(step):
        return pltpu.make_async_remote_copy(
            src_ref=sent.at[step],
            dst_ref=came.at[step],
            send_sem=send_sem.at[step],
            recv_sem=recv_sem.at[step],
            device_id={"dp": partner},
            device_id_type=MESH,
        )

    def out(step):
        rows = pl.ds(pl.multiple_of(step * height, height), height)
        return pltpu.make_async_copy(mine_buf.at[step], out_hbm.at[rows], out_sem.at[step])

    for part in range(2):
        left_in(0, 1 - mine, part).start()
    for f in range(piece):
        right_in(f).start()
    for half in (1 - mine, mine):
        for step in range(steps):
            for part in range(2):
                if half is mine or step > 0:
                    left_in(step, half, part).start()
    barrier = pltpu.get_barrier_semaphore()
    pl.semaphore_signal(barrier, inc=1, device_id={"dp": partner}, device_id_type=MESH)
    pl.semaphore_wait(barrier, 1)

    def turn(step, half):
        for part in range(2):
            left_in(step, half, part).wait()
            turned[part * block : (part + 1) * block, :] = jnp.transpose(left[2 * step + part, half])

    def other(step):
        turn(step, 1 - mine)

        def part(f):
            @pl.when(step == 0)
            def _():
                right_in(f).wait()

            place = columns(f, across)
            sent[step, :, place] = dot_nn(turned[...], right[:, place]).astype(BF16)

        loop(piece, part)
        swap(step).start()

    loop(steps, other)

    def own(step):
        turn(step, mine)
        swap(step).wait_recv()

        def part(f):
            place = columns(f, across)
            total = dot_nn(turned[...], right[:, place]) + came[step, :, place].astype(F32)
            mine_buf[step, :, place] = total.astype(BF16)

        loop(piece, part)
        out(step).start()

    loop(steps, own)

    def drain(step):
        swap(step).wait_send()
        out(step).wait()

    loop(steps, drain)


def finish_kernel(
    n, first_hbm, last_hbm, sums_ref,
    q_out, k_out, v_out, o_out, sums_out,
    own, core, right, left, by_core, by_plane, by_tensor,
    own_sem, core_send, core_recv, right_send, right_recv, left_send, left_recv, sum_send, sum_recv,
):
    _, pieces, height, width = own.shape
    me = lax.axis_index("dp")
    plane, mine = lax.div(me, CORES), lax.rem(me, CORES)
    partner = me + 1 - 2 * mine
    here, peers, peer_source = partners(n)
    planes_to = [lax.rem(plane + k, PLANES) for k in range(1, PLANES)]
    planes_from = [lax.rem(plane + PLANES - k, PLANES) for k in range(1, PLANES)]

    def dp_at(position):
        return position * CORES + mine

    def rows_of(position, half):
        return pl.ds(pl.multiple_of((position * CORES + half) * height, height), height)

    def block(position, half, p):
        if p < pieces - 1:
            return first_hbm.at[rows_of(position, half), p * width : (p + 1) * width]
        return last_hbm.at[rows_of(position, half)]

    def over_dp(source, target, send_sem, recv_sem, device):
        return pltpu.make_async_remote_copy(
            src_ref=source, dst_ref=target, send_sem=send_sem, recv_sem=recv_sem,
            device_id={"dp": device}, device_id_type=MESH,
        )

    def own_in(position, p):
        return pltpu.make_async_copy(
            block(position, mine, p), own.at[position, p], own_sem.at[position, p]
        )

    def core_in(position, p):
        return over_dp(
            block(position, 1 - mine, p), core.at[position, p],
            core_send.at[position, p], core_recv.at[position, p], partner,
        )

    def rightward(step, p):
        return over_dp(
            own.at[lax.rem(plane + PLANES - step, PLANES), p], right.at[step - 1, p],
            right_send.at[step - 1, p], right_recv.at[step - 1, p], lax.rem(me + CORES, PLANES * CORES),
        )

    def leftward(step, p):
        return over_dp(
            own.at[lax.rem(plane + step, PLANES), p], left.at[step - 1, p],
            left_send.at[step - 1, p], left_recv.at[step - 1, p],
            lax.rem(me + (PLANES - 1) * CORES, PLANES * CORES),
        )

    order = (3, 0, 2, 1)
    for position in order:
        for p in range(pieces):
            own_in(position, p).start()

    barrier = pltpu.get_barrier_semaphore()
    pl.semaphore_signal(barrier, inc=1, device_id={"dp": partner}, device_id_type=MESH)
    for k in range(PLANES - 1):
        pl.semaphore_signal(
            barrier, inc=1, device_id={"dp": dp_at(planes_to[k])}, device_id_type=MESH
        )
    for k in range(n - 1):
        pl.semaphore_signal(barrier, inc=1, device_id={"tensor": peers[k]}, device_id_type=MESH)
    pl.semaphore_wait(barrier, 1 + PLANES - 1 + n - 1)

    by_core[mine] = jnp.sum(sums_ref[...], axis=1)
    over_dp(
        by_core.at[mine], by_core.at[mine], sum_send.at[0], sum_recv.at[0], partner
    ).start()
    for position in order:
        for p in range(pieces):
            core_in(position, p).start()
    over_dp(
        by_core.at[1 - mine], by_core.at[1 - mine], sum_send.at[0], sum_recv.at[0], partner
    ).wait_recv()
    by_plane[plane] = by_core[0] + by_core[1]

    def plane_sums(k, at):
        return over_dp(
            by_plane.at[at], by_plane.at[at], sum_send.at[1 + k], sum_recv.at[1 + k],
            dp_at(planes_to[k]),
        )

    def tensor_sums(k, at):
        at = by_tensor.at[at]
        return remote(at, at, sum_send.at[PLANES + k], sum_recv.at[PLANES + k], peers[k])

    for k in range(PLANES - 1):
        plane_sums(k, plane).start()

    def gather_pair(position):
        def piece(p):
            pltpu.make_async_copy(
                own.at[position, p], own.at[position, p], own_sem.at[position, p]
            ).wait()
            over_dp(
                core.at[position, p], core.at[position, p],
                core_send.at[position, p], core_recv.at[position, p], partner,
            ).wait_recv()
            add(own.at[position, p], core.at[position, p])

        loop(pieces, piece)

    def add(target, source):
        def part(r):
            rows = local_rows(r)
            target[rows, :] = (target[rows, :].astype(F32) + source[rows, :].astype(F32)).astype(BF16)

        loop(height // ROWS, part)

    def send_step(step):
        def piece(p):
            @pl.when(plane <= step - 1)
            def _():
                if step >= 2:

                    @pl.when(plane >= 1)
                    def _():
                        rightward(step - 1, p).wait_recv()
                        add(own.at[lax.rem(plane + PLANES - step, PLANES), p], right.at[step - 2, p])

                rightward(step, p).start()

            @pl.when(plane >= PLANES - step)
            def _():
                if step >= 2:

                    @pl.when(plane <= PLANES - 2)
                    def _():
                        leftward(step - 1, p).wait_recv()
                        add(own.at[lax.rem(plane + step, PLANES), p], left.at[step - 2, p])

                leftward(step, p).start()

        loop(pieces, piece)

    gather_pair(3)
    gather_pair(0)
    send_step(1)
    gather_pair(2)
    gather_pair(1)
    for k in range(PLANES - 1):
        plane_sums(k, planes_from[k]).wait_recv()
    by_tensor[here] = sum((by_plane[i] for i in range(1, PLANES)), by_plane[0])
    for k in range(n - 1):
        tensor_sums(k, here).start()
    for step in range(2, PLANES):
        send_step(step)
    for k in range(n - 1):
        tensor_sums(k, peer_source[k]).wait_recv()
    sums_out[...] = sum((by_tensor[i] for i in range(1, n)), by_tensor[0])

    for p, target in enumerate((q_out, k_out, v_out, o_out)):
        steps = PLANES - 2

        @pl.when(plane >= 1)
        def _():
            rightward(PLANES - 1, p).wait_recv()

        @pl.when(plane <= PLANES - 2)
        def _():
            leftward(PLANES - 1, p).wait_recv()

        total = own[plane, p].astype(F32)
        total += jnp.where(plane >= 1, right[steps, p].astype(F32), 0.0)
        total += jnp.where(plane <= PLANES - 2, left[steps, p].astype(F32), 0.0)
        target[...] = total if p < pieces - 1 else jnp.transpose(total)

    over_dp(by_core.at[mine], by_core.at[mine], sum_send.at[0], sum_recv.at[0], partner).wait_send()
    for k in range(PLANES - 1):
        plane_sums(k, plane).wait_send()
    for k in range(n - 1):
        tensor_sums(k, here).wait_send()
    for p in range(pieces):
        for position in range(PLANES):
            core_in(position, p).wait_send()
        for step in range(1, PLANES):

            @pl.when(plane <= step - 1)
            def _():
                rightward(step, p).wait_send()

            @pl.when(plane >= PLANES - step)
            def _():
                leftward(step, p).wait_send()


def on_device(
    n,
    replicas,
    streams,
    segments,
    positions,
    mix_in1,
    mix_res1,
    mix_out1,
    mix_in2,
    mix_res2,
    mix_out2,
    w_query,
    w_key,
    w_value,
    w_output,
    w_gate,
    w_up,
    w_down,
    cotangent,
):
    tokens, stream_count, width = streams.shape
    features = w_query.shape[0]
    units = w_gate.shape[1]
    chunks = tokens // CHUNK
    assert tokens == LENGTH == 4 * CHUNK and stream_count == 4
    any_spec = pl.BlockSpec(memory_space=pl.ANY)
    vmem = pl.BlockSpec(memory_space=pltpu.VMEM)
    smem = pl.BlockSpec(memory_space=pltpu.SMEM)

    def array(shape, dtype):
        return jax.ShapeDtypeStruct(shape, dtype)

    def dma(*shape):
        return pltpu.SemaphoreType.DMA(shape)

    def pair(lanes):
        return [dma(lanes, chunks), dma(lanes, chunks)]

    gather_sems = pair(4 if n == 4 else n - 1)
    scatter_sems = pair(6 if n == 4 else n - 1)
    stats_sems = pair(n - 1)

    def lasts(micros):
        return pl.CostEstimate(
            flops=int(micros * 1.0e9), bytes_accessed=int(micros * 3.6e6), transcendentals=0
        )

    def params(identity, mib):
        return pltpu.CompilerParams(
            collective_id=identity, has_side_effects=True, vmem_limit_bytes=mib * MIB
        )

    planes = jnp.transpose(streams, (1, 0, 2))
    mixes = (mix_in1, mix_out1, mix_in2, mix_out2, mix_res1, mix_res2)

    def stats_scratch():
        return [
            pltpu.VMEM((CHUNK, 128), F32),
            pltpu.VMEM((CHUNK, 128), F32),
            pltpu.VMEM((chunks, 16, CHUNK), F32),
            pltpu.VMEM((n - 1, chunks, 16, CHUNK), F32),
        ]

    (
        normed1, queries, keys, values, stand1, scale1, grad_branch2, cot_planes,
        cos_table, sin_table, seg_column, seg_row,
    ) = pl.pallas_call(
        functools.partial(project_kernel, n),
        name="project",
        cost_estimate=lasts(100),
        out_shape=[
            array((tokens, features), BF16),
            array((tokens, width), BF16),
            array((tokens, width), BF16),
            array((tokens, width), BF16),
            array((tokens, width), F32),
            array((tokens, 128), F32),
            array((tokens, features), BF16),
            array((stream_count, tokens, width), BF16),
            array((tokens, HEAD), F32),
            array((tokens, HEAD), F32),
            array((tokens, 128), F32),
            array((8, tokens), F32),
        ],
        in_specs=[smem, smem, vmem, vmem] + [any_spec] * 5,
        out_specs=[any_spec] + [vmem] * 5 + [any_spec] * 2 + [vmem] * 4,
        scratch_shapes=[
            pltpu.VMEM((stream_count, tokens, width), BF16),
            pltpu.VMEM((tokens, stream_count, width), BF16),
            pltpu.VMEM((stream_count, tokens, width), BF16),
            pltpu.VMEM((3, features, width), BF16),
            pltpu.VMEM((tokens, features), BF16),
            pltpu.VMEM((tokens, features), BF16),
        ]
        + stats_scratch()
        + [dma(2, chunks), dma(3), dma(3, chunks)]
        + gather_sems
        + gather_sems
        + stats_sems,
        compiler_params=params(0, 56),
    )(
        mix_in1, mix_out2,
        positions.reshape(tokens // 128, 128), segments.reshape(tokens // 128, 128),
        planes, cotangent, w_query, w_key, w_value,
    )

    extent = window(0, tokens)[1]
    attended, branch1, normed2, stand2, scale2, hidden, grad_acts, _ = pl.pallas_call(
        functools.partial(attend_kernel, n),
        name="attend",
        cost_estimate=lasts(100),
        out_shape=[
            array((tokens, width), BF16),
            array((tokens, width), F32),
            array((tokens, features), BF16),
            array((tokens, width), F32),
            array((tokens, 128), F32),
            array((tokens, units), BF16),
            array((tokens, 2 * units), BF16),
            array((tokens, units), BF16),
        ],
        in_specs=[smem] * 6 + [vmem] * 6 + [any_spec] * 5,
        out_specs=[vmem, vmem, any_spec, vmem, vmem, any_spec, any_spec, any_spec],
        scratch_shapes=[
            pltpu.VMEM((2, stream_count, CHUNK, width), BF16),
            pltpu.VMEM((2, CHUNK, features), BF16),
            pltpu.VMEM((features, units), BF16),
            pltpu.VMEM((features, units), BF16),
            pltpu.VMEM((units, features), BF16),
            pltpu.VMEM((2, CHUNK, units), BF16),
            pltpu.VMEM((2, CHUNK, units), BF16),
            pltpu.VMEM((2, CHUNK, units), BF16),
            pltpu.VMEM((tokens, features), BF16),
            pltpu.VMEM((n - 1, tokens, width), BF16),
            pltpu.VMEM((tokens, features), BF16),
        ]
        + stats_scratch()
        + [pltpu.VMEM((CHUNK, extent), F32), dma(2), dma(2), dma(2, 2)]
        + [dma(3), dma(chunks), dma(3, 2)]
        + scatter_sems
        + gather_sems
        + stats_sems,
        compiler_params=params(1, 62),
    )(
        *mixes, queries, keys, values, seg_column, seg_row, w_output, planes,
        grad_branch2, w_gate, w_up, w_down,
    )

    def over_dp(partial, dimension):
        return lax.psum_scatter(partial, "dp", scatter_dimension=dimension, tiled=True)

    height = features // replicas
    paired = replicas == PLANES * CORES

    def weight_sum(identity, left, right):
        if not paired:
            partial = contract_rows(left, right).astype(BF16)
            return over_dp(partial, 0), partial
        steps, columns_in = PLANES // 2, right.shape[1]
        pieces = max(columns_in // 1024, 1)
        partial = pl.pallas_call(
            pair_kernel,
            name="pair",
            cost_estimate=lasts(20),
            out_shape=array((features // CORES, columns_in), BF16),
            in_specs=[any_spec, any_spec],
            out_specs=any_spec,
            scratch_shapes=[
                pltpu.VMEM((PLANES, CORES, tokens, height), BF16),
                pltpu.VMEM((tokens, columns_in), BF16),
                pltpu.VMEM((2 * height, tokens), BF16),
                pltpu.VMEM((steps, 2 * height, columns_in), BF16),
                pltpu.VMEM((steps, 2 * height, columns_in), BF16),
                pltpu.VMEM((steps, 2 * height, columns_in), BF16),
                dma(PLANES, CORES),
                dma(pieces),
                dma(steps),
                dma(steps),
                dma(steps),
            ],
            compiler_params=params(identity, 56),
        )(left, right)
        groups = [[CORES * plane + c for plane in range(PLANES)] for c in range(CORES)]
        total = lax.psum_scatter(
            partial, "dp", scatter_dimension=0, tiled=True, axis_index_groups=groups
        )
        return total, partial

    grad_down, part_down = weight_sum(5, grad_branch2, hidden)
    part_gate_up = contract_rows(normed2, grad_acts).astype(BF16)
    grad_gate_up = over_dp(part_gate_up, 0)
    grad_w_down = pl.pallas_call(
        turn_kernel,
        name="turn",
        cost_estimate=lasts(2),
        out_shape=array((units, height), F32),
        in_specs=[vmem],
        out_specs=vmem,
        compiler_params=pltpu.CompilerParams(vmem_limit_bytes=32 * MIB),
    )(grad_down)
    grad_w_gate = grad_gate_up[:, :units].astype(F32)
    grad_w_up = grad_gate_up[:, units:].astype(F32)

    grad_entry2, grad_branch1 = pl.pallas_call(
        functools.partial(units_back_kernel, n),
        name="units_back",
        cost_estimate=lasts(400),
        out_shape=[array((tokens, width), F32), array((tokens, features), BF16)],
        in_specs=[smem] * 6 + [vmem] + [any_spec] * 8,
        out_specs=[vmem, any_spec],
        scratch_shapes=[
            pltpu.VMEM((tokens, 2 * units), BF16),
            pltpu.VMEM((features, units), BF16),
            pltpu.VMEM((features, units), BF16),
            pltpu.VMEM((tokens, features), BF16),
            pltpu.VMEM((tokens, width), F32),
            pltpu.VMEM((stream_count, tokens, width), BF16),
            pltpu.VMEM((CHUNK, features), F32),
            pltpu.VMEM((CHUNK, 128), F32),
            pltpu.VMEM((CHUNK, 128), F32),
            pltpu.VMEM((tokens, features), BF16),
            pltpu.VMEM((n - 1, tokens, width), BF16),
            pltpu.VMEM((chunks, 16, CHUNK), F32),
            pltpu.VMEM((n - 1, chunks, 16, CHUNK), F32),
            pltpu.VMEM((tokens, features), BF16),
            dma(chunks),
            dma(5),
            dma(chunks),
        ]
        + scatter_sems
        + stats_sems
        + gather_sems,
        compiler_params=params(2, 60),
    )(
        *mixes, scale2, grad_acts, w_gate, w_up, normed2, stand2, cot_planes,
        part_down, part_gate_up,
    )

    part_output = contract_rows(grad_branch1, attended).astype(BF16)

    grad_lin, branch2, grad_entry1 = pl.pallas_call(
        functools.partial(attend_back_kernel, n),
        name="attend_back",
        cost_estimate=lasts(2),
        out_shape=[array((tokens, 3 * width), BF16)] + [array((tokens, width), F32)] * 2,
        in_specs=[vmem] * 8 + [any_spec] * 11,
        out_specs=[vmem] * 3,
        scratch_shapes=[
            pltpu.VMEM((width, features), BF16),
            pltpu.VMEM((features, width), BF16),
            pltpu.VMEM((features, width), BF16),
            pltpu.VMEM((features, width), BF16),
            pltpu.VMEM((units, features), BF16),
            pltpu.VMEM((tokens, width), F32),
            pltpu.VMEM((2, CHUNK, features), BF16),
            pltpu.VMEM((2, CHUNK, units), BF16),
            pltpu.VMEM((2, CHUNK, features), BF16),
            pltpu.VMEM((CHUNK, extent), F32),
            pltpu.VMEM((width, tokens), F32),
            pltpu.VMEM((width, tokens), F32),
            pltpu.VMEM((CHUNK, features), F32),
            pltpu.VMEM((CHUNK, 128), F32),
            pltpu.VMEM((CHUNK, 128), F32),
            pltpu.VMEM((tokens, features), BF16),
            pltpu.VMEM((n - 1, tokens, width), BF16),
            pltpu.VMEM((tokens, features), BF16),
            pltpu.VMEM((n - 1, tokens, width), BF16),
            pltpu.VMEM((chunks, 16, CHUNK), F32),
            pltpu.VMEM((n - 1, chunks, 16, CHUNK), F32),
            dma(3, 2),
            dma(6),
        ]
        + scatter_sems
        + scatter_sems
        + stats_sems,
        compiler_params=params(3, 60),
    )(
        queries, keys, values, seg_column, seg_row, cos_table, sin_table, scale1,
        w_output, w_query, w_key, w_value, w_down, stand1,
        grad_branch1, hidden, normed1, part_output, grad_w_down,
    )

    part_lin = contract_rows(normed1, grad_lin).astype(BF16)

    rows = 128
    plane_spec = pl.BlockSpec((stream_count, rows, width), lambda t: (0, t, 0))
    field_spec = pl.BlockSpec((rows, width), lambda t: (t, 0))
    stream_spec = pl.BlockSpec((rows, stream_count, width), lambda t: (t, 0, 0))
    new_streams, stream_grad, sums = pl.pallas_call(
        streams_kernel,
        name="streams",
        cost_estimate=lasts(2),
        grid=(tokens // rows,),
        out_shape=[
            array(streams.shape, BF16),
            array(streams.shape, F32),
            array((SUMS, 8, 128), F32),
        ],
        in_specs=[smem] * 6 + [plane_spec, plane_spec] + [field_spec] * 4,
        out_specs=[
            stream_spec,
            stream_spec,
            pl.BlockSpec((SUMS, 8, 128), lambda t: (0, 0, 0)),
        ],
        scratch_shapes=[pltpu.VMEM((PRODUCTS, 8, 128), F32)],
        compiler_params=pltpu.CompilerParams(vmem_limit_bytes=48 * MIB),
    )(*mixes, planes, cot_planes, branch1, branch2, grad_entry1, grad_entry2)
    if paired:
        steps = PLANES - 1
        grad_w_query, grad_w_key, grad_w_value, grad_w_output, sums = pl.pallas_call(
            functools.partial(finish_kernel, n),
            name="finish",
            cost_estimate=lasts(2),
            out_shape=[array((height, width), F32)] * 3
            + [array((width, height), F32), array((SUMS, 128), F32)],
            in_specs=[any_spec, any_spec, vmem],
            out_specs=[vmem] * 5,
            scratch_shapes=[
                pltpu.VMEM((PLANES, 4, height, width), BF16),
                pltpu.VMEM((PLANES, 4, height, width), BF16),
                pltpu.VMEM((steps, 4, height, width), BF16),
                pltpu.VMEM((steps, 4, height, width), BF16),
                pltpu.VMEM((CORES, SUMS, 128), F32),
                pltpu.VMEM((PLANES, SUMS, 128), F32),
                pltpu.VMEM((n, SUMS, 128), F32),
                dma(PLANES, 4),
                dma(PLANES, 4),
                dma(PLANES, 4),
                dma(steps, 4),
                dma(steps, 4),
                dma(steps, 4),
                dma(steps, 4),
                dma(PLANES + n - 1),
                dma(PLANES + n - 1),
            ],
            compiler_params=params(4, 48),
        )(part_lin, part_output, sums)
        sums = jnp.sum(sums, axis=1)
    else:
        grad_w_query, grad_w_key, grad_w_value = (
            over_dp(part_lin[:, width * j : width * (j + 1)], 0).astype(F32) for j in range(3)
        )
        grad_w_output = jnp.transpose(over_dp(part_output, 0)).astype(F32)
        sums = lax.psum(jnp.sum(sums, axis=(1, 2)), ("dp", "tensor"))
    grad_mix_in1, grad_mix_res1 = sums[0:4], sums[4:20].reshape(4, 4)
    grad_mix_out1, grad_mix_in2 = sums[20:24], sums[24:28]
    grad_mix_res2, grad_mix_out2 = sums[28:44].reshape(4, 4), sums[44:48]
    return (
        new_streams,
        stream_grad,
        grad_w_query,
        grad_w_key,
        grad_w_value,
        grad_w_output,
        grad_w_gate,
        grad_w_up,
        grad_w_down,
        grad_mix_in1,
        grad_mix_res1,
        grad_mix_out1,
        grad_mix_in2,
        grad_mix_res2,
        grad_mix_out2,
    )


def solution(mesh):
    return jax.shard_map(
        functools.partial(on_device, mesh.shape["tensor"], mesh.shape["dp"]),
        mesh=mesh,
        in_specs=(
            P("dp", None, "tensor"),
            P("dp"),
            P("dp"),
            P(),
            P(),
            P(),
            P(),
            P(),
            P(),
            P(None, "tensor"),
            P(None, "tensor"),
            P(None, "tensor"),
            P("tensor", None),
            P(None, "tensor"),
            P(None, "tensor"),
            P("tensor", None),
            P("dp", None, "tensor"),
        ),
        out_specs=(
            P("dp", None, "tensor"),
            P("dp", None, "tensor"),
            P("dp", "tensor"),
            P("dp", "tensor"),
            P("dp", "tensor"),
            P("tensor", "dp"),
            P("dp", "tensor"),
            P("dp", "tensor"),
            P("tensor", "dp"),
            P(),
            P(),
            P(),
            P(),
            P(),
            P(),
        ),
        check_vma=False,
    )
```

```python
import functools
import math

import jax
import jax.numpy as jnp
from jax import lax
from jax.experimental import pallas as pl
from jax.experimental.pallas import tpu as pltpu
from jax.sharding import PartitionSpec as P

HEAD = 128
LENGTH = 1024
LONGEST = 512
EPS = 1e-05
PRECISE = lax.Precision.HIGHEST
MASKED = -1e30
MESH = pl.DeviceIdType.MESH
BF16 = jnp.bfloat16
F32 = jnp.float32
CHUNK = 256
ROWS = 32
MIB = 1 << 20


def inner(left, right):
    total = left[0] * right[0]
    for a, b in zip(left[1:], right[1:]):
        total += a * b
    return total


class Mixing:
    def __init__(self, refs):
        vectors = [[ref[i] for i in range(4)] for ref in refs[:4]]
        self.in1, self.out1, self.in2, self.out2 = vectors
        self.res1, self.res2 = (
            [[ref[i, j] for j in range(4)] for i in range(4)] for ref in refs[4:]
        )
        self.entry = [inner(row, self.in2) for row in self.res1]
        self.branch = [inner(self.out1, column) for column in zip(*self.res2)]
        self.across = inner(self.out1, self.in2)

    def mixed(self, k, j):
        return inner(self.res1[k], [row[j] for row in self.res2])


def contract_rows(left, right):
    return lax.dot_general(
        left, right, (((0,), (0,)), ((), ())), preferred_element_type=F32
    )


def dot_nn(left, right):
    return jnp.dot(left, right, preferred_element_type=F32)


def dot_nt(left, right):
    return lax.dot_general(
        left, right, (((1,), (1,)), ((), ())), preferred_element_type=F32
    )


def partners(n):
    me = lax.axis_index("tensor")
    if n == 4:
        both = (me + 1 - 2 * lax.rem(me, 2), lax.rem(me + 2, 4), 3 - me)
        return me, both, both
    to = tuple(lax.rem(me + k, n) for k in range(1, n))
    source = tuple(lax.rem(me + n - k, n) for k in range(1, n))
    return me, to, source


def enter(n, to):
    barrier = pltpu.get_barrier_semaphore()
    for target in to:
        pl.semaphore_signal(
            barrier, inc=1, device_id={"tensor": target}, device_id_type=MESH
        )
    pl.semaphore_wait(barrier, n - 1)


def remote(source, target, send_sem, recv_sem, device):
    return pltpu.make_async_remote_copy(
        src_ref=source,
        dst_ref=target,
        send_sem=send_sem,
        recv_sem=recv_sem,
        device_id={"tensor": device},
        device_id_type=MESH,
    )


def columns(index, width):
    return pl.ds(pl.multiple_of(index * width, 128), width)


def chunk_rows(c):
    return pl.ds(pl.multiple_of(c * CHUNK, CHUNK), CHUNK)


def half_rows(c, half):
    return pl.ds(pl.multiple_of(c * CHUNK + half * (CHUNK // 2), CHUNK // 2), CHUNK // 2)


class Gather:
    def __init__(self, n, buf, width, send_sem, recv_sem):
        self.n, self.buf, self.width = n, buf, width
        self.me, self.to, self.source = partners(n)
        self.send_sem, self.recv_sem = send_sem, recv_sem

    def own(self):
        return columns(self.me, self.width)

    def copy(self, rows, owner, k, c, target):
        view = self.buf.at[rows, columns(owner, self.width)]
        return remote(view, view, self.send_sem.at[k, c], self.recv_sem.at[k, c], target)

    def direct(self):
        return 2 if self.n == 4 else self.n - 1

    def handed(self, c):
        side, up, _ = self.to
        return (
            self.copy(half_rows(c, 0), side, 2, c, up),
            self.copy(half_rows(c, 1), up, 3, c, side),
        )

    def start(self, c):
        for k in range(self.direct()):
            self.copy(chunk_rows(c), self.me, k, c, self.to[k]).start()

    def relay(self, c):
        if self.n == 4:
            for k, copy in enumerate(self.handed(c)):
                self.copy(chunk_rows(c), self.source[k], k, c, self.to[k]).wait_recv()
                copy.start()

    def arrive(self, c):
        if self.n == 4:
            side, up, across = self.to
            self.copy(half_rows(c, 0), across, 2, c, up).wait_recv()
            self.copy(half_rows(c, 1), across, 3, c, side).wait_recv()
        else:
            for k in range(self.n - 1):
                self.copy(chunk_rows(c), self.source[k], k, c, self.to[k]).wait_recv()

    def finish(self, c):
        for k in range(self.direct()):
            self.copy(chunk_rows(c), self.me, k, c, self.to[k]).wait_send()
        if self.n == 4:
            for copy in self.handed(c):
                copy.wait_send()


class Scatter:
    def __init__(self, n, part, came, width, send_sem, recv_sem):
        self.n, self.part, self.came, self.width = n, part, came, width
        self.me, self.to, self.source = partners(n)
        self.send_sem, self.recv_sem = send_sem, recv_sem

    def copy(self, rows, owner, slot, k, c, target):
        return remote(
            self.part.at[rows, columns(owner, self.width)],
            self.came.at[slot, rows],
            self.send_sem.at[k, c],
            self.recv_sem.at[k, c],
            target,
        )

    def first(self, c):
        if self.n != 4:
            return tuple(
                (chunk_rows(c), self.to[k], k, k, c, self.to[k]) for k in range(self.n - 1)
            )
        side, up, across = self.to
        return (
            (half_rows(c, 0), across, 2, 0, c, side),
            (half_rows(c, 1), across, 2, 1, c, up),
            (half_rows(c, 0), side, 0, 2, c, side),
            (half_rows(c, 1), up, 1, 3, c, up),
        )

    def second(self, c):
        if self.n != 4:
            return ()
        side, up, _ = self.to
        return (
            (half_rows(c, 0), up, 1, 4, c, up),
            (half_rows(c, 1), side, 0, 5, c, side),
        )

    def start(self, c):
        for place in self.first(c):
            self.copy(*place).start()

    def relay(self, c):
        second = self.second(c)
        first = self.first(c)
        for half in range(len(second)):
            self.copy(*first[half]).wait_recv()
            owner = columns(self.to[1 - half], self.width)
            base = c * CHUNK + half * (CHUNK // 2)

            def add(r):
                rows = pl.ds(pl.multiple_of(base + r * ROWS, ROWS), ROWS)
                total = self.part[rows, owner].astype(F32) + self.came[2, rows].astype(F32)
                self.part[rows, owner] = total.astype(BF16)

            loop(CHUNK // 2 // ROWS, add)
            self.copy(*second[half]).start()

    def arrive(self, c):
        places = self.first(c)
        if self.n == 4:
            places = places[2:] + self.second(c)
        for place in places:
            self.copy(*place).wait_recv()

    def finish(self, c):
        for place in self.first(c) + self.second(c):
            self.copy(*place).wait_send()

    def total(self, rows):
        total = self.part[rows, columns(self.me, self.width)].astype(F32)
        for k in range(2 if self.n == 4 else self.n - 1):
            total += self.came[k, rows].astype(F32)
        return total


class Stats:
    def __init__(self, n, mine, came, send_sem, recv_sem):
        self.n, self.mine, self.came = n, mine, came
        self.me, self.to, self.source = partners(n)
        self.send_sem, self.recv_sem = send_sem, recv_sem

    def copy(self, c, k):
        return remote(
            self.mine.at[c], self.came.at[k, c], self.send_sem.at[k, c], self.recv_sem.at[k, c], self.to[k]
        )

    def start(self, c):
        for k in range(self.n - 1):
            self.copy(c, k).start()

    def arrive(self, c):
        for k in range(self.n - 1):
            self.copy(c, k).wait_recv()

    def finish(self, c):
        for k in range(self.n - 1):
            self.copy(c, k).wait_send()

    def put(self, c, first, second):
        ones = jnp.ones((8, 128), F32)
        for place, field in ((0, first), (8, second)):
            self.mine[c, place : place + 8] = lax.dot_general(
                ones, field, (((1,), (1,)), ((), ())), precision=PRECISE, preferred_element_type=F32
            )

    def moments(self, c, width):
        pieces = [self.mine[c]] + [self.came[k, c] for k in range(self.n - 1)]
        count = float(self.n * width)
        mean = sum(piece[0:8] for piece in pieces) * (1.0 / count)
        squares = sum(
            piece[8:16] + width * (piece[0:8] * (1.0 / width) - mean) ** 2 for piece in pieces
        )
        share = jnp.full((8, 128), 0.125, F32)
        return tuple(
            lax.dot_general(
                row, share, (((0,), (0,)), ((), ())), precision=PRECISE, preferred_element_type=F32
            )
            for row in (mean, lax.rsqrt(squares * (1.0 / count) + EPS))
        )

    def means(self, c, features):
        total = self.mine[c]
        for k in range(self.n - 1):
            total += self.came[k, c]
        share = jnp.full((8, 128), 1.0 / (8 * features), F32)
        return tuple(
            lax.dot_general(
                total[place : place + 8],
                share,
                (((0,), (0,)), ((), ())),
                precision=PRECISE,
                preferred_element_type=F32,
            )
            for place in (0, 8)
        )


def loop(count, body):
    def step(i, carry):
        body(i)
        return carry

    lax.fori_loop(0, count, step, 0)


def sub_rows(c, r):
    return pl.ds(pl.multiple_of(c * CHUNK + r * ROWS, ROWS), ROWS)


def repeat_lanes(field, width):
    return jnp.concatenate([field] * (width // 128), axis=1)


def fold_lanes(field):
    total = field[:, 0:128]
    for j in range(1, field.shape[1] // 128):
        total += field[:, 128 * j : 128 * (j + 1)]
    return total


def local_rows(r):
    return pl.ds(pl.multiple_of(r * ROWS, ROWS), ROWS)


def fold_entry(entry, first, second, rows):
    first[rows, :] = fold_lanes(entry)
    centered = entry - jnp.sum(entry, axis=1, keepdims=True) * (1.0 / entry.shape[1])
    second[rows, :] = fold_lanes(centered * centered)


def standardize(c, stats, gather, first, second, stand_ref, scale_ref):
    width = stand_ref.shape[1]
    stats.arrive(c)
    first[...], second[...] = stats.moments(c, width)

    def piece(r):
        rows, local = sub_rows(c, r), local_rows(r)
        scaling = second[local, :]
        stand = (stand_ref[rows, :] - repeat_lanes(first[local, :], width)) * repeat_lanes(
            scaling, width
        )
        stand_ref[rows, :] = stand
        scale_ref[rows, :] = scaling
        gather.buf[rows, gather.own()] = stand.astype(BF16)

    loop(CHUNK // ROWS, piece)
    gather.start(c)


def rotate(field, cos_rows, sin_rows, sign):
    turned = pltpu.roll(field, HEAD // 2, 1)
    return field * cos_rows + (sign * turned) * sin_rows


def spread(row):
    share = jnp.full((8, 128), 0.125, F32)
    return lax.dot_general(
        jnp.broadcast_to(row, (8, 128)),
        share,
        (((0,), (0,)), ((), ())),
        precision=PRECISE,
        preferred_element_type=F32,
    )


def project_kernel(
    n, in1, out2, positions_ref, segments_ref, s_hbm, c_hbm, wq_hbm, wk_hbm, wv_hbm,
    normed_hbm, q_ref, k_ref, v_ref, stand_ref, scale_ref, gb2_hbm, cot_hbm,
    cos_ref, sin_ref, segc_ref, segr_ref,
    s_buf, c_buf, cot_planes, w_buf, all1, all2, first, second, mine, others,
    in_sem, w_sem, out_sem, send1, recv1, send2, recv2, send3, recv3,
):
    streams, tokens, width = s_buf.shape
    count = tokens // CHUNK
    heads = width // HEAD
    weights = (wq_hbm, wk_hbm, wv_hbm)

    def s_in(c):
        return pltpu.make_async_copy(
            s_hbm.at[:, chunk_rows(c)], s_buf.at[:, chunk_rows(c)], in_sem.at[0, c]
        )

    def c_in(c):
        return pltpu.make_async_copy(
            c_hbm.at[chunk_rows(c)], c_buf.at[chunk_rows(c)], in_sem.at[1, c]
        )

    def w_in(j):
        return pltpu.make_async_copy(weights[j], w_buf.at[j], w_sem.at[j])

    def out(c, i):
        rows = chunk_rows(c)
        source, target = (
            (all1.at[rows], normed_hbm.at[rows]),
            (all2.at[rows], gb2_hbm.at[rows]),
            (cot_planes.at[:, rows], cot_hbm.at[:, rows]),
        )[i]
        return pltpu.make_async_copy(source, target, out_sem.at[i, c])

    loop(count, lambda c: s_in(c).start())
    loop(count, lambda c: c_in(c).start())
    for j in range(3):
        w_in(j).start()
    gather = Gather(n, all1, width, send1, recv1)
    incoming = Gather(n, all2, width, send2, recv2)
    stats = Stats(n, mine, others, send3, recv3)
    enter(n, gather.to)

    def entry(c):
        s_in(c).wait()

        def piece(r):
            rows = sub_rows(c, r)
            field = in1[0] * s_buf[0, rows].astype(F32)
            for i in range(1, streams):
                field += in1[i] * s_buf[i, rows].astype(F32)
            stand_ref[sub_rows(c, r), :] = field
            fold_entry(field, first, second, local_rows(r))

        loop(CHUNK // ROWS, piece)
        stats.put(c, first[...], second[...])
        stats.start(c)

    def send(c):
        standardize(c, stats, gather, first, second, stand_ref, scale_ref)

    def grad(c):
        c_in(c).wait()

        def piece(r):
            rows = sub_rows(c, r)
            block = c_buf[rows].astype(F32)
            total = None
            for i in range(streams):
                field = block[:, i, :]
                cot_planes[i, rows] = field.astype(BF16)
                total = out2[i] * field if total is None else total + out2[i] * field
            all2[rows, incoming.own()] = total.astype(BF16)

        loop(CHUNK // ROWS, piece)
        incoming.start(c)
        out(c, 2).start()

    entry(0)

    def ahead(c):
        entry(c + 1)
        send(c)

    loop(count - 1, ahead)
    send(count - 1)
    grad(0)
    gather.relay(0)
    grad(1)
    gather.relay(1)
    incoming.relay(0)

    segr_ref[...] = jnp.concatenate(
        [
            jnp.broadcast_to(segments_ref[a : a + 1, :].astype(F32), (8, 128))
            for a in range(tokens // 128)
        ],
        axis=1,
    )
    lane = lax.broadcasted_iota(jnp.int32, (128, 128), 1)
    exponent = lax.rem(lane, HEAD // 2).astype(F32) * (-2.0 / HEAD * math.log(10000.0))
    inverse = jnp.exp(exponent)
    for a in range(tokens // 128):
        rows = slice(128 * a, 128 * (a + 1))
        segc_ref[rows, :] = spread(segments_ref[a : a + 1, :].astype(F32))
        angles = spread(positions_ref[a : a + 1, :].astype(F32)) * inverse
        cos_ref[rows, :] = jnp.cos(angles)
        sine = jnp.sin(angles)
        sin_ref[rows, :] = jnp.where(lane < HEAD // 2, -sine, sine)
    grad(2)
    gather.relay(2)
    grad(3)
    gather.relay(3)
    incoming.relay(1)
    for j in range(3):
        w_in(j).wait()

    def work(c):
        gather.arrive(c)
        out(c, 0).start()
        rows = chunk_rows(c)
        block = all1[rows, :]
        cos_rows, sin_rows = cos_ref[rows, :], sin_ref[rows, :]
        for j, target in ((0, q_ref), (1, k_ref)):
            lin = dot_nn(block, w_buf[j])
            for h in range(heads):
                place = slice(HEAD * h, HEAD * (h + 1))
                target[rows, place] = rotate(lin[:, place], cos_rows, sin_rows, 1.0).astype(BF16)
        v_ref[rows, :] = dot_nn(block, w_buf[2]).astype(BF16)

        @pl.when(c + 2 < count)
        def _():
            incoming.relay(c + 2)

    loop(count, work)

    def end(c):
        incoming.arrive(c)
        out(c, 1).start()

    loop(count, end)

    def drain(c):
        for i in range(3):
            out(c, i).wait()
        stats.finish(c)
        gather.finish(c)
        incoming.finish(c)

    loop(count, drain)


def window_bias(c, start, extent, segc_ref, segr_ref, bias):
    def part(r):
        rows = pl.ds(pl.multiple_of(r * ROWS, ROWS), ROWS)
        row = c * CHUNK + r * ROWS + lax.broadcasted_iota(jnp.int32, (ROWS, extent), 0)
        column = start + lax.broadcasted_iota(jnp.int32, (ROWS, extent), 1)
        same = segc_ref[sub_rows(c, r), 0:1] == segr_ref[0:1, pl.ds(start, extent)]
        bias[rows, :] = jnp.where((row >= column) & same, 0.0, MASKED)

    loop(CHUNK // ROWS, part)


def window(c, tokens):
    extent = min(tokens, CHUNK * (-(-(LONGEST - 1) // CHUNK) + 1))
    back = extent // CHUNK - 1
    return pl.multiple_of(jnp.maximum(c - back, 0) * CHUNK, CHUNK), extent


def attend_kernel(
    n, in1, out1, in2, out2, res1, res2, q_ref, k_ref, v_ref, segc_ref, segr_ref, wo_ref,
    s_hbm, gb2_hbm, wg_hbm, wu_hbm, wd_hbm,
    attended_ref, branch_ref, normed_hbm, stand_ref, scale_ref, hidden_hbm, acts_hbm, grads_hbm,
    s_buf, gb2_buf, wg_buf, wu_buf, wd_buf, hidden_buf, gate_buf, up_buf,
    part, came, all2, first, second, mine, others, bias,
    s_sem, gb2_sem, grad_sem, w_sem, normed_sem, out_sem, send1, recv1, send2, recv2, send3, recv3,
):
    tokens, width = q_ref.shape
    units = wg_buf.shape[1]
    count = tokens // CHUNK
    heads = width // HEAD
    block = min(units, 512)
    mixing = Mixing((in1, out1, in2, out2, res1, res2))

    def s_in(c):
        slot = lax.rem(c, 2)
        return pltpu.make_async_copy(s_hbm.at[:, chunk_rows(c)], s_buf.at[slot], s_sem.at[slot])

    def gb2_in(c):
        slot = lax.rem(c, 2)
        return pltpu.make_async_copy(gb2_hbm.at[chunk_rows(c)], gb2_buf.at[slot], gb2_sem.at[slot])

    def grads_out(c):
        slot = lax.rem(c, 2)
        return pltpu.make_async_copy(
            gate_buf.at[slot], grads_hbm.at[chunk_rows(c)], grad_sem.at[0, slot]
        )

    def grads_in(c):
        slot = lax.rem(c, 2)
        return pltpu.make_async_copy(
            grads_hbm.at[chunk_rows(c)], gb2_buf.at[slot, :, 0:units], grad_sem.at[1, slot]
        )

    def normed_out(c):
        return pltpu.make_async_copy(
            all2.at[chunk_rows(c)], normed_hbm.at[chunk_rows(c)], normed_sem.at[c]
        )

    def outs(c):
        slot, rows = lax.rem(c, 2), chunk_rows(c)
        return tuple(
            pltpu.make_async_copy(buf.at[slot], target, out_sem.at[i, slot])
            for i, (buf, target) in enumerate(
                (
                    (hidden_buf, hidden_hbm.at[rows]),
                    (gate_buf, acts_hbm.at[rows, 0:units]),
                    (up_buf, acts_hbm.at[rows, units : 2 * units]),
                )
            )
        )

    weights = tuple(
        pltpu.make_async_copy(source, target, w_sem.at[i])
        for i, (source, target) in enumerate(
            ((wd_hbm, wd_buf), (wg_hbm, wg_buf), (wu_hbm, wu_buf))
        )
    )
    s_in(0).start()
    gb2_in(0).start()
    gb2_in(1).start()
    for copy in weights:
        copy.start()
    scatter = Scatter(n, part, came, width, send1, recv1)
    gather = Gather(n, all2, width, send2, recv2)
    stats = Stats(n, mine, others, send3, recv3)
    enter(n, gather.to)

    def attend(c):
        rows = chunk_rows(c)
        start, extent = window(c, tokens)
        window_bias(c, start, extent, segc_ref, segr_ref, bias)
        for h in range(heads):
            place = slice(HEAD * h, HEAD * (h + 1))
            scores = dot_nt(q_ref[rows, place], k_ref[pl.ds(start, extent), place])
            scores = scores * HEAD ** (-0.5) + bias[...]
            raised = jnp.exp(scores - jnp.max(scores, axis=1, keepdims=True))
            inverse = 1.0 / jnp.sum(raised, axis=1, keepdims=True)
            probs = (raised * inverse).astype(BF16)
            attended_ref[rows, place] = dot_nn(probs, v_ref[pl.ds(start, extent), place]).astype(BF16)
        part[rows, :] = dot_nn(attended_ref[rows, :], wo_ref[...]).astype(BF16)

    def middle(c):
        @pl.when(c + 1 < count)
        def _():
            s_in(c + 1).start()

        s_in(c).wait()
        slot = lax.rem(c, 2)
        scatter.arrive(c)

        def piece(r):
            rows = sub_rows(c, r)
            branch = scatter.total(rows)
            branch_ref[rows, :] = branch
            entry = mixing.across * branch
            for i in range(s_buf.shape[1]):
                entry += mixing.entry[i] * s_buf[slot, i, local_rows(r)].astype(F32)
            stand_ref[rows, :] = entry
            fold_entry(entry, first, second, local_rows(r))

        loop(CHUNK // ROWS, piece)
        stats.put(c, first[...], second[...])
        stats.start(c)

    def send(c):
        standardize(c, stats, gather, first, second, stand_ref, scale_ref)

    def work(c):
        gather.arrive(c)
        normed_out(c).start()
        slot = lax.rem(c, 2)

        @pl.when(c >= 2)
        def _():
            for copy in outs(c - 2):
                copy.wait()

        grads_in(c).wait()

        def piece(f):
            place = columns(f, block)
            gate = dot_nn(all2[chunk_rows(c), :], wg_buf[:, place])
            up = dot_nn(all2[chunk_rows(c), :], wu_buf[:, place])
            grad = gb2_buf[slot, :, place].astype(F32)
            sig = jax.nn.sigmoid(gate)
            act = gate * sig
            hidden_buf[slot, :, place] = (act * up).astype(BF16)
            gate_buf[slot, :, place] = (grad * up * sig * (1.0 + gate * (1.0 - sig))).astype(BF16)
            up_buf[slot, :, place] = (grad * act).astype(BF16)

        loop(units // block, piece)
        for copy in outs(c):
            copy.start()

        @pl.when(c + 2 < count)
        def _():
            grads_in(c + 2).start()
            gather.relay(c + 2)

    def grads(c):
        slot = lax.rem(c, 2)
        if c >= 2:
            grads_out(c - 2).wait()
        gb2_in(c).wait()

        def piece(f):
            place = columns(f, block)
            gate_buf[slot, :, place] = dot_nt(gb2_buf[slot], wd_buf[place, :]).astype(BF16)

        loop(units // block, piece)
        grads_out(c).start()
        if c + 2 < count:
            gb2_in(c + 2).start()

    def attend_send(c):
        attend(c)
        scatter.start(c)

        @pl.when(c >= 1)
        def _():
            scatter.relay(c - 1)

    loop(count, attend_send)
    middle(0)
    weights[0].wait()
    grads(0)
    scatter.relay(3)
    middle(1)
    send(0)
    grads(1)
    middle(2)
    send(1)
    grads(2)
    middle(3)
    grads(3)
    gather.relay(0)
    send(2)
    gather.relay(1)
    send(3)
    grads_out(2).wait()
    grads_out(3).wait()
    grads_in(0).start()
    grads_in(1).start()
    weights[1].wait()
    weights[2].wait()
    loop(count, work)
    for c in range(max(count - 2, 0), count):
        for copy in outs(c):
            copy.wait()

    def drain(c):
        normed_out(c).wait()
        scatter.finish(c)
        stats.finish(c)
        gather.finish(c)

    loop(count, drain)


def stats_part(part32, normed, normed_rows, part, c, first, second):
    def piece(r):
        rows = pl.ds(pl.multiple_of(r * ROWS, ROWS), ROWS)
        field = part32[rows, :]
        first[rows, :] = fold_lanes(field)
        second[rows, :] = fold_lanes(field * normed[normed_rows(r), :].astype(F32))
        part[sub_rows(c, r), :] = field.astype(BF16)

    loop(CHUNK // ROWS, piece)


def units_back_kernel(
    n, in1, out1, in2, out2, res1, res2, scale_ref, acts_hbm, wg_hbm, wu_hbm, normed_hbm, stand_hbm, c_hbm, _down, _gate_up,
    entry_ref, gb1_hbm,
    acts_ref, wg_ref, wu_ref, normed_ref, stand_ref, c_buf, part32, first, second, part, came, mine, others, all1, acts_sem, in_sem, out_sem,
    send1, recv1, send2, recv2, send3, recv3,
):
    tokens, features = normed_ref.shape
    width = entry_ref.shape[1]
    count = tokens // CHUNK
    mixing = Mixing((in1, out1, in2, out2, res1, res2))

    def acts_in(c):
        return pltpu.make_async_copy(
            acts_hbm.at[chunk_rows(c)], acts_ref.at[chunk_rows(c)], acts_sem.at[c]
        )

    wg_in, wu_in, normed_in, stand_in, c_in = (
        pltpu.make_async_copy(source, target, in_sem.at[i])
        for i, (source, target) in enumerate(
            (
                (wg_hbm, wg_ref),
                (wu_hbm, wu_ref),
                (normed_hbm, normed_ref),
                (stand_hbm, stand_ref),
                (c_hbm, c_buf),
            )
        )
    )
    acts_in(0).start()
    wg_in.start()
    wu_in.start()
    normed_in.start()
    loop(count - 1, lambda c: acts_in(c + 1).start())
    stand_in.start()
    c_in.start()
    scatter = Scatter(n, part, came, width, send1, recv1)
    stats = Stats(n, mine, others, send2, recv2)
    gather = Gather(n, all1, width, send3, recv3)
    enter(n, gather.to)

    def work(c):
        rows = chunk_rows(c)
        units = wg_ref.shape[1]
        acts_in(c).wait()

        @pl.when(c == 0)
        def _():
            wg_in.wait()

        part32[...] = dot_nt(acts_ref[rows, 0:units], wg_ref[...])

        @pl.when(c == 0)
        def _():
            wu_in.wait()
            normed_in.wait()

        part32[...] += dot_nt(acts_ref[rows, units : 2 * units], wu_ref[...])
        stats_part(part32, normed_ref, lambda r: sub_rows(c, r), part, c, first, second)
        stats.put(c, first[...], second[...])
        stats.start(c)
        scatter.start(c)

        @pl.when(c >= 1)
        def _():
            scatter.relay(c - 1)

    def middle(c):
        scatter.arrive(c)
        stats.arrive(c)
        first[...], second[...] = stats.means(c, features)

        def piece(r):
            rows = sub_rows(c, r)
            local = pl.ds(pl.multiple_of(r * ROWS, ROWS), ROWS)
            standard = stand_ref[rows, :]
            entry = repeat_lanes(scale_ref[rows, :], width) * (
                scatter.total(rows)
                - repeat_lanes(first[local, :], width)
                - standard * repeat_lanes(second[local, :], width)
            )
            entry_ref[rows, :] = entry
            grad = mixing.across * entry
            for i in range(c_buf.shape[0]):
                grad += mixing.branch[i] * c_buf[i, rows].astype(F32)
            all1[rows, gather.own()] = grad.astype(BF16)

        loop(CHUNK // ROWS, piece)
        gather.start(c)

    def ahead(c):
        work(c)

        @pl.when(c == 1)
        def _():
            stand_in.wait()
            c_in.wait()

        @pl.when(c >= 2)
        def _():
            middle(c - 2)

    loop(count, ahead)
    scatter.relay(count - 1)
    middle(count - 2)
    gather.relay(0)
    middle(count - 1)
    for c in range(1, count):
        gather.relay(c)

    def gb1_out(c):
        return pltpu.make_async_copy(
            all1.at[chunk_rows(c)], gb1_hbm.at[chunk_rows(c)], out_sem.at[c]
        )

    def last(c):
        gather.arrive(c)
        gb1_out(c).start()

    loop(count, last)

    def drain(c):
        gb1_out(c).wait()
        scatter.finish(c)
        stats.finish(c)
        gather.finish(c)

    loop(count, drain)


def attend_back_kernel(
    n, q_ref, k_ref, v_ref, segc_ref, segr_ref, cos_ref, sin_ref, scale_ref,
    wo_hbm, wq_hbm, wk_hbm, wv_hbm, wd_hbm, stand_hbm, gb1_hbm, hidden_hbm, normed_hbm, _output, _down,
    lin_ref, branch_ref, entry_ref,
    wo_ref, wq_ref, wk_ref, wv_ref, wd_ref, stand_ref, gb1_buf, hidden_buf, normed_buf, bias, dk_t, dv_t, part32, first, second,
    part1, came1, part2, came2, mine, others, in_sem, w_sem,
    send1, recv1, send2, recv2, send3, recv3,
):
    tokens, width = q_ref.shape
    features = part1.shape[1]
    count = tokens // CHUNK
    heads = width // HEAD
    factor = HEAD ** (-0.5)
    down = Scatter(n, part2, came2, width, send1, recv1)
    scatter = Scatter(n, part1, came1, width, send2, recv2)
    stats = Stats(n, mine, others, send3, recv3)

    def inputs(c, slot):
        return tuple(
            pltpu.make_async_copy(source.at[chunk_rows(c)], target.at[slot], in_sem.at[i, slot])
            for i, (source, target) in enumerate(
                ((gb1_hbm, gb1_buf), (hidden_hbm, hidden_buf), (normed_hbm, normed_buf))
            )
        )

    wd_in, wo_in, wq_in, wk_in, wv_in, stand_in = (
        pltpu.make_async_copy(source, target, w_sem.at[i])
        for i, (source, target) in enumerate(
            (
                (wd_hbm, wd_ref),
                (wo_hbm, wo_ref),
                (wq_hbm, wq_ref),
                (wk_hbm, wk_ref),
                (wv_hbm, wv_ref),
                (stand_hbm, stand_ref),
            )
        )
    )
    for copy in inputs(count - 1, 0):
        copy.start()
    for copy in (wd_in, wo_in, wq_in, wk_in, wv_in, stand_in):
        copy.start()
    dk_t[...] = jnp.zeros_like(dk_t)
    dv_t[...] = jnp.zeros_like(dv_t)
    enter(n, scatter.to)

    def work(i):
        c = count - 1 - i
        slot = lax.rem(i, 2)

        @pl.when(i < count - 1)
        def _():
            for copy in inputs(c - 1, 1 - slot):
                copy.start()

        for copy in inputs(c, slot):
            copy.wait()
        rows = chunk_rows(c)

        @pl.when(i == 0)
        def _():
            wd_in.wait()

        part2[rows, :] = dot_nn(hidden_buf[slot], wd_ref[...]).astype(BF16)
        down.start(c)

        @pl.when(i == 0)
        def _():
            for copy in (wo_in, wq_in, wk_in, wv_in):
                copy.wait()

        grad = dot_nt(gb1_buf[slot], wo_ref[...]).astype(BF16)
        start, extent = window(c, tokens)
        keys = pl.ds(start, extent)
        window_bias(c, start, extent, segc_ref, segr_ref, bias)
        cos_rows, sin_rows = cos_ref[rows, :], sin_ref[rows, :]
        for h in range(heads):
            place = slice(HEAD * h, HEAD * (h + 1))
            query, grad_h = q_ref[rows, place], grad[:, place]
            scores = dot_nt(query, k_ref[keys, place]) * factor + bias[...]
            raised = jnp.exp(scores - jnp.max(scores, axis=1, keepdims=True))
            inverse = 1.0 / jnp.sum(raised, axis=1, keepdims=True)
            probs = raised * inverse
            grad_probs = dot_nt(grad_h, v_ref[keys, place])
            centre = jnp.sum(probs * grad_probs, axis=1, keepdims=True)
            grad_scores = (probs * (grad_probs - centre)).astype(BF16)
            dv_t[place, keys] += dot_nn(jnp.transpose(grad_h), probs.astype(BF16))
            dk_t[place, keys] += dot_nn(jnp.transpose(query), grad_scores)
            dq = dot_nn(grad_scores, k_ref[keys, place]) * factor
            lin_ref[rows, place] = rotate(dq, cos_rows, sin_rows, -1.0).astype(BF16)
            dk = jnp.transpose(dk_t[place, rows]) * factor
            lin_ref[rows, slice(width + HEAD * h, width + HEAD * (h + 1))] = rotate(dk, cos_rows, sin_rows, -1.0).astype(BF16)
            lin_ref[rows, slice(2 * width + HEAD * h, 2 * width + HEAD * (h + 1))] = jnp.transpose(dv_t[place, rows]).astype(BF16)
        part32[...] = dot_nt(lin_ref[rows, 0:width], wq_ref[...])
        part32[...] += dot_nt(lin_ref[rows, width : 2 * width], wk_ref[...])
        part32[...] += dot_nt(lin_ref[rows, 2 * width : 3 * width], wv_ref[...])
        stats_part(
            part32,
            normed_buf.at[slot],
            lambda r: pl.ds(pl.multiple_of(r * ROWS, ROWS), ROWS),
            part1,
            c,
            first,
            second,
        )
        stats.put(c, first[...], second[...])
        stats.start(c)
        scatter.start(c)
        down.relay(c)

        @pl.when(i >= 1)
        def _():
            scatter.relay(c + 1)

    loop(count, work)
    scatter.relay(0)
    stand_in.wait()

    def last(i):
        c = count - 1 - i
        down.arrive(c)

        def sums(r):
            branch_ref[sub_rows(c, r), :] = down.total(sub_rows(c, r))

        loop(CHUNK // ROWS, sums)
        scatter.arrive(c)
        stats.arrive(c)
        first[...], second[...] = stats.means(c, features)

        def piece(r):
            rows = sub_rows(c, r)
            local = pl.ds(pl.multiple_of(r * ROWS, ROWS), ROWS)
            entry_ref[rows, :] = repeat_lanes(scale_ref[rows, :], width) * (
                scatter.total(rows)
                - repeat_lanes(first[local, :], width)
                - stand_ref[rows, :] * repeat_lanes(second[local, :], width)
            )

        loop(CHUNK // ROWS, piece)

    loop(count, last)

    def drain(c):
        down.finish(c)
        scatter.finish(c)
        stats.finish(c)

    loop(count, drain)


def turn_kernel(source_ref, target_ref):
    target_ref[...] = jnp.transpose(source_ref[...].astype(F32))


def streams_kernel(
    in1, out1, in2, out2, res1, res2, s_ref, c_ref, b1_ref, b2_ref, e1_ref, e2_ref,
    new_ref, grad_ref, mix_ref, sums_ref,
):
    @pl.when(pl.program_id(0) == 0)
    def _():
        sums_ref[...] = jnp.zeros_like(sums_ref)

    count = s_ref.shape[0]
    mixing = Mixing((in1, out1, in2, out2, res1, res2))
    mixed = [[mixing.mixed(k, j) for j in range(count)] for k in range(count)]

    def fold(field):
        field = fold_lanes(field)
        total = field[0:8]
        for j in range(1, field.shape[0] // 8):
            total += field[8 * j : 8 * (j + 1)]
        return total

    def piece(r):
        rows = local_rows(r)
        s = [s_ref[i, rows].astype(F32) for i in range(count)]
        c = [c_ref[i, rows].astype(F32) for i in range(count)]
        b1, b2, e1, e2 = b1_ref[rows, :], b2_ref[rows, :], e1_ref[rows, :], e2_ref[rows, :]
        for j in range(count):
            new = mixing.branch[j] * b1 + mixing.out2[j] * b2
            grad = mixing.entry[j] * e2 + mixing.in1[j] * e1
            for k in range(count):
                new += mixed[k][j] * s[k]
                grad += mixed[j][k] * c[k]
            new_ref[rows, j, :] = new.astype(BF16)
            grad_ref[rows, j, :] = grad
        pairs = [(s[i], c[j]) for i in range(count) for j in range(count)]
        pairs += [(s[i], e1) for i in range(count)] + [(s[i], e2) for i in range(count)]
        pairs += [(c[i], b1) for i in range(count)] + [(c[i], b2) for i in range(count)]
        pairs += [(b1, e2)]
        for place, (left, right) in enumerate(pairs):
            sums_ref[place] += fold(left * right)

    loop(s_ref.shape[1] // ROWS, piece)

    @pl.when(pl.program_id(0) == pl.num_programs(0) - 1)
    def _():
        sums = [sums_ref[place] for place in range(PRODUCTS)]
        s_c = [sums[count * i : count * (i + 1)] for i in range(count)]
        s_e1, s_e2, c_b1, c_b2 = (sums[16 + 4 * k : 20 + 4 * k] for k in range(4))
        b_e = sums[32]
        every = range(count)
        row1, row2 = mixing.res1, mixing.res2
        grads = [s_e1[i] for i in every]
        grads += [inner(row2[j], s_c[i]) + mixing.in2[j] * s_e2[i] for i in every for j in every]
        grads += [inner(row2[j], c_b1) + mixing.in2[j] * b_e for j in every]
        turned1 = [[row1[k][i] for k in every] for i in every]
        grads += [inner(turned1[i], s_e2) + mixing.out1[i] * b_e for i in every]
        grads += [
            inner(turned1[i], [s_c[k][j] for k in every]) + mixing.out1[i] * c_b1[j]
            for i in every
            for j in every
        ]
        grads += [c_b2[j] for j in every]
        for place, field in enumerate(grads):
            mix_ref[place] = field


PLANES = 4
CORES = 2
PRODUCTS = 33
SUMS = 48


def pair_kernel(
    left_hbm, right_hbm, out_hbm, left, right, turned, sent, came, mine_buf,
    left_sem, right_sem, out_sem, send_sem, recv_sem,
):
    steps, height, width = came.shape
    block = height // 2
    piece = right_sem.shape[0]
    across = width // piece
    me = lax.axis_index("dp")
    mine = lax.rem(me, CORES)
    partner = me + 1 - 2 * mine

    def left_in(step, half, part):
        index = (2 * step + part) * CORES + half
        return pltpu.make_async_copy(
            left_hbm.at[:, columns(index, block)],
            left.at[2 * step + part, half],
            left_sem.at[2 * step + part, half],
        )

    def right_in(f):
        return pltpu.make_async_copy(
            right_hbm.at[:, columns(f, across)], right.at[:, columns(f, across)], right_sem.at[f]
        )

    def swap(step):
        return pltpu.make_async_remote_copy(
            src_ref=sent.at[step],
            dst_ref=came.at[step],
            send_sem=send_sem.at[step],
            recv_sem=recv_sem.at[step],
            device_id={"dp": partner},
            device_id_type=MESH,
        )

    def out(step):
        rows = pl.ds(pl.multiple_of(step * height, height), height)
        return pltpu.make_async_copy(mine_buf.at[step], out_hbm.at[rows], out_sem.at[step])

    for part in range(2):
        left_in(0, 1 - mine, part).start()
    for f in range(piece):
        right_in(f).start()
    for half in (1 - mine, mine):
        for step in range(steps):
            for part in range(2):
                if half is mine or step > 0:
                    left_in(step, half, part).start()
    barrier = pltpu.get_barrier_semaphore()
    pl.semaphore_signal(barrier, inc=1, device_id={"dp": partner}, device_id_type=MESH)
    pl.semaphore_wait(barrier, 1)

    def turn(step, half):
        for part in range(2):
            left_in(step, half, part).wait()
            turned[part * block : (part + 1) * block, :] = jnp.transpose(left[2 * step + part, half])

    def other(step):
        turn(step, 1 - mine)

        def part(f):
            @pl.when(step == 0)
            def _():
                right_in(f).wait()

            place = columns(f, across)
            sent[step, :, place] = dot_nn(turned[...], right[:, place]).astype(BF16)

        loop(piece, part)
        swap(step).start()

    loop(steps, other)

    def own(step):
        turn(step, mine)
        swap(step).wait_recv()

        def part(f):
            place = columns(f, across)
            total = dot_nn(turned[...], right[:, place]) + came[step, :, place].astype(F32)
            mine_buf[step, :, place] = total.astype(BF16)

        loop(piece, part)
        out(step).start()

    loop(steps, own)

    def drain(step):
        swap(step).wait_send()
        out(step).wait()

    loop(steps, drain)


def finish_kernel(
    n, first_hbm, last_hbm, sums_ref,
    q_out, k_out, v_out, o_out, sums_out,
    own, core, right, left, by_core, by_plane, by_tensor,
    own_sem, core_send, core_recv, right_send, right_recv, left_send, left_recv, sum_send, sum_recv,
):
    _, pieces, height, width = own.shape
    me = lax.axis_index("dp")
    plane, mine = lax.div(me, CORES), lax.rem(me, CORES)
    partner = me + 1 - 2 * mine
    here, peers, peer_source = partners(n)
    planes_to = [lax.rem(plane + k, PLANES) for k in range(1, PLANES)]
    planes_from = [lax.rem(plane + PLANES - k, PLANES) for k in range(1, PLANES)]

    def dp_at(position):
        return position * CORES + mine

    def rows_of(position, half):
        return pl.ds(pl.multiple_of((position * CORES + half) * height, height), height)

    def block(position, half, p):
        if p < pieces - 1:
            return first_hbm.at[rows_of(position, half), p * width : (p + 1) * width]
        return last_hbm.at[rows_of(position, half)]

    def over_dp(source, target, send_sem, recv_sem, device):
        return pltpu.make_async_remote_copy(
            src_ref=source, dst_ref=target, send_sem=send_sem, recv_sem=recv_sem,
            device_id={"dp": device}, device_id_type=MESH,
        )

    def own_in(position, p):
        return pltpu.make_async_copy(
            block(position, mine, p), own.at[position, p], own_sem.at[position, p]
        )

    def core_in(position, p):
        return over_dp(
            block(position, 1 - mine, p), core.at[position, p],
            core_send.at[position, p], core_recv.at[position, p], partner,
        )

    def rightward(step, p):
        return over_dp(
            own.at[lax.rem(plane + PLANES - step, PLANES), p], right.at[step - 1, p],
            right_send.at[step - 1, p], right_recv.at[step - 1, p], lax.rem(me + CORES, PLANES * CORES),
        )

    def leftward(step, p):
        return over_dp(
            own.at[lax.rem(plane + step, PLANES), p], left.at[step - 1, p],
            left_send.at[step - 1, p], left_recv.at[step - 1, p],
            lax.rem(me + (PLANES - 1) * CORES, PLANES * CORES),
        )

    order = (3, 0, 2, 1)
    for position in order:
        for p in range(pieces):
            own_in(position, p).start()

    barrier = pltpu.get_barrier_semaphore()
    pl.semaphore_signal(barrier, inc=1, device_id={"dp": partner}, device_id_type=MESH)
    for k in range(PLANES - 1):
        pl.semaphore_signal(
            barrier, inc=1, device_id={"dp": dp_at(planes_to[k])}, device_id_type=MESH
        )
    for k in range(n - 1):
        pl.semaphore_signal(barrier, inc=1, device_id={"tensor": peers[k]}, device_id_type=MESH)
    pl.semaphore_wait(barrier, 1 + PLANES - 1 + n - 1)

    by_core[mine] = jnp.sum(sums_ref[...], axis=1)
    over_dp(
        by_core.at[mine], by_core.at[mine], sum_send.at[0], sum_recv.at[0], partner
    ).start()
    for position in order:
        for p in range(pieces):
            core_in(position, p).start()
    over_dp(
        by_core.at[1 - mine], by_core.at[1 - mine], sum_send.at[0], sum_recv.at[0], partner
    ).wait_recv()
    by_plane[plane] = by_core[0] + by_core[1]

    def plane_sums(k, at):
        return over_dp(
            by_plane.at[at], by_plane.at[at], sum_send.at[1 + k], sum_recv.at[1 + k],
            dp_at(planes_to[k]),
        )

    def tensor_sums(k, at):
        at = by_tensor.at[at]
        return remote(at, at, sum_send.at[PLANES + k], sum_recv.at[PLANES + k], peers[k])

    for k in range(PLANES - 1):
        plane_sums(k, plane).start()

    def gather_pair(position):
        def piece(p):
            pltpu.make_async_copy(
                own.at[position, p], own.at[position, p], own_sem.at[position, p]
            ).wait()
            over_dp(
                core.at[position, p], core.at[position, p],
                core_send.at[position, p], core_recv.at[position, p], partner,
            ).wait_recv()
            add(own.at[position, p], core.at[position, p])

        loop(pieces, piece)

    def add(target, source):
        def part(r):
            rows = local_rows(r)
            target[rows, :] = (target[rows, :].astype(F32) + source[rows, :].astype(F32)).astype(BF16)

        loop(height // ROWS, part)

    def send_step(step):
        def piece(p):
            @pl.when(plane <= step - 1)
            def _():
                if step >= 2:

                    @pl.when(plane >= 1)
                    def _():
                        rightward(step - 1, p).wait_recv()
                        add(own.at[lax.rem(plane + PLANES - step, PLANES), p], right.at[step - 2, p])

                rightward(step, p).start()

            @pl.when(plane >= PLANES - step)
            def _():
                if step >= 2:

                    @pl.when(plane <= PLANES - 2)
                    def _():
                        leftward(step - 1, p).wait_recv()
                        add(own.at[lax.rem(plane + step, PLANES), p], left.at[step - 2, p])

                leftward(step, p).start()

        loop(pieces, piece)

    gather_pair(3)
    gather_pair(0)
    send_step(1)
    gather_pair(2)
    gather_pair(1)
    for k in range(PLANES - 1):
        plane_sums(k, planes_from[k]).wait_recv()
    by_tensor[here] = sum((by_plane[i] for i in range(1, PLANES)), by_plane[0])
    for k in range(n - 1):
        tensor_sums(k, here).start()
    for step in range(2, PLANES):
        send_step(step)
    for k in range(n - 1):
        tensor_sums(k, peer_source[k]).wait_recv()
    sums_out[...] = sum((by_tensor[i] for i in range(1, n)), by_tensor[0])

    for p, target in enumerate((q_out, k_out, v_out, o_out)):
        steps = PLANES - 2

        @pl.when(plane >= 1)
        def _():
            rightward(PLANES - 1, p).wait_recv()

        @pl.when(plane <= PLANES - 2)
        def _():
            leftward(PLANES - 1, p).wait_recv()

        total = own[plane, p].astype(F32)
        total += jnp.where(plane >= 1, right[steps, p].astype(F32), 0.0)
        total += jnp.where(plane <= PLANES - 2, left[steps, p].astype(F32), 0.0)
        target[...] = total if p < pieces - 1 else jnp.transpose(total)

    over_dp(by_core.at[mine], by_core.at[mine], sum_send.at[0], sum_recv.at[0], partner).wait_send()
    for k in range(PLANES - 1):
        plane_sums(k, plane).wait_send()
    for k in range(n - 1):
        tensor_sums(k, here).wait_send()
    for p in range(pieces):
        for position in range(PLANES):
            core_in(position, p).wait_send()
        for step in range(1, PLANES):

            @pl.when(plane <= step - 1)
            def _():
                rightward(step, p).wait_send()

            @pl.when(plane >= PLANES - step)
            def _():
                leftward(step, p).wait_send()


def on_device(
    n,
    replicas,
    streams,
    segments,
    positions,
    mix_in1,
    mix_res1,
    mix_out1,
    mix_in2,
    mix_res2,
    mix_out2,
    w_query,
    w_key,
    w_value,
    w_output,
    w_gate,
    w_up,
    w_down,
    cotangent,
):
    tokens, stream_count, width = streams.shape
    features = w_query.shape[0]
    units = w_gate.shape[1]
    chunks = tokens // CHUNK
    assert tokens == LENGTH == 4 * CHUNK and stream_count == 4
    any_spec = pl.BlockSpec(memory_space=pl.ANY)
    vmem = pl.BlockSpec(memory_space=pltpu.VMEM)
    smem = pl.BlockSpec(memory_space=pltpu.SMEM)

    def array(shape, dtype):
        return jax.ShapeDtypeStruct(shape, dtype)

    def dma(*shape):
        return pltpu.SemaphoreType.DMA(shape)

    def pair(lanes):
        return [dma(lanes, chunks), dma(lanes, chunks)]

    gather_sems = pair(4 if n == 4 else n - 1)
    scatter_sems = pair(6 if n == 4 else n - 1)
    stats_sems = pair(n - 1)

    def lasts(micros):
        return pl.CostEstimate(
            flops=int(micros * 1.0e9), bytes_accessed=int(micros * 3.6e6), transcendentals=0
        )

    def params(identity, mib):
        return pltpu.CompilerParams(
            collective_id=identity, has_side_effects=True, vmem_limit_bytes=mib * MIB
        )

    planes = jnp.transpose(streams, (1, 0, 2))
    mixes = (mix_in1, mix_out1, mix_in2, mix_out2, mix_res1, mix_res2)

    def stats_scratch():
        return [
            pltpu.VMEM((CHUNK, 128), F32),
            pltpu.VMEM((CHUNK, 128), F32),
            pltpu.VMEM((chunks, 16, CHUNK), F32),
            pltpu.VMEM((n - 1, chunks, 16, CHUNK), F32),
        ]

    (
        normed1, queries, keys, values, stand1, scale1, grad_branch2, cot_planes,
        cos_table, sin_table, seg_column, seg_row,
    ) = pl.pallas_call(
        functools.partial(project_kernel, n),
        name="project",
        cost_estimate=lasts(100),
        out_shape=[
            array((tokens, features), BF16),
            array((tokens, width), BF16),
            array((tokens, width), BF16),
            array((tokens, width), BF16),
            array((tokens, width), F32),
            array((tokens, 128), F32),
            array((tokens, features), BF16),
            array((stream_count, tokens, width), BF16),
            array((tokens, HEAD), F32),
            array((tokens, HEAD), F32),
            array((tokens, 128), F32),
            array((8, tokens), F32),
        ],
        in_specs=[smem, smem, vmem, vmem] + [any_spec] * 5,
        out_specs=[any_spec] + [vmem] * 5 + [any_spec] * 2 + [vmem] * 4,
        scratch_shapes=[
            pltpu.VMEM((stream_count, tokens, width), BF16),
            pltpu.VMEM((tokens, stream_count, width), BF16),
            pltpu.VMEM((stream_count, tokens, width), BF16),
            pltpu.VMEM((3, features, width), BF16),
            pltpu.VMEM((tokens, features), BF16),
            pltpu.VMEM((tokens, features), BF16),
        ]
        + stats_scratch()
        + [dma(2, chunks), dma(3), dma(3, chunks)]
        + gather_sems
        + gather_sems
        + stats_sems,
        compiler_params=params(0, 56),
    )(
        mix_in1, mix_out2,
        positions.reshape(tokens // 128, 128), segments.reshape(tokens // 128, 128),
        planes, cotangent, w_query, w_key, w_value,
    )

    extent = window(0, tokens)[1]
    attended, branch1, normed2, stand2, scale2, hidden, grad_acts, _ = pl.pallas_call(
        functools.partial(attend_kernel, n),
        name="attend",
        cost_estimate=lasts(100),
        out_shape=[
            array((tokens, width), BF16),
            array((tokens, width), F32),
            array((tokens, features), BF16),
            array((tokens, width), F32),
            array((tokens, 128), F32),
            array((tokens, units), BF16),
            array((tokens, 2 * units), BF16),
            array((tokens, units), BF16),
        ],
        in_specs=[smem] * 6 + [vmem] * 6 + [any_spec] * 5,
        out_specs=[vmem, vmem, any_spec, vmem, vmem, any_spec, any_spec, any_spec],
        scratch_shapes=[
            pltpu.VMEM((2, stream_count, CHUNK, width), BF16),
            pltpu.VMEM((2, CHUNK, features), BF16),
            pltpu.VMEM((features, units), BF16),
            pltpu.VMEM((features, units), BF16),
            pltpu.VMEM((units, features), BF16),
            pltpu.VMEM((2, CHUNK, units), BF16),
            pltpu.VMEM((2, CHUNK, units), BF16),
            pltpu.VMEM((2, CHUNK, units), BF16),
            pltpu.VMEM((tokens, features), BF16),
            pltpu.VMEM((n - 1, tokens, width), BF16),
            pltpu.VMEM((tokens, features), BF16),
        ]
        + stats_scratch()
        + [pltpu.VMEM((CHUNK, extent), F32), dma(2), dma(2), dma(2, 2)]
        + [dma(3), dma(chunks), dma(3, 2)]
        + scatter_sems
        + gather_sems
        + stats_sems,
        compiler_params=params(1, 62),
    )(
        *mixes, queries, keys, values, seg_column, seg_row, w_output, planes,
        grad_branch2, w_gate, w_up, w_down,
    )

    def over_dp(partial, dimension):
        return lax.psum_scatter(partial, "dp", scatter_dimension=dimension, tiled=True)

    height = features // replicas
    paired = replicas == PLANES * CORES

    def weight_sum(identity, left, right):
        if not paired:
            partial = contract_rows(left, right).astype(BF16)
            return over_dp(partial, 0), partial
        steps, columns_in = PLANES // 2, right.shape[1]
        pieces = max(columns_in // 1024, 1)
        partial = pl.pallas_call(
            pair_kernel,
            name="pair",
            cost_estimate=lasts(20),
            out_shape=array((features // CORES, columns_in), BF16),
            in_specs=[any_spec, any_spec],
            out_specs=any_spec,
            scratch_shapes=[
                pltpu.VMEM((PLANES, CORES, tokens, height), BF16),
                pltpu.VMEM((tokens, columns_in), BF16),
                pltpu.VMEM((2 * height, tokens), BF16),
                pltpu.VMEM((steps, 2 * height, columns_in), BF16),
                pltpu.VMEM((steps, 2 * height, columns_in), BF16),
                pltpu.VMEM((steps, 2 * height, columns_in), BF16),
                dma(PLANES, CORES),
                dma(pieces),
                dma(steps),
                dma(steps),
                dma(steps),
            ],
            compiler_params=params(identity, 56),
        )(left, right)
        groups = [[CORES * plane + c for plane in range(PLANES)] for c in range(CORES)]
        total = lax.psum_scatter(
            partial, "dp", scatter_dimension=0, tiled=True, axis_index_groups=groups
        )
        return total, partial

    grad_down, part_down = weight_sum(5, grad_branch2, hidden)
    part_gate_up = contract_rows(normed2, grad_acts).astype(BF16)
    grad_gate_up = over_dp(part_gate_up, 0)
    grad_w_down = pl.pallas_call(
        turn_kernel,
        name="turn",
        cost_estimate=lasts(2),
        out_shape=array((units, height), F32),
        in_specs=[vmem],
        out_specs=vmem,
        compiler_params=pltpu.CompilerParams(vmem_limit_bytes=32 * MIB),
    )(grad_down)
    grad_w_gate = grad_gate_up[:, :units].astype(F32)
    grad_w_up = grad_gate_up[:, units:].astype(F32)

    grad_entry2, grad_branch1 = pl.pallas_call(
        functools.partial(units_back_kernel, n),
        name="units_back",
        cost_estimate=lasts(400),
        out_shape=[array((tokens, width), F32), array((tokens, features), BF16)],
        in_specs=[smem] * 6 + [vmem] + [any_spec] * 8,
        out_specs=[vmem, any_spec],
        scratch_shapes=[
            pltpu.VMEM((tokens, 2 * units), BF16),
            pltpu.VMEM((features, units), BF16),
            pltpu.VMEM((features, units), BF16),
            pltpu.VMEM((tokens, features), BF16),
            pltpu.VMEM((tokens, width), F32),
            pltpu.VMEM((stream_count, tokens, width), BF16),
            pltpu.VMEM((CHUNK, features), F32),
            pltpu.VMEM((CHUNK, 128), F32),
            pltpu.VMEM((CHUNK, 128), F32),
            pltpu.VMEM((tokens, features), BF16),
            pltpu.VMEM((n - 1, tokens, width), BF16),
            pltpu.VMEM((chunks, 16, CHUNK), F32),
            pltpu.VMEM((n - 1, chunks, 16, CHUNK), F32),
            pltpu.VMEM((tokens, features), BF16),
            dma(chunks),
            dma(5),
            dma(chunks),
        ]
        + scatter_sems
        + stats_sems
        + gather_sems,
        compiler_params=params(2, 60),
    )(
        *mixes, scale2, grad_acts, w_gate, w_up, normed2, stand2, cot_planes,
        part_down, part_gate_up,
    )

    part_output = contract_rows(grad_branch1, attended).astype(BF16)

    grad_lin, branch2, grad_entry1 = pl.pallas_call(
        functools.partial(attend_back_kernel, n),
        name="attend_back",
        cost_estimate=lasts(2),
        out_shape=[array((tokens, 3 * width), BF16)] + [array((tokens, width), F32)] * 2,
        in_specs=[vmem] * 8 + [any_spec] * 11,
        out_specs=[vmem] * 3,
        scratch_shapes=[
            pltpu.VMEM((width, features), BF16),
            pltpu.VMEM((features, width), BF16),
            pltpu.VMEM((features, width), BF16),
            pltpu.VMEM((features, width), BF16),
            pltpu.VMEM((units, features), BF16),
            pltpu.VMEM((tokens, width), F32),
            pltpu.VMEM((2, CHUNK, features), BF16),
            pltpu.VMEM((2, CHUNK, units), BF16),
            pltpu.VMEM((2, CHUNK, features), BF16),
            pltpu.VMEM((CHUNK, extent), F32),
            pltpu.VMEM((width, tokens), F32),
            pltpu.VMEM((width, tokens), F32),
            pltpu.VMEM((CHUNK, features), F32),
            pltpu.VMEM((CHUNK, 128), F32),
            pltpu.VMEM((CHUNK, 128), F32),
            pltpu.VMEM((tokens, features), BF16),
            pltpu.VMEM((n - 1, tokens, width), BF16),
            pltpu.VMEM((tokens, features), BF16),
            pltpu.VMEM((n - 1, tokens, width), BF16),
            pltpu.VMEM((chunks, 16, CHUNK), F32),
            pltpu.VMEM((n - 1, chunks, 16, CHUNK), F32),
            dma(3, 2),
            dma(6),
        ]
        + scatter_sems
        + scatter_sems
        + stats_sems,
        compiler_params=params(3, 60),
    )(
        queries, keys, values, seg_column, seg_row, cos_table, sin_table, scale1,
        w_output, w_query, w_key, w_value, w_down, stand1,
        grad_branch1, hidden, normed1, part_output, grad_w_down,
    )

    part_lin = contract_rows(normed1, grad_lin).astype(BF16)

    rows = 128
    plane_spec = pl.BlockSpec((stream_count, rows, width), lambda t: (0, t, 0))
    field_spec = pl.BlockSpec((rows, width), lambda t: (t, 0))
    stream_spec = pl.BlockSpec((rows, stream_count, width), lambda t: (t, 0, 0))
    new_streams, stream_grad, sums = pl.pallas_call(
        streams_kernel,
        name="streams",
        cost_estimate=lasts(2),
        grid=(tokens // rows,),
        out_shape=[
            array(streams.shape, BF16),
            array(streams.shape, F32),
            array((SUMS, 8, 128), F32),
        ],
        in_specs=[smem] * 6 + [plane_spec, plane_spec] + [field_spec] * 4,
        out_specs=[
            stream_spec,
            stream_spec,
            pl.BlockSpec((SUMS, 8, 128), lambda t: (0, 0, 0)),
        ],
        scratch_shapes=[pltpu.VMEM((PRODUCTS, 8, 128), F32)],
        compiler_params=pltpu.CompilerParams(vmem_limit_bytes=48 * MIB),
    )(*mixes, planes, cot_planes, branch1, branch2, grad_entry1, grad_entry2)
    if paired:
        steps = PLANES - 1
        grad_w_query, grad_w_key, grad_w_value, grad_w_output, sums = pl.pallas_call(
            functools.partial(finish_kernel, n),
            name="finish",
            cost_estimate=lasts(2),
            out_shape=[array((height, width), F32)] * 3
            + [array((width, height), F32), array((SUMS, 128), F32)],
            in_specs=[any_spec, any_spec, vmem],
            out_specs=[vmem] * 5,
            scratch_shapes=[
                pltpu.VMEM((PLANES, 4, height, width), BF16),
                pltpu.VMEM((PLANES, 4, height, width), BF16),
                pltpu.VMEM((steps, 4, height, width), BF16),
                pltpu.VMEM((steps, 4, height, width), BF16),
                pltpu.VMEM((CORES, SUMS, 128), F32),
                pltpu.VMEM((PLANES, SUMS, 128), F32),
                pltpu.VMEM((n, SUMS, 128), F32),
                dma(PLANES, 4),
                dma(PLANES, 4),
                dma(PLANES, 4),
                dma(steps, 4),
                dma(steps, 4),
                dma(steps, 4),
                dma(steps, 4),
                dma(PLANES + n - 1),
                dma(PLANES + n - 1),
            ],
            compiler_params=params(4, 48),
        )(part_lin, part_output, sums)
        sums = jnp.sum(sums, axis=1)
    else:
        grad_w_query, grad_w_key, grad_w_value = (
            over_dp(part_lin[:, width * j : width * (j + 1)], 0).astype(F32) for j in range(3)
        )
        grad_w_output = jnp.transpose(over_dp(part_output, 0)).astype(F32)
        sums = lax.psum(jnp.sum(sums, axis=(1, 2)), ("dp", "tensor"))
    grad_mix_in1, grad_mix_res1 = sums[0:4], sums[4:20].reshape(4, 4)
    grad_mix_out1, grad_mix_in2 = sums[20:24], sums[24:28]
    grad_mix_res2, grad_mix_out2 = sums[28:44].reshape(4, 4), sums[44:48]
    return (
        new_streams,
        stream_grad,
        grad_w_query,
        grad_w_key,
        grad_w_value,
        grad_w_output,
        grad_w_gate,
        grad_w_up,
        grad_w_down,
        grad_mix_in1,
        grad_mix_res1,
        grad_mix_out1,
        grad_mix_in2,
        grad_mix_res2,
        grad_mix_out2,
    )


def solution(mesh):
    return jax.shard_map(
        functools.partial(on_device, mesh.shape["tensor"], mesh.shape["dp"]),
        mesh=mesh,
        in_specs=(
            P("dp", None, "tensor"),
            P("dp"),
            P("dp"),
            P(),
            P(),
            P(),
            P(),
            P(),
            P(),
            P(None, "tensor"),
            P(None, "tensor"),
            P(None, "tensor"),
            P("tensor", None),
            P(None, "tensor"),
            P(None, "tensor"),
            P("tensor", None),
            P("dp", None, "tensor"),
        ),
        out_specs=(
            P("dp", None, "tensor"),
            P("dp", None, "tensor"),
            P("dp", "tensor"),
            P("dp", "tensor"),
            P("dp", "tensor"),
            P("tensor", "dp"),
            P("dp", "tensor"),
            P("dp", "tensor"),
            P("tensor", "dp"),
            P(),
            P(),
            P(),
            P(),
            P(),
            P(),
        ),
        check_vma=False,
    )
```
